32 devices in a mesh: batch: 4 (over z), col: 8 (over y, x, core).
Axes of the slice: x: 2, y: 2, z: 4, core: 2. Of those that a mesh axis runs over, the one named last changes fastest.
Arguments:
- views: bfloat16 [2, 512, 4096], P(None, 'batch', 'col'), may hold values from -132 to 132
- norm_scale_gain: float32 [4096], P('col'), may hold values from 0.5 to 1.5
- norm_shift_bias: float32 [4096], P('col'), may hold values from -3 to 3
- weight: bfloat16 [4096, 8192], P(None, 'col'), may hold values from -0.09375 to 0.09375
Outputs:
- loss: float32 [], replicated
- grad_weight: float32 [4096, 8192], P('batch', 'col')
- grad_gain: float32 [4096], P('col')
- grad_bias: float32 [4096], P('col')
- views_gradient: float32 [2, 512, 4096], P(None, 'batch', 'col')
The draws below stay inside these ranges and needn't reach their ends.
All inputs are finite; a program needn't handle non-finite values.
Results may differ from the reference program's by a relative error of at most 0.0027.
Values may be sent and summed in bfloat16 or wider, within the bound.
No kernel may reach another device: no remote copies, remote signals or barrier semaphores. Data moves between devices by JAX's collectives and lax.ppermute only.
A program may use at most 64 MiB of HBM per device.

```python
import jax
import jax.numpy as jnp
from jax import lax

H = 4096
E = 8192
PAIRS = 512


def draw_views(key, part):
    keys = jax.random.split(key, 6)
    rank = jnp.arange(PAIRS, dtype=jnp.float32) / float(PAIRS - 1)
    row_noise = jax.random.uniform(keys[0], (2, PAIRS, 1), dtype=jnp.float32)
    row_scale = jnp.exp(jnp.log(3.0) * rank[None, :, None] + jnp.log(3.5) * row_noise)
    col_scale = 0.3 * jnp.exp(jnp.log(10.0) * jax.random.uniform(keys[1], (1, 1, H), dtype=jnp.float32))
    noise = jax.random.truncated_normal(keys[2], -4.0, 4.0, (2, PAIRS, H), dtype=jnp.float32)
    centre = jax.random.uniform(keys[5], (1, 1, H), dtype=jnp.float32, minval=-2.0, maxval=2.0)
    return (col_scale * (row_scale * noise + centre)).astype(jnp.bfloat16)


def shard_levels(own_key, dims, cuts, smallest, largest):
    gain = 1.0
    for position, parts in cuts:
        steps = jax.random.uniform(jax.random.fold_in(jax.random.fold_in(own_key, 6), position), (parts,), jnp.float32, smallest / len(cuts), largest / len(cuts))
        gain = gain * jnp.repeat(jnp.exp(steps), dims[position] // parts).reshape((-1,) + (1,) * (len(dims) - 1 - position))
    return gain


def bell_draw(own_key, dims, scale, most, cuts=(), kind=jnp.bfloat16):
    values = jax.random.normal(own_key, dims, jnp.float32) * scale
    if len(cuts) > 0:
        values = shard_levels(own_key, dims, cuts, -0.22, 0.18) * values
    return jnp.clip(values, min=-most, max=most).astype(kind)


def setup_inputs(seed: int = 0) -> dict:
    splits = jax.random.split(jax.random.key(seed), 5)
    views = draw_views(jax.random.fold_in(splits[4], 71), 0)
    norm_scale_gain = jnp.clip(1.0 + 0.1 * jax.random.normal(splits[1], (H,), jnp.float32), 0.5, 1.5)
    norm_shift_bias = bell_draw(splits[2], (H,), 0.5, 3.0, ((0, 8),), jnp.float32)
    weight = bell_draw(splits[3], (H, E), H ** -0.5, 0.09375, ((1, 8),))
    return dict(views=views, norm_scale_gain=norm_scale_gain, norm_shift_bias=norm_shift_bias, weight=weight)


eps_norm = 1e-05
eps_std = 0.0001

def gelu_slope(preactivation):
    value, pullback = jax.vjp(lambda t: jax.nn.gelu(t, approximate=True), preactivation)
    return pullback(jnp.ones_like(value))[0]

def reference(views, norm_scale_gain, norm_shift_bias, weight):
    sample_count = PAIRS
    scale = PAIRS * E / 128.0
    hidden_float = views.astype(jnp.float32)
    batch_average = lax.optimization_barrier(jnp.mean(hidden_float, axis=1, keepdims=True))
    var = lax.optimization_barrier(jnp.mean((hidden_float - batch_average) * (hidden_float - batch_average), axis=1, keepdims=True))
    inverse_deviation = 1.0 / jnp.sqrt(var + eps_norm)
    normalised_input = (hidden_float - batch_average) * inverse_deviation
    preactivation = norm_scale_gain * normalised_input + norm_shift_bias
    act = jax.nn.gelu(preactivation, approximate=True).astype(jnp.bfloat16)
    z = jnp.stack([jnp.dot(act[v], weight, preferred_element_type=jnp.float32) for v in range(2)]).astype(jnp.bfloat16)
    zf = z.astype(jnp.float32)
    zmean = lax.optimization_barrier(jnp.mean(zf, axis=1, keepdims=True))
    zc = zf - zmean
    zvar = lax.optimization_barrier(jnp.sum(zc * zc, axis=1, keepdims=True)) / (sample_count - 1)
    std = jnp.sqrt(zvar + eps_std)
    zcb = zc.astype(jnp.bfloat16)
    diff = zf[0] - zf[1]
    invariance = jnp.sum(diff * diff) / (sample_count * E)
    hinge = jnp.sum(jnp.maximum(1.0 - std, 0.0)) / (2 * E)
    denom = float((sample_count - 1) ** 2 * E)
    coef = 4.0 * scale / denom
    hinge_coef = 25.0 * scale / (2.0 * E * (sample_count - 1))
    loss_cov = jnp.float32(0.0)
    grads = []
    for v in range(2):
        kernel = jnp.dot(zcb[v], zcb[v].T, preferred_element_type=jnp.float32)
        diag = lax.optimization_barrier(jnp.sum(jnp.square(zcb[v].astype(jnp.float32)), axis=0, keepdims=True))
        loss_cov = loss_cov + (jnp.sum(kernel * kernel) - jnp.sum(diag * diag)) / denom
        moved = jnp.dot(kernel.astype(jnp.bfloat16), zcb[v], preferred_element_type=jnp.float32)
        g_cov = coef * (moved - zcb[v].astype(jnp.float32) * diag)
        mask = jnp.where(std[v] < 1.0, 1.0, 0.0)
        g_var = -hinge_coef * mask * zc[v] / std[v]
        summed = g_cov + g_var
        grads.append(summed - lax.optimization_barrier(jnp.mean(summed, axis=0, keepdims=True)))
    g_inv = 50.0 * scale / (sample_count * E) * diff
    dz = (jnp.stack(grads) + jnp.stack([g_inv, -g_inv])).astype(jnp.bfloat16)
    loss = 25.0 * invariance + 25.0 * hinge + loss_cov
    act_flat = act.reshape(2 * sample_count, H)
    dz_flat = dz.reshape(2 * sample_count, E)
    grad_weight = jnp.dot(act_flat.T, dz_flat, preferred_element_type=jnp.float32)
    d_act = jnp.dot(dz_flat, weight.T, preferred_element_type=jnp.float32).reshape(2, sample_count, H)
    preactivation_gradient = d_act * gelu_slope(preactivation)
    bias_gradient_sum = lax.optimization_barrier(jnp.sum(preactivation_gradient, axis=1, keepdims=True))
    gain_gradient_sum = lax.optimization_barrier(jnp.sum(preactivation_gradient * normalised_input, axis=1, keepdims=True))
    grad_bias = lax.optimization_barrier(jnp.sum(bias_gradient_sum, axis=(0, 1)))
    grad_gain = lax.optimization_barrier(jnp.sum(gain_gradient_sum, axis=(0, 1)))
    views_gradient = norm_scale_gain * (preactivation_gradient - bias_gradient_sum / sample_count - normalised_input * gain_gradient_sum / sample_count) * inverse_deviation
    return (loss, grad_weight, grad_gain, grad_bias, views_gradient)
```

```python
import jax
import jax.numpy as jnp
from jax import lax
from jax.sharding import PartitionSpec as P

eps_norm = 1e-05
eps_std = 0.0001
f32 = jnp.float32
bf16 = jnp.bfloat16


def gelu_slope(preactivation):
    value, pullback = jax.vjp(lambda t: jax.nn.gelu(t, approximate=True), preactivation)
    return pullback(jnp.ones_like(value))[0]


def xor_send(x, axis, k):
    n = lax.axis_size(axis)
    return lax.ppermute(x, axis, [(i, i ^ k) for i in range(n)])


def low_bit(k):
    return k & -k


def high_bit(k):
    return 1 << (k.bit_length() - 1)


def ring_order(n):
    return list(range(0, n, 2)) + list(range(1, n, 2))[::-1]


def ring_send(x, axis):
    order = ring_order(lax.axis_size(axis))
    n = len(order)
    return lax.ppermute(x, axis, [(order[i], order[(i + 1) % n]) for i in range(n)])


def exchange(x, axis):
    n = lax.axis_size(axis)
    me = lax.axis_index(axis)
    slots = [x]
    for d in range(1, n):
        slots.append(lax.ppermute(x, axis, [(i, (i + d) % n) for i in range(n)]))
    ordered = []
    for a in range(n):
        value = slots[0]
        for d in range(1, n):
            value = jnp.where((me - a) % n == d, slots[d], value)
        ordered.append(value)
    return ordered


def gather_pieces(x, axis):
    n = lax.axis_size(axis)
    pieces = {0: x}
    half = x.shape[0] // 2
    for k in sorted(range(2, n, 2), key=lambda k: (bin(k).count("1"), k)):
        lo, hi = low_bit(k), high_bit(k)
        if lo == hi:
            pieces[k] = xor_send(x, axis, k)
        else:
            first = xor_send(pieces[k ^ lo][:half], axis, lo)
            second = xor_send(pieces[k ^ hi][half:], axis, hi)
            pieces[k] = jnp.concatenate([first, second])
    for k in range(0, n, 2):
        pieces[k + 1] = xor_send(pieces[k], axis, 1)
    return [pieces[k] for k in range(n)]


def scatter_pieces(parts, axis, wire):
    n = lax.axis_size(axis)
    total = []
    for k in range(0, n, 2):
        got = xor_send(parts[k + 1].astype(wire), axis, 1)
        total.append(parts[k] + got.astype(f32))
    result = total[0]
    for k in range(2, n, 2):
        result = result + xor_send(total[k // 2].astype(wire), axis, k).astype(f32)
    return result


def shards(views, norm_scale_gain, norm_shift_bias, weight):
    n_batch = lax.axis_size("batch")
    n_col = lax.axis_size("col")
    b = lax.axis_index("batch")
    c = lax.axis_index("col")
    n_view, local_rows, width = views.shape
    columns = weight.shape[1]
    E = columns * n_col
    rows = local_rows * n_batch
    scale = rows * E / 128.0
    with jax.named_scope("norm_stats"):
        hidden = views.astype(f32)
        local_mean = jnp.mean(hidden, axis=1)
        local_centred = hidden - local_mean[:, None, :]
        local_spread = jnp.sum(local_centred * local_centred, axis=1)
        stats = exchange(jnp.concatenate([local_mean, local_spread]), "batch")
        mean = sum(s[:n_view] for s in stats) / n_batch
        spread = sum(s[n_view:] + local_rows * jnp.square(s[:n_view] - mean) for s in stats)
        var = spread / rows
        inverse_deviation = (1.0 / jnp.sqrt(var + eps_norm))[:, None, :]
        normalised = (hidden - mean[:, None, :]) * inverse_deviation
        preactivation = norm_scale_gain * normalised + norm_shift_bias
        act = jax.nn.gelu(preactivation, approximate=True).astype(bf16)
    with jax.named_scope("weight_order"):
        blocks = weight.reshape(n_col, width, columns)
        weight_xor = jnp.concatenate(
            [lax.dynamic_index_in_dim(blocks, c ^ k, 0, keepdims=True) for k in range(n_col)]
        ).reshape(n_col * width, columns)
    with jax.named_scope("act_gather"):
        slots = [act]
        for _ in range(1, n_batch):
            slots.append(ring_send(slots[-1], "batch"))
        pieces = [gather_pieces(s, "col") for s in slots]
    with jax.named_scope("z"):
        acts = [jnp.concatenate(p, axis=2) for p in pieces]
        z = jnp.concatenate(
            [
                jnp.einsum("vrk,kj->vrj", a, weight_xor, preferred_element_type=f32).astype(bf16)
                for a in acts
            ],
            axis=1,
        )
    with jax.named_scope("z_stats"):
        zf = z.astype(f32)
        zc = zf - jnp.mean(zf, axis=1, keepdims=True)
        zvar = jnp.sum(zc * zc, axis=1, keepdims=True) / (rows - 1)
        std = jnp.sqrt(zvar + eps_std)
        zcb = zc.astype(bf16)
        diag = jnp.sum(jnp.square(zcb.astype(f32)), axis=1, keepdims=True)
    with jax.named_scope("kernel"):
        kernel_part = jnp.einsum("vrj,vmj->vrm", zcb, zcb, preferred_element_type=f32)
        strip = rows // n_col
        parts = [
            lax.dynamic_slice_in_dim(kernel_part, (c ^ k) * strip, strip, 1) for k in range(n_col)
        ]
        kernel = scatter_pieces(parts, "col", f32)
        kernel_b = jnp.zeros((n_view, rows, rows), bf16)
        for k, piece in enumerate(gather_pieces(kernel.astype(bf16), "col")):
            kernel_b = lax.dynamic_update_slice_in_dim(kernel_b, piece, (c ^ k) * strip, 1)
    denom = float((rows - 1) ** 2 * E)
    coef = 4.0 * scale / denom
    hinge_coef = 25.0 * scale / (2.0 * E * (rows - 1))
    with jax.named_scope("dz"):
        mask = jnp.where(std < 1.0, 1.0, 0.0)
        moved = jnp.einsum("vrm,vmj->vrj", kernel_b, zcb, preferred_element_type=f32)
        summed = coef * (moved - zcb.astype(f32) * diag) - hinge_coef * mask * zc / std
        diff = zf[0] - zf[1]
        g_inv = 50.0 * scale / (rows * E) * diff
        dz = summed - jnp.mean(summed, axis=1, keepdims=True) + jnp.stack([g_inv, -g_inv])
        dzb = dz.astype(bf16)
    with jax.named_scope("loss"):
        inv_share = jnp.sum(diff * diff) / (rows * E)
        hinge_share = jnp.sum(jnp.maximum(1.0 - std, 0.0)) / (2 * E)
        block_share = jnp.sum(kernel * kernel) / denom
        diag_share = jnp.sum(diag * diag) / denom
        share = 25.0 * inv_share + 25.0 * hinge_share - diag_share + block_share
        share = jnp.broadcast_to(share, (8, 128))
        for axis, n in (("col", n_col), ("batch", n_batch)):
            k = 1
            while k < n:
                share = share + xor_send(share, axis, k)
                k *= 2
        loss = share[0, 0] / n_batch
    with jax.named_scope("d_act"):
        d_parts = [
            jnp.einsum(
                "vrj,kj->vrk",
                dzb[:, :local_rows],
                weight_xor[k * width : (k + 1) * width],
                preferred_element_type=f32,
            )
            for k in range(n_col)
        ]
        d_act = scatter_pieces(d_parts, "col", bf16)
    with jax.named_scope("grad_weight"):
        share_pieces = n_col // n_batch
        wanted = jnp.concatenate(
            [
                jnp.concatenate(
                    [
                        lax.dynamic_slice_in_dim(
                            a, (c ^ (b * share_pieces + i)) * width, width, 2
                        )
                        for i in range(share_pieces)
                    ],
                    axis=2,
                )
                for a in acts
            ],
            axis=1,
        )
        grad_weight = jnp.einsum("vnk,vnj->kj", wanted, dzb, preferred_element_type=f32)
    with jax.named_scope("norm_backward"):
        d_pre = d_act * gelu_slope(preactivation)
        sums = jnp.concatenate(
            [
                jnp.sum(d_pre, axis=1),
                jnp.sum(d_pre * normalised, axis=1),
            ]
        )
        everyone = exchange(sums, "batch")
        both = sum(everyone)
        sum_b, sum_g = both[:n_view], both[n_view : 2 * n_view]
        grad_bias = jnp.sum(sum_b, axis=0)
        grad_gain = jnp.sum(sum_g, axis=0)
        views_gradient = (
            norm_scale_gain
            * (d_pre - sum_b[:, None, :] / rows - normalised * sum_g[:, None, :] / rows)
            * inverse_deviation
        )
    return (loss, grad_weight, grad_gain, grad_bias, views_gradient)


def solution(mesh):
    placed = (P(None, "batch", "col"), P("col"), P("col"), P(None, "col"))
    return jax.shard_map(
        shards,
        mesh=mesh,
        in_specs=placed,
        out_specs=(P(), P("batch", "col"), P("col"), P("col"), P(None, "batch", "col")),
        check_vma=False,
    )
```

```python
import functools

import jax
import jax.numpy as jnp
from jax import lax
from jax.experimental import pallas as pl
from jax.experimental.pallas import tpu as pltpu
from jax.sharding import PartitionSpec as P

eps_norm = 1e-05
eps_std = 0.0001
f32 = jnp.float32
bf16 = jnp.bfloat16
VMEM_LIMIT = 40 * 1024 * 1024


def gelu_slope(preactivation):
    value, pullback = jax.vjp(lambda t: jax.nn.gelu(t, approximate=True), preactivation)
    return pullback(jnp.ones_like(value))[0]


def xor_send(x, axis, k):
    n = lax.axis_size(axis)
    return lax.ppermute(x, axis, [(i, i ^ k) for i in range(n)])


def ring_order(n):
    return list(range(0, n, 2)) + list(range(1, n, 2))[::-1]


def ring_send(x, axis, d):
    order = ring_order(lax.axis_size(axis))
    n = len(order)
    return lax.ppermute(x, axis, [(order[i], order[(i + d) % n]) for i in range(n)])


def exchange(x, axis):
    n = lax.axis_size(axis)
    me = lax.axis_index(axis)
    slots = [x]
    for d in range(1, n):
        slots.append(lax.ppermute(x, axis, [(i, (i + d) % n) for i in range(n)]))
    ordered = []
    for a in range(n):
        value = slots[0]
        for d in range(1, n):
            value = jnp.where((me - a) % n == d, slots[d], value)
        ordered.append(value)
    return ordered


def params():
    return pltpu.CompilerParams(vmem_limit_bytes=VMEM_LIMIT)


def cost(flops, moved):
    return pl.CostEstimate(flops=flops, bytes_accessed=moved, transcendentals=0)


def whole(shape):
    return pl.BlockSpec(shape, lambda i, index: (0,) * len(shape))


def z_kernel(count, first, last, index_ref, *refs):
    pieces, rest = refs[:count], list(refs[count:])
    w_ref = rest.pop(0)
    before = None if first else rest.pop(0)
    i = pl.program_id(0)
    if last:
        z_ref, sum_ref, total = rest
    else:
        (total,) = rest

    for j in range(count):

        @pl.when(i == j)
        def _():
            part = jnp.dot(pieces[j][...], w_ref[0], preferred_element_type=f32)
            if j > 0:
                total[...] += part
            elif first:
                total[...] = part
            else:
                total[...] = before[...] + part

    if last:

        @pl.when(i == count - 1)
        def _():
            z = total[...].astype(bf16)
            z_ref[...] = z
            zf = z.astype(f32)
            half = zf.shape[0] // 2
            sum_ref[0:1, :] = jnp.sum(zf[:half], axis=0, keepdims=True)
            sum_ref[1:2, :] = jnp.sum(zf[half:], axis=0, keepdims=True)


def z_call(index, pieces, blocks, before, last):
    count = len(pieces)
    rows, width = pieces[0].shape
    columns = blocks.shape[2]
    in_specs = [whole((rows, width)) for _ in pieces]
    in_specs.append(pl.BlockSpec((1, width, columns), lambda i, index: (index[i], 0, 0)))
    operands = list(pieces) + [blocks]
    if before is not None:
        in_specs.append(whole((rows, columns)))
        operands.append(before)
    scratch = []
    if last:
        out_shape = (
            jax.ShapeDtypeStruct((rows, columns), bf16),
            jax.ShapeDtypeStruct((2, columns), f32),
        )
        out_specs = (whole((rows, columns)), whole((2, columns)))
        scratch = [pltpu.VMEM((rows, columns), f32)]
    else:
        out_shape = jax.ShapeDtypeStruct((rows, columns), f32)
        out_specs = whole((rows, columns))
    return pl.pallas_call(
        functools.partial(z_kernel, count, before is None, last),
        out_shape=out_shape,
        grid_spec=pltpu.PrefetchScalarGridSpec(
            num_scalar_prefetch=1,
            grid=(count,),
            in_specs=in_specs,
            out_specs=out_specs,
            scratch_shapes=scratch,
        ),
        compiler_params=params(),
        cost_estimate=cost(
            2 * rows * width * columns * count, 2 * count * width * (columns + rows)
        ),
        name="z_matmul",
    )(index, *operands)


def strip_kernel(n_slots, n_sums, rows, n_col, index_ref, *refs):
    z_refs, sum_refs = refs[:n_slots], refs[n_slots : n_slots + n_sums]
    even_ref, odd_ref, strip = refs[n_slots + n_sums :]
    local_rows = z_refs[0].shape[0] // 2
    mean = sum(s[...] for s in sum_refs) / rows
    for v in range(2):
        here = pl.ds(v * local_rows, local_rows)
        rounded = [(z[here, :].astype(f32) - mean[v : v + 1]).astype(bf16) for z in z_refs]
        for u in range(n_slots):
            strip[here, pl.ds(u * local_rows, local_rows)] = lax.dot_general(
                rounded[0], rounded[u], (((1,), (1,)), ((), ())), preferred_element_type=f32
            )
    part = 2 * local_rows // n_col
    for k in range(n_col):
        start = pl.multiple_of(index_ref[k] * part, part)
        (odd_ref if k % 2 else even_ref)[k // 2] = strip[pl.ds(start, part), :]


def strip_call(index, z_slots, sums, rows, n_col):
    tall, columns = z_slots[0].shape
    wide = len(z_slots) * tall // 2
    part = jax.ShapeDtypeStruct((n_col // 2, tall // n_col, wide), f32)
    specs = [whole((tall, columns)) for _ in z_slots] + [whole((2, columns)) for _ in sums]
    return pl.pallas_call(
        functools.partial(strip_kernel, len(z_slots), len(sums), rows, n_col),
        out_shape=(part, part),
        grid_spec=pltpu.PrefetchScalarGridSpec(
            num_scalar_prefetch=1,
            grid=(1,),
            in_specs=specs,
            out_specs=(whole(part.shape), whole(part.shape)),
            scratch_shapes=[pltpu.VMEM((tall, wide), f32)],
        ),
        compiler_params=params(),
        cost_estimate=cost(2 * tall * wide * columns, 2 * tall * columns * len(z_slots)),
        name="kernel_strip",
    )(index, *z_slots, *sums)


def dz_kernel(n_batch, n_col, coef, hinge_coef, inv_coef, inv_share, hinge_share, diag_share, index_ref, *refs):
    strip_refs = refs[:n_col]
    z_refs = refs[n_col : n_col + n_batch]
    dz_ref, share_ref, strips, full, centred = refs[n_col + n_batch :]
    local_rows = z_refs[0].shape[0] // 2
    rows = local_rows * n_batch
    reach = n_batch // 2

    @pl.when(pl.program_id(0) == 0)
    def _():
        share_ref[...] = jnp.zeros_like(share_ref)
        part = 2 * local_rows // n_col
        for k in range(n_col):
            start = pl.multiple_of(index_ref[k] * part, part)
            for s in range(n_batch):
                strips[s, pl.ds(start, part), :] = strip_refs[k][s].astype(f32)
        for v in range(2):
            for s in range(n_batch):
                for u in range(reach + 1):
                    t = (s + u) % n_batch
                    block = strips[s, pl.ds(v * local_rows, local_rows), pl.ds(u * local_rows, local_rows)]
                    full[v, pl.ds(s * local_rows, local_rows), pl.ds(t * local_rows, local_rows)] = block.astype(bf16)
                    if 0 < u < n_batch - reach:
                        full[v, pl.ds(t * local_rows, local_rows), pl.ds(s * local_rows, local_rows)] = jnp.transpose(block).astype(bf16)

    share = jnp.zeros((1, 1), f32)
    grads = []
    z_views = []
    for v in range(2):
        zf = jnp.concatenate(
            [z[pl.ds(v * local_rows, local_rows), :].astype(f32) for z in z_refs], axis=0
        )
        z_views.append(zf)
        zc = zf - jnp.sum(zf, axis=0, keepdims=True) / rows
        std = jnp.sqrt(jnp.sum(zc * zc, axis=0, keepdims=True) / (rows - 1) + eps_std)
        zcb = zc.astype(bf16)
        centred[...] = zcb
        rounded = zcb.astype(f32)
        diag = jnp.sum(rounded * rounded, axis=0, keepdims=True)
        moved = jnp.dot(full[v], centred[...], preferred_element_type=f32)
        pull = jnp.where(std < 1.0, hinge_coef, 0.0) / std
        summed = coef * (moved - rounded * diag) - zc * pull
        grads.append(summed - jnp.sum(summed, axis=0, keepdims=True) / rows)
        share += hinge_share * jnp.sum(jnp.maximum(1.0 - std, 0.0), axis=1, keepdims=True)
        share -= diag_share * jnp.sum(diag * diag, axis=1, keepdims=True)
    diff = z_views[0] - z_views[1]
    share += inv_share * jnp.sum(jnp.sum(diff * diff, axis=0, keepdims=True), axis=1, keepdims=True)
    share_ref[...] += jnp.broadcast_to(share, share_ref.shape)
    dz_ref[0] = (grads[0] + inv_coef * diff).astype(bf16)
    dz_ref[1] = (grads[1] - inv_coef * diff).astype(bf16)


def dz_call(index, strips, z_slots, constants):
    n_col, n_batch = len(strips), len(z_slots)
    tall, columns = z_slots[0].shape
    rows = tall // 2 * n_batch
    tile = min(256, columns)
    part = strips[0].shape
    return pl.pallas_call(
        functools.partial(dz_kernel, n_batch, n_col, *constants),
        out_shape=(
            jax.ShapeDtypeStruct((2, rows, columns), bf16),
            jax.ShapeDtypeStruct((8, 128), f32),
        ),
        grid_spec=pltpu.PrefetchScalarGridSpec(
            num_scalar_prefetch=1,
            grid=(columns // tile,),
            in_specs=[whole(part) for _ in strips]
            + [pl.BlockSpec((tall, tile), lambda j, index: (0, j)) for _ in z_slots],
            out_specs=(
                pl.BlockSpec((2, rows, tile), lambda j, index: (0, 0, j)),
                whole((8, 128)),
            ),
            scratch_shapes=[
                pltpu.VMEM((n_batch, tall, part[2]), f32),
                pltpu.VMEM((2, rows, rows), bf16),
                pltpu.VMEM((rows, tile), bf16),
            ],
        ),
        compiler_params=params(),
        cost_estimate=cost(4 * rows * rows * columns, 8 * rows * columns),
        name="embedding_gradient",
    )(index, *strips, *z_slots)


def d_act_kernel(count, adds, index_ref, dz_ref, w_ref, *refs):
    i = pl.program_id(0)
    outs = refs[1:] if adds else refs
    two, local_rows, columns = dz_ref.shape
    dz = dz_ref[...].reshape(two * local_rows, columns)
    part = lax.dot_general(dz, w_ref[0], (((1,), (1,)), ((), ())), preferred_element_type=f32)
    if adds:
        part = part + refs[0][0].astype(f32)
    for j in range(count):

        @pl.when(i == j)
        def _():
            outs[j][...] = part.astype(outs[j].dtype)


def d_act_call(index, dz, blocks, local_rows, ks, got, kind):
    count = len(ks)
    _, width, columns = blocks.shape
    tall = 2 * local_rows
    in_specs = [
        pl.BlockSpec((2, local_rows, columns), lambda i, index: (0, 0, 0)),
        pl.BlockSpec((1, width, columns), lambda i, index: (index[i], 0, 0)),
    ]
    operands = [dz, blocks]
    if got is not None:
        first = ks[0] // 2
        in_specs.append(pl.BlockSpec((1, tall, width), lambda i, index: (first + i, 0, 0)))
        operands.append(got)
    if got is None:
        out_shape = (jax.ShapeDtypeStruct((count, tall, width), kind),)
        out_specs = (pl.BlockSpec((1, tall, width), lambda i, index: (i, 0, 0)),)
    else:
        out_shape = tuple(jax.ShapeDtypeStruct((tall, width), kind) for _ in ks)
        out_specs = tuple(whole((tall, width)) for _ in ks)

    def body(index_ref, dz_ref, w_ref, *refs):
        if got is None:
            d_act_kernel(1, False, index_ref, dz_ref, w_ref, *refs)
        else:
            d_act_kernel(count, True, index_ref, dz_ref, w_ref, *refs)

    def body_stacked(index_ref, dz_ref, w_ref, out_ref):
        two, r, n = dz_ref.shape
        part = lax.dot_general(
            dz_ref[...].reshape(two * r, n), w_ref[0], (((1,), (1,)), ((), ())), preferred_element_type=f32
        )
        out_ref[0] = part.astype(out_ref.dtype)

    return pl.pallas_call(
        body_stacked if got is None else body,
        out_shape=out_shape,
        grid_spec=pltpu.PrefetchScalarGridSpec(
            num_scalar_prefetch=1, grid=(count,), in_specs=in_specs, out_specs=out_specs
        ),
        compiler_params=params(),
        cost_estimate=cost(2 * tall * width * columns * count, 2 * count * width * (columns + tall)),
        name="d_act_matmul",
    )(index, *operands)


def weight_grad_kernel(act_ref, dz_ref, out_ref):
    out_ref[...] = lax.dot_general(
        act_ref[...], dz_ref[...], (((0,), (0,)), ((), ())), preferred_element_type=f32
    )


def weight_grad_call(act, dz):
    rows, features = act.shape
    columns = dz.shape[1]
    tile = min(256, features)
    return pl.pallas_call(
        weight_grad_kernel,
        out_shape=jax.ShapeDtypeStruct((features, columns), f32),
        grid=(features // tile,),
        in_specs=[
            pl.BlockSpec((rows, tile), lambda i: (0, i)),
            pl.BlockSpec((rows, columns), lambda i: (0, 0)),
        ],
        out_specs=pl.BlockSpec((tile, columns), lambda i: (i, 0)),
        compiler_params=params(),
        cost_estimate=cost(2 * rows * features * columns, 4 * features * columns),
        name="weight_gradient",
    )(act, dz)


def shards(views, norm_scale_gain, norm_shift_bias, weight):
    n_batch = lax.axis_size("batch")
    n_col = lax.axis_size("col")
    b = lax.axis_index("batch")
    c = lax.axis_index("col")
    n_view, local_rows, width = views.shape
    columns = weight.shape[1]
    E = columns * n_col
    rows = local_rows * n_batch
    tall = n_view * local_rows
    scale = rows * E / 128.0
    denom = float((rows - 1) ** 2 * E)
    evens = list(range(0, n_col, 2))
    far = evens[1:]
    blocks = weight.reshape(n_col, width, columns)

    def places(ks):
        return jnp.stack([c ^ k for k in ks]).astype(jnp.int32)

    with jax.named_scope("norm_stats"):
        hidden = views.astype(f32)
        local_mean = jnp.mean(hidden, axis=1)
        local_centred = hidden - local_mean[:, None, :]
        local_spread = jnp.sum(local_centred * local_centred, axis=1)
        stats = exchange(jnp.concatenate([local_mean, local_spread]), "batch")
        mean = sum(s[:n_view] for s in stats) / n_batch
        spread = sum(s[n_view:] + local_rows * jnp.square(s[:n_view] - mean) for s in stats)
        var = spread / rows
        inverse_deviation = (1.0 / jnp.sqrt(var + eps_norm))[:, None, :]
        normalised = (hidden - mean[:, None, :]) * inverse_deviation
        preactivation = norm_scale_gain * normalised + norm_shift_bias
        act = jax.nn.gelu(preactivation, approximate=True).astype(bf16)
    with jax.named_scope("act_gather"):
        pieces = {0: act.reshape(tall, width)}
        for k in far:
            pieces[k] = xor_send(pieces[0], "col", k)
        for k in evens:
            pieces[k + 1] = xor_send(pieces[k], "col", 1)
    with jax.named_scope("z"):
        z = z_call(places([0, 1]), [pieces[0], pieces[1]], blocks, None, False)
        z = z_call(places(far), [pieces[k] for k in far], blocks, z, False)
        odd = [k + 1 for k in far]
        z, z_sum = z_call(places(odd), [pieces[k] for k in odd], blocks, z, True)
    with jax.named_scope("z_ring"):
        sums = [z_sum] + [ring_send(z_sum, "batch", d) for d in range(1, n_batch)]
        slots = [z]
        for _ in range(1, n_batch):
            slots.append(ring_send(slots[-1], "batch", 1))
    with jax.named_scope("kernel"):
        reach = n_batch // 2
        everyone = places(range(n_col))
        even_part, odd_part = strip_call(everyone, slots[: reach + 1], sums, rows, n_col)
        even_part = even_part + xor_send(odd_part, "col", 1)
        strip = even_part[0]
        for k in far:
            strip = strip + xor_send(even_part[k // 2], "col", k)
        block = lax.broadcasted_iota(jnp.int32, (1, strip.shape[1]), 1) // local_rows
        twice = jnp.where((block > 0) & (block < n_batch - reach), 2.0, 1.0)
        block_share = jnp.sum(strip * strip * twice) / denom
        mine = strip.astype(bf16)
        mine = jnp.stack([mine] + [ring_send(mine, "batch", d) for d in range(1, n_batch)])
        strips = {0: mine}
        for k in far:
            strips[k] = xor_send(mine, "col", k)
        for k in evens:
            strips[k + 1] = xor_send(strips[k], "col", 1)
    with jax.named_scope("dz"):
        constants = (
            4.0 * scale / denom,
            25.0 * scale / (2.0 * E * (rows - 1)),
            50.0 * scale / (rows * E),
            25.0 / (rows * E) / n_batch,
            25.0 / (2 * E) / n_batch,
            1.0 / denom / n_batch,
        )
        dz, share = dz_call(everyone, [strips[k] for k in range(n_col)], slots, constants)
    with jax.named_scope("d_act"):
        odds = [k + 1 for k in evens]
        (away,) = d_act_call(places(odds), dz, blocks, local_rows, odds, None, bf16)
        got = xor_send(away, "col", 1)
        sends = d_act_call(places(far), dz, blocks, local_rows, far, got, bf16)
        arrived = [xor_send(part, "col", k) for k, part in zip(far, sends)]
        (d_act,) = d_act_call(places([0]), dz, blocks, local_rows, [0], got, f32)
    with jax.named_scope("grad_weight"):
        per_plane = n_col // n_batch
        order = jnp.array(ring_order(n_batch), jnp.int32)
        position = jnp.where(b % 2 == 0, b // 2, n_batch - 1 - b // 2)
        stacked = jnp.stack([pieces[k] for k in evens])

        def held(plane, i):
            k = (per_plane * plane + 2 * i) ^ (c - c % 2)
            return lax.dynamic_index_in_dim(stacked, k // 2, 0, keepdims=False)

        halves = []
        for i in range(per_plane // 2):
            own = [held(b, i)]
            for d in range(1, n_batch):
                ahead = (position + d) % n_batch
                plane = jnp.where(ahead < (n_batch + 1) // 2, 2 * ahead, 2 * (n_batch - ahead) - 1)
                own.append(ring_send(held(plane, i), "batch", d))
            own = jnp.concatenate([o.reshape(n_view, local_rows, width) for o in own], axis=1)
            other = xor_send(own, "col", 1)
            halves.append(jnp.where(c % 2 == 0, own, other))
            halves.append(jnp.where(c % 2 == 0, other, own))
        wanted = jnp.concatenate(halves, axis=2).reshape(n_view * rows, per_plane * width)
        grad_weight = weight_grad_call(wanted, dz.reshape(n_view * rows, columns))
    with jax.named_scope("loss"):
        share = share + block_share
        k = 1
        while k < n_col:
            share = share + xor_send(share, "col", k)
            k *= 2
    with jax.named_scope("norm_backward"):
        arrived, d_act, grad_weight = lax.optimization_barrier((arrived, d_act, grad_weight))
        for part in arrived:
            d_act = d_act + part.astype(f32)
        d_pre = d_act.reshape(n_view, local_rows, width) * gelu_slope(preactivation)
        sums = jnp.concatenate([jnp.sum(d_pre, axis=1), jnp.sum(d_pre * normalised, axis=1)])
        last = exchange(sums, "batch")
        loss = sum(exchange(share, "batch"))[0, 0]
        both = sum(last)
        sum_b, sum_g = both[:n_view], both[n_view:]
        grad_bias = jnp.sum(sum_b, axis=0)
        grad_gain = jnp.sum(sum_g, axis=0)
        views_gradient = (
            norm_scale_gain
            * (d_pre - sum_b[:, None, :] / rows - normalised * sum_g[:, None, :] / rows)
            * inverse_deviation
        )
    return (loss, grad_weight, grad_gain, grad_bias, views_gradient)


def solution(mesh):
    placed = (P(None, "batch", "col"), P("col"), P("col"), P(None, "col"))
    return jax.shard_map(
        shards,
        mesh=mesh,
        in_specs=placed,
        out_specs=(P(), P("batch", "col"), P("col"), P("col"), P(None, "batch", "col")),
        check_vma=False,
    )
```

```python
import functools

import jax
import jax.numpy as jnp
from jax import lax
from jax.experimental import pallas as pl
from jax.experimental.pallas import tpu as pltpu
from jax.sharding import PartitionSpec as P

eps_norm = 1e-05
eps_std = 0.0001
f32 = jnp.float32
bf16 = jnp.bfloat16
VMEM_LIMIT = 40 * 1024 * 1024


def gelu_slope(preactivation):
    value, pullback = jax.vjp(lambda t: jax.nn.gelu(t, approximate=True), preactivation)
    return pullback(jnp.ones_like(value))[0]


def xor_send(x, axis, k):
    n = lax.axis_size(axis)
    return lax.ppermute(x, axis, [(i, i ^ k) for i in range(n)])


def ring_order(n):
    return list(range(0, n, 2)) + list(range(1, n, 2))[::-1]


def ring_send(x, axis, d):
    order = ring_order(lax.axis_size(axis))
    n = len(order)
    return lax.ppermute(x, axis, [(order[i], order[(i + d) % n]) for i in range(n)])


def exchange(x, axis):
    n = lax.axis_size(axis)
    me = lax.axis_index(axis)
    slots = [x]
    for d in range(1, n):
        slots.append(lax.ppermute(x, axis, [(i, (i + d) % n) for i in range(n)]))
    ordered = []
    for a in range(n):
        value = slots[0]
        for d in range(1, n):
            value = jnp.where((me - a) % n == d, slots[d], value)
        ordered.append(value)
    return ordered


def params():
    return pltpu.CompilerParams(vmem_limit_bytes=VMEM_LIMIT)


def cost(flops, moved):
    return pl.CostEstimate(flops=flops, bytes_accessed=moved, transcendentals=0)


def whole(shape):
    return pl.BlockSpec(shape, lambda i, index: (0,) * len(shape))


def z_kernel(count, first, last, index_ref, *refs):
    pieces, rest = refs[:count], list(refs[count:])
    w_ref = rest.pop(0)
    before = None if first else rest.pop(0)
    i = pl.program_id(0)
    if last:
        z0_ref, z1_ref, sum_ref, total = rest
    else:
        (total,) = rest

    for j in range(count):

        @pl.when(i == j)
        def _():
            part = jnp.dot(pieces[j][...], w_ref[...], preferred_element_type=f32)
            if j > 0:
                total[...] += part
            elif first:
                total[...] = part
            else:
                total[...] = before[...] + part

    if last:

        @pl.when(i == count - 1)
        def _():
            z = total[...].astype(bf16)
            half = z.shape[0] // 2
            for v, ref in enumerate((z0_ref, z1_ref)):
                mine = z[v * half : (v + 1) * half]
                ref[...] = mine
                sum_ref[v : v + 1, :] = jnp.sum(mine.astype(f32), axis=0, keepdims=True)


def z_call(index, pieces, weight, before, last):
    count = len(pieces)
    rows, width = pieces[0].shape
    columns = weight.shape[1]
    in_specs = [whole((rows, width)) for _ in pieces]
    in_specs.append(pl.BlockSpec((width, columns), lambda i, index: (index[i], 0)))
    operands = list(pieces) + [weight]
    if before is not None:
        in_specs.append(whole((rows, columns)))
        operands.append(before)
    scratch = []
    if last:
        out_shape = (
            jax.ShapeDtypeStruct((rows // 2, columns), bf16),
            jax.ShapeDtypeStruct((rows // 2, columns), bf16),
            jax.ShapeDtypeStruct((2, columns), f32),
        )
        out_specs = (whole((rows // 2, columns)), whole((rows // 2, columns)), whole((2, columns)))
        scratch = [pltpu.VMEM((rows, columns), f32)]
    else:
        out_shape = jax.ShapeDtypeStruct((rows, columns), f32)
        out_specs = whole((rows, columns))
    return pl.pallas_call(
        functools.partial(z_kernel, count, before is None, last),
        out_shape=out_shape,
        grid_spec=pltpu.PrefetchScalarGridSpec(
            num_scalar_prefetch=1,
            grid=(count,),
            in_specs=in_specs,
            out_specs=out_specs,
            scratch_shapes=scratch,
        ),
        compiler_params=params(),
        cost_estimate=cost(
            2 * rows * width * columns * count, 2 * count * width * (columns + rows)
        ),
        name="z_matmul",
    )(index, *operands)


def strip_kernel(n_slots, n_sums, rows, n_col, index_ref, *refs):
    z_refs, sum_refs = refs[: 2 * n_slots], refs[2 * n_slots : 2 * n_slots + n_sums]
    even_ref, odd_ref, strip = refs[2 * n_slots + n_sums :]
    local_rows = z_refs[0].shape[0]
    mean = sum(s[...] for s in sum_refs) / rows
    for v in range(2):
        here = pl.ds(v * local_rows, local_rows)
        rounded = [(z[...].astype(f32) - mean[v : v + 1]).astype(bf16) for z in z_refs[v::2]]
        for u in range(n_slots):
            strip[here, pl.ds(u * local_rows, local_rows)] = lax.dot_general(
                rounded[0], rounded[u], (((1,), (1,)), ((), ())), preferred_element_type=f32
            )
    part = 2 * local_rows // n_col
    for k in range(n_col):
        start = pl.multiple_of(index_ref[k] * part, part)
        (odd_ref if k % 2 else even_ref)[k // 2] = strip[pl.ds(start, part), :]


def strip_call(index, z_slots, sums, rows, n_col):
    local_rows, columns = z_slots[0][0].shape
    tall = 2 * local_rows
    wide = len(z_slots) * local_rows
    part = jax.ShapeDtypeStruct((n_col // 2, tall // n_col, wide), f32)
    operands = [z for slot in z_slots for z in slot] + list(sums)
    specs = [whole(x.shape) for x in operands]
    return pl.pallas_call(
        functools.partial(strip_kernel, len(z_slots), len(sums), rows, n_col),
        out_shape=(part, part),
        grid_spec=pltpu.PrefetchScalarGridSpec(
            num_scalar_prefetch=1,
            grid=(1,),
            in_specs=specs,
            out_specs=(whole(part.shape), whole(part.shape)),
            scratch_shapes=[pltpu.VMEM((tall, wide), f32)],
        ),
        compiler_params=params(),
        cost_estimate=cost(2 * tall * wide * columns, 2 * tall * columns * len(z_slots)),
        name="kernel_strip",
    )(index, *operands)


def dz_kernel(n_batch, n_col, coef, hinge_coef, inv_coef, inv_share, hinge_share, diag_share, index_ref, *refs):
    strip_refs = refs[:n_col]
    z_refs = refs[n_col : n_col + 2 * n_batch]
    dz_ref, share_ref, strips, full, centred = refs[n_col + 2 * n_batch :]
    local_rows = z_refs[0].shape[0]
    rows = local_rows * n_batch
    reach = n_batch // 2

    @pl.when(pl.program_id(0) == 0)
    def _():
        share_ref[...] = jnp.zeros_like(share_ref)
        part = 2 * local_rows // n_col
        for k in range(n_col):
            start = pl.multiple_of(index_ref[k] * part, part)
            for s in range(n_batch):
                strips[s, pl.ds(start, part), :] = strip_refs[k][s].astype(f32)
        for v in range(2):
            for s in range(n_batch):
                for u in range(reach + 1):
                    t = (s + u) % n_batch
                    block = strips[s, pl.ds(v * local_rows, local_rows), pl.ds(u * local_rows, local_rows)]
                    full[v, pl.ds(s * local_rows, local_rows), pl.ds(t * local_rows, local_rows)] = block.astype(bf16)
                    if 0 < u < n_batch - reach:
                        full[v, pl.ds(t * local_rows, local_rows), pl.ds(s * local_rows, local_rows)] = jnp.transpose(block).astype(bf16)

    share = jnp.zeros((1, 1), f32)
    grads = []
    z_views = []
    for v in range(2):
        zf = jnp.concatenate([z[...].astype(f32) for z in z_refs[v::2]], axis=0)
        z_views.append(zf)
        zc = zf - jnp.sum(zf, axis=0, keepdims=True) / rows
        std = jnp.sqrt(jnp.sum(zc * zc, axis=0, keepdims=True) / (rows - 1) + eps_std)
        zcb = zc.astype(bf16)
        centred[...] = zcb
        rounded = zcb.astype(f32)
        diag = jnp.sum(rounded * rounded, axis=0, keepdims=True)
        moved = jnp.dot(full[v], centred[...], preferred_element_type=f32)
        pull = jnp.where(std < 1.0, hinge_coef, 0.0) / std
        summed = coef * (moved - rounded * diag) - zc * pull
        grads.append(summed - jnp.sum(summed, axis=0, keepdims=True) / rows)
        share += hinge_share * jnp.sum(jnp.maximum(1.0 - std, 0.0), axis=1, keepdims=True)
        share -= diag_share * jnp.sum(diag * diag, axis=1, keepdims=True)
    diff = z_views[0] - z_views[1]
    share += inv_share * jnp.sum(jnp.sum(diff * diff, axis=0, keepdims=True), axis=1, keepdims=True)
    share_ref[...] += jnp.broadcast_to(share, share_ref.shape)
    dz_ref[0] = (grads[0] + inv_coef * diff).astype(bf16)
    dz_ref[1] = (grads[1] - inv_coef * diff).astype(bf16)


def dz_call(index, strips, z_slots, constants):
    n_col, n_batch = len(strips), len(z_slots)
    local_rows, columns = z_slots[0][0].shape
    tall = 2 * local_rows
    rows = local_rows * n_batch
    tile = min(256, columns)
    part = strips[0].shape
    return pl.pallas_call(
        functools.partial(dz_kernel, n_batch, n_col, *constants),
        out_shape=(
            jax.ShapeDtypeStruct((2, rows, columns), bf16),
            jax.ShapeDtypeStruct((8, 128), f32),
        ),
        grid_spec=pltpu.PrefetchScalarGridSpec(
            num_scalar_prefetch=1,
            grid=(columns // tile,),
            in_specs=[whole(part) for _ in strips]
            + [pl.BlockSpec((local_rows, tile), lambda j, index: (0, j)) for _ in range(2 * n_batch)],
            out_specs=(
                pl.BlockSpec((2, rows, tile), lambda j, index: (0, 0, j)),
                whole((8, 128)),
            ),
            scratch_shapes=[
                pltpu.VMEM((n_batch, tall, part[2]), f32),
                pltpu.VMEM((2, rows, rows), bf16),
                pltpu.VMEM((rows, tile), bf16),
            ],
        ),
        compiler_params=params(),
        cost_estimate=cost(4 * rows * rows * columns, 8 * rows * columns),
        name="embedding_gradient",
    )(index, *strips, *[z for slot in z_slots for z in slot])


def d_act_kernel(count, adds, index_ref, dz_ref, w_ref, *refs):
    i = pl.program_id(0)
    two, local_rows, columns = dz_ref.shape
    part = lax.dot_general(
        dz_ref[...].reshape(two * local_rows, columns),
        w_ref[...],
        (((1,), (1,)), ((), ())),
        preferred_element_type=f32,
    )
    if not adds:
        refs[0][0] = part.astype(refs[0].dtype)
        return
    part = part + refs[0][0].astype(f32)
    for j in range(count):

        @pl.when(i == j)
        def _():
            refs[j + 1][...] = part.astype(refs[j + 1].dtype)


def d_act_call(index, dz, weight, local_rows, width, got, first, count, kind):
    columns = weight.shape[1]
    tall = 2 * local_rows
    in_specs = [
        pl.BlockSpec((2, local_rows, columns), lambda i, index: (0, 0, 0)),
        pl.BlockSpec((width, columns), lambda i, index: (index[i], 0)),
    ]
    operands = [dz, weight]
    if got is None:
        out_shape = (jax.ShapeDtypeStruct((count, tall, width), kind),)
        out_specs = (pl.BlockSpec((1, tall, width), lambda i, index: (i, 0, 0)),)
    else:
        in_specs.append(pl.BlockSpec((1, tall, width), lambda i, index: (first + i, 0, 0)))
        operands.append(got)
        out_shape = (jax.ShapeDtypeStruct((tall, width), kind),) * count
        out_specs = (whole((tall, width)),) * count
    return pl.pallas_call(
        functools.partial(d_act_kernel, count, got is not None),
        out_shape=out_shape,
        grid_spec=pltpu.PrefetchScalarGridSpec(
            num_scalar_prefetch=1, grid=(count,), in_specs=in_specs, out_specs=out_specs
        ),
        compiler_params=params(),
        cost_estimate=cost(2 * tall * width * columns * count, 2 * count * width * (columns + tall)),
        name="d_act_matmul",
    )(index, *operands)


def weight_grad_kernel(act_ref, dz_ref, out_ref):
    out_ref[...] = lax.dot_general(
        act_ref[...], dz_ref[...], (((0,), (0,)), ((), ())), preferred_element_type=f32
    )


def weight_grad_call(act, dz):
    rows, features = act.shape
    columns = dz.shape[1]
    tile = min(256, features)
    return pl.pallas_call(
        weight_grad_kernel,
        out_shape=jax.ShapeDtypeStruct((features, columns), f32),
        grid=(features // tile,),
        in_specs=[
            pl.BlockSpec((rows, tile), lambda i: (0, i)),
            pl.BlockSpec((rows, columns), lambda i: (0, 0)),
        ],
        out_specs=pl.BlockSpec((tile, columns), lambda i: (i, 0)),
        compiler_params=params(),
        cost_estimate=cost(2 * rows * features * columns, 4 * features * columns),
        name="weight_gradient",
    )(act, dz)


def shards(views, norm_scale_gain, norm_shift_bias, weight):
    n_batch = lax.axis_size("batch")
    n_col = lax.axis_size("col")
    b = lax.axis_index("batch")
    c = lax.axis_index("col")
    n_view, local_rows, width = views.shape
    columns = weight.shape[1]
    E = columns * n_col
    rows = local_rows * n_batch
    tall = n_view * local_rows
    scale = rows * E / 128.0
    denom = float((rows - 1) ** 2 * E)
    evens = list(range(0, n_col, 2))
    far = evens[1:]
    blocks = pltpu.with_memory_space_constraint(weight, pltpu.HBM)

    def places(ks):
        return jnp.stack([c ^ k for k in ks]).astype(jnp.int32)

    with jax.named_scope("norm_stats"):
        hidden = views.astype(f32)
        local_mean = jnp.mean(hidden, axis=1)
        local_centred = hidden - local_mean[:, None, :]
        local_spread = jnp.sum(local_centred * local_centred, axis=1)
        stats = exchange(jnp.concatenate([local_mean, local_spread]), "batch")
        mean = sum(s[:n_view] for s in stats) / n_batch
        spread = sum(s[n_view:] + local_rows * jnp.square(s[:n_view] - mean) for s in stats)
        var = spread / rows
        inverse_deviation = (1.0 / jnp.sqrt(var + eps_norm))[:, None, :]
        normalised = (hidden - mean[:, None, :]) * inverse_deviation
        preactivation = norm_scale_gain * normalised + norm_shift_bias
        act = jax.nn.gelu(preactivation, approximate=True).astype(bf16)
    with jax.named_scope("act_gather"):
        pieces = {0: act.reshape(tall, width)}
        for k in far:
            pieces[k] = xor_send(pieces[0], "col", k)
        for k in evens:
            pieces[k + 1] = xor_send(pieces[k], "col", 1)
    with jax.named_scope("z"):
        z = z_call(places([0, 1]), [pieces[0], pieces[1]], blocks, None, False)
        z = z_call(places(far), [pieces[k] for k in far], blocks, z, False)
        odd = [k + 1 for k in far]
        *z, z_sum = z_call(places(odd), [pieces[k] for k in odd], blocks, z, True)
    with jax.named_scope("z_ring"):
        sums = [z_sum] + [ring_send(z_sum, "batch", d) for d in range(1, n_batch)]
        slots = [z]
        for _ in range(1, n_batch):
            slots.append([ring_send(x, "batch", 1) for x in slots[-1]])
    with jax.named_scope("kernel"):
        reach = n_batch // 2
        everyone = places(range(n_col))
        even_part, odd_part = strip_call(everyone, slots[: reach + 1], sums, rows, n_col)
        even_part = even_part + xor_send(odd_part, "col", 1)
        strip = even_part[0]
        for k in far:
            strip = strip + xor_send(even_part[k // 2], "col", k)
        block = lax.broadcasted_iota(jnp.int32, (1, strip.shape[1]), 1) // local_rows
        twice = jnp.where((block > 0) & (block < n_batch - reach), 2.0, 1.0)
        block_share = jnp.sum(strip * strip * twice) / denom
        mine = strip.astype(bf16)
        mine = jnp.stack([mine] + [ring_send(mine, "batch", d) for d in range(1, n_batch)])
        mine, held_back = lax.optimization_barrier((mine, [pieces[k] for k in evens]))
        strips = {0: mine}
        for k in far:
            strips[k] = xor_send(mine, "col", k)
        for k in evens:
            strips[k + 1] = xor_send(strips[k], "col", 1)
    with jax.named_scope("dz"):
        constants = (
            4.0 * scale / denom,
            25.0 * scale / (2.0 * E * (rows - 1)),
            50.0 * scale / (rows * E),
            25.0 / (rows * E) / n_batch,
            25.0 / (2 * E) / n_batch,
            1.0 / denom / n_batch,
        )
        dz, share = dz_call(everyone, [strips[k] for k in range(n_col)], slots, constants)
    with jax.named_scope("d_act"):
        half = len(evens)
        (away,) = d_act_call(
            places([k + 1 for k in evens]), dz, blocks, local_rows, width, None, 0, half, bf16
        )
        got = xor_send(away, "col", 1)
        sends = d_act_call(places(far), dz, blocks, local_rows, width, got, 1, half - 1, bf16)
        arrived = [xor_send(part, "col", k) for k, part in zip(far, sends)]
        (d_act,) = d_act_call(places([0]), dz, blocks, local_rows, width, got, 0, 1, f32)
    with jax.named_scope("grad_weight"):
        per_plane = n_col // n_batch
        order = jnp.array(ring_order(n_batch), jnp.int32)
        position = jnp.where(b % 2 == 0, b // 2, n_batch - 1 - b // 2)
        stacked = jnp.stack(held_back)

        def held(plane, i):
            k = (per_plane * plane + 2 * i) ^ (c - c % 2)
            return lax.dynamic_index_in_dim(stacked, k // 2, 0, keepdims=False)

        halves = []
        for i in range(per_plane // 2):
            own = [held(b, i)]
            for d in range(1, n_batch):
                ahead = (position + d) % n_batch
                plane = jnp.where(ahead < (n_batch + 1) // 2, 2 * ahead, 2 * (n_batch - ahead) - 1)
                own.append(ring_send(held(plane, i), "batch", d))
            own = jnp.concatenate([o.reshape(n_view, local_rows, width) for o in own], axis=1)
            other = xor_send(own, "col", 1)
            halves.append(jnp.where(c % 2 == 0, own, other))
            halves.append(jnp.where(c % 2 == 0, other, own))
        wanted = jnp.concatenate(halves, axis=2).reshape(n_view * rows, per_plane * width)
        grad_weight = weight_grad_call(wanted, dz.reshape(n_view * rows, columns))
    with jax.named_scope("loss"):
        share = share + block_share
        k = 1
        while k < n_col:
            share = share + xor_send(share, "col", k)
            k *= 2
    with jax.named_scope("norm_backward"):
        arrived, d_act, grad_weight = lax.optimization_barrier((arrived, d_act, grad_weight))
        for part in arrived:
            d_act = d_act + part.astype(f32)
        d_pre = d_act.reshape(n_view, local_rows, width) * gelu_slope(preactivation)
        sums = jnp.concatenate(
            [
                jnp.sum(d_pre, axis=1),
                jnp.sum(d_pre * normalised, axis=1),
                jnp.broadcast_to(share[:1, :1], (2 * n_view, width)),
            ]
        )
        both = sum(exchange(sums, "batch"))
        sum_b, sum_g = both[:n_view], both[n_view : 2 * n_view]
        loss = jnp.max(both[2 * n_view :])
        grad_bias = jnp.sum(sum_b, axis=0)
        grad_gain = jnp.sum(sum_g, axis=0)
        views_gradient = (
            norm_scale_gain
            * (d_pre - sum_b[:, None, :] / rows - normalised * sum_g[:, None, :] / rows)
            * inverse_deviation
        )
    return (loss, grad_weight, grad_gain, grad_bias, views_gradient)


def solution(mesh):
    placed = (P(None, "batch", "col"), P("col"), P("col"), P(None, "col"))
    return jax.shard_map(
        shards,
        mesh=mesh,
        in_specs=placed,
        out_specs=(P(), P("batch", "col"), P("col"), P("col"), P(None, "batch", "col")),
        check_vma=False,
    )
```

```python
import functools

import jax
import jax.numpy as jnp
from jax import lax
from jax.experimental import pallas as pl
from jax.experimental.pallas import tpu as pltpu
from jax.sharding import PartitionSpec as P

eps_norm = 1e-05
eps_std = 0.0001
f32 = jnp.float32
bf16 = jnp.bfloat16
VMEM_LIMIT = 40 * 1024 * 1024


def gelu_slope(preactivation):
    value, pullback = jax.vjp(lambda t: jax.nn.gelu(t, approximate=True), preactivation)
    return pullback(jnp.ones_like(value))[0]


def xor_send(x, axis, k):
    n = lax.axis_size(axis)
    return lax.ppermute(x, axis, [(i, i ^ k) for i in range(n)])


def ring_order(n):
    return list(range(0, n, 2)) + list(range(1, n, 2))[::-1]


def ring_send(x, axis, d):
    order = ring_order(lax.axis_size(axis))
    n = len(order)
    return lax.ppermute(x, axis, [(order[i], order[(i + d) % n]) for i in range(n)])


def exchange(x, axis):
    n = lax.axis_size(axis)
    me = lax.axis_index(axis)
    slots = [x]
    for d in range(1, n):
        slots.append(lax.ppermute(x, axis, [(i, (i + d) % n) for i in range(n)]))
    ordered = []
    for a in range(n):
        value = slots[0]
        for d in range(1, n):
            value = jnp.where((me - a) % n == d, slots[d], value)
        ordered.append(value)
    return ordered


def params():
    return pltpu.CompilerParams(vmem_limit_bytes=VMEM_LIMIT)


def cost(flops, moved):
    return pl.CostEstimate(flops=flops // 1000, bytes_accessed=moved // 1000, transcendentals=0)


def whole(shape):
    return pl.BlockSpec(shape, lambda i, index: (0,) * len(shape))


SPLITS = 4


def weight_copies(index_ref, w_ref, buffer, sems, j):
    width = buffer.shape[1]
    step = width // SPLITS
    start = pl.multiple_of(index_ref[j] * width, width)
    return [
        pltpu.make_async_copy(
            w_ref.at[pl.ds(start + q * step, step)],
            buffer.at[j, pl.ds(q * step, step)],
            sems.at[j, q],
        )
        for q in range(SPLITS)
    ]


def weight_scratch(count, width, columns):
    return [pltpu.VMEM((count, width, columns), bf16), pltpu.SemaphoreType.DMA((count, SPLITS))]


def z_kernel(count, first, last, index_ref, *refs):
    pieces, rest = refs[:count], list(refs[count:])
    w_ref = rest.pop(0)
    before = None if first else rest.pop(0)
    buffer, sems = rest[-2:]
    for j in range(count):
        for copy in weight_copies(index_ref, w_ref, buffer, sems, j):
            copy.start()
    total = None if first else before[...]
    for j in range(count):
        for copy in weight_copies(index_ref, w_ref, buffer, sems, j):
            copy.wait()
        part = jnp.dot(pieces[j][...], buffer[j], preferred_element_type=f32)
        total = part if total is None else total + part
    if not last:
        rest[0][...] = total
        return
    z0_ref, z1_ref, sum_ref = rest[:3]
    z = total.astype(bf16)
    half = z.shape[0] // 2
    for v, ref in enumerate((z0_ref, z1_ref)):
        mine = z[v * half : (v + 1) * half]
        ref[...] = mine
        sum_ref[v : v + 1, :] = jnp.sum(mine.astype(f32), axis=0, keepdims=True)


def z_call(index, pieces, weight, before, last):
    count = len(pieces)
    rows, width = pieces[0].shape
    columns = weight.shape[1]
    in_specs = [whole((rows, width)) for _ in pieces]
    in_specs.append(pl.BlockSpec(memory_space=pl.ANY))
    operands = list(pieces) + [weight]
    if before is not None:
        in_specs.append(whole((rows, columns)))
        operands.append(before)
    if last:
        out_shape = (
            jax.ShapeDtypeStruct((rows // 2, columns), bf16),
            jax.ShapeDtypeStruct((rows // 2, columns), bf16),
            jax.ShapeDtypeStruct((2, columns), f32),
        )
        out_specs = (whole((rows // 2, columns)), whole((rows // 2, columns)), whole((2, columns)))
    else:
        out_shape = jax.ShapeDtypeStruct((rows, columns), f32)
        out_specs = whole((rows, columns))
    return pl.pallas_call(
        functools.partial(z_kernel, count, before is None, last),
        out_shape=out_shape,
        grid_spec=pltpu.PrefetchScalarGridSpec(
            num_scalar_prefetch=1,
            grid=(1,),
            in_specs=in_specs,
            out_specs=out_specs,
            scratch_shapes=weight_scratch(count, width, columns),
        ),
        compiler_params=params(),
        cost_estimate=cost(
            2 * rows * width * columns * count, 2 * count * width * (columns + rows)
        ),
        name="z_matmul",
    )(index, *operands)


def strip_kernel(n_slots, n_sums, rows, n_col, index_ref, *refs):
    z_refs, sum_refs = refs[: 2 * n_slots], refs[2 * n_slots : 2 * n_slots + n_sums]
    even_ref, odd_ref, strip = refs[2 * n_slots + n_sums :]
    local_rows = z_refs[0].shape[0]
    mean = sum(s[...] for s in sum_refs) / rows
    for v in range(2):
        here = pl.ds(v * local_rows, local_rows)
        rounded = [(z[...].astype(f32) - mean[v : v + 1]).astype(bf16) for z in z_refs[v::2]]
        for u in range(n_slots):
            strip[here, pl.ds(u * local_rows, local_rows)] = lax.dot_general(
                rounded[0], rounded[u], (((1,), (1,)), ((), ())), preferred_element_type=f32
            )
    part = 2 * local_rows // n_col
    for k in range(n_col):
        start = pl.multiple_of(index_ref[k] * part, part)
        (odd_ref if k % 2 else even_ref)[k // 2] = strip[pl.ds(start, part), :]


def strip_call(index, z_slots, sums, rows, n_col):
    local_rows, columns = z_slots[0][0].shape
    tall = 2 * local_rows
    wide = len(z_slots) * local_rows
    part = jax.ShapeDtypeStruct((n_col // 2, tall // n_col, wide), f32)
    operands = [z for slot in z_slots for z in slot] + list(sums)
    specs = [whole(x.shape) for x in operands]
    return pl.pallas_call(
        functools.partial(strip_kernel, len(z_slots), len(sums), rows, n_col),
        out_shape=(part, part),
        grid_spec=pltpu.PrefetchScalarGridSpec(
            num_scalar_prefetch=1,
            grid=(1,),
            in_specs=specs,
            out_specs=(whole(part.shape), whole(part.shape)),
            scratch_shapes=[pltpu.VMEM((tall, wide), f32)],
        ),
        compiler_params=params(),
        cost_estimate=cost(2 * tall * wide * columns, 2 * tall * columns * len(z_slots)),
        name="kernel_strip",
    )(index, *operands)


def dz_kernel(n_batch, n_col, coef, hinge_coef, inv_coef, inv_share, hinge_share, diag_share, index_ref, *refs):
    strip_refs = refs[:n_col]
    z_refs = refs[n_col : n_col + 2 * n_batch]
    dz_ref, share_ref, strips, full, centred = refs[n_col + 2 * n_batch :]
    local_rows = z_refs[0].shape[0]
    rows = local_rows * n_batch
    reach = n_batch // 2

    @pl.when(pl.program_id(0) == 0)
    def _():
        share_ref[...] = jnp.zeros_like(share_ref)
        part = 2 * local_rows // n_col
        for k in range(n_col):
            start = pl.multiple_of(index_ref[k] * part, part)
            for s in range(n_batch):
                strips[s, pl.ds(start, part), :] = strip_refs[k][s].astype(f32)
        for v in range(2):
            for s in range(n_batch):
                for u in range(reach + 1):
                    t = (s + u) % n_batch
                    block = strips[s, pl.ds(v * local_rows, local_rows), pl.ds(u * local_rows, local_rows)]
                    full[v, pl.ds(s * local_rows, local_rows), pl.ds(t * local_rows, local_rows)] = block.astype(bf16)
                    if 0 < u < n_batch - reach:
                        full[v, pl.ds(t * local_rows, local_rows), pl.ds(s * local_rows, local_rows)] = jnp.transpose(block).astype(bf16)

    share = jnp.zeros((1, 1), f32)
    grads = []
    z_views = []
    for v in range(2):
        zf = jnp.concatenate([z[...].astype(f32) for z in z_refs[v::2]], axis=0)
        z_views.append(zf)
        zc = zf - jnp.sum(zf, axis=0, keepdims=True) / rows
        std = jnp.sqrt(jnp.sum(zc * zc, axis=0, keepdims=True) / (rows - 1) + eps_std)
        zcb = zc.astype(bf16)
        centred[...] = zcb
        rounded = zcb.astype(f32)
        diag = jnp.sum(rounded * rounded, axis=0, keepdims=True)
        moved = jnp.dot(full[v], centred[...], preferred_element_type=f32)
        pull = jnp.where(std < 1.0, hinge_coef, 0.0) / std
        summed = coef * (moved - rounded * diag) - zc * pull
        grads.append(summed - jnp.sum(summed, axis=0, keepdims=True) / rows)
        share += hinge_share * jnp.sum(jnp.maximum(1.0 - std, 0.0), axis=1, keepdims=True)
        share -= diag_share * jnp.sum(diag * diag, axis=1, keepdims=True)
    diff = z_views[0] - z_views[1]
    share += inv_share * jnp.sum(jnp.sum(diff * diff, axis=0, keepdims=True), axis=1, keepdims=True)
    share_ref[...] += jnp.broadcast_to(share, share_ref.shape)
    dz_ref[0] = (grads[0] + inv_coef * diff).astype(bf16)
    dz_ref[1] = (grads[1] - inv_coef * diff).astype(bf16)


def dz_call(index, strips, z_slots, constants):
    n_col, n_batch = len(strips), len(z_slots)
    local_rows, columns = z_slots[0][0].shape
    tall = 2 * local_rows
    rows = local_rows * n_batch
    tile = min(256, columns)
    part = strips[0].shape
    return pl.pallas_call(
        functools.partial(dz_kernel, n_batch, n_col, *constants),
        out_shape=(
            jax.ShapeDtypeStruct((2, rows, columns), bf16),
            jax.ShapeDtypeStruct((8, 128), f32),
        ),
        grid_spec=pltpu.PrefetchScalarGridSpec(
            num_scalar_prefetch=1,
            grid=(columns // tile,),
            in_specs=[whole(part) for _ in strips]
            + [pl.BlockSpec((local_rows, tile), lambda j, index: (0, j)) for _ in range(2 * n_batch)],
            out_specs=(
                pl.BlockSpec((2, rows, tile), lambda j, index: (0, 0, j)),
                whole((8, 128)),
            ),
            scratch_shapes=[
                pltpu.VMEM((n_batch, tall, part[2]), f32),
                pltpu.VMEM((2, rows, rows), bf16),
                pltpu.VMEM((rows, tile), bf16),
            ],
        ),
        compiler_params=params(),
        cost_estimate=cost(4 * rows * rows * columns, 8 * rows * columns),
        name="embedding_gradient",
    )(index, *strips, *[z for slot in z_slots for z in slot])


EXTRA = 16


def share_rows(share, width, kind):
    high = share.astype(bf16).astype(f32)
    middle = (share - high).astype(bf16).astype(f32)
    low = share - high - middle
    row = lax.broadcasted_iota(jnp.int32, (EXTRA, width), 0)
    rows = jnp.where(row == 0, high, jnp.where(row == 1, middle, jnp.where(row == 2, low, 0.0)))
    return rows.astype(kind)


def share_of(rows):
    return rows[0:1].astype(f32) + rows[1:2].astype(f32) + rows[2:3].astype(f32)


def d_act_kernel(count, first, index_ref, dz_ref, share_ref, w_ref, *refs):
    buffer, sems = refs[-2:]
    for j in range(count):
        for copy in weight_copies(index_ref, w_ref, buffer, sems, j):
            copy.start()
    two, local_rows, columns = dz_ref.shape
    dz = dz_ref[...].reshape(two * local_rows, columns)
    for j in range(count):
        for copy in weight_copies(index_ref, w_ref, buffer, sems, j):
            copy.wait()
        part = lax.dot_general(
            dz, buffer[j], (((1,), (1,)), ((), ())), preferred_element_type=f32
        )
        tall, width = part.shape
        share = share_ref[0:1, 0:1]
        if first is None:
            refs[0][j, :tall] = part.astype(refs[0].dtype)
            refs[0][j, tall:] = share_rows(share, width, refs[0].dtype)
        else:
            out_ref = refs[j + 1]
            out_ref[:tall] = (part + refs[0][first + j, :tall].astype(f32)).astype(out_ref.dtype)
            share = share + share_of(refs[0][first + j, tall:])[:, 0:1]
            out_ref[tall:] = share_rows(share, width, out_ref.dtype)


def d_act_call(index, dz, share, weight, local_rows, width, got, first, count, kind):
    columns = weight.shape[1]
    tall = 2 * local_rows
    in_specs = [
        pl.BlockSpec((2, local_rows, columns), lambda i, index: (0, 0, 0)),
        whole(share.shape),
        pl.BlockSpec(memory_space=pl.ANY),
    ]
    operands = [dz, share, weight]
    long = tall + EXTRA
    if got is None:
        out_shape = (jax.ShapeDtypeStruct((count, long, width), kind),)
        out_specs = (whole((count, long, width)),)
    else:
        in_specs.append(whole(got.shape))
        operands.append(got)
        out_shape = (jax.ShapeDtypeStruct((long, width), kind),) * count
        out_specs = (whole((long, width)),) * count
    return pl.pallas_call(
        functools.partial(d_act_kernel, count, None if got is None else first),
        out_shape=out_shape,
        grid_spec=pltpu.PrefetchScalarGridSpec(
            num_scalar_prefetch=1,
            grid=(1,),
            in_specs=in_specs,
            out_specs=out_specs,
            scratch_shapes=weight_scratch(count, width, columns),
        ),
        compiler_params=params(),
        cost_estimate=cost(2 * tall * width * columns * count, 2 * count * width * (columns + tall)),
        name="d_act_matmul",
    )(index, *operands)


def weight_grad_kernel(act_ref, dz_ref, out_ref):
    out_ref[...] = lax.dot_general(
        act_ref[...], dz_ref[...], (((0,), (0,)), ((), ())), preferred_element_type=f32
    )


def weight_grad_call(act, dz):
    rows, features = act.shape
    columns = dz.shape[1]
    tile = min(256, features)
    return pl.pallas_call(
        weight_grad_kernel,
        out_shape=jax.ShapeDtypeStruct((features, columns), f32),
        grid=(features // tile,),
        in_specs=[
            pl.BlockSpec((rows, tile), lambda i: (0, i)),
            pl.BlockSpec((rows, columns), lambda i: (0, 0)),
        ],
        out_specs=pl.BlockSpec((tile, columns), lambda i: (i, 0)),
        compiler_params=params(),
        cost_estimate=cost(2 * rows * features * columns, 4 * features * columns),
        name="weight_gradient",
    )(act, dz)


def shards(views, norm_scale_gain, norm_shift_bias, weight):
    n_batch = lax.axis_size("batch")
    n_col = lax.axis_size("col")
    b = lax.axis_index("batch")
    c = lax.axis_index("col")
    n_view, local_rows, width = views.shape
    columns = weight.shape[1]
    E = columns * n_col
    rows = local_rows * n_batch
    tall = n_view * local_rows
    scale = rows * E / 128.0
    denom = float((rows - 1) ** 2 * E)
    evens = list(range(0, n_col, 2))
    far = evens[1:]
    blocks = pltpu.with_memory_space_constraint(weight, pltpu.HBM)

    def places(ks):
        return jnp.stack([c ^ k for k in ks]).astype(jnp.int32)

    with jax.named_scope("norm_stats"):
        hidden = views.astype(f32)
        local_mean = jnp.mean(hidden, axis=1)
        local_centred = hidden - local_mean[:, None, :]
        local_spread = jnp.sum(local_centred * local_centred, axis=1)
        stats = exchange(jnp.concatenate([local_mean, local_spread]), "batch")
        mean = sum(s[:n_view] for s in stats) / n_batch
        spread = sum(s[n_view:] + local_rows * jnp.square(s[:n_view] - mean) for s in stats)
        var = spread / rows
        inverse_deviation = (1.0 / jnp.sqrt(var + eps_norm))[:, None, :]
        normalised = (hidden - mean[:, None, :]) * inverse_deviation
        preactivation = norm_scale_gain * normalised + norm_shift_bias
        act = jax.nn.gelu(preactivation, approximate=True).astype(bf16)
    with jax.named_scope("act_gather"):
        pieces = {0: act.reshape(tall, width)}
        for k in far:
            pieces[k] = xor_send(pieces[0], "col", k)
        for k in evens:
            pieces[k + 1] = xor_send(pieces[k], "col", 1)
    with jax.named_scope("z"):
        z = z_call(places([0, 1]), [pieces[0], pieces[1]], blocks, None, False)
        z = z_call(places(far), [pieces[k] for k in far], blocks, z, False)
        odd = [k + 1 for k in far]
        *z, z_sum = z_call(places(odd), [pieces[k] for k in odd], blocks, z, True)
    with jax.named_scope("z_ring"):
        sums = [z_sum] + [ring_send(z_sum, "batch", d) for d in range(1, n_batch)]
        slots = [z]
        for _ in range(1, n_batch):
            slots.append([ring_send(x, "batch", 1) for x in slots[-1]])
    with jax.named_scope("kernel"):
        reach = n_batch // 2
        everyone = places(range(n_col))
        even_part, odd_part = strip_call(everyone, slots[: reach + 1], sums, rows, n_col)
        even_part = even_part + xor_send(odd_part, "col", 1)
        strip = even_part[0]
        for k in far:
            strip = strip + xor_send(even_part[k // 2], "col", k)
        strip, slots[reach + 1 :] = lax.optimization_barrier((strip, slots[reach + 1 :]))
        block = lax.broadcasted_iota(jnp.int32, (1, strip.shape[1]), 1) // local_rows
        twice = jnp.where((block > 0) & (block < n_batch - reach), 2.0, 1.0)
        block_share = jnp.sum(strip * strip * twice) / denom
        mine = strip.astype(bf16)
        mine = jnp.stack([mine] + [ring_send(mine, "batch", d) for d in range(1, n_batch)])
        strips = {0: mine}
        for k in far:
            strips[k] = xor_send(mine, "col", k)
        for k in evens:
            strips[k + 1] = xor_send(strips[k], "col", 1)
        strips, held_back = lax.optimization_barrier((strips, [pieces[k] for k in evens]))
    with jax.named_scope("dz"):
        constants = (
            4.0 * scale / denom,
            25.0 * scale / (2.0 * E * (rows - 1)),
            50.0 * scale / (rows * E),
            25.0 / (rows * E) / n_batch,
            25.0 / (2 * E) / n_batch,
            1.0 / denom / n_batch,
        )
        dz, share = dz_call(everyone, [strips[k] for k in range(n_col)], slots, constants)
        share = share + block_share
    with jax.named_scope("d_act"):
        half = len(evens)
        (away,) = d_act_call(
            places([k + 1 for k in evens]), dz, share, blocks, local_rows, width, None, 0, half, bf16
        )
        got = xor_send(away, "col", 1)
        sends = d_act_call(places(far), dz, share, blocks, local_rows, width, got, 1, half - 1, bf16)
        arrived = [xor_send(part, "col", k) for k, part in zip(far, sends)]
        got, _ = lax.optimization_barrier((got, sends))
        (d_act,) = d_act_call(places([0]), dz, share, blocks, local_rows, width, got, 0, 1, f32)
    with jax.named_scope("grad_weight"):
        per_plane = n_col // n_batch
        order = jnp.array(ring_order(n_batch), jnp.int32)
        position = jnp.where(b % 2 == 0, b // 2, n_batch - 1 - b // 2)
        stacked = jnp.stack(held_back)

        def held(plane, i):
            k = (per_plane * plane + 2 * i) ^ (c - c % 2)
            return lax.dynamic_index_in_dim(stacked, k // 2, 0, keepdims=False)

        halves = []
        for i in range(per_plane // 2):
            own = [held(b, i)]
            for d in range(1, n_batch):
                ahead = (position + d) % n_batch
                plane = jnp.where(ahead < (n_batch + 1) // 2, 2 * ahead, 2 * (n_batch - ahead) - 1)
                own.append(ring_send(held(plane, i), "batch", d))
            own, d_act = lax.optimization_barrier((own, d_act))
            own = jnp.concatenate([o.reshape(n_view, local_rows, width) for o in own], axis=1)
            other = xor_send(own, "col", 1)
            halves.append(jnp.where(c % 2 == 0, own, other))
            halves.append(jnp.where(c % 2 == 0, other, own))
        wanted = jnp.concatenate(halves, axis=2).reshape(n_view * rows, per_plane * width)
        grad_weight = weight_grad_call(wanted, dz.reshape(n_view * rows, columns))
    with jax.named_scope("norm_backward"):
        arrived, d_act, grad_weight = lax.optimization_barrier((arrived, d_act, grad_weight))
        shares = [share_of(part[tall:]) for part in [d_act] + arrived]
        while len(shares) > 1:
            shares = [x + y for x, y in zip(shares[::2], shares[1::2])]
        d_act = d_act[:tall]
        for part in arrived:
            d_act = d_act + part[:tall].astype(f32)
        d_pre = d_act.reshape(n_view, local_rows, width) * gelu_slope(preactivation)
        sums = jnp.concatenate(
            [
                jnp.sum(d_pre, axis=1),
                jnp.sum(d_pre * normalised, axis=1),
                jnp.broadcast_to(shares[0], (2 * n_view, width)),
            ]
        )
        both = sum(exchange(sums, "batch"))
        sum_b, sum_g = both[:n_view], both[n_view : 2 * n_view]
        loss = jnp.max(both[2 * n_view :])
        grad_bias = jnp.sum(sum_b, axis=0)
        grad_gain = jnp.sum(sum_g, axis=0)
        views_gradient = (
            norm_scale_gain
            * (d_pre - sum_b[:, None, :] / rows - normalised * sum_g[:, None, :] / rows)
            * inverse_deviation
        )
    return (loss, grad_weight, grad_gain, grad_bias, views_gradient)


def solution(mesh):
    placed = (P(None, "batch", "col"), P("col"), P("col"), P(None, "col"))
    return jax.shard_map(
        shards,
        mesh=mesh,
        in_specs=placed,
        out_specs=(P(), P("batch", "col"), P("col"), P("col"), P(None, "batch", "col")),
        check_vma=False,
    )
```

```python
import functools

import jax
import jax.numpy as jnp
from jax import lax
from jax.experimental import pallas as pl
from jax.experimental.pallas import tpu as pltpu
from jax.sharding import PartitionSpec as P

eps_norm = 1e-05
eps_std = 0.0001
f32 = jnp.float32
bf16 = jnp.bfloat16
MIB = 1024 * 1024


def gelu_slope(preactivation):
    value, pullback = jax.vjp(lambda t: jax.nn.gelu(t, approximate=True), preactivation)
    return pullback(jnp.ones_like(value))[0]


def xor_send(x, axis, k):
    n = lax.axis_size(axis)
    return lax.ppermute(x, axis, [(i, i ^ k) for i in range(n)])


def ring_order(n):
    return list(range(0, n, 2)) + list(range(1, n, 2))[::-1]


def ring_send(x, axis, d):
    order = ring_order(lax.axis_size(axis))
    n = len(order)
    return lax.ppermute(x, axis, [(order[i], order[(i + d) % n]) for i in range(n)])


def exchange(x, axis):
    n = lax.axis_size(axis)
    me = lax.axis_index(axis)
    slots = [x]
    for d in range(1, n):
        slots.append(lax.ppermute(x, axis, [(i, (i + d) % n) for i in range(n)]))
    ordered = []
    for a in range(n):
        value = slots[0]
        for d in range(1, n):
            value = jnp.where((me - a) % n == d, slots[d], value)
        ordered.append(value)
    return ordered


def params(limit):
    return pltpu.CompilerParams(vmem_limit_bytes=limit * MIB)


def cost(flops, moved):
    return pl.CostEstimate(flops=flops, bytes_accessed=moved, transcendentals=0)


IN_SMEM = pl.BlockSpec(memory_space=pltpu.SMEM)
IN_VMEM = pl.BlockSpec(memory_space=pltpu.VMEM)
ANYWHERE = pl.BlockSpec(memory_space=pl.ANY)
LOADS = 8


def load_kernel(w_ref, out_ref, sems):
    step = w_ref.shape[0] // LOADS
    copies = [
        pltpu.make_async_copy(
            w_ref.at[pl.ds(i * step, step)], out_ref.at[pl.ds(i * step, step)], sems.at[i]
        )
        for i in range(LOADS)
    ]
    for copy in copies:
        copy.start()
    for copy in copies:
        copy.wait()


def load_call(weight):
    return pl.pallas_call(
        load_kernel,
        out_shape=pltpu.VMEM(weight.shape, weight.dtype),
        in_specs=[ANYWHERE],
        out_specs=IN_VMEM,
        scratch_shapes=[pltpu.SemaphoreType.DMA((LOADS,))],
        compiler_params=params(4),
        cost_estimate=cost(0, 4 * weight.size),
        name="weight_load",
    )(pltpu.with_memory_space_constraint(weight, pltpu.HBM))


def weight_rows(index_ref, w_ref, j, width):
    return w_ref[pl.ds(pl.multiple_of(index_ref[j] * width, width), width), :]


def z_kernel(count, first, last, local_rows, index_ref, *refs):
    pieces, rest = refs[:count], list(refs[count:])
    w_ref = rest.pop(0)
    total = None if first else rest.pop(0)[...]
    width = pieces[0].shape[1]
    for j in range(count):
        part = jnp.dot(
            pieces[j][...], weight_rows(index_ref, w_ref, j, width), preferred_element_type=f32
        )
        total = part if total is None else total + part
    if not last:
        rest[0][...] = total
        return
    z = total.astype(bf16)
    *z_refs, sum_ref = rest
    for v, ref in enumerate(z_refs):
        mine = z[v * local_rows : (v + 1) * local_rows]
        ref[...] = mine
        sum_ref[v : v + 1, :] = jnp.sum(mine.astype(f32), axis=0, keepdims=True)


def z_call(index, pieces, weight, before, last, local_rows):
    count = len(pieces)
    tall, width = pieces[0].shape
    columns = weight.shape[1]
    operands = [index] + list(pieces) + [weight] + ([] if before is None else [before])
    if last:
        groups = tall // local_rows
        out_shape = (jax.ShapeDtypeStruct((local_rows, columns), bf16),) * groups
        out_shape += (jax.ShapeDtypeStruct((groups, columns), f32),)
    else:
        out_shape = jax.ShapeDtypeStruct((tall, columns), f32)
    return pl.pallas_call(
        functools.partial(z_kernel, count, before is None, last, local_rows),
        out_shape=out_shape,
        in_specs=[IN_SMEM] + [IN_VMEM] * (len(operands) - 1),
        out_specs=jax.tree.map(lambda _: IN_VMEM, out_shape),
        compiler_params=params(8),
        cost_estimate=cost(2 * tall * width * columns * count, 2 * tall * columns),
        name="z_matmul",
    )(*operands)


def strip_kernel(n_slots, n_sums, rows, n_col, index_ref, *refs):
    z_refs, sum_refs = refs[: 2 * n_slots], refs[2 * n_slots : 2 * n_slots + n_sums]
    even_ref, odd_ref, strip = refs[2 * n_slots + n_sums :]
    local_rows = z_refs[0].shape[0]
    mean = sum(s[...] for s in sum_refs) / rows
    for v in range(2):
        here = pl.ds(v * local_rows, local_rows)
        rounded = [(z[...].astype(f32) - mean[v : v + 1]).astype(bf16) for z in z_refs[v::2]]
        for u in range(n_slots):
            strip[here, pl.ds(u * local_rows, local_rows)] = lax.dot_general(
                rounded[0], rounded[u], (((1,), (1,)), ((), ())), preferred_element_type=f32
            )
    part = 2 * local_rows // n_col
    for k in range(n_col):
        start = pl.multiple_of(index_ref[k] * part, part)
        (odd_ref if k % 2 else even_ref)[k // 2] = strip[pl.ds(start, part), :]


def strip_call(index, z_slots, sums, rows, n_col):
    local_rows, columns = z_slots[0][0].shape
    tall = 2 * local_rows
    wide = len(z_slots) * local_rows
    part = jax.ShapeDtypeStruct((n_col // 2, tall // n_col, wide), f32)
    operands = [index] + [z for slot in z_slots for z in slot] + list(sums)
    return pl.pallas_call(
        functools.partial(strip_kernel, len(z_slots), len(sums), rows, n_col),
        out_shape=(part, part),
        in_specs=[IN_SMEM] + [IN_VMEM] * (len(operands) - 1),
        out_specs=(IN_VMEM, IN_VMEM),
        scratch_shapes=[pltpu.VMEM((tall, wide), f32)],
        compiler_params=params(10),
        cost_estimate=cost(2 * tall * wide * columns, 2 * tall * columns * len(z_slots)),
        name="kernel_strip",
    )(*operands)


def dz_kernel(n_batch, n_col, tile, constants, index_ref, *refs):
    coef, hinge_coef, inv_coef, inv_share, hinge_share, diag_share = constants
    strip_refs = refs[:n_col]
    z_refs = refs[n_col : n_col + 2 * n_batch]
    dz_ref, share_ref, strips, full, centred = refs[n_col + 2 * n_batch :]
    local_rows, columns = z_refs[0].shape
    rows = local_rows * n_batch
    reach = n_batch // 2
    share_ref[...] = jnp.zeros_like(share_ref)
    part = 2 * local_rows // n_col
    for k in range(n_col):
        start = pl.multiple_of(index_ref[k] * part, part)
        for s in range(n_batch):
            strips[s, pl.ds(start, part), :] = strip_refs[k][s].astype(f32)
    for v in range(2):
        for s in range(n_batch):
            here = pl.ds(s * local_rows, local_rows)
            for u in range(reach + 1):
                t = (s + u) % n_batch
                there = pl.ds(t * local_rows, local_rows)
                block = strips[
                    s, pl.ds(v * local_rows, local_rows), pl.ds(u * local_rows, local_rows)
                ]
                full[v, here, there] = block.astype(bf16)
                if 0 < u < n_batch - reach:
                    full[v, there, here] = jnp.transpose(block).astype(bf16)

    def one_tile(j, carry):
        here = pl.ds(pl.multiple_of(j * tile, tile), tile)
        share = jnp.zeros((1, 1), f32)
        grads = []
        z_views = []
        for v in range(2):
            zf = jnp.concatenate([z[:, here].astype(f32) for z in z_refs[v::2]], axis=0)
            z_views.append(zf)
            zc = zf - jnp.sum(zf, axis=0, keepdims=True) / rows
            std = jnp.sqrt(jnp.sum(zc * zc, axis=0, keepdims=True) / (rows - 1) + eps_std)
            zcb = zc.astype(bf16)
            centred[...] = zcb
            rounded = zcb.astype(f32)
            diag = jnp.sum(rounded * rounded, axis=0, keepdims=True)
            moved = jnp.dot(full[v], centred[...], preferred_element_type=f32)
            pull = jnp.where(std < 1.0, hinge_coef, 0.0) / std
            summed = coef * (moved - rounded * diag) - zc * pull
            grads.append(summed - jnp.sum(summed, axis=0, keepdims=True) / rows)
            share += hinge_share * jnp.sum(jnp.maximum(1.0 - std, 0.0), axis=1, keepdims=True)
            share -= diag_share * jnp.sum(diag * diag, axis=1, keepdims=True)
        diff = z_views[0] - z_views[1]
        share += inv_share * jnp.sum(
            jnp.sum(diff * diff, axis=0, keepdims=True), axis=1, keepdims=True
        )
        share_ref[...] += jnp.broadcast_to(share, share_ref.shape)
        dz_ref[0, :, here] = (grads[0] + inv_coef * diff).astype(bf16)
        dz_ref[1, :, here] = (grads[1] - inv_coef * diff).astype(bf16)
        return carry

    lax.fori_loop(0, columns // tile, one_tile, 0)


def dz_call(index, strips, z_slots, constants):
    n_col, n_batch = len(strips), len(z_slots)
    local_rows, columns = z_slots[0][0].shape
    tall = 2 * local_rows
    rows = local_rows * n_batch
    tile = min(256, columns)
    operands = [index] + list(strips) + [z for slot in z_slots for z in slot]
    return pl.pallas_call(
        functools.partial(dz_kernel, n_batch, n_col, tile, constants),
        out_shape=(
            jax.ShapeDtypeStruct((2, rows, columns), bf16),
            jax.ShapeDtypeStruct((8, 128), f32),
        ),
        in_specs=[IN_SMEM] + [IN_VMEM] * (len(operands) - 1),
        out_specs=(IN_VMEM, IN_VMEM),
        scratch_shapes=[
            pltpu.VMEM((n_batch, tall, strips[0].shape[2]), f32),
            pltpu.VMEM((2, rows, rows), bf16),
            pltpu.VMEM((rows, tile), bf16),
        ],
        compiler_params=params(24),
        cost_estimate=cost(4 * rows * rows * columns, 8 * rows * columns),
        name="embedding_gradient",
    )(*operands)


EXTRA = 16


def share_rows(share, width, kind):
    high = share.astype(bf16).astype(f32)
    middle = (share - high).astype(bf16).astype(f32)
    low = share - high - middle
    row = lax.broadcasted_iota(jnp.int32, (EXTRA, width), 0)
    rows = jnp.where(row == 0, high, jnp.where(row == 1, middle, jnp.where(row == 2, low, 0.0)))
    return rows.astype(kind)


def share_of(rows):
    return rows[0:1].astype(f32) + rows[1:2].astype(f32) + rows[2:3].astype(f32)


def d_act_kernel(count, adds, index_ref, dz_ref, share_ref, w_ref, *refs):
    local_rows, columns = dz_ref.shape[1] // adds[1], dz_ref.shape[2]
    tall = 2 * local_rows
    dz = jnp.concatenate([dz_ref[0, :local_rows], dz_ref[1, :local_rows]], axis=0)
    width = w_ref.shape[0] // adds[2]
    share = share_ref[0:1, 0:1]
    for j in range(count):
        part = lax.dot_general(
            dz,
            weight_rows(index_ref, w_ref, j, width),
            (((1,), (1,)), ((), ())),
            preferred_element_type=f32,
        )
        if not adds[0]:
            refs[0][j, :tall] = part.astype(refs[0].dtype)
            refs[0][j, tall:] = share_rows(share, width, refs[0].dtype)
        else:
            got = refs[0]
            out_ref = refs[j + 1]
            slot = (j + 1) % count
            out_ref[:tall] = (part + got[slot, :tall].astype(f32)).astype(out_ref.dtype)
            whole_share = share + share_of(got[slot, tall:])[:, 0:1]
            out_ref[tall:] = share_rows(whole_share, width, out_ref.dtype)


def d_act_call(index, dz, share, weight, n_batch, n_col, got):
    columns = weight.shape[1]
    width = weight.shape[0] // n_col
    tall = 2 * dz.shape[1] // n_batch
    count = n_col // 2
    operands = [index, dz, share, weight] + ([] if got is None else [got])
    if got is None:
        out_shape = (jax.ShapeDtypeStruct((count, tall + EXTRA, width), bf16),)
    else:
        out_shape = (jax.ShapeDtypeStruct((tall + EXTRA, width), bf16),) * (count - 1)
        out_shape += (jax.ShapeDtypeStruct((tall + EXTRA, width), f32),)
    return pl.pallas_call(
        functools.partial(d_act_kernel, count, (got is not None, n_batch, n_col)),
        out_shape=out_shape,
        in_specs=[IN_SMEM] + [IN_VMEM] * (len(operands) - 1),
        out_specs=(IN_VMEM,) * len(out_shape),
        compiler_params=params(8),
        cost_estimate=cost(2 * tall * width * columns * count, 2 * count * width * tall),
        name="d_act_matmul",
    )(*operands)


def weight_grad_kernel(groups, half, tile, place_ref, *refs):
    n_far, aliased = groups[-2:]
    near = [refs[g * half : (g + 1) * half] for g in range(3)]
    arrived = refs[3 * half : 3 * half + n_far]
    dz_ref = refs[3 * half + n_far]
    out_ref, act, product, sems = refs[3 * half + n_far + 1 + aliased :]
    local_rows = near[0][0].shape[0] // 2
    rows = dz_ref.shape[1]
    for e in range(half):

        @pl.when(place_ref[0] == e)
        def _():
            act[pl.ds(0, local_rows)] = near[0][e][:local_rows]
            act[pl.ds(rows, local_rows)] = near[0][e][local_rows:]
            at = local_rows
            for group in near[1:]:
                size = group[e].shape[0]
                act[pl.ds(at, size)] = group[e][...]
                at += size

    for s in range(n_far):
        act[pl.ds(rows + (s + 1) * local_rows, local_rows)] = arrived[s][...]
    width = act.shape[1]
    copies = []
    for i in range(width // tile):
        total = None
        for v in range(2):
            part = lax.dot_general(
                act[pl.ds(v * rows, rows), pl.ds(i * tile, tile)],
                dz_ref[v],
                (((0,), (0,)), ((), ())),
                preferred_element_type=f32,
            )
            total = part if total is None else total + part
        product[pl.ds(i * tile, tile)] = total
        start = pl.multiple_of(place_ref[1] * width + i * tile, tile)
        copies.append(
            pltpu.make_async_copy(
                product.at[pl.ds(i * tile, tile)], out_ref.at[pl.ds(start, tile)], sems.at[i]
            )
        )
        copies[-1].start()
    for copy in copies:
        copy.wait()


def weight_grad_call(place, near, arrived, dz, features, before):
    half = len(near[0])
    width = near[0][0].shape[1]
    _, rows, columns = dz.shape
    tile = min(256, width)
    operands = [place] + [x for group in near for x in group] + list(arrived) + [dz]
    specs = [IN_SMEM] + [IN_VMEM] * (len(operands) - 1)
    aliases = {}
    if before is not None:
        aliases = {len(operands): 0}
        operands.append(before)
        specs.append(ANYWHERE)
    return pl.pallas_call(
        functools.partial(
            weight_grad_kernel, (len(arrived), int(before is not None)), half, tile
        ),
        out_shape=jax.ShapeDtypeStruct((features, columns), f32),
        in_specs=specs,
        out_specs=ANYWHERE,
        scratch_shapes=[
            pltpu.VMEM((2 * rows, width), bf16),
            pltpu.VMEM((width, columns), f32),
            pltpu.SemaphoreType.DMA((width // tile,)),
        ],
        input_output_aliases=aliases,
        compiler_params=params(12),
        cost_estimate=cost(4 * rows * width * columns, 4 * width * columns),
        name="weight_gradient",
    )(*operands)


def gather_pieces(x, n_col):
    pieces = {0: x}
    for k in range(2, n_col, 2):
        pieces[k] = xor_send(x, "col", k)
    for k in range(0, n_col, 2):
        pieces[k + 1] = xor_send(pieces[k], "col", 1)
    return pieces


def shards(views, norm_scale_gain, norm_shift_bias, weight):
    n_batch = lax.axis_size("batch")
    n_col = lax.axis_size("col")
    b = lax.axis_index("batch")
    c = lax.axis_index("col")
    n_view, local_rows, width = views.shape
    features, columns = weight.shape
    E = columns * n_col
    rows = local_rows * n_batch
    tall = n_view * local_rows
    reach = n_batch // 2
    scale = rows * E / 128.0
    denom = float((rows - 1) ** 2 * E)
    evens = list(range(0, n_col, 2))
    odds = [k + 1 for k in evens]
    far = evens[1:]

    def places(ks):
        return jnp.stack([c ^ k for k in ks]).astype(jnp.int32)

    with jax.named_scope("weight_load"):
        held_weight = load_call(weight)
    with jax.named_scope("norm_stats"):
        hidden = views.astype(f32)
        local_mean = jnp.mean(hidden, axis=1)
        local_centred = hidden - local_mean[:, None, :]
        local_spread = jnp.sum(local_centred * local_centred, axis=1)
        stats = exchange(jnp.concatenate([local_mean, local_spread]), "batch")
        mean = sum(s[:n_view] for s in stats) / n_batch
        spread = sum(s[n_view:] + local_rows * jnp.square(s[:n_view] - mean) for s in stats)
        var = spread / rows
        inverse_deviation = (1.0 / jnp.sqrt(var + eps_norm))[:, None, :]
        normalised = (hidden - mean[:, None, :]) * inverse_deviation
        preactivation = norm_scale_gain * normalised + norm_shift_bias
        act = jax.nn.gelu(preactivation, approximate=True).astype(bf16)
    with jax.named_scope("act_gather"):
        pieces = gather_pieces(act.reshape(tall, width), n_col)
        ring = [act[0]]
        for _ in range(1, n_batch):
            ring.append(ring_send(ring[-1], "batch", 1))
        ring = lax.optimization_barrier(ring)
        near_pieces = gather_pieces(jnp.concatenate(ring[1 : reach + 1]), n_col)
        last_pieces = gather_pieces(jnp.concatenate(ring[reach + 1 :]), n_col)
    with jax.named_scope("z"):

        def z_of(source, groups):
            total = None
            for i, ks in enumerate(groups):
                total = z_call(
                    places(ks),
                    [source[k] for k in ks],
                    held_weight,
                    total,
                    i == len(groups) - 1,
                    local_rows,
                )
            return total

        z_own0, z_own1, z_sum = z_of(pieces, [[0, 1], far, [k + 1 for k in far]])
        *z_near, _ = z_of(near_pieces, [evens, odds])
        *z_last, _ = z_of(last_pieces, [evens, odds])
    with jax.named_scope("z_ring"):
        z_ring = [z_own1]
        for _ in range(1, n_batch):
            z_ring.append(ring_send(z_ring[-1], "batch", 1))
        sums = [z_sum] + [ring_send(z_sum, "batch", d) for d in range(1, n_batch)]
        slots = [list(pair) for pair in zip([z_own0] + z_near + z_last, z_ring)]
    with jax.named_scope("kernel"):
        everyone = places(range(n_col))
        even_part, odd_part = strip_call(everyone, slots[: reach + 1], sums, rows, n_col)
        even_part = even_part + xor_send(odd_part, "col", 1)
        strip = even_part[0]
        for k in far:
            strip = strip + xor_send(even_part[k // 2], "col", k)
        strip, slots[reach + 1 :] = lax.optimization_barrier((strip, slots[reach + 1 :]))
        block = lax.broadcasted_iota(jnp.int32, (1, strip.shape[1]), 1) // local_rows
        twice = jnp.where((block > 0) & (block < n_batch - reach), 2.0, 1.0)
        block_share = jnp.sum(strip * strip * twice) / denom
        mine = strip.astype(bf16)
        mine = jnp.stack([mine] + [ring_send(mine, "batch", d) for d in range(1, n_batch)])
        strips = gather_pieces(mine, n_col)
        strips, held_back = lax.optimization_barrier((strips, [pieces[k] for k in evens]))
    with jax.named_scope("dz"):
        constants = (
            4.0 * scale / denom,
            25.0 * scale / (2.0 * E * (rows - 1)),
            50.0 * scale / (rows * E),
            25.0 / (rows * E) / n_batch,
            25.0 / (2 * E) / n_batch,
            1.0 / denom / n_batch,
        )
        dz, share = dz_call(everyone, [strips[k] for k in range(n_col)], slots, constants)
        share = share + block_share
    with jax.named_scope("d_act"):
        (away,) = d_act_call(places(odds), dz, share, held_weight, n_batch, n_col, None)
        got = xor_send(away, "col", 1)
        *sends, d_act = d_act_call(
            places(far + [0]), dz, share, held_weight, n_batch, n_col, got
        )
        arrived = [xor_send(part, "col", k) for k, part in zip(far, sends)]
    with jax.named_scope("grad_weight"):
        per_plane = n_col // n_batch
        position = jnp.where(b % 2 == 0, b // 2, n_batch - 1 - b // 2)

        def held_place(plane, i):
            return ((per_plane * plane + 2 * i) ^ (c - c % 2)) // 2

        grad_weight = None
        for i in range(per_plane // 2):
            mine = []
            for d in range(1, n_batch):
                ahead = (position + d) % n_batch
                plane = jnp.where(ahead < (n_batch + 1) // 2, 2 * ahead, 2 * (n_batch - ahead) - 1)
                place = held_place(plane, i)
                block = held_back[0][local_rows:]
                for e in range(1, n_col // 2):
                    block = jnp.where(place == e, held_back[e][local_rows:], block)
                mine.append(ring_send(block, "batch", d))
            mine, d_act = lax.optimization_barrier((mine, d_act))
            other = [xor_send(x, "col", 1) for x in mine]
            for parity, ks, blocks in ((0, evens, mine), (1, odds, other)):
                row = 2 * i + (c % 2 if parity == 0 else 1 - c % 2)
                grad_weight = weight_grad_call(
                    jnp.stack([held_place(b, i), row]).astype(jnp.int32),
                    [[group[k] for k in ks] for group in (pieces, near_pieces, last_pieces)],
                    blocks,
                    dz,
                    features // n_batch,
                    grad_weight,
                )
    with jax.named_scope("norm_backward"):
        arrived, d_act, grad_weight = lax.optimization_barrier((arrived, d_act, grad_weight))
        shares = [share_of(part[tall:]) for part in [d_act] + arrived]
        while len(shares) > 1:
            shares = [x + y for x, y in zip(shares[::2], shares[1::2])]
        d_act = d_act[:tall]
        for part in arrived:
            d_act = d_act + part[:tall].astype(f32)
        d_pre = d_act.reshape(n_view, local_rows, width) * gelu_slope(preactivation)
        sums = jnp.concatenate(
            [
                jnp.sum(d_pre, axis=1),
                jnp.sum(d_pre * normalised, axis=1),
                jnp.broadcast_to(shares[0], (2 * n_view, width)),
            ]
        )
        both = sum(exchange(sums, "batch"))
        sum_b, sum_g = both[:n_view], both[n_view : 2 * n_view]
        loss = jnp.max(both[2 * n_view :])
        grad_bias = jnp.sum(sum_b, axis=0)
        grad_gain = jnp.sum(sum_g, axis=0)
        views_gradient = (
            norm_scale_gain
            * (d_pre - sum_b[:, None, :] / rows - normalised * sum_g[:, None, :] / rows)
            * inverse_deviation
        )
    return (loss, grad_weight, grad_gain, grad_bias, views_gradient)


def solution(mesh):
    placed = (P(None, "batch", "col"), P("col"), P("col"), P(None, "col"))
    return jax.shard_map(
        shards,
        mesh=mesh,
        in_specs=placed,
        out_specs=(P(), P("batch", "col"), P("col"), P("col"), P(None, "batch", "col")),
        check_vma=False,
    )
```

```python
import functools

import jax
import jax.numpy as jnp
from jax import lax
from jax.experimental import pallas as pl
from jax.experimental.pallas import tpu as pltpu
from jax.sharding import PartitionSpec as P

eps_norm = 1e-05
eps_std = 0.0001
f32 = jnp.float32
bf16 = jnp.bfloat16
MIB = 1024 * 1024


def gelu_slope(preactivation):
    value, pullback = jax.vjp(lambda t: jax.nn.gelu(t, approximate=True), preactivation)
    return pullback(jnp.ones_like(value))[0]


def xor_send(x, axis, k):
    n = lax.axis_size(axis)
    return lax.ppermute(x, axis, [(i, i ^ k) for i in range(n)])


def ring_order(n):
    return list(range(0, n, 2)) + list(range(1, n, 2))[::-1]


def ring_send(x, axis, d):
    order = ring_order(lax.axis_size(axis))
    n = len(order)
    return lax.ppermute(x, axis, [(order[i], order[(i + d) % n]) for i in range(n)])


def exchange_sum(parts):
    parts = list(parts)
    while len(parts) > 1:
        parts = [x + y for x, y in zip(parts[::2], parts[1::2])]
    return parts[0]


def exchange(x, axis):
    return [x] + [xor_send(x, axis, k) for k in range(1, lax.axis_size(axis))]


def params(limit):
    return pltpu.CompilerParams(vmem_limit_bytes=limit * MIB)


def cost(flops, moved):
    return pl.CostEstimate(flops=flops, bytes_accessed=moved, transcendentals=0)


IN_SMEM = pl.BlockSpec(memory_space=pltpu.SMEM)
IN_VMEM = pl.BlockSpec(memory_space=pltpu.VMEM)
ANYWHERE = pl.BlockSpec(memory_space=pl.ANY)
LOADS = 8


def load_kernel(w_ref, out_ref, sems):
    step = w_ref.shape[0] // LOADS
    copies = [
        pltpu.make_async_copy(
            w_ref.at[pl.ds(i * step, step)], out_ref.at[pl.ds(i * step, step)], sems.at[i]
        )
        for i in range(LOADS)
    ]
    for copy in copies:
        copy.start()
    for copy in copies:
        copy.wait()


def load_call(weight):
    return pl.pallas_call(
        load_kernel,
        out_shape=pltpu.VMEM(weight.shape, weight.dtype),
        in_specs=[ANYWHERE],
        out_specs=IN_VMEM,
        scratch_shapes=[pltpu.SemaphoreType.DMA((LOADS,))],
        compiler_params=params(4),
        cost_estimate=cost(0, 4 * weight.size),
        name="weight_load",
    )(pltpu.with_memory_space_constraint(weight, pltpu.HBM))


def weight_rows(place_ref, w_ref, k, width):
    return w_ref[pl.ds(pl.multiple_of((place_ref[1] ^ k) * width, width), width), :]


def z_kernel(ks, first, last, local_rows, place_ref, *refs):
    count = len(ks)
    pieces, rest = refs[:count], list(refs[count:])
    w_ref = rest.pop(0)
    total = None if first else rest.pop(0)[...]
    width = pieces[0].shape[1]
    for j in range(count):
        part = jnp.dot(
            pieces[j][...], weight_rows(place_ref, w_ref, ks[j], width), preferred_element_type=f32
        )
        total = part if total is None else total + part
    if not last:
        rest[0][...] = total
        return
    z = total.astype(bf16)
    *z_refs, sum_ref = rest
    for v, ref in enumerate(z_refs):
        mine = z[v * local_rows : (v + 1) * local_rows]
        ref[...] = mine
        sum_ref[v : v + 1, :] = jnp.sum(mine.astype(f32), axis=0, keepdims=True)


def z_call(place, ks, pieces, weight, before, last, local_rows):
    count = len(ks)
    tall, width = pieces[0].shape
    columns = weight.shape[1]
    operands = [place] + list(pieces) + [weight] + ([] if before is None else [before])
    if last:
        groups = tall // local_rows
        out_shape = (jax.ShapeDtypeStruct((local_rows, columns), bf16),) * groups
        out_shape += (jax.ShapeDtypeStruct((groups, columns), f32),)
    else:
        out_shape = jax.ShapeDtypeStruct((tall, columns), f32)
    return pl.pallas_call(
        functools.partial(z_kernel, tuple(ks), before is None, last, local_rows),
        out_shape=out_shape,
        in_specs=[IN_SMEM] + [IN_VMEM] * (len(operands) - 1),
        out_specs=jax.tree.map(lambda _: IN_VMEM, out_shape),
        compiler_params=params(8),
        cost_estimate=cost(2 * tall * width * columns * count, 2 * tall * columns),
        name="z_matmul",
    )(*operands)


def strip_kernel(n_slots, n_sums, rows, n_col, place_ref, *refs):
    z_refs, sum_refs = refs[: 2 * n_slots], refs[2 * n_slots : 2 * n_slots + n_sums]
    even_ref, odd_ref, strip = refs[2 * n_slots + n_sums :]
    local_rows = z_refs[0].shape[0]
    mean = sum(s[...] for s in sum_refs) / rows
    for v in range(2):
        here = pl.ds(v * local_rows, local_rows)
        rounded = [(z[...].astype(f32) - mean[v : v + 1]).astype(bf16) for z in z_refs[v::2]]
        for u in range(n_slots):
            strip[here, pl.ds(u * local_rows, local_rows)] = lax.dot_general(
                rounded[0], rounded[u], (((1,), (1,)), ((), ())), preferred_element_type=f32
            )
    part = 2 * local_rows // n_col
    for k in range(n_col):
        start = pl.multiple_of((place_ref[1] ^ k) * part, part)
        (odd_ref if k % 2 else even_ref)[k // 2] = strip[pl.ds(start, part), :]


def strip_call(place, z_slots, sums, rows, n_col):
    local_rows, columns = z_slots[0][0].shape
    tall = 2 * local_rows
    wide = len(z_slots) * local_rows
    part = jax.ShapeDtypeStruct((n_col // 2, tall // n_col, wide), f32)
    operands = [place] + [z for slot in z_slots for z in slot] + list(sums)
    return pl.pallas_call(
        functools.partial(strip_kernel, len(z_slots), len(sums), rows, n_col),
        out_shape=(part, part),
        in_specs=[IN_SMEM] + [IN_VMEM] * (len(operands) - 1),
        out_specs=(IN_VMEM, IN_VMEM),
        scratch_shapes=[pltpu.VMEM((tall, wide), f32)],
        compiler_params=params(10),
        cost_estimate=cost(2 * tall * wide * columns, 2 * tall * columns * len(z_slots)),
        name="kernel_strip",
    )(*operands)


def dz_kernel(n_batch, n_col, tile, constants, place_ref, own_ref, *refs):
    coef, hinge_coef, inv_coef, inv_share, hinge_share, diag_share, block_share = constants
    strip_refs = refs[:n_col]
    z_refs = refs[n_col : n_col + 2 * n_batch]
    dz_ref, share_ref, strips, full, centred = refs[n_col + 2 * n_batch :]
    local_rows, columns = z_refs[0].shape
    rows = local_rows * n_batch
    reach = n_batch // 2
    own = own_ref[...]
    block = lax.broadcasted_iota(jnp.int32, own.shape, 1) // local_rows
    own = own * own * jnp.where((block > 0) & (block < n_batch - reach), 2.0, 1.0)
    own = jnp.sum(jnp.sum(own, axis=0, keepdims=True), axis=1, keepdims=True)
    share_ref[...] = jnp.broadcast_to(block_share * own, share_ref.shape)
    part = 2 * local_rows // n_col
    for k in range(n_col):
        start = pl.multiple_of((place_ref[1] ^ k) * part, part)
        for s in range(n_batch):
            strips[s, pl.ds(start, part), :] = strip_refs[k][s].astype(f32)
    for v in range(2):
        for s in range(n_batch):
            here = pl.ds(s * local_rows, local_rows)
            for u in range(reach + 1):
                t = (s + u) % n_batch
                there = pl.ds(t * local_rows, local_rows)
                block = strips[
                    s, pl.ds(v * local_rows, local_rows), pl.ds(u * local_rows, local_rows)
                ]
                full[v, here, there] = block.astype(bf16)
                if 0 < u < n_batch - reach:
                    full[v, there, here] = jnp.transpose(block).astype(bf16)

    def one_tile(j, carry):
        here = pl.ds(pl.multiple_of(j * tile, tile), tile)
        share = jnp.zeros((1, 1), f32)
        grads = []
        z_views = []
        for v in range(2):
            zf = jnp.concatenate([z[:, here].astype(f32) for z in z_refs[v::2]], axis=0)
            z_views.append(zf)
            zc = zf - jnp.sum(zf, axis=0, keepdims=True) / rows
            std = jnp.sqrt(jnp.sum(zc * zc, axis=0, keepdims=True) / (rows - 1) + eps_std)
            zcb = zc.astype(bf16)
            centred[...] = zcb
            rounded = zcb.astype(f32)
            diag = jnp.sum(rounded * rounded, axis=0, keepdims=True)
            moved = jnp.dot(full[v], centred[...], preferred_element_type=f32)
            pull = jnp.where(std < 1.0, hinge_coef, 0.0) / std
            summed = coef * (moved - rounded * diag) - zc * pull
            grads.append(summed - jnp.sum(summed, axis=0, keepdims=True) / rows)
            share += hinge_share * jnp.sum(jnp.maximum(1.0 - std, 0.0), axis=1, keepdims=True)
            share -= diag_share * jnp.sum(diag * diag, axis=1, keepdims=True)
        diff = z_views[0] - z_views[1]
        share += inv_share * jnp.sum(
            jnp.sum(diff * diff, axis=0, keepdims=True), axis=1, keepdims=True
        )
        share_ref[...] += jnp.broadcast_to(share, share_ref.shape)
        dz_ref[0, :, here] = (grads[0] + inv_coef * diff).astype(bf16)
        dz_ref[1, :, here] = (grads[1] - inv_coef * diff).astype(bf16)
        return carry

    lax.fori_loop(0, columns // tile, one_tile, 0)


def dz_call(place, own, strips, z_slots, constants):
    n_col, n_batch = len(strips), len(z_slots)
    local_rows, columns = z_slots[0][0].shape
    tall = 2 * local_rows
    rows = local_rows * n_batch
    tile = min(256, columns)
    operands = [place, own] + list(strips) + [z for slot in z_slots for z in slot]
    return pl.pallas_call(
        functools.partial(dz_kernel, n_batch, n_col, tile, constants),
        out_shape=(
            jax.ShapeDtypeStruct((2, rows, columns), bf16),
            jax.ShapeDtypeStruct((8, 128), f32),
        ),
        in_specs=[IN_SMEM] + [IN_VMEM] * (len(operands) - 1),
        out_specs=(IN_VMEM, IN_VMEM),
        scratch_shapes=[
            pltpu.VMEM((n_batch, tall, strips[0].shape[2]), f32),
            pltpu.VMEM((2, rows, rows), bf16),
            pltpu.VMEM((rows, tile), bf16),
        ],
        compiler_params=params(24),
        cost_estimate=cost(4 * rows * rows * columns, 8 * rows * columns),
        name="embedding_gradient",
    )(*operands)


EXTRA = 16


def share_rows(share, width, kind):
    high = share.astype(bf16).astype(f32)
    middle = (share - high).astype(bf16).astype(f32)
    low = share - high - middle
    row = lax.broadcasted_iota(jnp.int32, (EXTRA, width), 0)
    rows = jnp.where(row == 0, high, jnp.where(row == 1, middle, jnp.where(row == 2, low, 0.0)))
    return rows.astype(kind)


def share_of(rows):
    return rows[0:1].astype(f32) + rows[1:2].astype(f32) + rows[2:3].astype(f32)


def d_act_kernel(count, adds, place_ref, dz_ref, share_ref, w_ref, *refs):
    local_rows, columns = dz_ref.shape[1] // adds[1], dz_ref.shape[2]
    tall = 2 * local_rows
    dz = jnp.concatenate([dz_ref[0, :local_rows], dz_ref[1, :local_rows]], axis=0)
    width = w_ref.shape[0] // adds[2]
    share = share_ref[0:1, 0:1]
    for j in range(count):
        k = 2 * ((j + 1) % count) if adds[0] else 2 * j + 1
        part = lax.dot_general(
            dz,
            weight_rows(place_ref, w_ref, k, width),
            (((1,), (1,)), ((), ())),
            preferred_element_type=f32,
        )
        if not adds[0]:
            refs[0][j, :tall] = part.astype(refs[0].dtype)
            refs[0][j, tall:] = share_rows(share, width, refs[0].dtype)
        else:
            got = refs[0]
            out_ref = refs[j + 1]
            slot = (j + 1) % count
            out_ref[:tall] = (part + got[slot, :tall].astype(f32)).astype(out_ref.dtype)
            whole_share = share + share_of(got[slot, tall:])[:, 0:1]
            out_ref[tall:] = share_rows(whole_share, width, out_ref.dtype)


def d_act_call(place, dz, share, weight, n_batch, n_col, got):
    columns = weight.shape[1]
    width = weight.shape[0] // n_col
    tall = 2 * dz.shape[1] // n_batch
    count = n_col // 2
    operands = [place, dz, share, weight] + ([] if got is None else [got])
    if got is None:
        out_shape = (jax.ShapeDtypeStruct((count, tall + EXTRA, width), bf16),)
    else:
        out_shape = (jax.ShapeDtypeStruct((tall + EXTRA, width), bf16),) * (count - 1)
        out_shape += (jax.ShapeDtypeStruct((tall + EXTRA, width), f32),)
    return pl.pallas_call(
        functools.partial(d_act_kernel, count, (got is not None, n_batch, n_col)),
        out_shape=out_shape,
        in_specs=[IN_SMEM] + [IN_VMEM] * (len(operands) - 1),
        out_specs=(IN_VMEM,) * len(out_shape),
        compiler_params=params(8),
        cost_estimate=cost(2 * tall * width * columns * count, 2 * count * width * tall),
        name="d_act_matmul",
    )(*operands)


def held_place(plane, c, block, n_col, n_batch):
    return (((n_col // n_batch) * plane + 2 * block) ^ (c - (c & 1))) >> 1


def pick_kernel(n_batch, n_col, local_rows, place_ref, *refs):
    half = n_col // 2
    pieces, outs = refs[:half], refs[half:]
    b, c = place_ref[0], place_ref[1]
    position = jnp.where((b & 1) == 0, b >> 1, n_batch - 1 - (b >> 1))
    i = 0
    for block in range(n_col // n_batch // 2):
        for d in range(1, n_batch):
            ahead = position + d
            ahead = jnp.where(ahead >= n_batch, ahead - n_batch, ahead)
            plane = jnp.where(2 * ahead < n_batch, 2 * ahead, 2 * (n_batch - ahead) - 1)
            chosen = held_place(plane, c, block, n_col, n_batch)
            for e in range(half):

                @pl.when(chosen == e)
                def _():
                    outs[i][...] = pieces[e][local_rows:]

            i += 1


def pick_call(place, pieces, n_batch, n_col):
    tall, width = pieces[0].shape
    count = n_col // n_batch // 2 * (n_batch - 1)
    out_shape = (jax.ShapeDtypeStruct((tall // 2, width), bf16),) * count
    return pl.pallas_call(
        functools.partial(pick_kernel, n_batch, n_col, tall // 2),
        out_shape=out_shape,
        in_specs=[IN_SMEM] + [IN_VMEM] * len(pieces),
        out_specs=(IN_VMEM,) * count,
        compiler_params=params(4),
        cost_estimate=cost(0, tall * width * count),
        name="pick_blocks",
    )(place, *pieces)


def weight_grad_kernel(n_far, aliased, half, tile, which, place_ref, *refs):
    near = [refs[:half], refs[half : 2 * half]]
    arrived = refs[2 * half : 2 * half + n_far]
    dz_ref = refs[2 * half + n_far]
    out_ref, act, product, sems = refs[2 * half + n_far + 1 + aliased :]
    block, parity = which
    chosen = held_place(place_ref[0], place_ref[1], block, 2 * half, n_far + 1)
    out_row = 2 * block + ((place_ref[1] & 1) ^ parity)
    local_rows = near[0][0].shape[0] // 2
    rows = dz_ref.shape[1]
    for e in range(half):

        @pl.when(chosen == e)
        def _():
            act[pl.ds(0, local_rows)] = near[0][e][:local_rows]
            act[pl.ds(rows, local_rows)] = near[0][e][local_rows:]
            act[pl.ds(local_rows, rows - local_rows)] = near[1][e][...]

    for s in range(n_far):
        act[pl.ds(rows + (s + 1) * local_rows, local_rows)] = arrived[s][...]
    width = act.shape[1]
    copies = []
    for i in range(width // tile):
        total = None
        for v in range(2):
            part = lax.dot_general(
                act[pl.ds(v * rows, rows), pl.ds(i * tile, tile)],
                dz_ref[v],
                (((0,), (0,)), ((), ())),
                preferred_element_type=f32,
            )
            total = part if total is None else total + part
        product[pl.ds(i * tile, tile)] = total
        start = pl.multiple_of(out_row * width + i * tile, tile)
        copies.append(
            pltpu.make_async_copy(
                product.at[pl.ds(i * tile, tile)], out_ref.at[pl.ds(start, tile)], sems.at[i]
            )
        )
        copies[-1].start()
    for copy in copies:
        copy.wait()


def weight_grad_call(place, which, near, arrived, dz, features, before):
    half = len(near[0])
    width = near[0][0].shape[1]
    _, rows, columns = dz.shape
    tile = min(256, width)
    operands = [place] + [x for group in near for x in group] + list(arrived) + [dz]
    specs = [IN_SMEM] + [IN_VMEM] * (len(operands) - 1)
    aliases = {}
    if before is not None:
        aliases = {len(operands): 0}
        operands.append(before)
        specs.append(ANYWHERE)
    return pl.pallas_call(
        functools.partial(
            weight_grad_kernel, len(arrived), int(before is not None), half, tile, which
        ),
        out_shape=jax.ShapeDtypeStruct((features, columns), f32),
        in_specs=specs,
        out_specs=ANYWHERE,
        scratch_shapes=[
            pltpu.VMEM((2 * rows, width), bf16),
            pltpu.VMEM((width, columns), f32),
            pltpu.SemaphoreType.DMA((width // tile,)),
        ],
        input_output_aliases=aliases,
        compiler_params=params(12),
        cost_estimate=cost(4 * rows * width * columns, 4 * width * columns),
        name="weight_gradient",
    )(*operands)


def gather_pieces(x, n_col):
    pieces = {0: x}
    for k in range(2, n_col, 2):
        pieces[k] = xor_send(x, "col", k)
    for k in range(0, n_col, 2):
        pieces[k + 1] = xor_send(pieces[k], "col", 1)
    return pieces


def shards(views, norm_scale_gain, norm_shift_bias, weight):
    n_batch = lax.axis_size("batch")
    n_col = lax.axis_size("col")
    place = jnp.stack([lax.axis_index("batch"), lax.axis_index("col")]).astype(jnp.int32)
    views, norm_scale_gain, norm_shift_bias, weight, place = lax.optimization_barrier(
        (views, norm_scale_gain, norm_shift_bias, weight, place)
    )
    n_view, local_rows, width = views.shape
    features, columns = weight.shape
    E = columns * n_col
    rows = local_rows * n_batch
    tall = n_view * local_rows
    reach = n_batch // 2
    scale = rows * E / 128.0
    denom = float((rows - 1) ** 2 * E)
    evens = list(range(0, n_col, 2))
    odds = [k + 1 for k in evens]
    far = evens[1:]

    with jax.named_scope("weight_load"):
        held_weight = load_call(weight)
    with jax.named_scope("norm_stats"):
        hidden = views.astype(f32)
        local_mean = jnp.mean(hidden, axis=1)
        local_centred = hidden - local_mean[:, None, :]
        local_spread = jnp.sum(local_centred * local_centred, axis=1)
        stats = exchange(jnp.concatenate([local_mean, local_spread]), "batch")
        mean = exchange_sum(s[:n_view] for s in stats) / n_batch
        spread = exchange_sum(
            s[n_view:] + local_rows * jnp.square(s[:n_view] - mean) for s in stats
        )
        var = spread / rows
        inverse_deviation = (1.0 / jnp.sqrt(var + eps_norm))[:, None, :]
        normalised = (hidden - mean[:, None, :]) * inverse_deviation
        preactivation = norm_scale_gain * normalised + norm_shift_bias
        act = jax.nn.gelu(preactivation, approximate=True).astype(bf16)
    with jax.named_scope("act_gather"):
        pieces = gather_pieces(act.reshape(tall, width), n_col)
        ring = [act[0]]
        for _ in range(1, n_batch):
            ring.append(ring_send(ring[-1], "batch", 1))
        far_pieces = gather_pieces(jnp.concatenate(ring[1:]), n_col)
    with jax.named_scope("z"):

        def z_of(source, groups):
            total = None
            for i, ks in enumerate(groups):
                total = z_call(
                    place,
                    ks,
                    [source[k] for k in ks],
                    held_weight,
                    total,
                    i == len(groups) - 1,
                    local_rows,
                )
            return total

        z_own0, z_own1, z_sum = z_of(pieces, [[0, 1], far, [k + 1 for k in far]])
        *z_far, _ = z_of(far_pieces, [evens, odds])
    with jax.named_scope("z_ring"):
        z_ring = [z_own1]
        for _ in range(1, n_batch):
            z_ring.append(ring_send(z_ring[-1], "batch", 1))
        sums = exchange(z_sum, "batch")
        slots = [list(pair) for pair in zip([z_own0] + z_far, z_ring)]
    with jax.named_scope("kernel"):
        even_part, odd_part = strip_call(place, slots[: reach + 1], sums, rows, n_col)
        even_part = even_part + xor_send(odd_part, "col", 1)
        strip = even_part[0]
        for k in far:
            strip = strip + xor_send(even_part[k // 2], "col", k)
        strip, z_ring[reach + 1 :] = lax.optimization_barrier((strip, z_ring[reach + 1 :]))
        slots = [list(pair) for pair in zip([z_own0] + z_far, z_ring)]
        mine = strip.astype(bf16)
        mine = jnp.stack([mine] + [ring_send(mine, "batch", d) for d in range(1, n_batch)])
        mine, held_back = lax.optimization_barrier((mine, [pieces[k] for k in evens]))
        strips = gather_pieces(mine, n_col)
        picked = pick_call(place, held_back, n_batch, n_col)
        blocks = [
            ring_send(x, "batch", 1 + i % (n_batch - 1)) for i, x in enumerate(picked)
        ]
        strips, blocks = lax.optimization_barrier((strips, blocks))
    with jax.named_scope("dz"):
        constants = (
            4.0 * scale / denom,
            25.0 * scale / (2.0 * E * (rows - 1)),
            50.0 * scale / (rows * E),
            25.0 / (rows * E) / n_batch,
            25.0 / (2 * E) / n_batch,
            1.0 / denom / n_batch,
            1.0 / denom,
        )
        dz, share = dz_call(place, strip, [strips[k] for k in range(n_col)], slots, constants)
    with jax.named_scope("d_act"):
        (away,) = d_act_call(place, dz, share, held_weight, n_batch, n_col, None)
        got = xor_send(away, "col", 1)
        *sends, d_act = d_act_call(place, dz, share, held_weight, n_batch, n_col, got)
        arrived = [xor_send(part, "col", k) for k, part in zip(far, sends)]
    with jax.named_scope("grad_weight"):
        grad_weight = None
        for block in range(n_col // n_batch // 2):
            mine = blocks[block * (n_batch - 1) : (block + 1) * (n_batch - 1)]
            other = [xor_send(x, "col", 1) for x in mine]
            for parity, ks, far_rows in ((0, evens, mine), (1, odds, other)):
                grad_weight = weight_grad_call(
                    place,
                    (block, parity),
                    [[group[k] for k in ks] for group in (pieces, far_pieces)],
                    far_rows,
                    dz,
                    features // n_batch,
                    grad_weight,
                )
    with jax.named_scope("norm_backward"):
        arrived, d_act, grad_weight = lax.optimization_barrier((arrived, d_act, grad_weight))
        share = exchange_sum(share_of(part[tall:]) for part in [d_act] + arrived)
        d_act = d_act[:tall]
        for part in arrived:
            d_act = d_act + part[:tall].astype(f32)
        d_pre = d_act.reshape(n_view, local_rows, width) * gelu_slope(preactivation)
        sums = jnp.concatenate(
            [
                jnp.sum(d_pre, axis=1),
                jnp.sum(d_pre * normalised, axis=1),
                jnp.broadcast_to(share, (2 * n_view, width)),
            ]
        )
        both = exchange_sum(exchange(sums, "batch"))
        sum_b, sum_g = both[:n_view], both[n_view : 2 * n_view]
        loss = jnp.max(both[2 * n_view :])
        grad_bias = jnp.sum(sum_b, axis=0)
        grad_gain = jnp.sum(sum_g, axis=0)
        views_gradient = (
            norm_scale_gain
            * (d_pre - sum_b[:, None, :] / rows - normalised * sum_g[:, None, :] / rows)
            * inverse_deviation
        )
    return (loss, grad_weight, grad_gain, grad_bias, views_gradient)


def solution(mesh):
    placed = (P(None, "batch", "col"), P("col"), P("col"), P(None, "col"))
    return jax.shard_map(
        shards,
        mesh=mesh,
        in_specs=placed,
        out_specs=(P(), P("batch", "col"), P("col"), P("col"), P(None, "batch", "col")),
        check_vma=False,
    )
```

```python
import functools

import jax
import jax.numpy as jnp
from jax import lax
from jax.experimental import pallas as pl
from jax.experimental.pallas import tpu as pltpu
from jax.sharding import PartitionSpec as P

eps_norm = 1e-05
eps_std = 0.0001
f32 = jnp.float32
bf16 = jnp.bfloat16
MIB = 1024 * 1024


def gelu_slope(preactivation):
    value, pullback = jax.vjp(lambda t: jax.nn.gelu(t, approximate=True), preactivation)
    return pullback(jnp.ones_like(value))[0]


def xor_send(x, axis, k):
    n = lax.axis_size(axis)
    return lax.ppermute(x, axis, [(i, i ^ k) for i in range(n)])


def ring_order(n):
    return list(range(0, n, 2)) + list(range(1, n, 2))[::-1]


def ring_send(x, axis, d):
    order = ring_order(lax.axis_size(axis))
    n = len(order)
    return lax.ppermute(x, axis, [(order[i], order[(i + d) % n]) for i in range(n)])


def exchange_sum(parts):
    parts = list(parts)
    while len(parts) > 1:
        parts = [x + y for x, y in zip(parts[::2], parts[1::2])]
    return parts[0]


def exchange(x, axis):
    return [x] + [xor_send(x, axis, k) for k in range(1, lax.axis_size(axis))]


def params(limit):
    return pltpu.CompilerParams(vmem_limit_bytes=limit * MIB)


def cost(flops, moved):
    return pl.CostEstimate(flops=flops, bytes_accessed=moved, transcendentals=0)


IN_SMEM = pl.BlockSpec(memory_space=pltpu.SMEM)
IN_VMEM = pl.BlockSpec(memory_space=pltpu.VMEM)
ANYWHERE = pl.BlockSpec(memory_space=pl.ANY)
LOADS = 8


def load_kernel(w_ref, out_ref, flag_ref, sems):
    flag_ref[...] = jnp.zeros_like(flag_ref)
    step = w_ref.shape[0] // LOADS
    copies = [
        pltpu.make_async_copy(
            w_ref.at[pl.ds(i * step, step)], out_ref.at[pl.ds(i * step, step)], sems.at[i]
        )
        for i in range(LOADS)
    ]
    for copy in copies:
        copy.start()
    for copy in copies:
        copy.wait()


def load_call(weight, flag_shape):
    return pl.pallas_call(
        load_kernel,
        out_shape=(
            pltpu.VMEM(weight.shape, weight.dtype),
            jax.ShapeDtypeStruct(flag_shape, f32),
        ),
        in_specs=[ANYWHERE],
        out_specs=(IN_VMEM, IN_VMEM),
        scratch_shapes=[pltpu.SemaphoreType.DMA((LOADS,))],
        compiler_params=params(4),
        cost_estimate=cost(0, 4 * weight.size),
        name="weight_load",
    )(pltpu.with_memory_space_constraint(weight, pltpu.HBM))


def weight_rows(place_ref, w_ref, k, width):
    return w_ref[pl.ds(pl.multiple_of((place_ref[1] ^ k) * width, width), width), :]


def z_kernel(ks, first, last, local_rows, place_ref, *refs):
    count = len(ks)
    pieces, rest = refs[:count], list(refs[count:])
    w_ref = rest.pop(0)
    total = None if first else rest.pop(0)[...]
    width = pieces[0].shape[1]
    for j in range(count):
        part = jnp.dot(
            pieces[j][...], weight_rows(place_ref, w_ref, ks[j], width), preferred_element_type=f32
        )
        total = part if total is None else total + part
    if not last:
        rest[0][...] = total
        return
    z = total.astype(bf16)
    *z_refs, sum_ref = rest
    for v, ref in enumerate(z_refs):
        mine = z[v * local_rows : (v + 1) * local_rows]
        ref[...] = mine
        sum_ref[v : v + 1, :] = jnp.sum(mine.astype(f32), axis=0, keepdims=True)


def z_call(place, ks, pieces, weight, before, last, local_rows):
    count = len(ks)
    tall, width = pieces[0].shape
    columns = weight.shape[1]
    operands = [place] + list(pieces) + [weight] + ([] if before is None else [before])
    if last:
        groups = tall // local_rows
        out_shape = (jax.ShapeDtypeStruct((local_rows, columns), bf16),) * groups
        out_shape += (jax.ShapeDtypeStruct((groups, columns), f32),)
    else:
        out_shape = jax.ShapeDtypeStruct((tall, columns), f32)
    return pl.pallas_call(
        functools.partial(z_kernel, tuple(ks), before is None, last, local_rows),
        out_shape=out_shape,
        in_specs=[IN_SMEM] + [IN_VMEM] * (len(operands) - 1),
        out_specs=jax.tree.map(lambda _: IN_VMEM, out_shape),
        compiler_params=params(8),
        cost_estimate=cost(2 * tall * width * columns * count, 2 * tall * columns),
        name="z_matmul",
    )(*operands)


def strip_kernel(n_batch, n_slots, rows, n_col, place_ref, *refs):
    z_refs = [refs[:n_batch], refs[n_batch : n_batch + n_slots]]
    sum_refs = refs[n_batch + n_slots : 2 * n_batch]
    even_ref, odd_ref, strip = refs[2 * n_batch :]
    local_rows = z_refs[0][0].shape[0]
    for v in range(2):
        here = pl.ds(v * local_rows, local_rows)
        zf = [z[...].astype(f32) for z in z_refs[v]]
        total = sum(jnp.sum(z, axis=0, keepdims=True) for z in zf)
        if v == 1:
            total = total + sum(s[1:2] for s in sum_refs)
        mean = total / rows
        rounded = [(z - mean).astype(bf16) for z in zf[:n_slots]]
        for u in range(n_slots):
            strip[here, pl.ds(u * local_rows, local_rows)] = lax.dot_general(
                rounded[0], rounded[u], (((1,), (1,)), ((), ())), preferred_element_type=f32
            )
    part = 2 * local_rows // n_col
    for k in range(n_col):
        start = pl.multiple_of((place_ref[1] ^ k) * part, part)
        (odd_ref if k % 2 else even_ref)[k // 2] = strip[pl.ds(start, part), :]


def strip_call(place, z0, z1, sums, rows, n_col):
    local_rows, columns = z0[0].shape
    tall = 2 * local_rows
    wide = len(z1) * local_rows
    part = jax.ShapeDtypeStruct((n_col // 2, tall // n_col, wide), f32)
    operands = [place] + list(z0) + list(z1) + list(sums)
    return pl.pallas_call(
        functools.partial(strip_kernel, len(z0), len(z1), rows, n_col),
        out_shape=(part, part),
        in_specs=[IN_SMEM] + [IN_VMEM] * (len(operands) - 1),
        out_specs=(IN_VMEM, IN_VMEM),
        scratch_shapes=[pltpu.VMEM((tall, wide), f32)],
        compiler_params=params(12),
        cost_estimate=cost(2 * tall * wide * columns, 2 * tall * columns * len(z0)),
        name="kernel_strip",
    )(*operands)


def dz_kernel(n_batch, n_col, tile, constants, place_ref, own_ref, *refs):
    coef, hinge_coef, inv_coef, inv_share, hinge_share, diag_share, block_share = constants
    strip_refs = refs[:n_col]
    z_refs = refs[n_col : n_col + 2 * n_batch]
    dz_ref, share_ref, strips, full, centred = refs[n_col + 2 * n_batch :]
    local_rows, columns = z_refs[0].shape
    rows = local_rows * n_batch
    reach = n_batch // 2
    own = own_ref[...]
    block = lax.broadcasted_iota(jnp.int32, own.shape, 1) // local_rows
    own = own * own * jnp.where((block > 0) & (block < n_batch - reach), 2.0, 1.0)
    own = jnp.sum(jnp.sum(own, axis=0, keepdims=True), axis=1, keepdims=True)
    share_ref[...] = jnp.broadcast_to(block_share * own, share_ref.shape)
    part = 2 * local_rows // n_col
    for k in range(n_col):
        start = pl.multiple_of((place_ref[1] ^ k) * part, part)
        for s in range(n_batch):
            strips[s, pl.ds(start, part), :] = strip_refs[k][s].astype(f32)
    for v in range(2):
        for s in range(n_batch):
            here = pl.ds(s * local_rows, local_rows)
            for u in range(reach + 1):
                t = (s + u) % n_batch
                there = pl.ds(t * local_rows, local_rows)
                block = strips[
                    s, pl.ds(v * local_rows, local_rows), pl.ds(u * local_rows, local_rows)
                ]
                full[v, here, there] = block.astype(bf16)
                if 0 < u < n_batch - reach:
                    full[v, there, here] = jnp.transpose(block).astype(bf16)

    def one_tile(j, carry):
        here = pl.ds(pl.multiple_of(j * tile, tile), tile)
        share = jnp.zeros((1, 1), f32)
        grads = []
        z_views = []
        for v in range(2):
            zf = jnp.concatenate([z[:, here].astype(f32) for z in z_refs[v::2]], axis=0)
            z_views.append(zf)
            zc = zf - jnp.sum(zf, axis=0, keepdims=True) / rows
            std = jnp.sqrt(jnp.sum(zc * zc, axis=0, keepdims=True) / (rows - 1) + eps_std)
            zcb = zc.astype(bf16)
            centred[...] = zcb
            rounded = zcb.astype(f32)
            diag = jnp.sum(rounded * rounded, axis=0, keepdims=True)
            moved = jnp.dot(full[v], centred[...], preferred_element_type=f32)
            pull = jnp.where(std < 1.0, hinge_coef, 0.0) / std
            summed = coef * (moved - rounded * diag) - zc * pull
            grads.append(summed - jnp.sum(summed, axis=0, keepdims=True) / rows)
            share += hinge_share * jnp.sum(jnp.maximum(1.0 - std, 0.0), axis=1, keepdims=True)
            share -= diag_share * jnp.sum(diag * diag, axis=1, keepdims=True)
        diff = z_views[0] - z_views[1]
        share += inv_share * jnp.sum(
            jnp.sum(diff * diff, axis=0, keepdims=True), axis=1, keepdims=True
        )
        share_ref[...] += jnp.broadcast_to(share, share_ref.shape)
        dz_ref[0, :, here] = (grads[0] + inv_coef * diff).astype(bf16)
        dz_ref[1, :, here] = (grads[1] - inv_coef * diff).astype(bf16)
        return carry

    lax.fori_loop(0, columns // tile, one_tile, 0)


def dz_call(place, own, strips, z_slots, constants):
    n_col, n_batch = len(strips), len(z_slots)
    local_rows, columns = z_slots[0][0].shape
    tall = 2 * local_rows
    rows = local_rows * n_batch
    tile = min(256, columns)
    operands = [place, own] + list(strips) + [z for slot in z_slots for z in slot]
    return pl.pallas_call(
        functools.partial(dz_kernel, n_batch, n_col, tile, constants),
        out_shape=(
            jax.ShapeDtypeStruct((2, rows, columns), bf16),
            jax.ShapeDtypeStruct((8, 128), f32),
        ),
        in_specs=[IN_SMEM] + [IN_VMEM] * (len(operands) - 1),
        out_specs=(IN_VMEM, IN_VMEM),
        scratch_shapes=[
            pltpu.VMEM((n_batch, tall, strips[0].shape[2]), f32),
            pltpu.VMEM((2, rows, rows), bf16),
            pltpu.VMEM((rows, tile), bf16),
        ],
        compiler_params=params(24),
        cost_estimate=cost(4 * rows * rows * columns, 8 * rows * columns),
        name="embedding_gradient",
    )(*operands)


EXTRA = 16


def share_rows(share, width, kind):
    high = share.astype(bf16).astype(f32)
    middle = (share - high).astype(bf16).astype(f32)
    low = share - high - middle
    row = lax.broadcasted_iota(jnp.int32, (EXTRA, width), 0)
    rows = jnp.where(row == 0, high, jnp.where(row == 1, middle, jnp.where(row == 2, low, 0.0)))
    return rows.astype(kind)


def share_of(rows):
    return rows[0:1].astype(f32) + rows[1:2].astype(f32) + rows[2:3].astype(f32)


def d_act_kernel(count, adds, place_ref, dz_ref, share_ref, w_ref, *refs):
    local_rows, columns = dz_ref.shape[1] // adds[1], dz_ref.shape[2]
    tall = 2 * local_rows
    dz = jnp.concatenate([dz_ref[0, :local_rows], dz_ref[1, :local_rows]], axis=0)
    width = w_ref.shape[0] // adds[2]
    share = share_ref[0:1, 0:1]
    for j in range(count):
        k = 2 * ((j + 1) % count) if adds[0] else 2 * j + 1
        part = lax.dot_general(
            dz,
            weight_rows(place_ref, w_ref, k, width),
            (((1,), (1,)), ((), ())),
            preferred_element_type=f32,
        )
        if not adds[0]:
            refs[0][j, :tall] = part.astype(refs[0].dtype)
            refs[0][j, tall:] = share_rows(share, width, refs[0].dtype)
        else:
            got = refs[0]
            out_ref = refs[j + 1]
            slot = (j + 1) % count
            out_ref[:tall] = (part + got[slot, :tall].astype(f32)).astype(out_ref.dtype)
            whole_share = share + share_of(got[slot, tall:])[:, 0:1]
            out_ref[tall:] = share_rows(whole_share, width, out_ref.dtype)


def d_act_call(place, dz, share, weight, n_batch, n_col, got):
    columns = weight.shape[1]
    width = weight.shape[0] // n_col
    tall = 2 * dz.shape[1] // n_batch
    count = n_col // 2
    operands = [place, dz, share, weight] + ([] if got is None else [got])
    if got is None:
        out_shape = (jax.ShapeDtypeStruct((count, tall + EXTRA, width), bf16),)
    else:
        out_shape = (jax.ShapeDtypeStruct((tall + EXTRA, width), bf16),) * (count - 1)
        out_shape += (jax.ShapeDtypeStruct((tall + EXTRA, width), f32),)
    return pl.pallas_call(
        functools.partial(d_act_kernel, count, (got is not None, n_batch, n_col)),
        out_shape=out_shape,
        in_specs=[IN_SMEM] + [IN_VMEM] * (len(operands) - 1),
        out_specs=(IN_VMEM,) * len(out_shape),
        compiler_params=params(8),
        cost_estimate=cost(2 * tall * width * columns * count, 2 * count * width * tall),
        name="d_act_matmul",
    )(*operands)


def held_place(plane, c, block, n_col, n_batch):
    return (((n_col // n_batch) * plane + 2 * block) ^ (c - (c & 1))) >> 1


def pick_kernel(n_batch, n_col, local_rows, place_ref, *refs):
    half = n_col // 2
    pieces, outs = refs[:half], refs[half:]
    b, c = place_ref[0], place_ref[1]
    position = jnp.where((b & 1) == 0, b >> 1, n_batch - 1 - (b >> 1))
    i = 0
    for block in range(n_col // n_batch // 2):
        for d in range(1, n_batch):
            ahead = position + d
            ahead = jnp.where(ahead >= n_batch, ahead - n_batch, ahead)
            plane = jnp.where(2 * ahead < n_batch, 2 * ahead, 2 * (n_batch - ahead) - 1)
            chosen = held_place(plane, c, block, n_col, n_batch)
            for e in range(half):

                @pl.when(chosen == e)
                def _():
                    outs[i][...] = pieces[e][local_rows:]

            i += 1


def pick_call(place, pieces, n_batch, n_col):
    tall, width = pieces[0].shape
    count = n_col // n_batch // 2 * (n_batch - 1)
    out_shape = (jax.ShapeDtypeStruct((tall // 2, width), bf16),) * count
    return pl.pallas_call(
        functools.partial(pick_kernel, n_batch, n_col, tall // 2),
        out_shape=out_shape,
        in_specs=[IN_SMEM] + [IN_VMEM] * len(pieces),
        out_specs=(IN_VMEM,) * count,
        compiler_params=params(4),
        cost_estimate=cost(0, tall * width * count),
        name="pick_blocks",
    )(place, *pieces)


def weight_grad_kernel(n_far, aliased, half, tile, which, place_ref, *refs):
    near = [refs[:half], refs[half : 2 * half]]
    arrived = refs[2 * half : 2 * half + n_far]
    dz_ref = refs[2 * half + n_far]
    out_ref, act, product, sems = refs[2 * half + n_far + 1 + aliased :]
    block, parity = which
    chosen = held_place(place_ref[0], place_ref[1], block, 2 * half, n_far + 1)
    out_row = 2 * block + ((place_ref[1] & 1) ^ parity)
    local_rows = near[0][0].shape[0] // 2
    rows = dz_ref.shape[1]
    for e in range(half):

        @pl.when(chosen == e)
        def _():
            act[pl.ds(0, local_rows)] = near[0][e][:local_rows]
            act[pl.ds(rows, local_rows)] = near[0][e][local_rows:]
            act[pl.ds(local_rows, rows - local_rows)] = near[1][e][...]

    for s in range(n_far):
        act[pl.ds(rows + (s + 1) * local_rows, local_rows)] = arrived[s][...]
    width = act.shape[1]
    copies = []
    for i in range(width // tile):
        total = None
        for v in range(2):
            part = lax.dot_general(
                act[pl.ds(v * rows, rows), pl.ds(i * tile, tile)],
                dz_ref[v],
                (((0,), (0,)), ((), ())),
                preferred_element_type=f32,
            )
            total = part if total is None else total + part
        product[pl.ds(i * tile, tile)] = total
        start = pl.multiple_of(out_row * width + i * tile, tile)
        copies.append(
            pltpu.make_async_copy(
                product.at[pl.ds(i * tile, tile)], out_ref.at[pl.ds(start, tile)], sems.at[i]
            )
        )
        copies[-1].start()
    for copy in copies:
        copy.wait()


def weight_grad_call(place, which, near, arrived, dz, features, before):
    half = len(near[0])
    width = near[0][0].shape[1]
    _, rows, columns = dz.shape
    tile = min(256, width)
    operands = [place] + [x for group in near for x in group] + list(arrived) + [dz]
    specs = [IN_SMEM] + [IN_VMEM] * (len(operands) - 1)
    aliases = {}
    if before is not None:
        aliases = {len(operands): 0}
        operands.append(before)
        specs.append(ANYWHERE)
    return pl.pallas_call(
        functools.partial(
            weight_grad_kernel, len(arrived), int(before is not None), half, tile, which
        ),
        out_shape=jax.ShapeDtypeStruct((features, columns), f32),
        in_specs=specs,
        out_specs=ANYWHERE,
        scratch_shapes=[
            pltpu.VMEM((2 * rows, width), bf16),
            pltpu.VMEM((width, columns), f32),
            pltpu.SemaphoreType.DMA((width // tile,)),
        ],
        input_output_aliases=aliases,
        compiler_params=params(12),
        cost_estimate=cost(4 * rows * width * columns, 4 * width * columns),
        name="weight_gradient",
    )(*operands)


def gather_pieces(x, n_col):
    return sibling_pieces(link_pieces(x, n_col), n_col)


def link_pieces(x, n_col):
    pieces = {0: x}
    for k in range(2, n_col, 2):
        pieces[k] = xor_send(x, "col", k)
    return pieces


def sibling_pieces(pieces, n_col):
    for k in range(0, n_col, 2):
        if k + 1 not in pieces:
            pieces[k + 1] = xor_send(pieces[k], "col", 1)
    return pieces


def shards(views, norm_scale_gain, norm_shift_bias, weight):
    n_batch = lax.axis_size("batch")
    n_col = lax.axis_size("col")
    place = jnp.stack([lax.axis_index("batch"), lax.axis_index("col")]).astype(jnp.int32)
    views, norm_scale_gain, norm_shift_bias, weight, place = lax.optimization_barrier(
        (views, norm_scale_gain, norm_shift_bias, weight, place)
    )
    n_view, local_rows, width = views.shape
    features, columns = weight.shape
    E = columns * n_col
    rows = local_rows * n_batch
    tall = n_view * local_rows
    reach = n_batch // 2
    scale = rows * E / 128.0
    denom = float((rows - 1) ** 2 * E)
    evens = list(range(0, n_col, 2))
    odds = [k + 1 for k in evens]
    far = evens[1:]

    with jax.named_scope("weight_load"):
        held_weight, loaded = load_call(weight, (2 * n_view, width))
    with jax.named_scope("norm_stats"):
        hidden = views.astype(f32)
        local_mean = jnp.mean(hidden, axis=1)
        local_centred = hidden - local_mean[:, None, :]
        local_spread = jnp.sum(local_centred * local_centred, axis=1)
        stats = exchange(jnp.concatenate([local_mean, local_spread]), "batch")
        stats[-1] = stats[-1] + loaded
        mean = exchange_sum(s[:n_view] for s in stats) / n_batch
        spread = exchange_sum(
            s[n_view:] + local_rows * jnp.square(s[:n_view] - mean) for s in stats
        )
        var = spread / rows
        inverse_deviation = (1.0 / jnp.sqrt(var + eps_norm))[:, None, :]
        normalised = (hidden - mean[:, None, :]) * inverse_deviation
        preactivation = norm_scale_gain * normalised + norm_shift_bias
        act = jax.nn.gelu(preactivation, approximate=True).astype(bf16)
    with jax.named_scope("act_gather"):
        pieces = link_pieces(act.reshape(tall, width), n_col)
        pieces[1] = xor_send(pieces[0], "col", 1)
        first, pieces[1] = lax.optimization_barrier((act[0], pieces[1]))
        others = [ring_send(first, "batch", d) for d in range(1, n_batch)]
        pieces = sibling_pieces(pieces, n_col)
        far_pieces = gather_pieces(jnp.concatenate(others), n_col)
    with jax.named_scope("z"):

        def z_of(source, groups):
            total = None
            for i, ks in enumerate(groups):
                total = z_call(
                    place,
                    ks,
                    [source[k] for k in ks],
                    held_weight,
                    total,
                    i == len(groups) - 1,
                    local_rows,
                )
            return total

        z_own0, z_own1, z_sum = z_of(pieces, [[0, 1], far, [k + 1 for k in far]])
        *z_far, _ = z_of(far_pieces, [evens, odds])
    with jax.named_scope("z_ring"):
        z_ring = [z_own1]
        for _ in range(1, n_batch):
            z_ring.append(ring_send(z_ring[-1], "batch", 1))
        sums = [ring_send(z_sum, "batch", d) for d in range(reach + 1, n_batch)]
        z_flat = [z_own0] + z_far
    with jax.named_scope("kernel"):
        even_part, odd_part = strip_call(place, z_flat, z_ring[: reach + 1], sums, rows, n_col)
        even_part = even_part + xor_send(odd_part, "col", 1)
        even_part, z_ring[reach + 1 :] = lax.optimization_barrier((even_part, z_ring[reach + 1 :]))
        strip = even_part[0]
        for k in far:
            strip = strip + xor_send(even_part[k // 2], "col", k)
        slots = list(zip(z_flat, z_ring))
        mine = strip.astype(bf16)
        mine = jnp.stack([mine] + [ring_send(mine, "batch", d) for d in range(1, n_batch)])
        mine, held_back = lax.optimization_barrier((mine, [pieces[k] for k in evens]))
        strips = gather_pieces(mine, n_col)
        picked = pick_call(place, held_back, n_batch, n_col)
        blocks = [
            ring_send(x, "batch", 1 + i % (n_batch - 1)) for i, x in enumerate(picked)
        ]
        strips, blocks[0] = lax.optimization_barrier((strips, blocks[0]))
    with jax.named_scope("dz"):
        constants = (
            4.0 * scale / denom,
            25.0 * scale / (2.0 * E * (rows - 1)),
            50.0 * scale / (rows * E),
            25.0 / (rows * E) / n_batch,
            25.0 / (2 * E) / n_batch,
            1.0 / denom / n_batch,
            1.0 / denom,
        )
        dz, share = dz_call(place, strip, [strips[k] for k in range(n_col)], slots, constants)
        dz, blocks[1:] = lax.optimization_barrier((dz, blocks[1:]))
    with jax.named_scope("d_act"):
        (away,) = d_act_call(place, dz, share, held_weight, n_batch, n_col, None)
        got = xor_send(away, "col", 1)
        *sends, d_act = d_act_call(place, dz, share, held_weight, n_batch, n_col, got)
        arrived = [xor_send(part, "col", k) for k, part in zip(far, sends)]
    with jax.named_scope("grad_weight"):
        grad_weight = None
        for block in range(n_col // n_batch // 2):
            mine = blocks[block * (n_batch - 1) : (block + 1) * (n_batch - 1)]
            other = [xor_send(x, "col", 1) for x in mine]
            for parity, ks, far_rows in ((0, evens, mine), (1, odds, other)):
                grad_weight = weight_grad_call(
                    place,
                    (block, parity),
                    [[group[k] for k in ks] for group in (pieces, far_pieces)],
                    far_rows,
                    dz,
                    features // n_batch,
                    grad_weight,
                )
    with jax.named_scope("norm_backward"):
        arrived, d_act, grad_weight = lax.optimization_barrier((arrived, d_act, grad_weight))
        share = exchange_sum(share_of(part[tall:]) for part in [d_act] + arrived)
        d_act = d_act[:tall]
        for part in arrived:
            d_act = d_act + part[:tall].astype(f32)
        d_pre = d_act.reshape(n_view, local_rows, width) * gelu_slope(preactivation)
        sums = jnp.concatenate(
            [
                jnp.sum(d_pre, axis=1),
                jnp.sum(d_pre * normalised, axis=1),
                jnp.broadcast_to(share, (2 * n_view, width)),
            ]
        )
        both = exchange_sum(exchange(sums, "batch"))
        sum_b, sum_g = both[:n_view], both[n_view : 2 * n_view]
        loss = jnp.max(both[2 * n_view :])
        grad_bias = jnp.sum(sum_b, axis=0)
        grad_gain = jnp.sum(sum_g, axis=0)
        views_gradient = (
            norm_scale_gain
            * (d_pre - sum_b[:, None, :] / rows - normalised * sum_g[:, None, :] / rows)
            * inverse_deviation
        )
    return (loss, grad_weight, grad_gain, grad_bias, views_gradient)


def solution(mesh):
    placed = (P(None, "batch", "col"), P("col"), P("col"), P(None, "col"))
    return jax.shard_map(
        shards,
        mesh=mesh,
        in_specs=placed,
        out_specs=(P(), P("batch", "col"), P("col"), P("col"), P(None, "batch", "col")),
        check_vma=False,
    )
```

```python
import functools

import jax
import jax.numpy as jnp
from jax import lax
from jax.experimental import pallas as pl
from jax.experimental.pallas import tpu as pltpu
from jax.sharding import PartitionSpec as P

eps_norm = 1e-05
eps_std = 0.0001
f32 = jnp.float32
bf16 = jnp.bfloat16
MIB = 1024 * 1024


def gelu_slope(preactivation):
    value, pullback = jax.vjp(lambda t: jax.nn.gelu(t, approximate=True), preactivation)
    return pullback(jnp.ones_like(value))[0]


def xor_send(x, axis, k):
    n = lax.axis_size(axis)
    return lax.ppermute(x, axis, [(i, i ^ k) for i in range(n)])


def ring_order(n):
    return list(range(0, n, 2)) + list(range(1, n, 2))[::-1]


def ring_send(x, axis, d):
    order = ring_order(lax.axis_size(axis))
    n = len(order)
    return lax.ppermute(x, axis, [(order[i], order[(i + d) % n]) for i in range(n)])


def exchange_sum(parts):
    parts = list(parts)
    while len(parts) > 1:
        parts = [x + y for x, y in zip(parts[::2], parts[1::2])]
    return parts[0]


def exchange(x, axis):
    return [x] + [xor_send(x, axis, k) for k in range(1, lax.axis_size(axis))]


def params(limit):
    return pltpu.CompilerParams(vmem_limit_bytes=limit * MIB)


def cost(flops, moved):
    return pl.CostEstimate(flops=flops, bytes_accessed=moved, transcendentals=0)


IN_SMEM = pl.BlockSpec(memory_space=pltpu.SMEM)
IN_VMEM = pl.BlockSpec(memory_space=pltpu.VMEM)
ANYWHERE = pl.BlockSpec(memory_space=pl.ANY)
LOADS = 8


def load_kernel(w_ref, out_ref, flag_ref, sems):
    flag_ref[...] = jnp.zeros_like(flag_ref)
    step = w_ref.shape[0] // LOADS
    copies = [
        pltpu.make_async_copy(
            w_ref.at[pl.ds(i * step, step)], out_ref.at[pl.ds(i * step, step)], sems.at[i]
        )
        for i in range(LOADS)
    ]
    for copy in copies:
        copy.start()
    for copy in copies:
        copy.wait()


def load_call(weight, flag_shape):
    return pl.pallas_call(
        load_kernel,
        out_shape=(
            pltpu.VMEM(weight.shape, weight.dtype),
            jax.ShapeDtypeStruct(flag_shape, f32),
        ),
        in_specs=[ANYWHERE],
        out_specs=(IN_VMEM, IN_VMEM),
        scratch_shapes=[pltpu.SemaphoreType.DMA((LOADS,))],
        compiler_params=params(4),
        cost_estimate=cost(0, 4 * weight.size),
        name="weight_load",
    )(pltpu.with_memory_space_constraint(weight, pltpu.HBM))


def weight_rows(place_ref, w_ref, k, width):
    return w_ref[pl.ds(pl.multiple_of((place_ref[1] ^ k) * width, width), width), :]


def z_kernel(ks, first, last, local_rows, place_ref, *refs):
    count = len(ks)
    pieces, rest = refs[:count], list(refs[count:])
    w_ref = rest.pop(0)
    total = None if first else rest.pop(0)[...]
    width = pieces[0].shape[1]
    for j in range(count):
        part = jnp.dot(
            pieces[j][...], weight_rows(place_ref, w_ref, ks[j], width), preferred_element_type=f32
        )
        total = part if total is None else total + part
    if not last:
        rest[0][...] = total
        return
    z = total.astype(bf16)
    *z_refs, sum_ref = rest
    for v, ref in enumerate(z_refs):
        mine = z[v * local_rows : (v + 1) * local_rows]
        ref[...] = mine
        sum_ref[v : v + 1, :] = jnp.sum(mine.astype(f32), axis=0, keepdims=True)


def z_call(place, ks, pieces, weight, before, last, local_rows):
    count = len(ks)
    tall, width = pieces[0].shape
    columns = weight.shape[1]
    operands = [place] + list(pieces) + [weight] + ([] if before is None else [before])
    if last:
        groups = tall // local_rows
        out_shape = (jax.ShapeDtypeStruct((local_rows, columns), bf16),) * groups
        out_shape += (jax.ShapeDtypeStruct((groups, columns), f32),)
    else:
        out_shape = jax.ShapeDtypeStruct((tall, columns), f32)
    return pl.pallas_call(
        functools.partial(z_kernel, tuple(ks), before is None, last, local_rows),
        out_shape=out_shape,
        in_specs=[IN_SMEM] + [IN_VMEM] * (len(operands) - 1),
        out_specs=jax.tree.map(lambda _: IN_VMEM, out_shape),
        compiler_params=params(8),
        cost_estimate=cost(2 * tall * width * columns * count, 2 * tall * columns),
        name="z_matmul",
    )(*operands)


def strip_kernel(n_batch, n_slots, rows, *refs):
    z_refs = [refs[:n_batch], refs[n_batch : n_batch + n_slots]]
    sum_refs = refs[n_batch + n_slots : 2 * n_batch]
    strip = refs[2 * n_batch]
    local_rows = z_refs[0][0].shape[0]
    for v in range(2):
        here = pl.ds(v * local_rows, local_rows)
        zf = [z[...].astype(f32) for z in z_refs[v]]
        total = sum(jnp.sum(z, axis=0, keepdims=True) for z in zf)
        if v == 1:
            total = total + sum(s[1:2] for s in sum_refs)
        mean = total / rows
        rounded = [(z - mean).astype(bf16) for z in zf[:n_slots]]
        for u in range(n_slots):
            strip[here, pl.ds(u * local_rows, local_rows)] = lax.dot_general(
                rounded[0], rounded[u], (((1,), (1,)), ((), ())), preferred_element_type=f32
            )


def strip_call(z0, z1, sums, rows):
    local_rows, columns = z0[0].shape
    tall = 2 * local_rows
    wide = len(z1) * local_rows
    operands = list(z0) + list(z1) + list(sums)
    return pl.pallas_call(
        functools.partial(strip_kernel, len(z0), len(z1), rows),
        out_shape=jax.ShapeDtypeStruct((tall, wide), f32),
        in_specs=[IN_VMEM] * len(operands),
        out_specs=IN_VMEM,
        compiler_params=params(12),
        cost_estimate=cost(2 * tall * wide * columns, 2 * tall * columns * len(z0)),
        name="kernel_strip",
    )(*operands)


def ring_position(plane, n):
    return jnp.where((plane & 1) == 0, plane >> 1, n - 1 - (plane >> 1))


def ring_plane(position, n):
    return jnp.where(2 * position < n, 2 * position, 2 * (n - position) - 1)


def dz_kernel(n_batch, n_col, tile, constants, place_ref, own_ref, *refs):
    coef, hinge_coef, inv_coef, inv_share, hinge_share, diag_share, block_share = constants
    strip_refs = refs[:n_col]
    z_refs = refs[n_col : n_col + 2 * n_batch]
    dz_ref, share_ref, strips, full, centred = refs[n_col + 2 * n_batch :]
    local_rows, columns = z_refs[0].shape
    rows = local_rows * n_batch
    reach = n_batch // 2
    own = own_ref[...]
    block = lax.broadcasted_iota(jnp.int32, own.shape, 1) // local_rows
    own = own * own * jnp.where((block > 0) & (block < n_batch - reach), 2.0, 1.0)
    own = jnp.sum(jnp.sum(own, axis=0, keepdims=True), axis=1, keepdims=True)
    share_ref[...] = jnp.broadcast_to(block_share * own, share_ref.shape)
    part = 2 * local_rows // n_col
    position = ring_position(place_ref[0], n_batch)
    for s in range(n_batch):
        behind = position - s
        plane = ring_plane(jnp.where(behind < 0, behind + n_batch, behind), n_batch)
        for k in range(n_col):
            start = pl.multiple_of((place_ref[1] ^ k) * part, part)
            strips[s, pl.ds(start, part), :] = strip_refs[k][plane].astype(f32)
    for v in range(2):
        for s in range(n_batch):
            here = pl.ds(s * local_rows, local_rows)
            for u in range(reach + 1):
                t = (s + u) % n_batch
                there = pl.ds(t * local_rows, local_rows)
                block = strips[
                    s, pl.ds(v * local_rows, local_rows), pl.ds(u * local_rows, local_rows)
                ]
                full[v, here, there] = block.astype(bf16)
                if 0 < u < n_batch - reach:
                    full[v, there, here] = jnp.transpose(block).astype(bf16)

    def one_tile(j, carry):
        here = pl.ds(pl.multiple_of(j * tile, tile), tile)
        share = jnp.zeros((1, 1), f32)
        grads = []
        z_views = []
        for v in range(2):
            zf = jnp.concatenate([z[:, here].astype(f32) for z in z_refs[v::2]], axis=0)
            z_views.append(zf)
            zc = zf - jnp.sum(zf, axis=0, keepdims=True) / rows
            std = jnp.sqrt(jnp.sum(zc * zc, axis=0, keepdims=True) / (rows - 1) + eps_std)
            zcb = zc.astype(bf16)
            centred[...] = zcb
            rounded = zcb.astype(f32)
            diag = jnp.sum(rounded * rounded, axis=0, keepdims=True)
            moved = jnp.dot(full[v], centred[...], preferred_element_type=f32)
            pull = jnp.where(std < 1.0, hinge_coef, 0.0) / std
            summed = coef * (moved - rounded * diag) - zc * pull
            grads.append(summed - jnp.sum(summed, axis=0, keepdims=True) / rows)
            share += hinge_share * jnp.sum(jnp.maximum(1.0 - std, 0.0), axis=1, keepdims=True)
            share -= diag_share * jnp.sum(diag * diag, axis=1, keepdims=True)
        diff = z_views[0] - z_views[1]
        share += inv_share * jnp.sum(
            jnp.sum(diff * diff, axis=0, keepdims=True), axis=1, keepdims=True
        )
        share_ref[...] += jnp.broadcast_to(share, share_ref.shape)
        dz_ref[0, :, here] = (grads[0] + inv_coef * diff).astype(bf16)
        dz_ref[1, :, here] = (grads[1] - inv_coef * diff).astype(bf16)
        return carry

    lax.fori_loop(0, columns // tile, one_tile, 0)


def dz_call(place, own, strips, z_slots, constants):
    n_col, n_batch = len(strips), len(z_slots)
    local_rows, columns = z_slots[0][0].shape
    tall = 2 * local_rows
    rows = local_rows * n_batch
    tile = min(256, columns)
    operands = [place, own] + list(strips) + [z for slot in z_slots for z in slot]
    return pl.pallas_call(
        functools.partial(dz_kernel, n_batch, n_col, tile, constants),
        out_shape=(
            jax.ShapeDtypeStruct((2, rows, columns), bf16),
            jax.ShapeDtypeStruct((8, 128), f32),
        ),
        in_specs=[IN_SMEM] + [IN_VMEM] * (len(operands) - 1),
        out_specs=(IN_VMEM, IN_VMEM),
        scratch_shapes=[
            pltpu.VMEM((n_batch, tall, strips[0].shape[2]), f32),
            pltpu.VMEM((2, rows, rows), bf16),
            pltpu.VMEM((rows, tile), bf16),
        ],
        compiler_params=params(24),
        cost_estimate=cost(4 * rows * rows * columns, 8 * rows * columns),
        name="embedding_gradient",
    )(*operands)


EXTRA = 16


def share_rows(share, width, kind):
    high = share.astype(bf16).astype(f32)
    middle = (share - high).astype(bf16).astype(f32)
    low = share - high - middle
    row = lax.broadcasted_iota(jnp.int32, (EXTRA, width), 0)
    rows = jnp.where(row == 0, high, jnp.where(row == 1, middle, jnp.where(row == 2, low, 0.0)))
    return rows.astype(kind)


def share_of(rows):
    return rows[0:1].astype(f32) + rows[1:2].astype(f32) + rows[2:3].astype(f32)


def d_act_kernel(count, adds, place_ref, dz_ref, share_ref, w_ref, *refs):
    local_rows, columns = dz_ref.shape[1] // adds[1], dz_ref.shape[2]
    tall = 2 * local_rows
    dz = jnp.concatenate([dz_ref[0, :local_rows], dz_ref[1, :local_rows]], axis=0)
    width = w_ref.shape[0] // adds[2]
    share = share_ref[0:1, 0:1]
    for j in range(count):
        k = 2 * ((j + 1) % count) if adds[0] else 2 * j + 1
        part = lax.dot_general(
            dz,
            weight_rows(place_ref, w_ref, k, width),
            (((1,), (1,)), ((), ())),
            preferred_element_type=f32,
        )
        if not adds[0]:
            refs[0][j, :tall] = part.astype(refs[0].dtype)
            refs[0][j, tall:] = share_rows(share, width, refs[0].dtype)
        else:
            got = refs[0]
            out_ref = refs[j + 1]
            slot = (j + 1) % count
            out_ref[:tall] = (part + got[slot, :tall].astype(f32)).astype(out_ref.dtype)
            whole_share = share + share_of(got[slot, tall:])[:, 0:1]
            out_ref[tall:] = share_rows(whole_share, width, out_ref.dtype)


def d_act_call(place, dz, share, weight, n_batch, n_col, got):
    columns = weight.shape[1]
    width = weight.shape[0] // n_col
    tall = 2 * dz.shape[1] // n_batch
    count = n_col // 2
    operands = [place, dz, share, weight] + ([] if got is None else [got])
    if got is None:
        out_shape = (jax.ShapeDtypeStruct((count, tall + EXTRA, width), bf16),)
    else:
        out_shape = (jax.ShapeDtypeStruct((tall + EXTRA, width), bf16),) * (count - 1)
        out_shape += (jax.ShapeDtypeStruct((tall + EXTRA, width), f32),)
    return pl.pallas_call(
        functools.partial(d_act_kernel, count, (got is not None, n_batch, n_col)),
        out_shape=out_shape,
        in_specs=[IN_SMEM] + [IN_VMEM] * (len(operands) - 1),
        out_specs=(IN_VMEM,) * len(out_shape),
        compiler_params=params(8),
        cost_estimate=cost(2 * tall * width * columns * count, 2 * count * width * tall),
        name="d_act_matmul",
    )(*operands)


def held_place(plane, c, block, n_col, n_batch):
    return (((n_col // n_batch) * plane + 2 * block) ^ (c - (c & 1))) >> 1


def pick_kernel(n_batch, n_col, local_rows, place_ref, *refs):
    half = n_col // 2
    pieces, outs = refs[:half], refs[half:]
    b, c = place_ref[0], place_ref[1]
    position = ring_position(b, n_batch)
    i = 0
    for block in range(n_col // n_batch // 2):
        for d in range(1, n_batch):
            ahead = position + d
            ahead = jnp.where(ahead >= n_batch, ahead - n_batch, ahead)
            plane = ring_plane(ahead, n_batch)
            chosen = held_place(plane, c, block, n_col, n_batch)
            for e in range(half):

                @pl.when(chosen == e)
                def _():
                    outs[i][...] = pieces[e][local_rows:]

            i += 1


def pick_call(place, pieces, n_batch, n_col):
    tall, width = pieces[0].shape
    count = n_col // n_batch // 2 * (n_batch - 1)
    out_shape = (jax.ShapeDtypeStruct((tall // 2, width), bf16),) * count
    return pl.pallas_call(
        functools.partial(pick_kernel, n_batch, n_col, tall // 2),
        out_shape=out_shape,
        in_specs=[IN_SMEM] + [IN_VMEM] * len(pieces),
        out_specs=(IN_VMEM,) * count,
        compiler_params=params(4),
        cost_estimate=cost(0, tall * width * count),
        name="pick_blocks",
    )(place, *pieces)


def weight_grad_kernel(n_far, aliased, half, tile, which, place_ref, *refs):
    near = [refs[:half], refs[half : 2 * half]]
    arrived = refs[2 * half : 2 * half + n_far]
    dz_ref = refs[2 * half + n_far]
    out_ref, act, product, sems = refs[2 * half + n_far + 1 + aliased :]
    block, parity = which
    chosen = held_place(place_ref[0], place_ref[1], block, 2 * half, n_far + 1)
    out_row = 2 * block + ((place_ref[1] & 1) ^ parity)
    local_rows = near[0][0].shape[0] // 2
    rows = dz_ref.shape[1]
    for e in range(half):

        @pl.when(chosen == e)
        def _():
            act[pl.ds(0, local_rows)] = near[0][e][:local_rows]
            act[pl.ds(rows, local_rows)] = near[0][e][local_rows:]
            act[pl.ds(local_rows, rows - local_rows)] = near[1][e][...]

    for s in range(n_far):
        act[pl.ds(rows + (s + 1) * local_rows, local_rows)] = arrived[s][...]
    width = act.shape[1]
    copies = []
    for i in range(width // tile):
        total = None
        for v in range(2):
            part = lax.dot_general(
                act[pl.ds(v * rows, rows), pl.ds(i * tile, tile)],
                dz_ref[v],
                (((0,), (0,)), ((), ())),
                preferred_element_type=f32,
            )
            total = part if total is None else total + part
        product[pl.ds(i * tile, tile)] = total
        start = pl.multiple_of(out_row * width + i * tile, tile)
        copies.append(
            pltpu.make_async_copy(
                product.at[pl.ds(i * tile, tile)], out_ref.at[pl.ds(start, tile)], sems.at[i]
            )
        )
        copies[-1].start()
    for copy in copies:
        copy.wait()


def weight_grad_call(place, which, near, arrived, dz, features, before):
    half = len(near[0])
    width = near[0][0].shape[1]
    _, rows, columns = dz.shape
    tile = min(256, width)
    operands = [place] + [x for group in near for x in group] + list(arrived) + [dz]
    specs = [IN_SMEM] + [IN_VMEM] * (len(operands) - 1)
    aliases = {}
    if before is not None:
        aliases = {len(operands): 0}
        operands.append(before)
        specs.append(ANYWHERE)
    return pl.pallas_call(
        functools.partial(
            weight_grad_kernel, len(arrived), int(before is not None), half, tile, which
        ),
        out_shape=jax.ShapeDtypeStruct((features, columns), f32),
        in_specs=specs,
        out_specs=ANYWHERE,
        scratch_shapes=[
            pltpu.VMEM((2 * rows, width), bf16),
            pltpu.VMEM((width, columns), f32),
            pltpu.SemaphoreType.DMA((width // tile,)),
        ],
        input_output_aliases=aliases,
        compiler_params=params(12),
        cost_estimate=cost(4 * rows * width * columns, 4 * width * columns),
        name="weight_gradient",
    )(*operands)


def gather_pieces(x, n_col):
    return sibling_pieces(link_pieces(x, n_col), n_col)


def link_pieces(x, n_col):
    pieces = {0: x}
    for k in range(2, n_col, 2):
        pieces[k] = xor_send(x, "col", k)
    return pieces


def sibling_pieces(pieces, n_col):
    for k in range(0, n_col, 2):
        if k + 1 not in pieces:
            pieces[k + 1] = xor_send(pieces[k], "col", 1)
    return pieces


def shards(views, norm_scale_gain, norm_shift_bias, weight):
    n_batch = lax.axis_size("batch")
    n_col = lax.axis_size("col")
    place = jnp.stack([lax.axis_index("batch"), lax.axis_index("col")]).astype(jnp.int32)
    views, norm_scale_gain, norm_shift_bias, weight, place = lax.optimization_barrier(
        (views, norm_scale_gain, norm_shift_bias, weight, place)
    )
    n_view, local_rows, width = views.shape
    features, columns = weight.shape
    E = columns * n_col
    rows = local_rows * n_batch
    tall = n_view * local_rows
    reach = n_batch // 2
    scale = rows * E / 128.0
    denom = float((rows - 1) ** 2 * E)
    evens = list(range(0, n_col, 2))
    odds = [k + 1 for k in evens]
    far = evens[1:]

    with jax.named_scope("weight_load"):
        held_weight, loaded = load_call(weight, (2 * n_view, width))
    with jax.named_scope("norm_stats"):
        hidden = views.astype(f32)
        local_mean = jnp.mean(hidden, axis=1)
        local_centred = hidden - local_mean[:, None, :]
        local_spread = jnp.sum(local_centred * local_centred, axis=1)
        stats = exchange(jnp.concatenate([local_mean, local_spread]), "batch")
        stats[-1] = stats[-1] + loaded
        mean = exchange_sum(s[:n_view] for s in stats) / n_batch
        spread = exchange_sum(
            s[n_view:] + local_rows * jnp.square(s[:n_view] - mean) for s in stats
        )
        var = spread / rows
        inverse_deviation = (1.0 / jnp.sqrt(var + eps_norm))[:, None, :]
        normalised = (hidden - mean[:, None, :]) * inverse_deviation
        preactivation = norm_scale_gain * normalised + norm_shift_bias
        act = jax.nn.gelu(preactivation, approximate=True).astype(bf16)
    with jax.named_scope("act_gather"):
        pieces = link_pieces(act.reshape(tall, width), n_col)
        pieces[1] = xor_send(pieces[0], "col", 1)
        first, pieces[1] = lax.optimization_barrier((act[0], pieces[1]))
        others = [ring_send(first, "batch", d) for d in range(1, n_batch)]
        pieces = sibling_pieces(pieces, n_col)
        far_pieces = link_pieces(jnp.concatenate(others), n_col)
    with jax.named_scope("z"):

        def z_of(source, groups, total=None):
            for i, ks in enumerate(groups):
                total = z_call(
                    place,
                    ks,
                    [source[k] for k in ks],
                    held_weight,
                    total,
                    i == len(groups) - 1,
                    local_rows,
                )
            return total

        z_own0, z_own1, z_sum = z_of(pieces, [[0, 1], far, [k + 1 for k in far]])
        z_sum, held_back = lax.optimization_barrier((z_sum, [pieces[k] for k in evens]))
    with jax.named_scope("z_ring"):
        z_ring = [z_own1, ring_send(z_own1, "batch", 1)]
        z_ring[1], far_pieces[far[-1]] = lax.optimization_barrier((z_ring[1], far_pieces[far[-1]]))
        z_ring.append(ring_send(z_ring[1], "batch", 1))
        sums = [ring_send(z_sum, "batch", d) for d in range(reach + 1, n_batch)]
        picked = pick_call(place, held_back, n_batch, n_col)
        blocks = [
            ring_send(x, "batch", 1 + i % (n_batch - 1)) for i, x in enumerate(picked)
        ]
    with jax.named_scope("z_far"):
        start = z_call(
            place, [0, far[-1]], [far_pieces[0], far_pieces[far[-1]]], held_weight, None, False, local_rows
        )
        start, far_pieces[far[0]], z_ring[2] = lax.optimization_barrier(
            (start, far_pieces[far[0]], z_ring[2])
        )
        far_pieces = sibling_pieces(far_pieces, n_col)
        for _ in range(3, n_batch):
            z_ring.append(ring_send(z_ring[-1], "batch", 1))
        *z_far, _ = z_of(far_pieces, [far[:-1], odds], start)
        z_flat = [z_own0] + z_far
    with jax.named_scope("kernel"):
        strip = strip_call(z_flat, z_ring[: reach + 1], sums, rows)
        part = tall // n_col
        parts = lax.all_to_all(strip.reshape(n_col, part, -1), "col", 0, 0, tiled=True)
        parts, z_ring[reach + 1 :], blocks = lax.optimization_barrier(
            (parts, z_ring[reach + 1 :], blocks)
        )
        slots = list(zip(z_flat, z_ring))
        strip = jnp.sum(parts, axis=0)
        mine = jnp.broadcast_to(strip.astype(bf16)[None], (n_batch,) + strip.shape)
        mine = lax.all_to_all(mine, "batch", 0, 0, tiled=True)
        strips = gather_pieces(mine, n_col)
    with jax.named_scope("dz"):
        constants = (
            4.0 * scale / denom,
            25.0 * scale / (2.0 * E * (rows - 1)),
            50.0 * scale / (rows * E),
            25.0 / (rows * E) / n_batch,
            25.0 / (2 * E) / n_batch,
            1.0 / denom / n_batch,
            1.0 / denom,
        )
        dz, share = dz_call(place, strip, [strips[k] for k in range(n_col)], slots, constants)
    with jax.named_scope("d_act"):
        (away,) = d_act_call(place, dz, share, held_weight, n_batch, n_col, None)
        got = xor_send(away, "col", 1)
        *sends, d_act = d_act_call(place, dz, share, held_weight, n_batch, n_col, got)
        arrived = [xor_send(part, "col", k) for k, part in zip(far, sends)]
    with jax.named_scope("grad_weight"):
        grad_weight = None
        for block in range(n_col // n_batch // 2):
            mine = blocks[block * (n_batch - 1) : (block + 1) * (n_batch - 1)]
            other = [xor_send(x, "col", 1) for x in mine]
            for parity, ks, far_rows in ((0, evens, mine), (1, odds, other)):
                grad_weight = weight_grad_call(
                    place,
                    (block, parity),
                    [[group[k] for k in ks] for group in (pieces, far_pieces)],
                    far_rows,
                    dz,
                    features // n_batch,
                    grad_weight,
                )
    with jax.named_scope("norm_backward"):
        arrived, d_act, grad_weight = lax.optimization_barrier((arrived, d_act, grad_weight))
        share = exchange_sum(share_of(part[tall:]) for part in [d_act] + arrived)
        d_act = d_act[:tall]
        for part in arrived:
            d_act = d_act + part[:tall].astype(f32)
        d_pre = d_act.reshape(n_view, local_rows, width) * gelu_slope(preactivation)
        sums = jnp.concatenate(
            [
                jnp.sum(d_pre, axis=1),
                jnp.sum(d_pre * normalised, axis=1),
                jnp.broadcast_to(share, (2 * n_view, width)),
            ]
        )
        both = exchange_sum(exchange(sums, "batch"))
        sum_b, sum_g = both[:n_view], both[n_view : 2 * n_view]
        loss = jnp.max(both[2 * n_view :])
        grad_bias = jnp.sum(sum_b, axis=0)
        grad_gain = jnp.sum(sum_g, axis=0)
        views_gradient = (
            norm_scale_gain
            * (d_pre - sum_b[:, None, :] / rows - normalised * sum_g[:, None, :] / rows)
            * inverse_deviation
        )
    return (loss, grad_weight, grad_gain, grad_bias, views_gradient)


def solution(mesh):
    placed = (P(None, "batch", "col"), P("col"), P("col"), P(None, "col"))
    return jax.shard_map(
        shards,
        mesh=mesh,
        in_specs=placed,
        out_specs=(P(), P("batch", "col"), P("col"), P("col"), P(None, "batch", "col")),
        check_vma=False,
    )
```

```python
import functools

import jax
import jax.numpy as jnp
from jax import lax
from jax.experimental import pallas as pl
from jax.experimental.pallas import tpu as pltpu
from jax.sharding import PartitionSpec as P

eps_norm = 1e-05
eps_std = 0.0001
f32 = jnp.float32
bf16 = jnp.bfloat16
MIB = 1024 * 1024


def gelu_slope(preactivation):
    value, pullback = jax.vjp(lambda t: jax.nn.gelu(t, approximate=True), preactivation)
    return pullback(jnp.ones_like(value))[0]


def xor_send(x, axis, k):
    n = lax.axis_size(axis)
    return lax.ppermute(x, axis, [(i, i ^ k) for i in range(n)])


def ring_order(n):
    return list(range(0, n, 2)) + list(range(1, n, 2))[::-1]


def ring_send(x, axis, d):
    order = ring_order(lax.axis_size(axis))
    n = len(order)
    return lax.ppermute(x, axis, [(order[i], order[(i + d) % n]) for i in range(n)])


def exchange_sum(parts):
    parts = list(parts)
    while len(parts) > 1:
        parts = [x + y for x, y in zip(parts[::2], parts[1::2])]
    return parts[0]


def exchange(x, axis):
    return [x] + [xor_send(x, axis, k) for k in range(1, lax.axis_size(axis))]


def params(limit):
    return pltpu.CompilerParams(vmem_limit_bytes=limit * MIB)


def cost(flops, moved):
    return pl.CostEstimate(flops=flops, bytes_accessed=moved, transcendentals=0)


IN_SMEM = pl.BlockSpec(memory_space=pltpu.SMEM)
IN_VMEM = pl.BlockSpec(memory_space=pltpu.VMEM)
ANYWHERE = pl.BlockSpec(memory_space=pl.ANY)
LOADS = 8


def load_kernel(w_ref, out_ref, flag_ref, sems):
    flag_ref[...] = jnp.zeros_like(flag_ref)
    step = w_ref.shape[0] // LOADS
    copies = [
        pltpu.make_async_copy(
            w_ref.at[pl.ds(i * step, step)], out_ref.at[pl.ds(i * step, step)], sems.at[i]
        )
        for i in range(LOADS)
    ]
    for copy in copies:
        copy.start()
    for copy in copies:
        copy.wait()


def load_call(weight, flag_shape):
    return pl.pallas_call(
        load_kernel,
        out_shape=(
            pltpu.VMEM(weight.shape, weight.dtype),
            jax.ShapeDtypeStruct(flag_shape, f32),
        ),
        in_specs=[ANYWHERE],
        out_specs=(IN_VMEM, IN_VMEM),
        scratch_shapes=[pltpu.SemaphoreType.DMA((LOADS,))],
        compiler_params=params(4),
        cost_estimate=cost(0, 4 * weight.size),
        name="weight_load",
    )(pltpu.with_memory_space_constraint(weight, pltpu.HBM))


def weight_rows(place_ref, w_ref, k, width):
    return w_ref[pl.ds(pl.multiple_of((place_ref[1] ^ k) * width, width), width), :]


def z_kernel(ks, first, last, local_rows, place_ref, *refs):
    count = len(ks)
    pieces, rest = refs[:count], list(refs[count:])
    w_ref = rest.pop(0)
    total = None if first else rest.pop(0)[...]
    width = pieces[0].shape[1]
    for j in range(count):
        part = jnp.dot(
            pieces[j][...], weight_rows(place_ref, w_ref, ks[j], width), preferred_element_type=f32
        )
        total = part if total is None else total + part
    if not last:
        rest[0][...] = total
        return
    z = total.astype(bf16)
    *z_refs, sum_ref = rest
    for v, ref in enumerate(z_refs):
        mine = z[v * local_rows : (v + 1) * local_rows]
        ref[...] = mine
        sum_ref[v : v + 1, :] = jnp.sum(mine.astype(f32), axis=0, keepdims=True)


def z_call(place, ks, pieces, weight, before, last, local_rows):
    count = len(ks)
    tall, width = pieces[0].shape
    columns = weight.shape[1]
    operands = [place] + list(pieces) + [weight] + ([] if before is None else [before])
    if last:
        groups = tall // local_rows
        out_shape = (jax.ShapeDtypeStruct((local_rows, columns), bf16),) * groups
        out_shape += (jax.ShapeDtypeStruct((groups, columns), f32),)
    else:
        out_shape = jax.ShapeDtypeStruct((tall, columns), f32)
    return pl.pallas_call(
        functools.partial(z_kernel, tuple(ks), before is None, last, local_rows),
        out_shape=out_shape,
        in_specs=[IN_SMEM] + [IN_VMEM] * (len(operands) - 1),
        out_specs=jax.tree.map(lambda _: IN_VMEM, out_shape),
        compiler_params=params(8),
        cost_estimate=cost(2 * tall * width * columns * count, 2 * tall * columns),
        name="z_matmul",
    )(*operands)


def strip_kernel(n_batch, n_slots, rows, n_col, place_ref, *refs):
    z_refs = [refs[:n_batch], refs[n_batch : n_batch + n_slots]]
    sum_refs = refs[n_batch + n_slots : 2 * n_batch]
    even_ref, odd_ref, strip = refs[2 * n_batch :]
    local_rows = z_refs[0][0].shape[0]
    for v in range(2):
        here = pl.ds(v * local_rows, local_rows)
        zf = [z[...].astype(f32) for z in z_refs[v]]
        total = sum(jnp.sum(z, axis=0, keepdims=True) for z in zf)
        if v == 1:
            total = total + sum(s[1:2] for s in sum_refs)
        mean = total / rows
        rounded = [(z - mean).astype(bf16) for z in zf[:n_slots]]
        for u in range(n_slots):
            strip[here, pl.ds(u * local_rows, local_rows)] = lax.dot_general(
                rounded[0], rounded[u], (((1,), (1,)), ((), ())), preferred_element_type=f32
            )
    part = 2 * local_rows // n_col
    for k in range(n_col):
        start = pl.multiple_of((place_ref[1] ^ k) * part, part)
        (odd_ref if k % 2 else even_ref)[k // 2] = strip[pl.ds(start, part), :]


def strip_call(place, z0, z1, sums, rows, n_col):
    local_rows, columns = z0[0].shape
    tall = 2 * local_rows
    wide = len(z1) * local_rows
    part = jax.ShapeDtypeStruct((n_col // 2, tall // n_col, wide), f32)
    operands = [place] + list(z0) + list(z1) + list(sums)
    return pl.pallas_call(
        functools.partial(strip_kernel, len(z0), len(z1), rows, n_col),
        out_shape=(part, part),
        in_specs=[IN_SMEM] + [IN_VMEM] * (len(operands) - 1),
        out_specs=(IN_VMEM, IN_VMEM),
        scratch_shapes=[pltpu.VMEM((tall, wide), f32)],
        compiler_params=params(12),
        cost_estimate=cost(2 * tall * wide * columns, 2 * tall * columns * len(z0)),
        name="kernel_strip",
    )(*operands)


def dz_kernel(n_batch, n_col, tile, constants, place_ref, own_ref, *refs):
    coef, hinge_coef, inv_coef, inv_share, hinge_share, diag_share, block_share = constants
    strip_refs = refs[:n_col]
    z_refs = refs[n_col : n_col + 2 * n_batch]
    dz_ref, share_ref, strips, full, centred = refs[n_col + 2 * n_batch :]
    local_rows, columns = z_refs[0].shape
    rows = local_rows * n_batch
    reach = n_batch // 2
    own = own_ref[...]
    block = lax.broadcasted_iota(jnp.int32, own.shape, 1) // local_rows
    own = own * own * jnp.where((block > 0) & (block < n_batch - reach), 2.0, 1.0)
    own = jnp.sum(jnp.sum(own, axis=0, keepdims=True), axis=1, keepdims=True)
    share_ref[...] = jnp.broadcast_to(block_share * own, share_ref.shape)
    part = 2 * local_rows // n_col
    for k in range(n_col):
        start = pl.multiple_of((place_ref[1] ^ k) * part, part)
        for s in range(n_batch):
            strips[s, pl.ds(start, part), :] = strip_refs[k][s].astype(f32)
    for v in range(2):
        for s in range(n_batch):
            here = pl.ds(s * local_rows, local_rows)
            for u in range(reach + 1):
                t = (s + u) % n_batch
                there = pl.ds(t * local_rows, local_rows)
                block = strips[
                    s, pl.ds(v * local_rows, local_rows), pl.ds(u * local_rows, local_rows)
                ]
                full[v, here, there] = block.astype(bf16)
                if 0 < u < n_batch - reach:
                    full[v, there, here] = jnp.transpose(block).astype(bf16)

    def one_tile(j, carry):
        here = pl.ds(pl.multiple_of(j * tile, tile), tile)
        share = jnp.zeros((1, 1), f32)
        grads = []
        z_views = []
        for v in range(2):
            zf = jnp.concatenate([z[:, here].astype(f32) for z in z_refs[v::2]], axis=0)
            z_views.append(zf)
            zc = zf - jnp.sum(zf, axis=0, keepdims=True) / rows
            std = jnp.sqrt(jnp.sum(zc * zc, axis=0, keepdims=True) / (rows - 1) + eps_std)
            zcb = zc.astype(bf16)
            centred[...] = zcb
            rounded = zcb.astype(f32)
            diag = jnp.sum(rounded * rounded, axis=0, keepdims=True)
            moved = jnp.dot(full[v], centred[...], preferred_element_type=f32)
            pull = jnp.where(std < 1.0, hinge_coef, 0.0) / std
            summed = coef * (moved - rounded * diag) - zc * pull
            grads.append(summed - jnp.sum(summed, axis=0, keepdims=True) / rows)
            share += hinge_share * jnp.sum(jnp.maximum(1.0 - std, 0.0), axis=1, keepdims=True)
            share -= diag_share * jnp.sum(diag * diag, axis=1, keepdims=True)
        diff = z_views[0] - z_views[1]
        share += inv_share * jnp.sum(
            jnp.sum(diff * diff, axis=0, keepdims=True), axis=1, keepdims=True
        )
        share_ref[...] += jnp.broadcast_to(share, share_ref.shape)
        dz_ref[0, :, here] = (grads[0] + inv_coef * diff).astype(bf16)
        dz_ref[1, :, here] = (grads[1] - inv_coef * diff).astype(bf16)
        return carry

    lax.fori_loop(0, columns // tile, one_tile, 0)


def dz_call(place, own, strips, z_slots, constants):
    n_col, n_batch = len(strips), len(z_slots)
    local_rows, columns = z_slots[0][0].shape
    tall = 2 * local_rows
    rows = local_rows * n_batch
    tile = min(256, columns)
    operands = [place, own] + list(strips) + [z for slot in z_slots for z in slot]
    return pl.pallas_call(
        functools.partial(dz_kernel, n_batch, n_col, tile, constants),
        out_shape=(
            jax.ShapeDtypeStruct((2, rows, columns), bf16),
            jax.ShapeDtypeStruct((8, 128), f32),
        ),
        in_specs=[IN_SMEM] + [IN_VMEM] * (len(operands) - 1),
        out_specs=(IN_VMEM, IN_VMEM),
        scratch_shapes=[
            pltpu.VMEM((n_batch, tall, strips[0].shape[2]), f32),
            pltpu.VMEM((2, rows, rows), bf16),
            pltpu.VMEM((rows, tile), bf16),
        ],
        compiler_params=params(24),
        cost_estimate=cost(4 * rows * rows * columns, 8 * rows * columns),
        name="embedding_gradient",
    )(*operands)


EXTRA = 16


def share_rows(share, width, kind):
    high = share.astype(bf16).astype(f32)
    middle = (share - high).astype(bf16).astype(f32)
    low = share - high - middle
    row = lax.broadcasted_iota(jnp.int32, (EXTRA, width), 0)
    rows = jnp.where(row == 0, high, jnp.where(row == 1, middle, jnp.where(row == 2, low, 0.0)))
    return rows.astype(kind)


def share_of(rows):
    return rows[0:1].astype(f32) + rows[1:2].astype(f32) + rows[2:3].astype(f32)


def d_act_kernel(count, adds, place_ref, dz_ref, share_ref, w_ref, *refs):
    local_rows, columns = dz_ref.shape[1] // adds[1], dz_ref.shape[2]
    tall = 2 * local_rows
    dz = jnp.concatenate([dz_ref[0, :local_rows], dz_ref[1, :local_rows]], axis=0)
    width = w_ref.shape[0] // adds[2]
    share = share_ref[0:1, 0:1]
    for j in range(count):
        k = 2 * ((j + 1) % count) if adds[0] else 2 * j + 1
        part = lax.dot_general(
            dz,
            weight_rows(place_ref, w_ref, k, width),
            (((1,), (1,)), ((), ())),
            preferred_element_type=f32,
        )
        if not adds[0]:
            refs[0][j, :tall] = part.astype(refs[0].dtype)
            refs[0][j, tall:] = share_rows(share, width, refs[0].dtype)
        else:
            got = refs[0]
            out_ref = refs[j + 1]
            slot = (j + 1) % count
            out_ref[:tall] = (part + got[slot, :tall].astype(f32)).astype(out_ref.dtype)
            whole_share = share + share_of(got[slot, tall:])[:, 0:1]
            out_ref[tall:] = share_rows(whole_share, width, out_ref.dtype)


def d_act_call(place, dz, share, weight, n_batch, n_col, got):
    columns = weight.shape[1]
    width = weight.shape[0] // n_col
    tall = 2 * dz.shape[1] // n_batch
    count = n_col // 2
    operands = [place, dz, share, weight] + ([] if got is None else [got])
    if got is None:
        out_shape = (jax.ShapeDtypeStruct((count, tall + EXTRA, width), bf16),)
    else:
        out_shape = (jax.ShapeDtypeStruct((tall + EXTRA, width), bf16),) * (count - 1)
        out_shape += (jax.ShapeDtypeStruct((tall + EXTRA, width), f32),)
    return pl.pallas_call(
        functools.partial(d_act_kernel, count, (got is not None, n_batch, n_col)),
        out_shape=out_shape,
        in_specs=[IN_SMEM] + [IN_VMEM] * (len(operands) - 1),
        out_specs=(IN_VMEM,) * len(out_shape),
        compiler_params=params(8),
        cost_estimate=cost(2 * tall * width * columns * count, 2 * count * width * tall),
        name="d_act_matmul",
    )(*operands)


def held_place(plane, c, block, n_col, n_batch):
    return (((n_col // n_batch) * plane + 2 * block) ^ (c - (c & 1))) >> 1


def pick_kernel(n_batch, n_col, local_rows, place_ref, *refs):
    half = n_col // 2
    pieces, outs = refs[:half], refs[half:]
    b, c = place_ref[0], place_ref[1]
    position = jnp.where((b & 1) == 0, b >> 1, n_batch - 1 - (b >> 1))
    i = 0
    for block in range(n_col // n_batch // 2):
        for d in range(1, n_batch):
            ahead = position + d
            ahead = jnp.where(ahead >= n_batch, ahead - n_batch, ahead)
            plane = jnp.where(2 * ahead < n_batch, 2 * ahead, 2 * (n_batch - ahead) - 1)
            chosen = held_place(plane, c, block, n_col, n_batch)
            for e in range(half):

                @pl.when(chosen == e)
                def _():
                    outs[i][...] = pieces[e][local_rows:]

            i += 1


def pick_call(place, pieces, n_batch, n_col):
    tall, width = pieces[0].shape
    count = n_col // n_batch // 2 * (n_batch - 1)
    out_shape = (jax.ShapeDtypeStruct((tall // 2, width), bf16),) * count
    return pl.pallas_call(
        functools.partial(pick_kernel, n_batch, n_col, tall // 2),
        out_shape=out_shape,
        in_specs=[IN_SMEM] + [IN_VMEM] * len(pieces),
        out_specs=(IN_VMEM,) * count,
        compiler_params=params(4),
        cost_estimate=cost(0, tall * width * count),
        name="pick_blocks",
    )(place, *pieces)


def rows_product(act, dz, width, tile, write):
    for i in range(width // tile):
        write(
            i,
            lax.dot_general(
                act[:, pl.ds(i * tile, tile)],
                dz[...],
                (((0,), (0,)), ((), ())),
                preferred_element_type=f32,
            ),
        )


def weight_grad_kernel(n_batch, half, tile, block, place_ref, *refs):
    own, far = refs[:half], refs[half : 2 * half]
    dz_ref, out_ref, act = refs[2 * half :]
    local_rows = own[0].shape[0] // 2
    chosen = held_place(place_ref[0], place_ref[1], block, 2 * half, n_batch)
    for e in range(half):

        @pl.when(chosen == e)
        def _():
            act[:local_rows] = own[e][:local_rows]
            act[local_rows:] = far[e][...]

    def write(i, product):
        out_ref[pl.ds(i * tile, tile)] = product

    rows_product(act, dz_ref.at[0], act.shape[1], tile, write)


def weight_grad_call(place, n_batch, block, own, far, dz):
    width = own[0].shape[1]
    _, rows, columns = dz.shape
    tile = min(256, width)
    operands = [place] + list(own) + list(far) + [dz]
    return pl.pallas_call(
        functools.partial(weight_grad_kernel, n_batch, len(own), tile, block),
        out_shape=jax.ShapeDtypeStruct((width, columns), f32),
        in_specs=[IN_SMEM] + [IN_VMEM] * (len(operands) - 1),
        out_specs=IN_VMEM,
        scratch_shapes=[pltpu.VMEM((rows, width), bf16)],
        compiler_params=params(8),
        cost_estimate=cost(2 * rows * width * columns, 2 * rows * columns),
        name="weight_gradient_0",
    )(*operands)


def weight_grad_last_kernel(n_batch, half, tile, aliased, which, place_ref, *refs):
    own, blocks = refs[:half], refs[half : half + n_batch - 1]
    dz_ref, before_ref = refs[half + n_batch - 1 : half + n_batch + 1]
    out_ref, act, product, sems = refs[half + n_batch + 1 + aliased :]
    local_rows = own[0].shape[0] // 2
    block, parity = which
    chosen = held_place(place_ref[0], place_ref[1], block, 2 * half, n_batch)
    out_row = 2 * block + ((place_ref[1] & 1) ^ parity)
    for e in range(half):

        @pl.when(chosen == e)
        def _():
            act[:local_rows] = own[e][local_rows:]

    for s in range(n_batch - 1):
        act[pl.ds((s + 1) * local_rows, local_rows)] = blocks[s][...]
    width = act.shape[1]
    copies = []

    def write(i, part):
        here = pl.ds(i * tile, tile)
        product[here] = before_ref[here] + part
        start = pl.multiple_of(out_row * width + i * tile, tile)
        copies.append(
            pltpu.make_async_copy(product.at[here], out_ref.at[pl.ds(start, tile)], sems.at[i])
        )
        copies[-1].start()

    rows_product(act, dz_ref.at[1], width, tile, write)
    for copy in copies:
        copy.wait()


def weight_grad_last_call(place, which, own, blocks, dz, product, features, before):
    width = own[0].shape[1]
    _, rows, columns = dz.shape
    tile = min(256, width)
    operands = [place] + list(own) + list(blocks) + [dz, product]
    specs = [IN_SMEM] + [IN_VMEM] * (len(operands) - 1)
    aliases = {}
    if before is not None:
        aliases = {len(operands): 0}
        operands.append(before)
        specs.append(ANYWHERE)
    return pl.pallas_call(
        functools.partial(
            weight_grad_last_kernel,
            len(blocks) + 1,
            len(own),
            tile,
            int(before is not None),
            which,
        ),
        out_shape=jax.ShapeDtypeStruct((features, columns), f32),
        in_specs=specs,
        out_specs=ANYWHERE,
        scratch_shapes=[
            pltpu.VMEM((rows, width), bf16),
            pltpu.VMEM((width, columns), f32),
            pltpu.SemaphoreType.DMA((width // tile,)),
        ],
        input_output_aliases=aliases,
        compiler_params=params(10),
        cost_estimate=cost(2 * rows * width * columns, 4 * width * columns),
        name="weight_gradient_1",
    )(*operands)


def gather_pieces(x, n_col):
    return sibling_pieces(link_pieces(x, n_col), n_col)


def link_pieces(x, n_col):
    pieces = {0: x}
    for k in range(2, n_col, 2):
        pieces[k] = xor_send(x, "col", k)
    return pieces


def sibling_pieces(pieces, n_col):
    for k in range(0, n_col, 2):
        if k + 1 not in pieces:
            pieces[k + 1] = xor_send(pieces[k], "col", 1)
    return pieces


def shards(views, norm_scale_gain, norm_shift_bias, weight):
    n_batch = lax.axis_size("batch")
    n_col = lax.axis_size("col")
    place = jnp.stack([lax.axis_index("batch"), lax.axis_index("col")]).astype(jnp.int32)
    views, norm_scale_gain, norm_shift_bias, weight, place = lax.optimization_barrier(
        (views, norm_scale_gain, norm_shift_bias, weight, place)
    )
    n_view, local_rows, width = views.shape
    features, columns = weight.shape
    E = columns * n_col
    rows = local_rows * n_batch
    tall = n_view * local_rows
    reach = n_batch // 2
    scale = rows * E / 128.0
    denom = float((rows - 1) ** 2 * E)
    evens = list(range(0, n_col, 2))
    odds = [k + 1 for k in evens]
    far = evens[1:]

    with jax.named_scope("weight_load"):
        held_weight, loaded = load_call(weight, (2 * n_view, width))
    with jax.named_scope("norm_stats"):
        hidden = views.astype(f32)
        local_mean = jnp.mean(hidden, axis=1)
        local_centred = hidden - local_mean[:, None, :]
        local_spread = jnp.sum(local_centred * local_centred, axis=1)
        stats = exchange(jnp.concatenate([local_mean, local_spread]), "batch")
        stats[-1] = stats[-1] + loaded
        mean = exchange_sum(s[:n_view] for s in stats) / n_batch
        spread = exchange_sum(
            s[n_view:] + local_rows * jnp.square(s[:n_view] - mean) for s in stats
        )
        var = spread / rows
        inverse_deviation = (1.0 / jnp.sqrt(var + eps_norm))[:, None, :]
        normalised = (hidden - mean[:, None, :]) * inverse_deviation
        preactivation = norm_scale_gain * normalised + norm_shift_bias
        act = jax.nn.gelu(preactivation, approximate=True).astype(bf16)
    with jax.named_scope("act_gather"):
        pieces = link_pieces(act.reshape(tall, width), n_col)
        pieces[1] = xor_send(pieces[0], "col", 1)
        first, pieces[1] = lax.optimization_barrier((act[0], pieces[1]))
        others = [ring_send(first, "batch", d) for d in range(1, n_batch)]
        pieces = sibling_pieces(pieces, n_col)
        far_pieces = link_pieces(jnp.concatenate(others), n_col)
    with jax.named_scope("z"):

        def z_of(source, groups, total=None):
            for i, ks in enumerate(groups):
                total = z_call(
                    place,
                    ks,
                    [source[k] for k in ks],
                    held_weight,
                    total,
                    i == len(groups) - 1,
                    local_rows,
                )
            return total

        z_own0, z_own1, z_sum = z_of(pieces, [[0, 1], far, [k + 1 for k in far]])
        z_sum, held_back = lax.optimization_barrier((z_sum, [pieces[k] for k in evens]))
    with jax.named_scope("z_ring"):
        z_ring = [z_own1, ring_send(z_own1, "batch", 1)]
        z_ring[1], far_pieces[far[-1]] = lax.optimization_barrier((z_ring[1], far_pieces[far[-1]]))
        z_ring.append(ring_send(z_ring[1], "batch", 1))
        sums = [ring_send(z_sum, "batch", d) for d in range(reach + 1, n_batch)]
        picked = pick_call(place, held_back, n_batch, n_col)
        blocks = [
            ring_send(x, "batch", 1 + i % (n_batch - 1)) for i, x in enumerate(picked)
        ]
    with jax.named_scope("z_far"):
        start = z_call(
            place, [0, far[-1]], [far_pieces[0], far_pieces[far[-1]]], held_weight, None, False, local_rows
        )
        start, far_pieces[far[0]], z_ring[2] = lax.optimization_barrier(
            (start, far_pieces[far[0]], z_ring[2])
        )
        far_pieces = sibling_pieces(far_pieces, n_col)
        for _ in range(3, n_batch):
            z_ring.append(ring_send(z_ring[-1], "batch", 1))
        *z_far, _ = z_of(far_pieces, [far[:-1], odds], start)
        z_flat = [z_own0] + z_far
    with jax.named_scope("kernel"):
        even_part, odd_part = strip_call(place, z_flat, z_ring[: reach + 1], sums, rows, n_col)
        even_part = even_part + xor_send(odd_part, "col", 1)
        strip = even_part[0]
        for k in far:
            strip = strip + xor_send(even_part[k // 2], "col", k)
        mine = strip.astype(bf16)
        mine = jnp.stack([mine] + [ring_send(mine, "batch", d) for d in range(1, n_batch)])
        strips = gather_pieces(mine, n_col)
        slots = list(zip(z_flat, z_ring))
    with jax.named_scope("dz"):
        constants = (
            4.0 * scale / denom,
            25.0 * scale / (2.0 * E * (rows - 1)),
            50.0 * scale / (rows * E),
            25.0 / (rows * E) / n_batch,
            25.0 / (2 * E) / n_batch,
            1.0 / denom / n_batch,
            1.0 / denom,
        )
        dz, share = dz_call(place, strip, [strips[k] for k in range(n_col)], slots, constants)
    with jax.named_scope("d_act"):
        (away,) = d_act_call(place, dz, share, held_weight, n_batch, n_col, None)
        got = xor_send(away, "col", 1)
        *sends, d_act = d_act_call(place, dz, share, held_weight, n_batch, n_col, got)
        arrived = [xor_send(part, "col", k) for k, part in zip(far, sends)]
    with jax.named_scope("grad_weight"):
        sides = ((0, evens), (1, odds))
        products = {}
        for block in range(n_col // n_batch // 2):
            for parity, ks in sides:
                products[block, parity] = weight_grad_call(
                    place, n_batch, block, [pieces[k] for k in ks], [far_pieces[k] for k in ks], dz
                )
        arrived, blocks, products = lax.optimization_barrier((arrived, blocks, products))
        grad_weight = None
        for block in range(n_col // n_batch // 2):
            mine = blocks[block * (n_batch - 1) : (block + 1) * (n_batch - 1)]
            other = [xor_send(x, "col", 1) for x in mine]
            for (parity, ks), far_rows in zip(sides, (mine, other)):
                grad_weight = weight_grad_last_call(
                    place,
                    (block, parity),
                    [pieces[k] for k in ks],
                    far_rows,
                    dz,
                    products[block, parity],
                    features // n_batch,
                    grad_weight,
                )
    with jax.named_scope("norm_backward"):
        share = exchange_sum(share_of(part[tall:]) for part in [d_act] + arrived)
        d_act = d_act[:tall]
        for part in arrived:
            d_act = d_act + part[:tall].astype(f32)
        d_pre = d_act.reshape(n_view, local_rows, width) * gelu_slope(preactivation)
        sums = jnp.concatenate(
            [
                jnp.sum(d_pre, axis=1),
                jnp.sum(d_pre * normalised, axis=1),
                jnp.broadcast_to(share, (2 * n_view, width)),
            ]
        )
        both = exchange_sum(exchange(sums, "batch"))
        sum_b, sum_g = both[:n_view], both[n_view : 2 * n_view]
        loss = jnp.max(both[2 * n_view :])
        grad_bias = jnp.sum(sum_b, axis=0)
        grad_gain = jnp.sum(sum_g, axis=0)
        views_gradient = (
            norm_scale_gain
            * (d_pre - sum_b[:, None, :] / rows - normalised * sum_g[:, None, :] / rows)
            * inverse_deviation
        )
    return (loss, grad_weight, grad_gain, grad_bias, views_gradient)


def solution(mesh):
    placed = (P(None, "batch", "col"), P("col"), P("col"), P(None, "col"))
    return jax.shard_map(
        shards,
        mesh=mesh,
        in_specs=placed,
        out_specs=(P(), P("batch", "col"), P("col"), P("col"), P(None, "batch", "col")),
        check_vma=False,
    )
```

```python
import functools

import jax
import jax.numpy as jnp
from jax import lax
from jax.experimental import pallas as pl
from jax.experimental.pallas import tpu as pltpu
from jax.sharding import PartitionSpec as P

eps_norm = 1e-05
eps_std = 0.0001
f32 = jnp.float32
bf16 = jnp.bfloat16
MIB = 1024 * 1024


def gelu_slope(preactivation):
    value, pullback = jax.vjp(lambda t: jax.nn.gelu(t, approximate=True), preactivation)
    return pullback(jnp.ones_like(value))[0]


def xor_send(x, axis, k):
    n = lax.axis_size(axis)
    return lax.ppermute(x, axis, [(i, i ^ k) for i in range(n)])


def ring_order(n):
    return list(range(0, n, 2)) + list(range(1, n, 2))[::-1]


def ring_send(x, axis, d):
    order = ring_order(lax.axis_size(axis))
    n = len(order)
    return lax.ppermute(x, axis, [(order[i], order[(i + d) % n]) for i in range(n)])


def exchange_sum(parts):
    parts = list(parts)
    while len(parts) > 1:
        parts = [x + y for x, y in zip(parts[::2], parts[1::2])]
    return parts[0]


def exchange(x, axis):
    return [x] + [xor_send(x, axis, k) for k in range(1, lax.axis_size(axis))]


def params(limit):
    return pltpu.CompilerParams(vmem_limit_bytes=limit * MIB)


def cost(flops, moved):
    return pl.CostEstimate(flops=flops, bytes_accessed=moved, transcendentals=0)


IN_SMEM = pl.BlockSpec(memory_space=pltpu.SMEM)
IN_VMEM = pl.BlockSpec(memory_space=pltpu.VMEM)
ANYWHERE = pl.BlockSpec(memory_space=pl.ANY)
LOADS = 8


def load_kernel(w_ref, out_ref, flag_ref, sems):
    flag_ref[...] = jnp.zeros_like(flag_ref)
    step = w_ref.shape[0] // LOADS
    copies = [
        pltpu.make_async_copy(
            w_ref.at[pl.ds(i * step, step)], out_ref.at[pl.ds(i * step, step)], sems.at[i]
        )
        for i in range(LOADS)
    ]
    for copy in copies:
        copy.start()
    for copy in copies:
        copy.wait()


def load_call(weight, flag_shape):
    return pl.pallas_call(
        load_kernel,
        out_shape=(
            pltpu.VMEM(weight.shape, weight.dtype),
            jax.ShapeDtypeStruct(flag_shape, f32),
        ),
        in_specs=[ANYWHERE],
        out_specs=(IN_VMEM, IN_VMEM),
        scratch_shapes=[pltpu.SemaphoreType.DMA((LOADS,))],
        compiler_params=params(4),
        cost_estimate=cost(0, 4 * weight.size),
        name="weight_load",
    )(pltpu.with_memory_space_constraint(weight, pltpu.HBM))


def weight_rows(place_ref, w_ref, k, width):
    return w_ref[pl.ds(pl.multiple_of((place_ref[1] ^ k) * width, width), width), :]


def z_kernel(ks, first, last, local_rows, place_ref, *refs):
    count = len(ks)
    pieces, rest = refs[:count], list(refs[count:])
    w_ref = rest.pop(0)
    total = None if first else rest.pop(0)[...]
    width = pieces[0].shape[1]
    for j in range(count):
        part = jnp.dot(
            pieces[j][...], weight_rows(place_ref, w_ref, ks[j], width), preferred_element_type=f32
        )
        total = part if total is None else total + part
    if not last:
        rest[0][...] = total
        return
    z = total.astype(bf16)
    for v, ref in enumerate(rest):
        ref[...] = z[v * local_rows : (v + 1) * local_rows]


def z_call(place, ks, pieces, weight, before, last, local_rows):
    count = len(ks)
    tall, width = pieces[0].shape
    columns = weight.shape[1]
    operands = [place] + list(pieces) + [weight] + ([] if before is None else [before])
    if last:
        groups = tall // local_rows
        out_shape = (jax.ShapeDtypeStruct((local_rows, columns), bf16),) * groups
    else:
        out_shape = jax.ShapeDtypeStruct((tall, columns), f32)
    return pl.pallas_call(
        functools.partial(z_kernel, tuple(ks), before is None, last, local_rows),
        out_shape=out_shape,
        in_specs=[IN_SMEM] + [IN_VMEM] * (len(operands) - 1),
        out_specs=jax.tree.map(lambda _: IN_VMEM, out_shape),
        compiler_params=params(8),
        cost_estimate=cost(2 * tall * width * columns * count, 2 * tall * columns),
        name="z_matmul",
    )(*operands)


def upper_blocks(n):
    return [(s, t) for s in range(n) for t in range(s, n)]


def strip_kernel(n_batch, n_col, place_ref, *refs):
    z_refs, (even_ref, odd_ref, strip) = refs[: 2 * n_batch], refs[2 * n_batch :]
    local_rows = z_refs[0].shape[0]
    rows = local_rows * n_batch
    for v in range(2):
        zf = [z[...].astype(f32) for z in z_refs[v::2]]
        mean = sum(jnp.sum(z, axis=0, keepdims=True) for z in zf) / rows
        rounded = jnp.concatenate([(z - mean).astype(bf16) for z in zf], axis=0)
        at = 0
        for s in range(n_batch):
            product = lax.dot_general(
                rounded[s * local_rows : (s + 1) * local_rows],
                rounded[s * local_rows :],
                (((1,), (1,)), ((), ())),
                preferred_element_type=f32,
            )
            strip[pl.ds(v * local_rows, local_rows), pl.ds(at, product.shape[1])] = product
            at += product.shape[1]
    part = 2 * local_rows // n_col
    for k in range(n_col):
        start = pl.multiple_of((place_ref[1] ^ k) * part, part)
        (odd_ref if k % 2 else even_ref)[k // 2] = strip[pl.ds(start, part), :]


def strip_call(place, z_slots, n_col):
    n_batch = len(z_slots)
    local_rows, columns = z_slots[0][0].shape
    tall = 2 * local_rows
    wide = len(upper_blocks(n_batch)) * local_rows
    part = jax.ShapeDtypeStruct((n_col // 2, tall // n_col, wide), f32)
    operands = [place] + [z for slot in z_slots for z in slot]
    return pl.pallas_call(
        functools.partial(strip_kernel, n_batch, n_col),
        out_shape=(part, part),
        in_specs=[IN_SMEM] + [IN_VMEM] * (len(operands) - 1),
        out_specs=(IN_VMEM, IN_VMEM),
        scratch_shapes=[pltpu.VMEM((tall, wide), f32)],
        compiler_params=params(18),
        cost_estimate=cost(2 * tall * wide * columns, 2 * tall * columns * n_batch),
        name="kernel_strip",
    )(*operands)


def dz_kernel(n_batch, n_col, tile, constants, place_ref, own_ref, *refs):
    coef, hinge_coef, inv_coef, inv_share, hinge_share, diag_share, block_share = constants
    strip_refs = refs[:n_col]
    z_refs = refs[n_col : n_col + 2 * n_batch]
    dz_ref, share_ref, strips, full, centred = refs[n_col + 2 * n_batch :]
    local_rows, columns = z_refs[0].shape
    rows = local_rows * n_batch
    own = own_ref[...]
    block = lax.broadcasted_iota(jnp.int32, own.shape, 1) // local_rows
    on_diagonal = functools.reduce(
        jnp.logical_or, [block == i for i, (s, t) in enumerate(upper_blocks(n_batch)) if s == t]
    )
    own = own * own * jnp.where(on_diagonal, 1.0, 2.0)
    own = jnp.sum(jnp.sum(own, axis=0, keepdims=True), axis=1, keepdims=True)
    share_ref[...] = jnp.broadcast_to(block_share * own, share_ref.shape)
    part = 2 * local_rows // n_col
    for k in range(n_col):
        start = pl.multiple_of((place_ref[1] ^ k) * part, part)
        strips[pl.ds(start, part), :] = strip_refs[k][...].astype(f32)
    for v in range(2):
        for i, (s, t) in enumerate(upper_blocks(n_batch)):
            here, there = pl.ds(s * local_rows, local_rows), pl.ds(t * local_rows, local_rows)
            block = strips[pl.ds(v * local_rows, local_rows), pl.ds(i * local_rows, local_rows)]
            full[v, here, there] = block.astype(bf16)
            if s < t:
                full[v, there, here] = jnp.transpose(block).astype(bf16)

    def one_tile(j, carry):
        here = pl.ds(pl.multiple_of(j * tile, tile), tile)
        share = jnp.zeros((1, 1), f32)
        grads = []
        z_views = []
        for v in range(2):
            zf = jnp.concatenate([z[:, here].astype(f32) for z in z_refs[v::2]], axis=0)
            z_views.append(zf)
            zc = zf - jnp.sum(zf, axis=0, keepdims=True) / rows
            std = jnp.sqrt(jnp.sum(zc * zc, axis=0, keepdims=True) / (rows - 1) + eps_std)
            zcb = zc.astype(bf16)
            centred[...] = zcb
            rounded = zcb.astype(f32)
            diag = jnp.sum(rounded * rounded, axis=0, keepdims=True)
            moved = jnp.dot(full[v], centred[...], preferred_element_type=f32)
            pull = jnp.where(std < 1.0, hinge_coef, 0.0) / std
            summed = coef * (moved - rounded * diag) - zc * pull
            grads.append(summed - jnp.sum(summed, axis=0, keepdims=True) / rows)
            share += hinge_share * jnp.sum(jnp.maximum(1.0 - std, 0.0), axis=1, keepdims=True)
            share -= diag_share * jnp.sum(diag * diag, axis=1, keepdims=True)
        diff = z_views[0] - z_views[1]
        share += inv_share * jnp.sum(
            jnp.sum(diff * diff, axis=0, keepdims=True), axis=1, keepdims=True
        )
        share_ref[...] += jnp.broadcast_to(share, share_ref.shape)
        dz_ref[0, :, here] = (grads[0] + inv_coef * diff).astype(bf16)
        dz_ref[1, :, here] = (grads[1] - inv_coef * diff).astype(bf16)
        return carry

    lax.fori_loop(0, columns // tile, one_tile, 0)


def dz_call(place, own, strips, z_slots, constants):
    n_col, n_batch = len(strips), len(z_slots)
    local_rows, columns = z_slots[0][0].shape
    tall = 2 * local_rows
    rows = local_rows * n_batch
    tile = min(256, columns)
    operands = [place, own] + list(strips) + [z for slot in z_slots for z in slot]
    return pl.pallas_call(
        functools.partial(dz_kernel, n_batch, n_col, tile, constants),
        out_shape=(
            jax.ShapeDtypeStruct((2, rows, columns), bf16),
            jax.ShapeDtypeStruct((8, 128), f32),
        ),
        in_specs=[IN_SMEM] + [IN_VMEM] * (len(operands) - 1),
        out_specs=(IN_VMEM, IN_VMEM),
        scratch_shapes=[
            pltpu.VMEM((tall, strips[0].shape[1]), f32),
            pltpu.VMEM((2, rows, rows), bf16),
            pltpu.VMEM((rows, tile), bf16),
        ],
        compiler_params=params(24),
        cost_estimate=cost(4 * rows * rows * columns, 8 * rows * columns),
        name="embedding_gradient",
    )(*operands)


EXTRA = 16


def share_rows(share, width, kind):
    high = share.astype(bf16).astype(f32)
    middle = (share - high).astype(bf16).astype(f32)
    low = share - high - middle
    row = lax.broadcasted_iota(jnp.int32, (EXTRA, width), 0)
    rows = jnp.where(row == 0, high, jnp.where(row == 1, middle, jnp.where(row == 2, low, 0.0)))
    return rows.astype(kind)


def share_of(rows):
    return rows[0:1].astype(f32) + rows[1:2].astype(f32) + rows[2:3].astype(f32)


def d_act_kernel(count, adds, place_ref, dz_ref, share_ref, w_ref, *refs):
    local_rows, columns = dz_ref.shape[1] // adds[1], dz_ref.shape[2]
    tall = 2 * local_rows
    dz = jnp.concatenate([dz_ref[0, :local_rows], dz_ref[1, :local_rows]], axis=0)
    width = w_ref.shape[0] // adds[2]
    share = share_ref[0:1, 0:1]
    for j in range(count):
        k = 2 * ((j + 1) % count) if adds[0] else 2 * j + 1
        part = lax.dot_general(
            dz,
            weight_rows(place_ref, w_ref, k, width),
            (((1,), (1,)), ((), ())),
            preferred_element_type=f32,
        )
        if not adds[0]:
            refs[0][j, :tall] = part.astype(refs[0].dtype)
            refs[0][j, tall:] = share_rows(share, width, refs[0].dtype)
        else:
            got = refs[0]
            out_ref = refs[j + 1]
            slot = (j + 1) % count
            out_ref[:tall] = (part + got[slot, :tall].astype(f32)).astype(out_ref.dtype)
            whole_share = share + share_of(got[slot, tall:])[:, 0:1]
            out_ref[tall:] = share_rows(whole_share, width, out_ref.dtype)


def d_act_call(place, dz, share, weight, n_batch, n_col, got):
    columns = weight.shape[1]
    width = weight.shape[0] // n_col
    tall = 2 * dz.shape[1] // n_batch
    count = n_col // 2
    operands = [place, dz, share, weight] + ([] if got is None else [got])
    if got is None:
        out_shape = (jax.ShapeDtypeStruct((count, tall + EXTRA, width), bf16),)
    else:
        out_shape = (jax.ShapeDtypeStruct((tall + EXTRA, width), bf16),) * (count - 1)
        out_shape += (jax.ShapeDtypeStruct((tall + EXTRA, width), f32),)
    return pl.pallas_call(
        functools.partial(d_act_kernel, count, (got is not None, n_batch, n_col)),
        out_shape=out_shape,
        in_specs=[IN_SMEM] + [IN_VMEM] * (len(operands) - 1),
        out_specs=(IN_VMEM,) * len(out_shape),
        compiler_params=params(8),
        cost_estimate=cost(2 * tall * width * columns * count, 2 * count * width * tall),
        name="d_act_matmul",
    )(*operands)


def held_place(plane, c, block, n_col, n_batch):
    return (((n_col // n_batch) * plane + 2 * block) ^ (c - (c & 1))) >> 1


def pick_kernel(n_batch, n_col, local_rows, place_ref, *refs):
    half = n_col // 2
    pieces, outs = refs[:half], refs[half:]
    b, c = place_ref[0], place_ref[1]
    position = jnp.where((b & 1) == 0, b >> 1, n_batch - 1 - (b >> 1))
    i = 0
    for block in range(n_col // n_batch // 2):
        for d in range(1, n_batch):
            ahead = position + d
            ahead = jnp.where(ahead >= n_batch, ahead - n_batch, ahead)
            plane = jnp.where(2 * ahead < n_batch, 2 * ahead, 2 * (n_batch - ahead) - 1)
            chosen = held_place(plane, c, block, n_col, n_batch)
            for e in range(half):

                @pl.when(chosen == e)
                def _():
                    outs[i][...] = pieces[e][local_rows:]

            i += 1


def pick_call(place, pieces, n_batch, n_col):
    tall, width = pieces[0].shape
    count = n_col // n_batch // 2 * (n_batch - 1)
    out_shape = (jax.ShapeDtypeStruct((tall // 2, width), bf16),) * count
    return pl.pallas_call(
        functools.partial(pick_kernel, n_batch, n_col, tall // 2),
        out_shape=out_shape,
        in_specs=[IN_SMEM] + [IN_VMEM] * len(pieces),
        out_specs=(IN_VMEM,) * count,
        compiler_params=params(4),
        cost_estimate=cost(0, tall * width * count),
        name="pick_blocks",
    )(place, *pieces)


def weight_grad_kernel(n_far, aliased, half, tile, which, place_ref, *refs):
    near = [refs[:half], refs[half : 2 * half]]
    arrived = refs[2 * half : 2 * half + n_far]
    dz_ref = refs[2 * half + n_far]
    out_ref, act, product, sems = refs[2 * half + n_far + 1 + aliased :]
    block, parity = which
    chosen = held_place(place_ref[0], place_ref[1], block, 2 * half, n_far + 1)
    out_row = 2 * block + ((place_ref[1] & 1) ^ parity)
    local_rows = near[0][0].shape[0] // 2
    rows = dz_ref.shape[1]
    for e in range(half):

        @pl.when(chosen == e)
        def _():
            act[pl.ds(0, local_rows)] = near[0][e][:local_rows]
            act[pl.ds(rows, local_rows)] = near[0][e][local_rows:]
            act[pl.ds(local_rows, rows - local_rows)] = near[1][e][...]

    for s in range(n_far):
        act[pl.ds(rows + (s + 1) * local_rows, local_rows)] = arrived[s][...]
    width = act.shape[1]
    copies = []
    for i in range(width // tile):
        total = None
        for v in range(2):
            part = lax.dot_general(
                act[pl.ds(v * rows, rows), pl.ds(i * tile, tile)],
                dz_ref[v],
                (((0,), (0,)), ((), ())),
                preferred_element_type=f32,
            )
            total = part if total is None else total + part
        product[pl.ds(i * tile, tile)] = total
        start = pl.multiple_of(out_row * width + i * tile, tile)
        copies.append(
            pltpu.make_async_copy(
                product.at[pl.ds(i * tile, tile)], out_ref.at[pl.ds(start, tile)], sems.at[i]
            )
        )
        copies[-1].start()
    for copy in copies:
        copy.wait()


def weight_grad_call(place, which, near, arrived, dz, features, before):
    half = len(near[0])
    width = near[0][0].shape[1]
    _, rows, columns = dz.shape
    tile = min(256, width)
    operands = [place] + [x for group in near for x in group] + list(arrived) + [dz]
    specs = [IN_SMEM] + [IN_VMEM] * (len(operands) - 1)
    aliases = {}
    if before is not None:
        aliases = {len(operands): 0}
        operands.append(before)
        specs.append(ANYWHERE)
    return pl.pallas_call(
        functools.partial(
            weight_grad_kernel, len(arrived), int(before is not None), half, tile, which
        ),
        out_shape=jax.ShapeDtypeStruct((features, columns), f32),
        in_specs=specs,
        out_specs=ANYWHERE,
        scratch_shapes=[
            pltpu.VMEM((2 * rows, width), bf16),
            pltpu.VMEM((width, columns), f32),
            pltpu.SemaphoreType.DMA((width // tile,)),
        ],
        input_output_aliases=aliases,
        compiler_params=params(12),
        cost_estimate=cost(4 * rows * width * columns, 4 * width * columns),
        name="weight_gradient",
    )(*operands)


def gather_pieces(x, n_col):
    return sibling_pieces(link_pieces(x, n_col), n_col)


def link_pieces(x, n_col):
    pieces = {0: x}
    for k in range(2, n_col, 2):
        pieces[k] = xor_send(x, "col", k)
    return pieces


def sibling_pieces(pieces, n_col):
    for k in range(0, n_col, 2):
        if k + 1 not in pieces:
            pieces[k + 1] = xor_send(pieces[k], "col", 1)
    return pieces


def shards(views, norm_scale_gain, norm_shift_bias, weight):
    n_batch = lax.axis_size("batch")
    n_col = lax.axis_size("col")
    place = jnp.stack([lax.axis_index("batch"), lax.axis_index("col")]).astype(jnp.int32)
    views, norm_scale_gain, norm_shift_bias, weight, place = lax.optimization_barrier(
        (views, norm_scale_gain, norm_shift_bias, weight, place)
    )
    n_view, local_rows, width = views.shape
    features, columns = weight.shape
    E = columns * n_col
    rows = local_rows * n_batch
    tall = n_view * local_rows
    scale = rows * E / 128.0
    denom = float((rows - 1) ** 2 * E)
    evens = list(range(0, n_col, 2))
    odds = [k + 1 for k in evens]
    far = evens[1:]

    with jax.named_scope("weight_load"):
        held_weight, loaded = load_call(weight, (2 * n_view, width))
    with jax.named_scope("norm_stats"):
        hidden = views.astype(f32)
        local_mean = jnp.mean(hidden, axis=1)
        local_centred = hidden - local_mean[:, None, :]
        local_spread = jnp.sum(local_centred * local_centred, axis=1)
        stats = exchange(jnp.concatenate([local_mean, local_spread]), "batch")
        stats[-1] = stats[-1] + loaded
        mean = exchange_sum(s[:n_view] for s in stats) / n_batch
        spread = exchange_sum(
            s[n_view:] + local_rows * jnp.square(s[:n_view] - mean) for s in stats
        )
        var = spread / rows
        inverse_deviation = (1.0 / jnp.sqrt(var + eps_norm))[:, None, :]
        normalised = (hidden - mean[:, None, :]) * inverse_deviation
        preactivation = norm_scale_gain * normalised + norm_shift_bias
        act = jax.nn.gelu(preactivation, approximate=True).astype(bf16)
    with jax.named_scope("act_gather"):
        pieces = link_pieces(act.reshape(tall, width), n_col)
        pieces[1] = xor_send(pieces[0], "col", 1)
        first, pieces[1] = lax.optimization_barrier((act[0], pieces[1]))
        others = [ring_send(first, "batch", d) for d in range(1, n_batch)]
        pieces = sibling_pieces(pieces, n_col)
        far_pieces = link_pieces(jnp.concatenate(others), n_col)
    with jax.named_scope("z"):

        def z_of(source, groups, total=None):
            for i, ks in enumerate(groups):
                total = z_call(
                    place,
                    ks,
                    [source[k] for k in ks],
                    held_weight,
                    total,
                    i == len(groups) - 1,
                    local_rows,
                )
            return total

        z_own0, z_own1 = z_of(pieces, [[0, 1], far, [k + 1 for k in far]])
    with jax.named_scope("z_ring"):
        z_ring = [z_own1, ring_send(z_own1, "batch", 1)]
        z_ring[1], far_pieces[far[-1]] = lax.optimization_barrier((z_ring[1], far_pieces[far[-1]]))
        z_ring.append(ring_send(z_ring[1], "batch", 1))
    with jax.named_scope("z_far"):
        start = z_call(
            place, [0, far[-1]], [far_pieces[0], far_pieces[far[-1]]], held_weight, None, False, local_rows
        )
        start, far_pieces[far[0]], z_ring[2] = lax.optimization_barrier(
            (start, far_pieces[far[0]], z_ring[2])
        )
        far_pieces = sibling_pieces(far_pieces, n_col)
        for _ in range(3, n_batch):
            z_ring.append(ring_send(z_ring[-1], "batch", 1))
        z_far = z_of(far_pieces, [far[:-1], odds], start)
        slots = list(zip([z_own0] + list(z_far), z_ring))
    with jax.named_scope("kernel"):
        even_part, odd_part = strip_call(place, slots, n_col)
        even_part = even_part + xor_send(odd_part, "col", 1)
        even_part, held_back = lax.optimization_barrier((even_part, [pieces[k] for k in evens]))
        strip = even_part[0]
        for k in far:
            strip = strip + xor_send(even_part[k // 2], "col", k)
        picked = pick_call(place, held_back, n_batch, n_col)
        blocks = [
            ring_send(x, "batch", 1 + i % (n_batch - 1)) for i, x in enumerate(picked)
        ]
        strips = gather_pieces(strip.astype(bf16), n_col)
        strips, blocks = lax.optimization_barrier((strips, blocks))
    with jax.named_scope("dz"):
        constants = (
            4.0 * scale / denom,
            25.0 * scale / (2.0 * E * (rows - 1)),
            50.0 * scale / (rows * E),
            25.0 / (rows * E) / n_batch,
            25.0 / (2 * E) / n_batch,
            1.0 / denom / n_batch,
            1.0 / denom / n_batch,
        )
        dz, share = dz_call(place, strip, [strips[k] for k in range(n_col)], slots, constants)
    with jax.named_scope("d_act"):
        (away,) = d_act_call(place, dz, share, held_weight, n_batch, n_col, None)
        got = xor_send(away, "col", 1)
        *sends, d_act = d_act_call(place, dz, share, held_weight, n_batch, n_col, got)
        arrived = [xor_send(part, "col", k) for k, part in zip(far, sends)]
    with jax.named_scope("grad_weight"):
        grad_weight = None
        for block in range(n_col // n_batch // 2):
            mine = blocks[block * (n_batch - 1) : (block + 1) * (n_batch - 1)]
            other = [xor_send(x, "col", 1) for x in mine]
            for parity, ks, far_rows in ((0, evens, mine), (1, odds, other)):
                grad_weight = weight_grad_call(
                    place,
                    (block, parity),
                    [[group[k] for k in ks] for group in (pieces, far_pieces)],
                    far_rows,
                    dz,
                    features // n_batch,
                    grad_weight,
                )
    with jax.named_scope("norm_backward"):
        share = exchange_sum(share_of(part[tall:]) for part in [d_act] + arrived)
        d_act = d_act[:tall]
        for part in arrived:
            d_act = d_act + part[:tall].astype(f32)
        d_pre = d_act.reshape(n_view, local_rows, width) * gelu_slope(preactivation)
        sums = jnp.concatenate(
            [
                jnp.sum(d_pre, axis=1),
                jnp.sum(d_pre * normalised, axis=1),
                jnp.broadcast_to(share, (2 * n_view, width)),
            ]
        )
        both = exchange_sum(exchange(sums, "batch"))
        sum_b, sum_g = both[:n_view], both[n_view : 2 * n_view]
        loss = jnp.max(both[2 * n_view :])
        grad_bias = jnp.sum(sum_b, axis=0)
        grad_gain = jnp.sum(sum_g, axis=0)
        views_gradient = (
            norm_scale_gain
            * (d_pre - sum_b[:, None, :] / rows - normalised * sum_g[:, None, :] / rows)
            * inverse_deviation
        )
    return (loss, grad_weight, grad_gain, grad_bias, views_gradient)


def solution(mesh):
    placed = (P(None, "batch", "col"), P("col"), P("col"), P(None, "col"))
    return jax.shard_map(
        shards,
        mesh=mesh,
        in_specs=placed,
        out_specs=(P(), P("batch", "col"), P("col"), P("col"), P(None, "batch", "col")),
        check_vma=False,
    )
```

```python
import functools

import jax
import jax.numpy as jnp
from jax import lax
from jax.experimental import pallas as pl
from jax.experimental.pallas import tpu as pltpu
from jax.sharding import PartitionSpec as P

eps_norm = 1e-05
eps_std = 0.0001
f32 = jnp.float32
bf16 = jnp.bfloat16
MIB = 1024 * 1024


def gelu_slope(preactivation):
    value, pullback = jax.vjp(lambda t: jax.nn.gelu(t, approximate=True), preactivation)
    return pullback(jnp.ones_like(value))[0]


def xor_send(x, axis, k):
    n = lax.axis_size(axis)
    return lax.ppermute(x, axis, [(i, i ^ k) for i in range(n)])


def ring_order(n):
    return list(range(0, n, 2)) + list(range(1, n, 2))[::-1]


def ring_send(x, axis, d):
    order = ring_order(lax.axis_size(axis))
    n = len(order)
    return lax.ppermute(x, axis, [(order[i], order[(i + d) % n]) for i in range(n)])


def exchange_sum(parts):
    parts = list(parts)
    while len(parts) > 1:
        parts = [x + y for x, y in zip(parts[::2], parts[1::2])]
    return parts[0]


def exchange(x, axis):
    return [x] + [xor_send(x, axis, k) for k in range(1, lax.axis_size(axis))]


def params(limit):
    return pltpu.CompilerParams(vmem_limit_bytes=limit * MIB)


def cost(flops, moved):
    return pl.CostEstimate(flops=flops, bytes_accessed=moved, transcendentals=0)


IN_SMEM = pl.BlockSpec(memory_space=pltpu.SMEM)
IN_VMEM = pl.BlockSpec(memory_space=pltpu.VMEM)
ANYWHERE = pl.BlockSpec(memory_space=pl.ANY)
LOADS = 8


def load_kernel(w_ref, out_ref, flag_ref, sems):
    flag_ref[...] = jnp.zeros_like(flag_ref)
    step = w_ref.shape[0] // LOADS
    copies = [
        pltpu.make_async_copy(
            w_ref.at[pl.ds(i * step, step)], out_ref.at[pl.ds(i * step, step)], sems.at[i]
        )
        for i in range(LOADS)
    ]
    for copy in copies:
        copy.start()
    for copy in copies:
        copy.wait()


def load_call(weight, flag_shape):
    return pl.pallas_call(
        load_kernel,
        out_shape=(
            pltpu.VMEM(weight.shape, weight.dtype),
            jax.ShapeDtypeStruct(flag_shape, f32),
        ),
        in_specs=[ANYWHERE],
        out_specs=(IN_VMEM, IN_VMEM),
        scratch_shapes=[pltpu.SemaphoreType.DMA((LOADS,))],
        compiler_params=params(4),
        cost_estimate=cost(0, 4 * weight.size),
        name="weight_load",
    )(pltpu.with_memory_space_constraint(weight, pltpu.HBM))


def weight_rows(place_ref, w_ref, k, width):
    return w_ref[pl.ds(pl.multiple_of((place_ref[1] ^ k) * width, width), width), :]


def z_kernel(ks, first, last, local_rows, place_ref, *refs):
    count = len(ks)
    pieces, rest = refs[:count], list(refs[count:])
    w_ref = rest.pop(0)
    total = None if first else rest.pop(0)[...]
    width = pieces[0].shape[1]
    for j in range(count):
        part = jnp.dot(
            pieces[j][...], weight_rows(place_ref, w_ref, ks[j], width), preferred_element_type=f32
        )
        total = part if total is None else total + part
    if not last:
        rest[0][...] = total
        return
    z = total.astype(bf16)
    for v, ref in enumerate(rest):
        ref[...] = z[v * local_rows : (v + 1) * local_rows]


def z_call(place, ks, pieces, weight, before, last, local_rows):
    count = len(ks)
    tall, width = pieces[0].shape
    columns = weight.shape[1]
    operands = [place] + list(pieces) + [weight] + ([] if before is None else [before])
    if last:
        groups = tall // local_rows
        out_shape = (jax.ShapeDtypeStruct((local_rows, columns), bf16),) * groups
    else:
        out_shape = jax.ShapeDtypeStruct((tall, columns), f32)
    return pl.pallas_call(
        functools.partial(z_kernel, tuple(ks), before is None, last, local_rows),
        out_shape=out_shape,
        in_specs=[IN_SMEM] + [IN_VMEM] * (len(operands) - 1),
        out_specs=jax.tree.map(lambda _: IN_VMEM, out_shape),
        compiler_params=params(8),
        cost_estimate=cost(2 * tall * width * columns * count, 2 * tall * columns),
        name="z_matmul",
    )(*operands)


def upper_blocks(n):
    return [(s, t) for s in range(n) for t in range(s, n)]


def strip_kernel(n_batch, n_col, place_ref, *refs):
    z_refs, (even_ref, odd_ref, strip) = refs[: 2 * n_batch], refs[2 * n_batch :]
    local_rows = z_refs[0].shape[0]
    rows = local_rows * n_batch
    for v in range(2):
        zf = [z[...].astype(f32) for z in z_refs[v::2]]
        mean = sum(jnp.sum(z, axis=0, keepdims=True) for z in zf) / rows
        rounded = jnp.concatenate([(z - mean).astype(bf16) for z in zf], axis=0)
        at = 0
        for s in range(n_batch):
            product = lax.dot_general(
                rounded[s * local_rows : (s + 1) * local_rows],
                rounded[s * local_rows :],
                (((1,), (1,)), ((), ())),
                preferred_element_type=f32,
            )
            strip[pl.ds(v * local_rows, local_rows), pl.ds(at, product.shape[1])] = product
            at += product.shape[1]
    part = 2 * local_rows // n_col
    for k in range(n_col):
        start = pl.multiple_of((place_ref[1] ^ k) * part, part)
        ref = odd_ref if k % 2 else even_ref
        ref[k // 2] = strip[pl.ds(start, part), :].astype(ref.dtype)


def strip_call(place, z_slots, n_col):
    n_batch = len(z_slots)
    local_rows, columns = z_slots[0][0].shape
    tall = 2 * local_rows
    wide = len(upper_blocks(n_batch)) * local_rows
    shape = (n_col // 2, tall // n_col, wide)
    operands = [place] + [z for slot in z_slots for z in slot]
    return pl.pallas_call(
        functools.partial(strip_kernel, n_batch, n_col),
        out_shape=(jax.ShapeDtypeStruct(shape, f32), jax.ShapeDtypeStruct(shape, bf16)),
        in_specs=[IN_SMEM] + [IN_VMEM] * (len(operands) - 1),
        out_specs=(IN_VMEM, IN_VMEM),
        scratch_shapes=[pltpu.VMEM((tall, wide), f32)],
        compiler_params=params(18),
        cost_estimate=cost(2 * tall * wide * columns, 2 * tall * columns * n_batch),
        name="kernel_strip",
    )(*operands)


def dz_kernel(n_batch, n_col, tile, constants, place_ref, own_ref, *refs):
    coef, hinge_coef, inv_coef, inv_share, hinge_share, diag_share, block_share = constants
    strip_refs = refs[:n_col]
    z_refs = refs[n_col : n_col + 2 * n_batch]
    dz_ref, share_ref, strips, full, centred = refs[n_col + 2 * n_batch :]
    local_rows, columns = z_refs[0].shape
    rows = local_rows * n_batch
    own = own_ref[...]
    block = lax.broadcasted_iota(jnp.int32, own.shape, 1) // local_rows
    on_diagonal = functools.reduce(
        jnp.logical_or, [block == i for i, (s, t) in enumerate(upper_blocks(n_batch)) if s == t]
    )
    own = own * own * jnp.where(on_diagonal, 1.0, 2.0)
    own = jnp.sum(jnp.sum(own, axis=0, keepdims=True), axis=1, keepdims=True)
    share_ref[...] = jnp.broadcast_to(block_share * own, share_ref.shape)
    part = 2 * local_rows // n_col
    for k in range(n_col):
        start = pl.multiple_of((place_ref[1] ^ k) * part, part)
        strips[pl.ds(start, part), :] = strip_refs[k][...].astype(f32)
    for v in range(2):
        for i, (s, t) in enumerate(upper_blocks(n_batch)):
            here, there = pl.ds(s * local_rows, local_rows), pl.ds(t * local_rows, local_rows)
            block = strips[pl.ds(v * local_rows, local_rows), pl.ds(i * local_rows, local_rows)]
            full[v, here, there] = block.astype(bf16)
            if s < t:
                full[v, there, here] = jnp.transpose(block).astype(bf16)

    def one_tile(j, carry):
        here = pl.ds(pl.multiple_of(j * tile, tile), tile)
        share = jnp.zeros((1, 1), f32)
        grads = []
        z_views = []
        for v in range(2):
            zf = jnp.concatenate([z[:, here].astype(f32) for z in z_refs[v::2]], axis=0)
            z_views.append(zf)
            zc = zf - jnp.sum(zf, axis=0, keepdims=True) / rows
            std = jnp.sqrt(jnp.sum(zc * zc, axis=0, keepdims=True) / (rows - 1) + eps_std)
            zcb = zc.astype(bf16)
            centred[...] = zcb
            rounded = zcb.astype(f32)
            diag = jnp.sum(rounded * rounded, axis=0, keepdims=True)
            moved = jnp.dot(full[v], centred[...], preferred_element_type=f32)
            pull = jnp.where(std < 1.0, hinge_coef, 0.0) / std
            summed = coef * (moved - rounded * diag) - zc * pull
            grads.append(summed - jnp.sum(summed, axis=0, keepdims=True) / rows)
            share += hinge_share * jnp.sum(jnp.maximum(1.0 - std, 0.0), axis=1, keepdims=True)
            share -= diag_share * jnp.sum(diag * diag, axis=1, keepdims=True)
        diff = z_views[0] - z_views[1]
        share += inv_share * jnp.sum(
            jnp.sum(diff * diff, axis=0, keepdims=True), axis=1, keepdims=True
        )
        share_ref[...] += jnp.broadcast_to(share, share_ref.shape)
        dz_ref[0, :, here] = (grads[0] + inv_coef * diff).astype(bf16)
        dz_ref[1, :, here] = (grads[1] - inv_coef * diff).astype(bf16)
        return carry

    lax.fori_loop(0, columns // tile, one_tile, 0)


def dz_call(place, own, strips, z_slots, constants):
    n_col, n_batch = len(strips), len(z_slots)
    local_rows, columns = z_slots[0][0].shape
    tall = 2 * local_rows
    rows = local_rows * n_batch
    tile = min(256, columns)
    operands = [place, own] + list(strips) + [z for slot in z_slots for z in slot]
    return pl.pallas_call(
        functools.partial(dz_kernel, n_batch, n_col, tile, constants),
        out_shape=(
            jax.ShapeDtypeStruct((2, rows, columns), bf16),
            jax.ShapeDtypeStruct((8, 128), f32),
        ),
        in_specs=[IN_SMEM] + [IN_VMEM] * (len(operands) - 1),
        out_specs=(IN_VMEM, IN_VMEM),
        scratch_shapes=[
            pltpu.VMEM((tall, strips[0].shape[1]), f32),
            pltpu.VMEM((2, rows, rows), bf16),
            pltpu.VMEM((rows, tile), bf16),
        ],
        compiler_params=params(24),
        cost_estimate=cost(4 * rows * rows * columns, 8 * rows * columns),
        name="embedding_gradient",
    )(*operands)


EXTRA = 16


def share_rows(share, width, kind):
    high = share.astype(bf16).astype(f32)
    middle = (share - high).astype(bf16).astype(f32)
    low = share - high - middle
    row = lax.broadcasted_iota(jnp.int32, (EXTRA, width), 0)
    rows = jnp.where(row == 0, high, jnp.where(row == 1, middle, jnp.where(row == 2, low, 0.0)))
    return rows.astype(kind)


def share_of(rows):
    return rows[0:1].astype(f32) + rows[1:2].astype(f32) + rows[2:3].astype(f32)


def d_act_kernel(count, adds, place_ref, dz_ref, share_ref, w_ref, *refs):
    local_rows, columns = dz_ref.shape[1] // adds[1], dz_ref.shape[2]
    tall = 2 * local_rows
    dz = jnp.concatenate([dz_ref[0, :local_rows], dz_ref[1, :local_rows]], axis=0)
    width = w_ref.shape[0] // adds[2]
    share = share_ref[0:1, 0:1]
    for j in range(count):
        k = 2 * ((j + 1) % count) if adds[0] else 2 * j + 1
        part = lax.dot_general(
            dz,
            weight_rows(place_ref, w_ref, k, width),
            (((1,), (1,)), ((), ())),
            preferred_element_type=f32,
        )
        if not adds[0]:
            refs[0][j, :tall] = part.astype(refs[0].dtype)
            refs[0][j, tall:] = share_rows(share, width, refs[0].dtype)
        else:
            got = refs[0]
            out_ref = refs[j + 1]
            slot = (j + 1) % count
            out_ref[:tall] = (part + got[slot, :tall].astype(f32)).astype(out_ref.dtype)
            whole_share = share + share_of(got[slot, tall:])[:, 0:1]
            out_ref[tall:] = share_rows(whole_share, width, out_ref.dtype)


def d_act_call(place, dz, share, weight, n_batch, n_col, got):
    columns = weight.shape[1]
    width = weight.shape[0] // n_col
    tall = 2 * dz.shape[1] // n_batch
    count = n_col // 2
    operands = [place, dz, share, weight] + ([] if got is None else [got])
    if got is None:
        out_shape = (jax.ShapeDtypeStruct((count, tall + EXTRA, width), bf16),)
    else:
        out_shape = (jax.ShapeDtypeStruct((tall + EXTRA, width), bf16),) * (count - 1)
        out_shape += (jax.ShapeDtypeStruct((tall + EXTRA, width), f32),)
    return pl.pallas_call(
        functools.partial(d_act_kernel, count, (got is not None, n_batch, n_col)),
        out_shape=out_shape,
        in_specs=[IN_SMEM] + [IN_VMEM] * (len(operands) - 1),
        out_specs=(IN_VMEM,) * len(out_shape),
        compiler_params=params(8),
        cost_estimate=cost(2 * tall * width * columns * count, 2 * count * width * tall),
        name="d_act_matmul",
    )(*operands)


def held_place(plane, c, block, n_col, n_batch):
    return (((n_col // n_batch) * plane + 2 * block) ^ (c - (c & 1))) >> 1


def pick_kernel(n_batch, n_col, local_rows, place_ref, *refs):
    half = n_col // 2
    pieces, outs = refs[:half], refs[half:]
    b, c = place_ref[0], place_ref[1]
    position = jnp.where((b & 1) == 0, b >> 1, n_batch - 1 - (b >> 1))
    i = 0
    for block in range(n_col // n_batch // 2):
        for d in range(1, n_batch):
            ahead = position + d
            ahead = jnp.where(ahead >= n_batch, ahead - n_batch, ahead)
            plane = jnp.where(2 * ahead < n_batch, 2 * ahead, 2 * (n_batch - ahead) - 1)
            chosen = held_place(plane, c, block, n_col, n_batch)
            for e in range(half):

                @pl.when(chosen == e)
                def _():
                    outs[i][...] = pieces[e][local_rows:]

            i += 1


def pick_call(place, pieces, n_batch, n_col):
    tall, width = pieces[0].shape
    count = n_col // n_batch // 2 * (n_batch - 1)
    out_shape = (jax.ShapeDtypeStruct((tall // 2, width), bf16),) * count
    return pl.pallas_call(
        functools.partial(pick_kernel, n_batch, n_col, tall // 2),
        out_shape=out_shape,
        in_specs=[IN_SMEM] + [IN_VMEM] * len(pieces),
        out_specs=(IN_VMEM,) * count,
        compiler_params=params(4),
        cost_estimate=cost(0, tall * width * count),
        name="pick_blocks",
    )(place, *pieces)


def weight_grad_kernel(n_far, aliased, half, tile, which, place_ref, *refs):
    near = [refs[:half], refs[half : 2 * half]]
    arrived = refs[2 * half : 2 * half + n_far]
    dz_ref = refs[2 * half + n_far]
    out_ref, act, product, sems = refs[2 * half + n_far + 1 + aliased :]
    block, parity = which
    chosen = held_place(place_ref[0], place_ref[1], block, 2 * half, n_far + 1)
    out_row = 2 * block + ((place_ref[1] & 1) ^ parity)
    local_rows = near[0][0].shape[0] // 2
    rows = dz_ref.shape[1]
    for e in range(half):

        @pl.when(chosen == e)
        def _():
            act[pl.ds(0, local_rows)] = near[0][e][:local_rows]
            act[pl.ds(rows, local_rows)] = near[0][e][local_rows:]
            act[pl.ds(local_rows, rows - local_rows)] = near[1][e][...]

    for s in range(n_far):
        act[pl.ds(rows + (s + 1) * local_rows, local_rows)] = arrived[s][...]
    width = act.shape[1]
    copies = []
    for i in range(width // tile):
        total = None
        for v in range(2):
            part = lax.dot_general(
                act[pl.ds(v * rows, rows), pl.ds(i * tile, tile)],
                dz_ref[v],
                (((0,), (0,)), ((), ())),
                preferred_element_type=f32,
            )
            total = part if total is None else total + part
        product[pl.ds(i * tile, tile)] = total
        start = pl.multiple_of(out_row * width + i * tile, tile)
        copies.append(
            pltpu.make_async_copy(
                product.at[pl.ds(i * tile, tile)], out_ref.at[pl.ds(start, tile)], sems.at[i]
            )
        )
        copies[-1].start()
    for copy in copies:
        copy.wait()


def weight_grad_call(place, which, near, arrived, dz, features, before):
    half = len(near[0])
    width = near[0][0].shape[1]
    _, rows, columns = dz.shape
    tile = min(256, width)
    operands = [place] + [x for group in near for x in group] + list(arrived) + [dz]
    specs = [IN_SMEM] + [IN_VMEM] * (len(operands) - 1)
    aliases = {}
    if before is not None:
        aliases = {len(operands): 0}
        operands.append(before)
        specs.append(ANYWHERE)
    return pl.pallas_call(
        functools.partial(
            weight_grad_kernel, len(arrived), int(before is not None), half, tile, which
        ),
        out_shape=jax.ShapeDtypeStruct((features, columns), f32),
        in_specs=specs,
        out_specs=ANYWHERE,
        scratch_shapes=[
            pltpu.VMEM((2 * rows, width), bf16),
            pltpu.VMEM((width, columns), f32),
            pltpu.SemaphoreType.DMA((width // tile,)),
        ],
        input_output_aliases=aliases,
        compiler_params=params(12),
        cost_estimate=cost(4 * rows * width * columns, 4 * width * columns),
        name="weight_gradient",
    )(*operands)


def gather_pieces(x, n_col):
    return sibling_pieces(link_pieces(x, n_col), n_col)


def link_pieces(x, n_col):
    pieces = {0: x}
    for k in range(2, n_col, 2):
        pieces[k] = xor_send(x, "col", k)
    return pieces


def sibling_pieces(pieces, n_col):
    for k in range(0, n_col, 2):
        if k + 1 not in pieces:
            pieces[k + 1] = xor_send(pieces[k], "col", 1)
    return pieces


def finish_kernel(n_batch, rows, *refs):
    sums, (d_pre, normalised, gain, deviation) = refs[:n_batch], refs[n_batch : n_batch + 4]
    loss_ref, gain_ref, bias_ref, out_ref = refs[n_batch + 4 :]
    both = exchange_sum(x[...] for x in sums)
    bias_ref[...] = both[0:1] + both[1:2]
    gain_ref[...] = both[2:3] + both[3:4]
    loss_ref[...] = both[4:5, 0:128]
    for v in range(2):
        factor = gain[...] * deviation[v : v + 1]
        mean_b, mean_g = both[v : v + 1] / rows, both[2 + v : 3 + v] / rows
        out_ref[v] = factor * (d_pre[v] - mean_b - normalised[v] * mean_g)


def finish_call(sums, d_pre, normalised, gain, deviation, rows):
    _, local_rows, width = d_pre.shape
    operands = list(sums) + [d_pre, normalised, gain[None], deviation[:, 0]]
    out_shape = (
        jax.ShapeDtypeStruct((1, 128), f32),
        jax.ShapeDtypeStruct((1, width), f32),
        jax.ShapeDtypeStruct((1, width), f32),
        jax.ShapeDtypeStruct(d_pre.shape, f32),
    )
    return pl.pallas_call(
        functools.partial(finish_kernel, len(sums), rows),
        out_shape=out_shape,
        in_specs=[IN_VMEM] * len(operands),
        out_specs=(IN_VMEM,) * 4,
        compiler_params=params(4),
        cost_estimate=cost(0, 8 * d_pre.size),
        name="views_gradient",
    )(*operands)


def shards(views, norm_scale_gain, norm_shift_bias, weight):
    n_batch = lax.axis_size("batch")
    n_col = lax.axis_size("col")
    place = jnp.stack([lax.axis_index("batch"), lax.axis_index("col")]).astype(jnp.int32)
    views, norm_scale_gain, norm_shift_bias, weight, place = lax.optimization_barrier(
        (views, norm_scale_gain, norm_shift_bias, weight, place)
    )
    n_view, local_rows, width = views.shape
    features, columns = weight.shape
    E = columns * n_col
    rows = local_rows * n_batch
    tall = n_view * local_rows
    scale = rows * E / 128.0
    denom = float((rows - 1) ** 2 * E)
    evens = list(range(0, n_col, 2))
    odds = [k + 1 for k in evens]
    far = evens[1:]

    with jax.named_scope("weight_load"):
        held_weight, loaded = load_call(weight, (2 * n_view, width))
    with jax.named_scope("norm_stats"):
        hidden = views.astype(f32)
        local_mean = jnp.mean(hidden, axis=1)
        local_centred = hidden - local_mean[:, None, :]
        local_spread = jnp.sum(local_centred * local_centred, axis=1)
        stats = exchange(jnp.concatenate([local_mean, local_spread]), "batch")
        stats[-1] = stats[-1] + loaded
        mean = exchange_sum(s[:n_view] for s in stats) / n_batch
        spread = exchange_sum(
            s[n_view:] + local_rows * jnp.square(s[:n_view] - mean) for s in stats
        )
        var = spread / rows
        inverse_deviation = (1.0 / jnp.sqrt(var + eps_norm))[:, None, :]
        normalised = (hidden - mean[:, None, :]) * inverse_deviation
        preactivation = norm_scale_gain * normalised + norm_shift_bias
        act = jax.nn.gelu(preactivation, approximate=True).astype(bf16)
    with jax.named_scope("act_gather"):
        others = [ring_send(act[0], "batch", d) for d in range(1, n_batch)]
        own = act.reshape(tall, width)
        sibling = xor_send(own, "col", 1)
        own, sibling = lax.optimization_barrier((own, sibling))
        pieces = link_pieces(own, n_col)
        pieces[1] = sibling
        others, pieces[far[0]] = lax.optimization_barrier((others, pieces[far[0]]))
        pieces = sibling_pieces(pieces, n_col)
        far_pieces = link_pieces(jnp.concatenate(others), n_col)
    with jax.named_scope("z"):

        def z_of(source, groups, total=None):
            for i, ks in enumerate(groups):
                total = z_call(
                    place,
                    ks,
                    [source[k] for k in ks],
                    held_weight,
                    total,
                    i == len(groups) - 1,
                    local_rows,
                )
            return total

        z_own0, z_own1 = z_of(pieces, [[0, 1], far, [k + 1 for k in far]])
    with jax.named_scope("z_ring"):
        z_ring = [z_own1, ring_send(z_own1, "batch", 1)]
        z_ring[1], far_pieces[far[-1]] = lax.optimization_barrier((z_ring[1], far_pieces[far[-1]]))
        z_ring.append(ring_send(z_ring[1], "batch", 1))
    with jax.named_scope("z_far"):
        start = z_call(
            place, [0, far[-1]], [far_pieces[0], far_pieces[far[-1]]], held_weight, None, False, local_rows
        )
        start, far_pieces[far[0]], z_ring[2] = lax.optimization_barrier(
            (start, far_pieces[far[0]], z_ring[2])
        )
        far_pieces = sibling_pieces(far_pieces, n_col)
        for _ in range(3, n_batch):
            z_ring.append(ring_send(z_ring[-1], "batch", 1))
        z_far = z_of(far_pieces, [far[:-1], odds], start)
        slots = list(zip([z_own0] + list(z_far), z_ring))
    with jax.named_scope("kernel"):
        even_part, odd_part = strip_call(place, slots, n_col)
        even_part = even_part + xor_send(odd_part, "col", 1).astype(f32)
        even_part, held_back = lax.optimization_barrier((even_part, [pieces[k] for k in evens]))
        strip = even_part[0]
        for k in far:
            strip = strip + xor_send(even_part[k // 2].astype(bf16), "col", k).astype(f32)
        picked = pick_call(place, held_back, n_batch, n_col)
        blocks = [
            ring_send(x, "batch", 1 + i % (n_batch - 1)) for i, x in enumerate(picked)
        ]
        strips = gather_pieces(strip.astype(bf16), n_col)
        strips, blocks[:-1] = lax.optimization_barrier((strips, blocks[:-1]))
    with jax.named_scope("dz"):
        constants = (
            4.0 * scale / denom,
            25.0 * scale / (2.0 * E * (rows - 1)),
            50.0 * scale / (rows * E),
            25.0 / (rows * E) / n_batch,
            25.0 / (2 * E) / n_batch,
            1.0 / denom / n_batch,
            1.0 / denom / n_batch,
        )
        dz, share = dz_call(place, strip, [strips[k] for k in range(n_col)], slots, constants)
        dz, blocks[-1] = lax.optimization_barrier((dz, blocks[-1]))
    with jax.named_scope("d_act"):
        (away,) = d_act_call(place, dz, share, held_weight, n_batch, n_col, None)
        got = xor_send(away, "col", 1)
        *sends, d_act = d_act_call(place, dz, share, held_weight, n_batch, n_col, got)
        arrived = [xor_send(part, "col", k) for k, part in zip(far, sends)]
    with jax.named_scope("grad_weight"):
        grad_weight = None
        for block in range(n_col // n_batch // 2):
            mine = blocks[block * (n_batch - 1) : (block + 1) * (n_batch - 1)]
            other = [xor_send(x, "col", 1) for x in mine]
            for parity, ks, far_rows in ((0, evens, mine), (1, odds, other)):
                grad_weight = weight_grad_call(
                    place,
                    (block, parity),
                    [[group[k] for k in ks] for group in (pieces, far_pieces)],
                    far_rows,
                    dz,
                    features // n_batch,
                    grad_weight,
                )
    with jax.named_scope("norm_backward"):
        share = exchange_sum(share_of(part[tall:]) for part in [d_act] + arrived)
        d_act = d_act[:tall]
        for part in arrived:
            d_act = d_act + part[:tall].astype(f32)
        d_pre = d_act.reshape(n_view, local_rows, width) * gelu_slope(preactivation)
        sums = jnp.concatenate(
            [
                jnp.sum(d_pre, axis=1),
                jnp.sum(d_pre * normalised, axis=1),
                jnp.broadcast_to(share, (2 * n_view, width)),
            ]
        )
        loss, grad_gain, grad_bias, views_gradient = finish_call(
            exchange(sums, "batch"), d_pre, normalised, norm_scale_gain, inverse_deviation, rows
        )
    return (loss[0, 0], grad_weight, grad_gain[0], grad_bias[0], views_gradient)


def solution(mesh):
    placed = (P(None, "batch", "col"), P("col"), P("col"), P(None, "col"))
    return jax.shard_map(
        shards,
        mesh=mesh,
        in_specs=placed,
        out_specs=(P(), P("batch", "col"), P("col"), P("col"), P(None, "batch", "col")),
        check_vma=False,
    )
```

```python
import functools

import jax
import jax.numpy as jnp
from jax import lax
from jax.experimental import pallas as pl
from jax.experimental.pallas import tpu as pltpu
from jax.sharding import PartitionSpec as P

eps_norm = 1e-05
eps_std = 0.0001
f32 = jnp.float32
bf16 = jnp.bfloat16
MIB = 1024 * 1024


def gelu_slope(preactivation):
    value, pullback = jax.vjp(lambda t: jax.nn.gelu(t, approximate=True), preactivation)
    return pullback(jnp.ones_like(value))[0]


def xor_send(x, axis, k):
    n = lax.axis_size(axis)
    return lax.ppermute(x, axis, [(i, i ^ k) for i in range(n)])


def ring_order(n):
    return list(range(0, n, 2)) + list(range(1, n, 2))[::-1]


def ring_send(x, axis, d):
    order = ring_order(lax.axis_size(axis))
    n = len(order)
    return lax.ppermute(x, axis, [(order[i], order[(i + d) % n]) for i in range(n)])


def exchange_sum(parts):
    parts = list(parts)
    while len(parts) > 1:
        parts = [x + y for x, y in zip(parts[::2], parts[1::2])]
    return parts[0]


def exchange(x, axis):
    return [x] + [xor_send(x, axis, k) for k in range(1, lax.axis_size(axis))]


def params(limit):
    return pltpu.CompilerParams(vmem_limit_bytes=limit * MIB)


def cost(flops, moved):
    return pl.CostEstimate(flops=flops, bytes_accessed=moved, transcendentals=0)


IN_SMEM = pl.BlockSpec(memory_space=pltpu.SMEM)
IN_VMEM = pl.BlockSpec(memory_space=pltpu.VMEM)
ANYWHERE = pl.BlockSpec(memory_space=pl.ANY)
LOADS = 8


def load_kernel(w_ref, out_ref, flag_ref, sems):
    flag_ref[...] = jnp.zeros_like(flag_ref)
    step = w_ref.shape[0] // LOADS
    copies = [
        pltpu.make_async_copy(
            w_ref.at[pl.ds(i * step, step)], out_ref.at[pl.ds(i * step, step)], sems.at[i]
        )
        for i in range(LOADS)
    ]
    for copy in copies:
        copy.start()
    for copy in copies:
        copy.wait()


def load_call(weight, flag_shape):
    return pl.pallas_call(
        load_kernel,
        out_shape=(
            pltpu.VMEM(weight.shape, weight.dtype),
            jax.ShapeDtypeStruct(flag_shape, f32),
        ),
        in_specs=[ANYWHERE],
        out_specs=(IN_VMEM, IN_VMEM),
        scratch_shapes=[pltpu.SemaphoreType.DMA((LOADS,))],
        compiler_params=params(4),
        cost_estimate=cost(0, 4 * weight.size),
        name="weight_load",
    )(pltpu.with_memory_space_constraint(weight, pltpu.HBM))


def weight_rows(place_ref, w_ref, k, width):
    return w_ref[pl.ds(pl.multiple_of((place_ref[1] ^ k) * width, width), width), :]


def z_kernel(ks, first, last, local_rows, place_ref, *refs):
    count = len(ks)
    pieces, rest = refs[:count], list(refs[count:])
    w_ref = rest.pop(0)
    total = None if first else rest.pop(0)[...]
    width = pieces[0].shape[1]
    for j in range(count):
        part = jnp.dot(
            pieces[j][...], weight_rows(place_ref, w_ref, ks[j], width), preferred_element_type=f32
        )
        total = part if total is None else total + part
    if not last:
        rest[0][...] = total
        return
    z = total.astype(bf16)
    for v, ref in enumerate(rest):
        ref[...] = z[v * local_rows : (v + 1) * local_rows]


def z_call(place, ks, pieces, weight, before, last, local_rows):
    count = len(ks)
    tall, width = pieces[0].shape
    columns = weight.shape[1]
    operands = [place] + list(pieces) + [weight] + ([] if before is None else [before])
    if last:
        groups = tall // local_rows
        out_shape = (jax.ShapeDtypeStruct((local_rows, columns), bf16),) * groups
    else:
        out_shape = jax.ShapeDtypeStruct((tall, columns), f32)
    return pl.pallas_call(
        functools.partial(z_kernel, tuple(ks), before is None, last, local_rows),
        out_shape=out_shape,
        in_specs=[IN_SMEM] + [IN_VMEM] * (len(operands) - 1),
        out_specs=jax.tree.map(lambda _: IN_VMEM, out_shape),
        compiler_params=params(8),
        cost_estimate=cost(2 * tall * width * columns * count, 2 * tall * columns),
        name="z_matmul",
    )(*operands)


def upper_blocks(n):
    return [(s, t) for s in range(n) for t in range(s, n)]


def strip_kernel(n_batch, n_col, place_ref, *refs):
    z_refs, (even_ref, odd_ref, strip) = refs[: 2 * n_batch], refs[2 * n_batch :]
    local_rows = z_refs[0].shape[0]
    rows = local_rows * n_batch
    for v in range(2):
        zf = [z[...].astype(f32) for z in z_refs[v::2]]
        mean = sum(jnp.sum(z, axis=0, keepdims=True) for z in zf) / rows
        rounded = jnp.concatenate([(z - mean).astype(bf16) for z in zf], axis=0)
        at = 0
        for s in range(n_batch):
            product = lax.dot_general(
                rounded[s * local_rows : (s + 1) * local_rows],
                rounded[s * local_rows :],
                (((1,), (1,)), ((), ())),
                preferred_element_type=f32,
            )
            strip[pl.ds(v * local_rows, local_rows), pl.ds(at, product.shape[1])] = product
            at += product.shape[1]
    part = 2 * local_rows // n_col
    for k in range(n_col):
        start = pl.multiple_of((place_ref[1] ^ k) * part, part)
        ref = odd_ref if k % 2 else even_ref
        ref[k // 2] = strip[pl.ds(start, part), :].astype(ref.dtype)


def strip_call(place, z_slots, n_col):
    n_batch = len(z_slots)
    local_rows, columns = z_slots[0][0].shape
    tall = 2 * local_rows
    wide = len(upper_blocks(n_batch)) * local_rows
    shape = (n_col // 2, tall // n_col, wide)
    operands = [place] + [z for slot in z_slots for z in slot]
    return pl.pallas_call(
        functools.partial(strip_kernel, n_batch, n_col),
        out_shape=(jax.ShapeDtypeStruct(shape, f32), jax.ShapeDtypeStruct(shape, bf16)),
        in_specs=[IN_SMEM] + [IN_VMEM] * (len(operands) - 1),
        out_specs=(IN_VMEM, IN_VMEM),
        scratch_shapes=[pltpu.VMEM((tall, wide), f32)],
        compiler_params=params(18),
        cost_estimate=cost(2 * tall * wide * columns, 2 * tall * columns * n_batch),
        name="kernel_strip",
    )(*operands)


def dz_kernel(n_batch, n_col, tile, constants, place_ref, own_ref, *refs):
    coef, hinge_coef, inv_coef, inv_share, hinge_share, diag_share, block_share = constants
    strip_refs = refs[:n_col]
    z_refs = refs[n_col : n_col + 2 * n_batch]
    dz_ref, share_ref, strips, full, centred = refs[n_col + 2 * n_batch :]
    local_rows, columns = z_refs[0].shape
    rows = local_rows * n_batch
    own = own_ref[...]
    block = lax.broadcasted_iota(jnp.int32, own.shape, 1) // local_rows
    on_diagonal = functools.reduce(
        jnp.logical_or, [block == i for i, (s, t) in enumerate(upper_blocks(n_batch)) if s == t]
    )
    own = own * own * jnp.where(on_diagonal, 1.0, 2.0)
    own = jnp.sum(jnp.sum(own, axis=0, keepdims=True), axis=1, keepdims=True)
    share_ref[...] = jnp.broadcast_to(block_share * own, share_ref.shape)
    part = 2 * local_rows // n_col
    for k in range(n_col):
        start = pl.multiple_of((place_ref[1] ^ k) * part, part)
        strips[pl.ds(start, part), :] = strip_refs[k][...].astype(f32)
    for v in range(2):
        for i, (s, t) in enumerate(upper_blocks(n_batch)):
            here, there = pl.ds(s * local_rows, local_rows), pl.ds(t * local_rows, local_rows)
            block = strips[pl.ds(v * local_rows, local_rows), pl.ds(i * local_rows, local_rows)]
            full[v, here, there] = block.astype(bf16)
            if s < t:
                full[v, there, here] = jnp.transpose(block).astype(bf16)

    def one_tile(j, carry):
        here = pl.ds(pl.multiple_of(j * tile, tile), tile)
        share = jnp.zeros((1, 1), f32)
        grads = []
        z_views = []
        for v in range(2):
            zf = jnp.concatenate([z[:, here].astype(f32) for z in z_refs[v::2]], axis=0)
            z_views.append(zf)
            zc = zf - jnp.sum(zf, axis=0, keepdims=True) / rows
            std = jnp.sqrt(jnp.sum(zc * zc, axis=0, keepdims=True) / (rows - 1) + eps_std)
            zcb = zc.astype(bf16)
            centred[...] = zcb
            rounded = zcb.astype(f32)
            diag = jnp.sum(rounded * rounded, axis=0, keepdims=True)
            moved = jnp.dot(full[v], centred[...], preferred_element_type=f32)
            pull = jnp.where(std < 1.0, hinge_coef, 0.0) / std
            summed = coef * (moved - rounded * diag) - zc * pull
            grads.append(summed - jnp.sum(summed, axis=0, keepdims=True) / rows)
            share += hinge_share * jnp.sum(jnp.maximum(1.0 - std, 0.0), axis=1, keepdims=True)
            share -= diag_share * jnp.sum(diag * diag, axis=1, keepdims=True)
        diff = z_views[0] - z_views[1]
        share += inv_share * jnp.sum(
            jnp.sum(diff * diff, axis=0, keepdims=True), axis=1, keepdims=True
        )
        share_ref[...] += jnp.broadcast_to(share, share_ref.shape)
        dz_ref[0, :, here] = (grads[0] + inv_coef * diff).astype(bf16)
        dz_ref[1, :, here] = (grads[1] - inv_coef * diff).astype(bf16)
        return carry

    lax.fori_loop(0, columns // tile, one_tile, 0)


def dz_call(place, own, strips, z_slots, constants):
    n_col, n_batch = len(strips), len(z_slots)
    local_rows, columns = z_slots[0][0].shape
    tall = 2 * local_rows
    rows = local_rows * n_batch
    tile = min(256, columns)
    operands = [place, own] + list(strips) + [z for slot in z_slots for z in slot]
    return pl.pallas_call(
        functools.partial(dz_kernel, n_batch, n_col, tile, constants),
        out_shape=(
            jax.ShapeDtypeStruct((2, rows, columns), bf16),
            jax.ShapeDtypeStruct((8, 128), f32),
        ),
        in_specs=[IN_SMEM] + [IN_VMEM] * (len(operands) - 1),
        out_specs=(IN_VMEM, IN_VMEM),
        scratch_shapes=[
            pltpu.VMEM((tall, strips[0].shape[1]), f32),
            pltpu.VMEM((2, rows, rows), bf16),
            pltpu.VMEM((rows, tile), bf16),
        ],
        compiler_params=params(24),
        cost_estimate=cost(4 * rows * rows * columns, 8 * rows * columns),
        name="embedding_gradient",
    )(*operands)


EXTRA = 16


def share_rows(share, width, kind):
    high = share.astype(bf16).astype(f32)
    middle = (share - high).astype(bf16).astype(f32)
    low = share - high - middle
    row = lax.broadcasted_iota(jnp.int32, (EXTRA, width), 0)
    rows = jnp.where(row == 0, high, jnp.where(row == 1, middle, jnp.where(row == 2, low, 0.0)))
    return rows.astype(kind)


def share_of(rows):
    return rows[0:1].astype(f32) + rows[1:2].astype(f32) + rows[2:3].astype(f32)


def d_act_kernel(count, adds, place_ref, dz_ref, share_ref, w_ref, *refs):
    local_rows, columns = dz_ref.shape[1] // adds[1], dz_ref.shape[2]
    tall = 2 * local_rows
    dz = jnp.concatenate([dz_ref[0, :local_rows], dz_ref[1, :local_rows]], axis=0)
    width = w_ref.shape[0] // adds[2]
    share = share_ref[0:1, 0:1]
    for j in range(count):
        k = 2 * ((j + 1) % count) if adds[0] else 2 * j + 1
        part = lax.dot_general(
            dz,
            weight_rows(place_ref, w_ref, k, width),
            (((1,), (1,)), ((), ())),
            preferred_element_type=f32,
        )
        if not adds[0]:
            refs[0][j, :tall] = part.astype(refs[0].dtype)
            refs[0][j, tall:] = share_rows(share, width, refs[0].dtype)
        else:
            got = refs[0]
            out_ref = refs[j + 1]
            slot = (j + 1) % count
            out_ref[:tall] = (part + got[slot, :tall].astype(f32)).astype(out_ref.dtype)
            whole_share = share + share_of(got[slot, tall:])[:, 0:1]
            out_ref[tall:] = share_rows(whole_share, width, out_ref.dtype)


def d_act_call(place, dz, share, weight, n_batch, n_col, got):
    columns = weight.shape[1]
    width = weight.shape[0] // n_col
    tall = 2 * dz.shape[1] // n_batch
    count = n_col // 2
    operands = [place, dz, share, weight] + ([] if got is None else [got])
    if got is None:
        out_shape = (jax.ShapeDtypeStruct((count, tall + EXTRA, width), bf16),)
    else:
        out_shape = (jax.ShapeDtypeStruct((tall + EXTRA, width), bf16),) * (count - 1)
        out_shape += (jax.ShapeDtypeStruct((tall + EXTRA, width), f32),)
    return pl.pallas_call(
        functools.partial(d_act_kernel, count, (got is not None, n_batch, n_col)),
        out_shape=out_shape,
        in_specs=[IN_SMEM] + [IN_VMEM] * (len(operands) - 1),
        out_specs=(IN_VMEM,) * len(out_shape),
        compiler_params=params(8),
        cost_estimate=cost(2 * tall * width * columns * count, 2 * count * width * tall),
        name="d_act_matmul",
    )(*operands)


def held_place(plane, c, block, n_col, n_batch):
    return (((n_col // n_batch) * plane + 2 * block) ^ (c - (c & 1))) >> 1


def pick_kernel(n_batch, n_col, local_rows, place_ref, *refs):
    half = n_col // 2
    pieces, outs = refs[:half], refs[half:]
    b, c = place_ref[0], place_ref[1]
    position = jnp.where((b & 1) == 0, b >> 1, n_batch - 1 - (b >> 1))
    i = 0
    for block in range(n_col // n_batch // 2):
        for d in range(1, n_batch):
            ahead = position + d
            ahead = jnp.where(ahead >= n_batch, ahead - n_batch, ahead)
            plane = jnp.where(2 * ahead < n_batch, 2 * ahead, 2 * (n_batch - ahead) - 1)
            chosen = held_place(plane, c, block, n_col, n_batch)
            for e in range(half):

                @pl.when(chosen == e)
                def _():
                    outs[i][...] = pieces[e][local_rows:]

            i += 1


def pick_call(place, pieces, n_batch, n_col):
    tall, width = pieces[0].shape
    count = n_col // n_batch // 2 * (n_batch - 1)
    out_shape = (jax.ShapeDtypeStruct((tall // 2, width), bf16),) * count
    return pl.pallas_call(
        functools.partial(pick_kernel, n_batch, n_col, tall // 2),
        out_shape=out_shape,
        in_specs=[IN_SMEM] + [IN_VMEM] * len(pieces),
        out_specs=(IN_VMEM,) * count,
        compiler_params=params(4),
        cost_estimate=cost(0, tall * width * count),
        name="pick_blocks",
    )(place, *pieces)


def rows_product(act, dz, width, tile, write):
    for i in range(width // tile):
        write(
            i,
            lax.dot_general(
                act[:, pl.ds(i * tile, tile)],
                dz[...],
                (((0,), (0,)), ((), ())),
                preferred_element_type=f32,
            ),
        )


def weight_grad_kernel(n_batch, half, tile, block, place_ref, *refs):
    own, far = refs[:half], refs[half : 2 * half]
    dz_ref, out_ref, act = refs[2 * half :]
    local_rows = own[0].shape[0] // 2
    chosen = held_place(place_ref[0], place_ref[1], block, 2 * half, n_batch)
    for e in range(half):

        @pl.when(chosen == e)
        def _():
            act[:local_rows] = own[e][:local_rows]
            act[local_rows:] = far[e][...]

    def write(i, product):
        out_ref[pl.ds(i * tile, tile)] = product

    rows_product(act, dz_ref.at[0], act.shape[1], tile, write)


def weight_grad_call(place, n_batch, block, own, far, dz):
    width = own[0].shape[1]
    _, rows, columns = dz.shape
    tile = min(256, width)
    operands = [place] + list(own) + list(far) + [dz]
    return pl.pallas_call(
        functools.partial(weight_grad_kernel, n_batch, len(own), tile, block),
        out_shape=jax.ShapeDtypeStruct((width, columns), f32),
        in_specs=[IN_SMEM] + [IN_VMEM] * (len(operands) - 1),
        out_specs=IN_VMEM,
        scratch_shapes=[pltpu.VMEM((rows, width), bf16)],
        compiler_params=params(8),
        cost_estimate=cost(2 * rows * width * columns, 2 * rows * columns),
        name="weight_gradient_0",
    )(*operands)


def weight_grad_last_kernel(n_batch, half, tile, aliased, which, place_ref, *refs):
    own, (blocks_ref, dz_ref, before_ref) = refs[:half], refs[half : half + 3]
    out_ref, act, product, sems = refs[half + 3 + aliased :]
    local_rows = own[0].shape[0] // 2
    block, parity = which
    chosen = held_place(place_ref[0], place_ref[1], block, 2 * half, n_batch)
    out_row = 2 * block + ((place_ref[1] & 1) ^ parity)
    for e in range(half):

        @pl.when(chosen == e)
        def _():
            act[:local_rows] = own[e][local_rows:]

    act[local_rows:] = blocks_ref[...]
    width = act.shape[1]
    copies = []

    def write(i, part):
        here = pl.ds(i * tile, tile)
        product[here] = before_ref[here] + part
        start = pl.multiple_of(out_row * width + i * tile, tile)
        copies.append(
            pltpu.make_async_copy(product.at[here], out_ref.at[pl.ds(start, tile)], sems.at[i])
        )
        copies[-1].start()

    rows_product(act, dz_ref.at[1], width, tile, write)
    for copy in copies:
        copy.wait()


def weight_grad_last_call(place, which, own, blocks, dz, product, features, before):
    width = own[0].shape[1]
    _, rows, columns = dz.shape
    tile = min(256, width)
    operands = [place] + list(own) + [blocks, dz, product]
    specs = [IN_SMEM] + [IN_VMEM] * (len(operands) - 1)
    aliases = {}
    if before is not None:
        aliases = {len(operands): 0}
        operands.append(before)
        specs.append(ANYWHERE)
    return pl.pallas_call(
        functools.partial(
            weight_grad_last_kernel,
            rows // (own[0].shape[0] // 2),
            len(own),
            tile,
            int(before is not None),
            which,
        ),
        out_shape=jax.ShapeDtypeStruct((features, columns), f32),
        in_specs=specs,
        out_specs=ANYWHERE,
        scratch_shapes=[
            pltpu.VMEM((rows, width), bf16),
            pltpu.VMEM((width, columns), f32),
            pltpu.SemaphoreType.DMA((width // tile,)),
        ],
        input_output_aliases=aliases,
        compiler_params=params(10),
        cost_estimate=cost(2 * rows * width * columns, 4 * width * columns),
        name="weight_gradient_1",
    )(*operands)


def link_pieces(x, n_col):
    pieces = {0: x}
    half = x.shape[0] // 2
    for k in sorted(range(2, n_col, 2), key=lambda k: (bin(k).count("1"), k)):
        low, high = k & -k, 1 << (k.bit_length() - 1)
        if low == high:
            pieces[k] = xor_send(x, "col", k)
        else:
            first = xor_send(pieces[k ^ low][:half], "col", low)
            second = xor_send(pieces[k ^ high][half:], "col", high)
            pieces[k] = jnp.concatenate([first, second])
    return pieces


def sibling_pieces(pieces, n_col):
    for k in range(0, n_col, 2):
        if k + 1 not in pieces:
            pieces[k + 1] = xor_send(pieces[k], "col", 1)
    return pieces


def finish_kernel(n_batch, rows, *refs):
    sums, (d_pre, normalised, gain, deviation) = refs[:n_batch], refs[n_batch : n_batch + 4]
    loss_ref, gain_ref, bias_ref, out_ref = refs[n_batch + 4 :]
    both = exchange_sum(x[...] for x in sums)
    bias_ref[...] = both[0:1] + both[1:2]
    gain_ref[...] = both[2:3] + both[3:4]
    loss_ref[...] = both[4:5, 0:128]
    for v in range(2):
        factor = gain[...] * deviation[v : v + 1]
        mean_b, mean_g = both[v : v + 1] / rows, both[2 + v : 3 + v] / rows
        out_ref[v] = factor * (d_pre[v] - mean_b - normalised[v] * mean_g)


def finish_call(sums, d_pre, normalised, gain, deviation, rows):
    _, local_rows, width = d_pre.shape
    operands = list(sums) + [d_pre, normalised, gain[None], deviation[:, 0]]
    out_shape = (
        jax.ShapeDtypeStruct((1, 128), f32),
        jax.ShapeDtypeStruct((1, width), f32),
        jax.ShapeDtypeStruct((1, width), f32),
        jax.ShapeDtypeStruct(d_pre.shape, f32),
    )
    return pl.pallas_call(
        functools.partial(finish_kernel, len(sums), rows),
        out_shape=out_shape,
        in_specs=[IN_VMEM] * len(operands),
        out_specs=(IN_VMEM,) * 4,
        compiler_params=params(4),
        cost_estimate=cost(0, 8 * d_pre.size),
        name="views_gradient",
    )(*operands)


def shards(views, norm_scale_gain, norm_shift_bias, weight):
    n_batch = lax.axis_size("batch")
    n_col = lax.axis_size("col")
    place = jnp.stack([lax.axis_index("batch"), lax.axis_index("col")]).astype(jnp.int32)
    views, norm_scale_gain, norm_shift_bias, weight, place = lax.optimization_barrier(
        (views, norm_scale_gain, norm_shift_bias, weight, place)
    )
    n_view, local_rows, width = views.shape
    features, columns = weight.shape
    E = columns * n_col
    rows = local_rows * n_batch
    tall = n_view * local_rows
    scale = rows * E / 128.0
    denom = float((rows - 1) ** 2 * E)
    evens = list(range(0, n_col, 2))
    odds = [k + 1 for k in evens]
    far = evens[1:]

    with jax.named_scope("weight_load"):
        held_weight, loaded = load_call(weight, (2 * n_view, width))
    with jax.named_scope("norm_stats"):
        hidden = views.astype(f32)
        local_mean = jnp.mean(hidden, axis=1)
        local_centred = hidden - local_mean[:, None, :]
        local_spread = jnp.sum(local_centred * local_centred, axis=1)
        stats = exchange(jnp.concatenate([local_mean, local_spread]), "batch")
        stats[-1] = stats[-1] + loaded
        mean = exchange_sum(s[:n_view] for s in stats) / n_batch
        spread = exchange_sum(
            s[n_view:] + local_rows * jnp.square(s[:n_view] - mean) for s in stats
        )
        var = spread / rows
        inverse_deviation = (1.0 / jnp.sqrt(var + eps_norm))[:, None, :]
        normalised = (hidden - mean[:, None, :]) * inverse_deviation
        preactivation = norm_scale_gain * normalised + norm_shift_bias
        act = jax.nn.gelu(preactivation, approximate=True).astype(bf16)
    with jax.named_scope("act_gather"):
        others = [ring_send(act[0], "batch", d) for d in range(1, n_batch)]
        own = act.reshape(tall, width)
        sibling = xor_send(own, "col", 1)
        own, sibling = lax.optimization_barrier((own, sibling))
        pieces = link_pieces(own, n_col)
        pieces[1] = sibling
        others, pieces[far[0]] = lax.optimization_barrier((others, pieces[far[0]]))
        pieces = sibling_pieces(pieces, n_col)
        far_pieces = link_pieces(jnp.concatenate(others), n_col)
    with jax.named_scope("z"):

        def z_of(source, groups, total=None):
            for i, ks in enumerate(groups):
                total = z_call(
                    place,
                    ks,
                    [source[k] for k in ks],
                    held_weight,
                    total,
                    i == len(groups) - 1,
                    local_rows,
                )
            return total

        z_own0, z_own1 = z_of(pieces, [[0, 1], far, [k + 1 for k in far]])
    with jax.named_scope("z_ring"):
        z_ring = [z_own1, ring_send(z_own1, "batch", 1)]
        z_ring[1], far_pieces[far[0]] = lax.optimization_barrier((z_ring[1], far_pieces[far[0]]))
        z_ring.append(ring_send(z_ring[1], "batch", 1))
    with jax.named_scope("z_far"):
        start = z_call(
            place, [0] + far[:-1], [far_pieces[k] for k in [0] + far[:-1]], held_weight, None, False, local_rows
        )
        picked = list(pick_call(place, [pieces[k] for k in evens], n_batch, n_col))
        start, far_pieces[far[-1]], z_ring[2], picked = lax.optimization_barrier(
            (start, far_pieces[far[-1]], z_ring[2], picked)
        )
        far_pieces = sibling_pieces(far_pieces, n_col)
        for _ in range(3, n_batch):
            z_ring.append(ring_send(z_ring[-1], "batch", 1))
        z_far = z_of(far_pieces, [odds[:-1] + far[-1:] + odds[-1:]], start)
        slots = list(zip([z_own0] + list(z_far), z_ring))
    with jax.named_scope("kernel"):
        even_part, odd_part = strip_call(place, slots, n_col)
        even_part = even_part + xor_send(odd_part, "col", 1).astype(f32)
        early = len(picked) // 3
        even_part, picked[:early] = lax.optimization_barrier((even_part, picked[:early]))

        def sent(i):
            return ring_send(picked[i], "batch", 1 + i % (n_batch - 1))

        strip = even_part[0]
        for k in far:
            strip = strip + xor_send(even_part[k // 2].astype(bf16), "col", k).astype(f32)
        strip_b = strip.astype(bf16)
        strips = {0: strip_b}
        for k in far:
            strips[k] = xor_send(strip_b, "col", k)
        strips = sibling_pieces(strips, n_col)
        blocks = [sent(i) for i in range(early)]
        strips, blocks = lax.optimization_barrier((strips, blocks))
    with jax.named_scope("dz"):
        constants = (
            4.0 * scale / denom,
            25.0 * scale / (2.0 * E * (rows - 1)),
            50.0 * scale / (rows * E),
            25.0 / (rows * E) / n_batch,
            25.0 / (2 * E) / n_batch,
            1.0 / denom / n_batch,
            1.0 / denom / n_batch,
        )
        dz, share = dz_call(place, strip, [strips[k] for k in range(n_col)], slots, constants)
        blocks += [sent(i) for i in range(early, 2 * early)]
        dz, blocks[early:] = lax.optimization_barrier((dz, blocks[early:]))
    with jax.named_scope("d_act"):
        (away,) = d_act_call(place, dz, share, held_weight, n_batch, n_col, None)
        got = xor_send(away, "col", 1)
        *sends, d_act = d_act_call(place, dz, share, held_weight, n_batch, n_col, got)
        arrived = [xor_send(part, "col", k) for k, part in zip(far, sends)]
    with jax.named_scope("grad_weight"):
        late = picked[2 * early :]
        d_act, picked[2 * early :] = lax.optimization_barrier((d_act, late))
        blocks += [sent(i) for i in range(2 * early, len(picked))]
        sides = ((0, evens), (1, odds))
        products = {}
        for block in range(n_col // n_batch // 2):
            for parity, ks in sides:
                products[block, parity] = weight_grad_call(
                    place, n_batch, block, [pieces[k] for k in ks], [far_pieces[k] for k in ks], dz
                )
        grad_weight = None
        for block in range(n_col // n_batch // 2):
            mine = jnp.concatenate(blocks[block * (n_batch - 1) : (block + 1) * (n_batch - 1)])
            other = xor_send(mine, "col", 1)
            for (parity, ks), far_rows in zip(sides, (mine, other)):
                grad_weight = weight_grad_last_call(
                    place,
                    (block, parity),
                    [pieces[k] for k in ks],
                    far_rows,
                    dz,
                    products[block, parity],
                    features // n_batch,
                    grad_weight,
                )
                if block == 0 and parity == 0:
                    arrived, grad_weight = lax.optimization_barrier((arrived, grad_weight))
    with jax.named_scope("norm_backward"):
        share = exchange_sum(share_of(part[tall:]) for part in [d_act] + arrived)
        d_act = d_act[:tall]
        for part in arrived:
            d_act = d_act + part[:tall].astype(f32)
        d_pre = d_act.reshape(n_view, local_rows, width) * gelu_slope(preactivation)
        sums = jnp.concatenate(
            [
                jnp.sum(d_pre, axis=1),
                jnp.sum(d_pre * normalised, axis=1),
                jnp.broadcast_to(share, (2 * n_view, width)),
            ]
        )
        loss, grad_gain, grad_bias, views_gradient = finish_call(
            exchange(sums, "batch"), d_pre, normalised, norm_scale_gain, inverse_deviation, rows
        )
    return (loss[0, 0], grad_weight, grad_gain[0], grad_bias[0], views_gradient)


def solution(mesh):
    placed = (P(None, "batch", "col"), P("col"), P("col"), P(None, "col"))
    return jax.shard_map(
        shards,
        mesh=mesh,
        in_specs=placed,
        out_specs=(P(), P("batch", "col"), P("col"), P("col"), P(None, "batch", "col")),
        check_vma=False,
    )
```

```python
import functools

import jax
import jax.numpy as jnp
from jax import lax
from jax.experimental import pallas as pl
from jax.experimental.pallas import tpu as pltpu
from jax.sharding import PartitionSpec as P

eps_norm = 1e-05
eps_std = 0.0001
f32 = jnp.float32
bf16 = jnp.bfloat16
MIB = 1024 * 1024


def gelu_slope(preactivation):
    value, pullback = jax.vjp(lambda t: jax.nn.gelu(t, approximate=True), preactivation)
    return pullback(jnp.ones_like(value))[0]


def xor_send(x, axis, k):
    n = lax.axis_size(axis)
    return lax.ppermute(x, axis, [(i, i ^ k) for i in range(n)])


def ring_order(n):
    return list(range(0, n, 2)) + list(range(1, n, 2))[::-1]


def ring_send(x, axis, d):
    order = ring_order(lax.axis_size(axis))
    n = len(order)
    return lax.ppermute(x, axis, [(order[i], order[(i + d) % n]) for i in range(n)])


def exchange_sum(parts):
    parts = list(parts)
    while len(parts) > 1:
        parts = [x + y for x, y in zip(parts[::2], parts[1::2])]
    return parts[0]


def exchange(x, axis):
    return [x] + [xor_send(x, axis, k) for k in range(1, lax.axis_size(axis))]


def params(limit):
    return pltpu.CompilerParams(vmem_limit_bytes=limit * MIB)


def cost(flops, moved):
    return pl.CostEstimate(flops=flops, bytes_accessed=moved, transcendentals=0)


IN_SMEM = pl.BlockSpec(memory_space=pltpu.SMEM)
IN_VMEM = pl.BlockSpec(memory_space=pltpu.VMEM)
ANYWHERE = pl.BlockSpec(memory_space=pl.ANY)
LOADS = 8


def load_kernel(w_ref, out_ref, flag_ref, sems):
    flag_ref[...] = jnp.zeros_like(flag_ref)
    step = w_ref.shape[0] // LOADS
    copies = [
        pltpu.make_async_copy(
            w_ref.at[pl.ds(i * step, step)], out_ref.at[pl.ds(i * step, step)], sems.at[i]
        )
        for i in range(LOADS)
    ]
    for copy in copies:
        copy.start()
    for copy in copies:
        copy.wait()


def load_call(weight, flag_shape):
    return pl.pallas_call(
        load_kernel,
        out_shape=(
            pltpu.VMEM(weight.shape, weight.dtype),
            jax.ShapeDtypeStruct(flag_shape, f32),
        ),
        in_specs=[ANYWHERE],
        out_specs=(IN_VMEM, IN_VMEM),
        scratch_shapes=[pltpu.SemaphoreType.DMA((LOADS,))],
        compiler_params=params(4),
        cost_estimate=cost(0, 4 * weight.size),
        name="weight_load",
    )(pltpu.with_memory_space_constraint(weight, pltpu.HBM))


def weight_rows(place_ref, w_ref, k, width):
    return w_ref[pl.ds(pl.multiple_of((place_ref[1] ^ k) * width, width), width), :]


def z_kernel(ks, first, last, local_rows, place_ref, *refs):
    count = len(ks)
    pieces, rest = refs[:count], list(refs[count:])
    w_ref = rest.pop(0)
    total = None if first else rest.pop(0)[...]
    width = pieces[0].shape[1]
    for j in range(count):
        part = jnp.dot(
            pieces[j][...], weight_rows(place_ref, w_ref, ks[j], width), preferred_element_type=f32
        )
        total = part if total is None else total + part
    if not last:
        rest[0][...] = total
        return
    z = total.astype(bf16)
    for v, ref in enumerate(rest):
        ref[...] = z[v * local_rows : (v + 1) * local_rows]


def z_call(place, ks, pieces, weight, before, last, local_rows):
    count = len(ks)
    tall, width = pieces[0].shape
    columns = weight.shape[1]
    operands = [place] + list(pieces) + [weight] + ([] if before is None else [before])
    if last:
        groups = tall // local_rows
        out_shape = (jax.ShapeDtypeStruct((local_rows, columns), bf16),) * groups
    else:
        out_shape = jax.ShapeDtypeStruct((tall, columns), f32)
    return pl.pallas_call(
        functools.partial(z_kernel, tuple(ks), before is None, last, local_rows),
        out_shape=out_shape,
        in_specs=[IN_SMEM] + [IN_VMEM] * (len(operands) - 1),
        out_specs=jax.tree.map(lambda _: IN_VMEM, out_shape),
        compiler_params=params(8),
        cost_estimate=cost(2 * tall * width * columns * count, 2 * tall * columns),
        name="z_matmul",
    )(*operands)


def upper_blocks(n):
    return [(s, t) for s in range(n) for t in range(s, n)]


def strip_kernel(n_batch, n_col, place_ref, *refs):
    z_refs, (even_ref, odd_ref, strip) = refs[: 2 * n_batch], refs[2 * n_batch :]
    local_rows = z_refs[0].shape[0]
    rows = local_rows * n_batch
    for v in range(2):
        zf = [z[...].astype(f32) for z in z_refs[v::2]]
        mean = sum(jnp.sum(z, axis=0, keepdims=True) for z in zf) / rows
        rounded = jnp.concatenate([(z - mean).astype(bf16) for z in zf], axis=0)
        at = 0
        for s in range(n_batch):
            product = lax.dot_general(
                rounded[s * local_rows : (s + 1) * local_rows],
                rounded[s * local_rows :],
                (((1,), (1,)), ((), ())),
                preferred_element_type=f32,
            )
            strip[pl.ds(v * local_rows, local_rows), pl.ds(at, product.shape[1])] = product
            at += product.shape[1]
    part = 2 * local_rows // n_col
    for k in range(n_col):
        start = pl.multiple_of((place_ref[1] ^ k) * part, part)
        ref = odd_ref if k % 2 else even_ref
        ref[k // 2] = strip[pl.ds(start, part), :].astype(ref.dtype)


def strip_call(place, z_slots, n_col):
    n_batch = len(z_slots)
    local_rows, columns = z_slots[0][0].shape
    tall = 2 * local_rows
    wide = len(upper_blocks(n_batch)) * local_rows
    shape = (n_col // 2, tall // n_col, wide)
    operands = [place] + [z for slot in z_slots for z in slot]
    return pl.pallas_call(
        functools.partial(strip_kernel, n_batch, n_col),
        out_shape=(jax.ShapeDtypeStruct(shape, f32), jax.ShapeDtypeStruct(shape, bf16)),
        in_specs=[IN_SMEM] + [IN_VMEM] * (len(operands) - 1),
        out_specs=(IN_VMEM, IN_VMEM),
        scratch_shapes=[pltpu.VMEM((tall, wide), f32)],
        compiler_params=params(18),
        cost_estimate=cost(2 * tall * wide * columns, 2 * tall * columns * n_batch),
        name="kernel_strip",
    )(*operands)


def dz_kernel(n_batch, n_col, tile, constants, place_ref, own_ref, *refs):
    coef, hinge_coef, inv_coef, inv_share, hinge_share, diag_share, block_share = constants
    strip_refs = refs[:n_col]
    z_refs = refs[n_col : n_col + 2 * n_batch]
    dz_ref, share_ref, strips, full, centred = refs[n_col + 2 * n_batch :]
    local_rows, columns = z_refs[0].shape
    rows = local_rows * n_batch
    own = own_ref[...]
    block = lax.broadcasted_iota(jnp.int32, own.shape, 1) // local_rows
    on_diagonal = functools.reduce(
        jnp.logical_or, [block == i for i, (s, t) in enumerate(upper_blocks(n_batch)) if s == t]
    )
    own = own * own * jnp.where(on_diagonal, 1.0, 2.0)
    own = jnp.sum(jnp.sum(own, axis=0, keepdims=True), axis=1, keepdims=True)
    share_ref[...] = jnp.broadcast_to(block_share * own, share_ref.shape)
    part = 2 * local_rows // n_col
    for k in range(n_col):
        start = pl.multiple_of((place_ref[1] ^ k) * part, part)
        strips[pl.ds(start, part), :] = strip_refs[k][...].astype(f32)
    for v in range(2):
        for i, (s, t) in enumerate(upper_blocks(n_batch)):
            here, there = pl.ds(s * local_rows, local_rows), pl.ds(t * local_rows, local_rows)
            block = strips[pl.ds(v * local_rows, local_rows), pl.ds(i * local_rows, local_rows)]
            full[v, here, there] = block.astype(bf16)
            if s < t:
                full[v, there, here] = jnp.transpose(block).astype(bf16)

    def one_tile(j, carry):
        here = pl.ds(pl.multiple_of(j * tile, tile), tile)
        share = jnp.zeros((1, 1), f32)
        grads = []
        z_views = []
        for v in range(2):
            zf = jnp.concatenate([z[:, here].astype(f32) for z in z_refs[v::2]], axis=0)
            z_views.append(zf)
            zc = zf - jnp.sum(zf, axis=0, keepdims=True) / rows
            std = jnp.sqrt(jnp.sum(zc * zc, axis=0, keepdims=True) / (rows - 1) + eps_std)
            zcb = zc.astype(bf16)
            centred[...] = zcb
            rounded = zcb.astype(f32)
            diag = jnp.sum(rounded * rounded, axis=0, keepdims=True)
            moved = jnp.dot(full[v], centred[...], preferred_element_type=f32)
            pull = jnp.where(std < 1.0, hinge_coef, 0.0) / std
            summed = coef * (moved - rounded * diag) - zc * pull
            grads.append(summed - jnp.sum(summed, axis=0, keepdims=True) / rows)
            share += hinge_share * jnp.sum(jnp.maximum(1.0 - std, 0.0), axis=1, keepdims=True)
            share -= diag_share * jnp.sum(diag * diag, axis=1, keepdims=True)
        diff = z_views[0] - z_views[1]
        share += inv_share * jnp.sum(
            jnp.sum(diff * diff, axis=0, keepdims=True), axis=1, keepdims=True
        )
        share_ref[...] += jnp.broadcast_to(share, share_ref.shape)
        dz_ref[0, :, here] = (grads[0] + inv_coef * diff).astype(bf16)
        dz_ref[1, :, here] = (grads[1] - inv_coef * diff).astype(bf16)
        return carry

    lax.fori_loop(0, columns // tile, one_tile, 0)


def dz_call(place, own, strips, z_slots, constants):
    n_col, n_batch = len(strips), len(z_slots)
    local_rows, columns = z_slots[0][0].shape
    tall = 2 * local_rows
    rows = local_rows * n_batch
    tile = min(256, columns)
    operands = [place, own] + list(strips) + [z for slot in z_slots for z in slot]
    return pl.pallas_call(
        functools.partial(dz_kernel, n_batch, n_col, tile, constants),
        out_shape=(
            jax.ShapeDtypeStruct((2, rows, columns), bf16),
            jax.ShapeDtypeStruct((8, 128), f32),
        ),
        in_specs=[IN_SMEM] + [IN_VMEM] * (len(operands) - 1),
        out_specs=(IN_VMEM, IN_VMEM),
        scratch_shapes=[
            pltpu.VMEM((tall, strips[0].shape[1]), f32),
            pltpu.VMEM((2, rows, rows), bf16),
            pltpu.VMEM((rows, tile), bf16),
        ],
        compiler_params=params(24),
        cost_estimate=cost(4 * rows * rows * columns, 8 * rows * columns),
        name="embedding_gradient",
    )(*operands)


EXTRA = 16


def share_rows(share, width, kind):
    high = share.astype(bf16).astype(f32)
    middle = (share - high).astype(bf16).astype(f32)
    low = share - high - middle
    row = lax.broadcasted_iota(jnp.int32, (EXTRA, width), 0)
    rows = jnp.where(row == 0, high, jnp.where(row == 1, middle, jnp.where(row == 2, low, 0.0)))
    return rows.astype(kind)


def share_of(rows):
    return rows[0:1].astype(f32) + rows[1:2].astype(f32) + rows[2:3].astype(f32)


def d_act_kernel(count, adds, place_ref, dz_ref, share_ref, w_ref, *refs):
    local_rows, columns = dz_ref.shape[1] // adds[1], dz_ref.shape[2]
    tall = 2 * local_rows
    dz = jnp.concatenate([dz_ref[0, :local_rows], dz_ref[1, :local_rows]], axis=0)
    width = w_ref.shape[0] // adds[2]
    share = share_ref[0:1, 0:1]
    for j in range(count):
        k = 2 * ((j + 1) % count) if adds[0] else 2 * j + 1
        part = lax.dot_general(
            dz,
            weight_rows(place_ref, w_ref, k, width),
            (((1,), (1,)), ((), ())),
            preferred_element_type=f32,
        )
        if not adds[0]:
            refs[0][j, :tall] = part.astype(refs[0].dtype)
            refs[0][j, tall:] = share_rows(share, width, refs[0].dtype)
        else:
            got = refs[0]
            out_ref = refs[j + 1]
            slot = (j + 1) % count
            out_ref[:tall] = (part + got[slot, :tall].astype(f32)).astype(out_ref.dtype)
            whole_share = share + share_of(got[slot, tall:])[:, 0:1]
            out_ref[tall:] = share_rows(whole_share, width, out_ref.dtype)


def d_act_call(place, dz, share, weight, n_batch, n_col, got):
    columns = weight.shape[1]
    width = weight.shape[0] // n_col
    tall = 2 * dz.shape[1] // n_batch
    count = n_col // 2
    operands = [place, dz, share, weight] + ([] if got is None else [got])
    if got is None:
        out_shape = (jax.ShapeDtypeStruct((count, tall + EXTRA, width), bf16),)
    else:
        out_shape = (jax.ShapeDtypeStruct((tall + EXTRA, width), bf16),) * (count - 1)
        out_shape += (jax.ShapeDtypeStruct((tall + EXTRA, width), f32),)
    return pl.pallas_call(
        functools.partial(d_act_kernel, count, (got is not None, n_batch, n_col)),
        out_shape=out_shape,
        in_specs=[IN_SMEM] + [IN_VMEM] * (len(operands) - 1),
        out_specs=(IN_VMEM,) * len(out_shape),
        compiler_params=params(8),
        cost_estimate=cost(2 * tall * width * columns * count, 2 * count * width * tall),
        name="d_act_matmul",
    )(*operands)


def held_place(plane, c, block, n_col, n_batch):
    return (((n_col // n_batch) * plane + 2 * block) ^ (c - (c & 1))) >> 1


def pick_kernel(n_batch, n_col, local_rows, place_ref, *refs):
    half = n_col // 2
    pieces, outs = refs[:half], refs[half:]
    b, c = place_ref[0], place_ref[1]
    position = jnp.where((b & 1) == 0, b >> 1, n_batch - 1 - (b >> 1))
    i = 0
    for block in range(n_col // n_batch // 2):
        for d in range(1, n_batch):
            ahead = position + d
            ahead = jnp.where(ahead >= n_batch, ahead - n_batch, ahead)
            plane = jnp.where(2 * ahead < n_batch, 2 * ahead, 2 * (n_batch - ahead) - 1)
            chosen = held_place(plane, c, block, n_col, n_batch)
            for e in range(half):

                @pl.when(chosen == e)
                def _():
                    outs[i][...] = pieces[e][local_rows:]

            i += 1


def pick_call(place, pieces, n_batch, n_col):
    tall, width = pieces[0].shape
    count = n_col // n_batch // 2 * (n_batch - 1)
    out_shape = (jax.ShapeDtypeStruct((tall // 2, width), bf16),) * count
    return pl.pallas_call(
        functools.partial(pick_kernel, n_batch, n_col, tall // 2),
        out_shape=out_shape,
        in_specs=[IN_SMEM] + [IN_VMEM] * len(pieces),
        out_specs=(IN_VMEM,) * count,
        compiler_params=params(4),
        cost_estimate=cost(0, tall * width * count),
        name="pick_blocks",
    )(place, *pieces)


def rows_product(act, dz, width, tile, write):
    for i in range(width // tile):
        write(
            i,
            lax.dot_general(
                act[:, pl.ds(i * tile, tile)],
                dz[...],
                (((0,), (0,)), ((), ())),
                preferred_element_type=f32,
            ),
        )


def weight_grad_kernel(n_batch, half, tile, block, place_ref, *refs):
    own, far = refs[:half], refs[half : 2 * half]
    dz_ref, out_ref, act = refs[2 * half :]
    local_rows = own[0].shape[0] // 2
    chosen = held_place(place_ref[0], place_ref[1], block, 2 * half, n_batch)
    for e in range(half):

        @pl.when(chosen == e)
        def _():
            act[:local_rows] = own[e][:local_rows]
            act[local_rows:] = far[e][...]

    def write(i, product):
        out_ref[pl.ds(i * tile, tile)] = product

    rows_product(act, dz_ref.at[0], act.shape[1], tile, write)


def weight_grad_call(place, n_batch, block, own, far, dz):
    width = own[0].shape[1]
    _, rows, columns = dz.shape
    tile = min(256, width)
    operands = [place] + list(own) + list(far) + [dz]
    return pl.pallas_call(
        functools.partial(weight_grad_kernel, n_batch, len(own), tile, block),
        out_shape=jax.ShapeDtypeStruct((width, columns), f32),
        in_specs=[IN_SMEM] + [IN_VMEM] * (len(operands) - 1),
        out_specs=IN_VMEM,
        scratch_shapes=[pltpu.VMEM((rows, width), bf16)],
        compiler_params=params(8),
        cost_estimate=cost(2 * rows * width * columns, 2 * rows * columns),
        name="weight_gradient_0",
    )(*operands)


def weight_grad_last_kernel(n_batch, half, tile, aliased, which, place_ref, *refs):
    own, (blocks_ref, dz_ref, before_ref) = refs[:half], refs[half : half + 3]
    out_ref, act, product, sems = refs[half + 3 + aliased :]
    local_rows = own[0].shape[0] // 2
    block, parity = which
    chosen = held_place(place_ref[0], place_ref[1], block, 2 * half, n_batch)
    out_row = 2 * block + ((place_ref[1] & 1) ^ parity)
    for e in range(half):

        @pl.when(chosen == e)
        def _():
            act[:local_rows] = own[e][local_rows:]

    act[local_rows:] = blocks_ref[...]
    width = act.shape[1]
    copies = []

    def write(i, part):
        here = pl.ds(i * tile, tile)
        product[here] = before_ref[here] + part
        start = pl.multiple_of(out_row * width + i * tile, tile)
        copies.append(
            pltpu.make_async_copy(product.at[here], out_ref.at[pl.ds(start, tile)], sems.at[i])
        )
        copies[-1].start()

    rows_product(act, dz_ref.at[1], width, tile, write)
    for copy in copies:
        copy.wait()


def weight_grad_last_call(place, which, own, blocks, dz, product, features, before):
    width = own[0].shape[1]
    _, rows, columns = dz.shape
    tile = min(256, width)
    operands = [place] + list(own) + [blocks, dz, product]
    specs = [IN_SMEM] + [IN_VMEM] * (len(operands) - 1)
    aliases = {}
    if before is not None:
        aliases = {len(operands): 0}
        operands.append(before)
        specs.append(ANYWHERE)
    return pl.pallas_call(
        functools.partial(
            weight_grad_last_kernel,
            rows // (own[0].shape[0] // 2),
            len(own),
            tile,
            int(before is not None),
            which,
        ),
        out_shape=jax.ShapeDtypeStruct((features, columns), f32),
        in_specs=specs,
        out_specs=ANYWHERE,
        scratch_shapes=[
            pltpu.VMEM((rows, width), bf16),
            pltpu.VMEM((width, columns), f32),
            pltpu.SemaphoreType.DMA((width // tile,)),
        ],
        input_output_aliases=aliases,
        compiler_params=params(10),
        cost_estimate=cost(2 * rows * width * columns, 4 * width * columns),
        name="weight_gradient_1",
    )(*operands)


def link_pieces(x, n_col):
    pieces = {0: x}
    half = x.shape[0] // 2
    for k in sorted(range(2, n_col, 2), key=lambda k: (bin(k).count("1"), k)):
        low, high = k & -k, 1 << (k.bit_length() - 1)
        if low == high:
            pieces[k] = xor_send(x, "col", k)
        else:
            first = xor_send(pieces[k ^ low][:half], "col", low)
            second = xor_send(pieces[k ^ high][half:], "col", high)
            pieces[k] = jnp.concatenate([first, second])
    return pieces


def sibling_pieces(pieces, n_col):
    for k in range(0, n_col, 2):
        if k + 1 not in pieces:
            pieces[k + 1] = xor_send(pieces[k], "col", 1)
    return pieces


def finish_kernel(n_batch, rows, *refs):
    sums, (d_pre, normalised, gain, deviation) = refs[:n_batch], refs[n_batch : n_batch + 4]
    loss_ref, gain_ref, bias_ref, out_ref = refs[n_batch + 4 :]
    both = exchange_sum(x[...] for x in sums)
    bias_ref[...] = both[0:1] + both[1:2]
    gain_ref[...] = both[2:3] + both[3:4]
    loss_ref[...] = both[4:5, 0:128]
    for v in range(2):
        factor = gain[...] * deviation[v : v + 1]
        mean_b, mean_g = both[v : v + 1] / rows, both[2 + v : 3 + v] / rows
        out_ref[v] = factor * (d_pre[v] - mean_b - normalised[v] * mean_g)


def finish_call(sums, d_pre, normalised, gain, deviation, rows):
    _, local_rows, width = d_pre.shape
    operands = list(sums) + [d_pre, normalised, gain[None], deviation[:, 0]]
    out_shape = (
        jax.ShapeDtypeStruct((1, 128), f32),
        jax.ShapeDtypeStruct((1, width), f32),
        jax.ShapeDtypeStruct((1, width), f32),
        jax.ShapeDtypeStruct(d_pre.shape, f32),
    )
    return pl.pallas_call(
        functools.partial(finish_kernel, len(sums), rows),
        out_shape=out_shape,
        in_specs=[IN_VMEM] * len(operands),
        out_specs=(IN_VMEM,) * 4,
        compiler_params=params(4),
        cost_estimate=cost(0, 8 * d_pre.size),
        name="views_gradient",
    )(*operands)


def shards(views, norm_scale_gain, norm_shift_bias, weight):
    n_batch = lax.axis_size("batch")
    n_col = lax.axis_size("col")
    place = jnp.stack([lax.axis_index("batch"), lax.axis_index("col")]).astype(jnp.int32)
    views, norm_scale_gain, norm_shift_bias, weight, place = lax.optimization_barrier(
        (views, norm_scale_gain, norm_shift_bias, weight, place)
    )
    n_view, local_rows, width = views.shape
    features, columns = weight.shape
    E = columns * n_col
    rows = local_rows * n_batch
    tall = n_view * local_rows
    scale = rows * E / 128.0
    denom = float((rows - 1) ** 2 * E)
    evens = list(range(0, n_col, 2))
    odds = [k + 1 for k in evens]
    far = evens[1:]

    with jax.named_scope("weight_load"):
        held_weight, loaded = load_call(weight, (2 * n_view, width))
    with jax.named_scope("norm_stats"):
        hidden = views.astype(f32)
        local_mean = jnp.mean(hidden, axis=1)
        local_centred = hidden - local_mean[:, None, :]
        local_spread = jnp.sum(local_centred * local_centred, axis=1)
        stats = exchange(jnp.concatenate([local_mean, local_spread]), "batch")
        stats[-1] = stats[-1] + loaded
        mean = exchange_sum(s[:n_view] for s in stats) / n_batch
        spread = exchange_sum(
            s[n_view:] + local_rows * jnp.square(s[:n_view] - mean) for s in stats
        )
        var = spread / rows
        inverse_deviation = (1.0 / jnp.sqrt(var + eps_norm))[:, None, :]
        normalised = (hidden - mean[:, None, :]) * inverse_deviation
        preactivation = norm_scale_gain * normalised + norm_shift_bias
        act = jax.nn.gelu(preactivation, approximate=True).astype(bf16)
    with jax.named_scope("act_gather"):
        own = act.reshape(tall, width)
        pieces = {0: own, 1: xor_send(own, "col", 1)}
        for k in far:
            pieces[k] = xor_send(own, "col", k)
        first, pieces[1] = lax.optimization_barrier((act[0], pieces[1]))
        others = [ring_send(first, "batch", d) for d in range(1, n_batch)]
        pieces = sibling_pieces(pieces, n_col)
    with jax.named_scope("z"):

        def z_part(source, ks, before, last=False):
            return z_call(
                place, ks, [source[k] for k in ks], held_weight, before, last, local_rows
            )

        z_own = z_part(pieces, far, z_part(pieces, [0, 1], None))
        z_own, others[-1] = lax.optimization_barrier((z_own, others[-1]))
        z_own0, z_own1 = z_part(pieces, [k + 1 for k in far], z_own, True)
        far_pieces = link_pieces(jnp.concatenate(others), n_col)
    with jax.named_scope("z_ring"):
        z_ring = [z_own1, ring_send(z_own1, "batch", 1)]
        z_ring[1], far_pieces[far[0]] = lax.optimization_barrier((z_ring[1], far_pieces[far[0]]))
        z_ring.append(ring_send(z_ring[1], "batch", 1))
    with jax.named_scope("z_far"):
        start = z_part(far_pieces, [0] + far[:-1], None)
        picked = list(pick_call(place, [pieces[k] for k in evens], n_batch, n_col))
        start, far_pieces[far[-1]], z_ring[2], picked = lax.optimization_barrier(
            (start, far_pieces[far[-1]], z_ring[2], picked)
        )
        far_pieces = sibling_pieces(far_pieces, n_col)
        for _ in range(3, n_batch):
            z_ring.append(ring_send(z_ring[-1], "batch", 1))
        z_far = z_part(far_pieces, odds[:-1] + far[-1:] + odds[-1:], start, True)
        slots = list(zip([z_own0] + list(z_far), z_ring))
    with jax.named_scope("kernel"):
        even_part, odd_part = strip_call(place, slots, n_col)
        even_part = even_part + xor_send(odd_part, "col", 1).astype(f32)
        strip = even_part[0]
        for k in far:
            strip = strip + xor_send(even_part[k // 2].astype(bf16), "col", k).astype(f32)
        strip_b = strip.astype(bf16)
        strips = {0: strip_b}
        for k in far:
            strips[k] = xor_send(strip_b, "col", k)
        strips = sibling_pieces(strips, n_col)
    with jax.named_scope("dz"):
        constants = (
            4.0 * scale / denom,
            25.0 * scale / (2.0 * E * (rows - 1)),
            50.0 * scale / (rows * E),
            25.0 / (rows * E) / n_batch,
            25.0 / (2 * E) / n_batch,
            1.0 / denom / n_batch,
            1.0 / denom / n_batch,
        )
        dz, share = dz_call(place, strip, [strips[k] for k in range(n_col)], slots, constants)
    with jax.named_scope("d_act"):
        (away,) = d_act_call(place, dz, share, held_weight, n_batch, n_col, None)
        got = xor_send(away, "col", 1)
        *sends, d_act = d_act_call(place, dz, share, held_weight, n_batch, n_col, got)
        arrived = [xor_send(part, "col", k) for k, part in zip(far, sends)]
    with jax.named_scope("grad_weight"):
        d_act, picked = lax.optimization_barrier((d_act, picked))
        blocks = [
            ring_send(x, "batch", 1 + i % (n_batch - 1)) for i, x in enumerate(picked)
        ]
        sides = ((0, evens), (1, odds))
        products = {}
        for block in range(n_col // n_batch // 2):
            for parity, ks in sides:
                products[block, parity] = weight_grad_call(
                    place, n_batch, block, [pieces[k] for k in ks], [far_pieces[k] for k in ks], dz
                )
        arrived, blocks, products = lax.optimization_barrier((arrived, blocks, products))
        grad_weight = None
        for block in range(n_col // n_batch // 2):
            mine = jnp.concatenate(blocks[block * (n_batch - 1) : (block + 1) * (n_batch - 1)])
            other = xor_send(mine, "col", 1)
            for (parity, ks), far_rows in zip(sides, (mine, other)):
                grad_weight = weight_grad_last_call(
                    place,
                    (block, parity),
                    [pieces[k] for k in ks],
                    far_rows,
                    dz,
                    products[block, parity],
                    features // n_batch,
                    grad_weight,
                )
    with jax.named_scope("norm_backward"):
        share = exchange_sum(share_of(part[tall:]) for part in [d_act] + arrived)
        d_act = d_act[:tall]
        for part in arrived:
            d_act = d_act + part[:tall].astype(f32)
        d_pre = d_act.reshape(n_view, local_rows, width) * gelu_slope(preactivation)
        sums = jnp.concatenate(
            [
                jnp.sum(d_pre, axis=1),
                jnp.sum(d_pre * normalised, axis=1),
                jnp.broadcast_to(share, (2 * n_view, width)),
            ]
        )
        loss, grad_gain, grad_bias, views_gradient = finish_call(
            exchange(sums, "batch"), d_pre, normalised, norm_scale_gain, inverse_deviation, rows
        )
    return (loss[0, 0], grad_weight, grad_gain[0], grad_bias[0], views_gradient)


def solution(mesh):
    placed = (P(None, "batch", "col"), P("col"), P("col"), P(None, "col"))
    return jax.shard_map(
        shards,
        mesh=mesh,
        in_specs=placed,
        out_specs=(P(), P("batch", "col"), P("col"), P("col"), P(None, "batch", "col")),
        check_vma=False,
    )
```

```python
import functools

import jax
import jax.numpy as jnp
from jax import lax
from jax.experimental import pallas as pl
from jax.experimental.pallas import tpu as pltpu
from jax.sharding import PartitionSpec as P

eps_norm = 1e-05
eps_std = 0.0001
f32 = jnp.float32
bf16 = jnp.bfloat16
MIB = 1024 * 1024


def gelu_slope(preactivation):
    value, pullback = jax.vjp(lambda t: jax.nn.gelu(t, approximate=True), preactivation)
    return pullback(jnp.ones_like(value))[0]


def xor_send(x, axis, k):
    n = lax.axis_size(axis)
    return lax.ppermute(x, axis, [(i, i ^ k) for i in range(n)])


def ring_order(n):
    return list(range(0, n, 2)) + list(range(1, n, 2))[::-1]


def ring_send(x, axis, d):
    order = ring_order(lax.axis_size(axis))
    n = len(order)
    return lax.ppermute(x, axis, [(order[i], order[(i + d) % n]) for i in range(n)])


def exchange_sum(parts):
    parts = list(parts)
    while len(parts) > 1:
        parts = [x + y for x, y in zip(parts[::2], parts[1::2])]
    return parts[0]


def exchange(x, axis):
    return [x] + [xor_send(x, axis, k) for k in range(1, lax.axis_size(axis))]


def params(limit):
    return pltpu.CompilerParams(vmem_limit_bytes=limit * MIB)


def cost(flops, moved):
    return pl.CostEstimate(flops=flops, bytes_accessed=moved, transcendentals=0)


IN_SMEM = pl.BlockSpec(memory_space=pltpu.SMEM)
IN_VMEM = pl.BlockSpec(memory_space=pltpu.VMEM)
ANYWHERE = pl.BlockSpec(memory_space=pl.ANY)
LOADS = 8


def load_kernel(w_ref, out_ref, flag_ref, sems):
    flag_ref[...] = jnp.zeros_like(flag_ref)
    step = w_ref.shape[0] // LOADS
    copies = [
        pltpu.make_async_copy(
            w_ref.at[pl.ds(i * step, step)], out_ref.at[pl.ds(i * step, step)], sems.at[i]
        )
        for i in range(LOADS)
    ]
    for copy in copies:
        copy.start()
    for copy in copies:
        copy.wait()


def load_call(weight, flag_shape):
    return pl.pallas_call(
        load_kernel,
        out_shape=(
            pltpu.VMEM(weight.shape, weight.dtype),
            jax.ShapeDtypeStruct(flag_shape, f32),
        ),
        in_specs=[ANYWHERE],
        out_specs=(IN_VMEM, IN_VMEM),
        scratch_shapes=[pltpu.SemaphoreType.DMA((LOADS,))],
        compiler_params=params(4),
        cost_estimate=cost(0, 4 * weight.size),
        name="weight_load",
    )(pltpu.with_memory_space_constraint(weight, pltpu.HBM))


def weight_rows(place_ref, w_ref, k, width):
    return w_ref[pl.ds(pl.multiple_of((place_ref[1] ^ k) * width, width), width), :]


def z_kernel(ks, first, last, local_rows, place_ref, *refs):
    count = len(ks)
    pieces, rest = refs[:count], list(refs[count:])
    w_ref = rest.pop(0)
    total = None if first else rest.pop(0)[...]
    width = pieces[0].shape[1]
    for j in range(count):
        part = jnp.dot(
            pieces[j][...], weight_rows(place_ref, w_ref, ks[j], width), preferred_element_type=f32
        )
        total = part if total is None else total + part
    if not last:
        rest[0][...] = total
        return
    z = total.astype(bf16)
    for v, ref in enumerate(rest):
        ref[...] = z[v * local_rows : (v + 1) * local_rows]


def z_call(place, ks, pieces, weight, before, last, local_rows):
    count = len(ks)
    tall, width = pieces[0].shape
    columns = weight.shape[1]
    operands = [place] + list(pieces) + [weight] + ([] if before is None else [before])
    if last:
        groups = tall // local_rows
        out_shape = (jax.ShapeDtypeStruct((local_rows, columns), bf16),) * groups
    else:
        out_shape = jax.ShapeDtypeStruct((tall, columns), f32)
    return pl.pallas_call(
        functools.partial(z_kernel, tuple(ks), before is None, last, local_rows),
        out_shape=out_shape,
        in_specs=[IN_SMEM] + [IN_VMEM] * (len(operands) - 1),
        out_specs=jax.tree.map(lambda _: IN_VMEM, out_shape),
        compiler_params=params(8),
        cost_estimate=cost(2 * tall * width * columns * count, 2 * tall * columns),
        name="z_matmul",
    )(*operands)


def upper_blocks(n):
    return [(s, t) for s in range(n) for t in range(s, n)]


def strip_kernel(n_batch, n_col, place_ref, *refs):
    z_refs, (even_ref, odd_ref, strip) = refs[: 2 * n_batch], refs[2 * n_batch :]
    local_rows = z_refs[0].shape[0]
    rows = local_rows * n_batch
    for v in range(2):
        zf = [z[...].astype(f32) for z in z_refs[v::2]]
        mean = sum(jnp.sum(z, axis=0, keepdims=True) for z in zf) / rows
        rounded = jnp.concatenate([(z - mean).astype(bf16) for z in zf], axis=0)
        at = 0
        for s in range(n_batch):
            product = lax.dot_general(
                rounded[s * local_rows : (s + 1) * local_rows],
                rounded[s * local_rows :],
                (((1,), (1,)), ((), ())),
                preferred_element_type=f32,
            )
            strip[pl.ds(v * local_rows, local_rows), pl.ds(at, product.shape[1])] = product
            at += product.shape[1]
    part = 2 * local_rows // n_col
    for k in range(n_col):
        start = pl.multiple_of((place_ref[1] ^ k) * part, part)
        ref = odd_ref if k % 2 else even_ref
        ref[k // 2] = strip[pl.ds(start, part), :].astype(ref.dtype)


def strip_call(place, z_slots, n_col):
    n_batch = len(z_slots)
    local_rows, columns = z_slots[0][0].shape
    tall = 2 * local_rows
    wide = len(upper_blocks(n_batch)) * local_rows
    shape = (n_col // 2, tall // n_col, wide)
    operands = [place] + [z for slot in z_slots for z in slot]
    return pl.pallas_call(
        functools.partial(strip_kernel, n_batch, n_col),
        out_shape=(jax.ShapeDtypeStruct(shape, f32), jax.ShapeDtypeStruct(shape, bf16)),
        in_specs=[IN_SMEM] + [IN_VMEM] * (len(operands) - 1),
        out_specs=(IN_VMEM, IN_VMEM),
        scratch_shapes=[pltpu.VMEM((tall, wide), f32)],
        compiler_params=params(18),
        cost_estimate=cost(2 * tall * wide * columns, 2 * tall * columns * n_batch),
        name="kernel_strip",
    )(*operands)


def dz_kernel(n_batch, n_col, tile, constants, place_ref, own_ref, *refs):
    coef, hinge_coef, inv_coef, inv_share, hinge_share, diag_share, block_share = constants
    strip_refs = refs[:n_col]
    z_refs = refs[n_col : n_col + 2 * n_batch]
    dz_ref, share_ref, strips, full, centred = refs[n_col + 2 * n_batch :]
    local_rows, columns = z_refs[0].shape
    rows = local_rows * n_batch
    own = own_ref[...]
    block = lax.broadcasted_iota(jnp.int32, own.shape, 1) // local_rows
    on_diagonal = functools.reduce(
        jnp.logical_or, [block == i for i, (s, t) in enumerate(upper_blocks(n_batch)) if s == t]
    )
    own = own * own * jnp.where(on_diagonal, 1.0, 2.0)
    own = jnp.sum(jnp.sum(own, axis=0, keepdims=True), axis=1, keepdims=True)
    share_ref[...] = jnp.broadcast_to(block_share * own, share_ref.shape)
    part = 2 * local_rows // n_col
    for k in range(n_col):
        start = pl.multiple_of((place_ref[1] ^ k) * part, part)
        strips[pl.ds(start, part), :] = strip_refs[k][...].astype(f32)
    for v in range(2):
        for i, (s, t) in enumerate(upper_blocks(n_batch)):
            here, there = pl.ds(s * local_rows, local_rows), pl.ds(t * local_rows, local_rows)
            block = strips[pl.ds(v * local_rows, local_rows), pl.ds(i * local_rows, local_rows)]
            full[v, here, there] = block.astype(bf16)
            if s < t:
                full[v, there, here] = jnp.transpose(block).astype(bf16)

    def one_tile(j, carry):
        here = pl.ds(pl.multiple_of(j * tile, tile), tile)
        share = jnp.zeros((1, 1), f32)
        grads = []
        z_views = []
        for v in range(2):
            zf = jnp.concatenate([z[:, here].astype(f32) for z in z_refs[v::2]], axis=0)
            z_views.append(zf)
            zc = zf - jnp.sum(zf, axis=0, keepdims=True) / rows
            std = jnp.sqrt(jnp.sum(zc * zc, axis=0, keepdims=True) / (rows - 1) + eps_std)
            zcb = zc.astype(bf16)
            centred[...] = zcb
            rounded = zcb.astype(f32)
            diag = jnp.sum(rounded * rounded, axis=0, keepdims=True)
            moved = jnp.dot(full[v], centred[...], preferred_element_type=f32)
            pull = jnp.where(std < 1.0, hinge_coef, 0.0) / std
            summed = coef * (moved - rounded * diag) - zc * pull
            grads.append(summed - jnp.sum(summed, axis=0, keepdims=True) / rows)
            share += hinge_share * jnp.sum(jnp.maximum(1.0 - std, 0.0), axis=1, keepdims=True)
            share -= diag_share * jnp.sum(diag * diag, axis=1, keepdims=True)
        diff = z_views[0] - z_views[1]
        share += inv_share * jnp.sum(
            jnp.sum(diff * diff, axis=0, keepdims=True), axis=1, keepdims=True
        )
        share_ref[...] += jnp.broadcast_to(share, share_ref.shape)
        dz_ref[0, :, here] = (grads[0] + inv_coef * diff).astype(bf16)
        dz_ref[1, :, here] = (grads[1] - inv_coef * diff).astype(bf16)
        return carry

    lax.fori_loop(0, columns // tile, one_tile, 0)


def dz_call(place, own, strips, z_slots, constants):
    n_col, n_batch = len(strips), len(z_slots)
    local_rows, columns = z_slots[0][0].shape
    tall = 2 * local_rows
    rows = local_rows * n_batch
    tile = min(256, columns)
    operands = [place, own] + list(strips) + [z for slot in z_slots for z in slot]
    return pl.pallas_call(
        functools.partial(dz_kernel, n_batch, n_col, tile, constants),
        out_shape=(
            jax.ShapeDtypeStruct((2, rows, columns), bf16),
            jax.ShapeDtypeStruct((8, 128), f32),
        ),
        in_specs=[IN_SMEM] + [IN_VMEM] * (len(operands) - 1),
        out_specs=(IN_VMEM, IN_VMEM),
        scratch_shapes=[
            pltpu.VMEM((tall, strips[0].shape[1]), f32),
            pltpu.VMEM((2, rows, rows), bf16),
            pltpu.VMEM((rows, tile), bf16),
        ],
        compiler_params=params(24),
        cost_estimate=cost(4 * rows * rows * columns, 8 * rows * columns),
        name="embedding_gradient",
    )(*operands)


EXTRA = 16


def share_rows(share, width, kind):
    high = share.astype(bf16).astype(f32)
    middle = (share - high).astype(bf16).astype(f32)
    low = share - high - middle
    row = lax.broadcasted_iota(jnp.int32, (EXTRA, width), 0)
    rows = jnp.where(row == 0, high, jnp.where(row == 1, middle, jnp.where(row == 2, low, 0.0)))
    return rows.astype(kind)


def share_of(rows):
    return rows[0:1].astype(f32) + rows[1:2].astype(f32) + rows[2:3].astype(f32)


def d_act_kernel(count, adds, place_ref, dz_ref, share_ref, w_ref, *refs):
    local_rows, columns = dz_ref.shape[1] // adds[1], dz_ref.shape[2]
    tall = 2 * local_rows
    dz = jnp.concatenate([dz_ref[0, :local_rows], dz_ref[1, :local_rows]], axis=0)
    width = w_ref.shape[0] // adds[2]
    share = share_ref[0:1, 0:1]
    for j in range(count):
        k = 2 * ((j + 1) % count) if adds[0] else 2 * j + 1
        part = lax.dot_general(
            dz,
            weight_rows(place_ref, w_ref, k, width),
            (((1,), (1,)), ((), ())),
            preferred_element_type=f32,
        )
        if not adds[0]:
            refs[0][j, :tall] = part.astype(refs[0].dtype)
            refs[0][j, tall:] = share_rows(share, width, refs[0].dtype)
        else:
            got = refs[0]
            out_ref = refs[j + 1]
            slot = (j + 1) % count
            out_ref[:tall] = (part + got[slot, :tall].astype(f32)).astype(out_ref.dtype)
            whole_share = share + share_of(got[slot, tall:])[:, 0:1]
            out_ref[tall:] = share_rows(whole_share, width, out_ref.dtype)


def d_act_call(place, dz, share, weight, n_batch, n_col, got):
    columns = weight.shape[1]
    width = weight.shape[0] // n_col
    tall = 2 * dz.shape[1] // n_batch
    count = n_col // 2
    operands = [place, dz, share, weight] + ([] if got is None else [got])
    if got is None:
        out_shape = (jax.ShapeDtypeStruct((count, tall + EXTRA, width), bf16),)
    else:
        out_shape = (jax.ShapeDtypeStruct((tall + EXTRA, width), bf16),) * (count - 1)
        out_shape += (jax.ShapeDtypeStruct((tall + EXTRA, width), f32),)
    return pl.pallas_call(
        functools.partial(d_act_kernel, count, (got is not None, n_batch, n_col)),
        out_shape=out_shape,
        in_specs=[IN_SMEM] + [IN_VMEM] * (len(operands) - 1),
        out_specs=(IN_VMEM,) * len(out_shape),
        compiler_params=params(8),
        cost_estimate=cost(2 * tall * width * columns * count, 2 * count * width * tall),
        name="d_act_matmul",
    )(*operands)


def held_place(plane, c, block, n_col, n_batch):
    return (((n_col // n_batch) * plane + 2 * block) ^ (c - (c & 1))) >> 1


def pick_kernel(n_batch, n_col, local_rows, place_ref, *refs):
    half = n_col // 2
    pieces, outs = refs[:half], refs[half:]
    b, c = place_ref[0], place_ref[1]
    position = jnp.where((b & 1) == 0, b >> 1, n_batch - 1 - (b >> 1))
    i = 0
    for block in range(n_col // n_batch // 2):
        for d in range(1, n_batch):
            ahead = position + d
            ahead = jnp.where(ahead >= n_batch, ahead - n_batch, ahead)
            plane = jnp.where(2 * ahead < n_batch, 2 * ahead, 2 * (n_batch - ahead) - 1)
            chosen = held_place(plane, c, block, n_col, n_batch)
            for e in range(half):

                @pl.when(chosen == e)
                def _():
                    outs[i][...] = pieces[e][local_rows:]

            i += 1


def pick_call(place, pieces, n_batch, n_col):
    tall, width = pieces[0].shape
    count = n_col // n_batch // 2 * (n_batch - 1)
    out_shape = (jax.ShapeDtypeStruct((tall // 2, width), bf16),) * count
    return pl.pallas_call(
        functools.partial(pick_kernel, n_batch, n_col, tall // 2),
        out_shape=out_shape,
        in_specs=[IN_SMEM] + [IN_VMEM] * len(pieces),
        out_specs=(IN_VMEM,) * count,
        compiler_params=params(4),
        cost_estimate=cost(0, tall * width * count),
        name="pick_blocks",
    )(place, *pieces)


def weight_grad_kernel(n_batch, aliased, half, tile, which, place_ref, *refs):
    near = [refs[:half], refs[half : 2 * half]]
    blocks_ref, dz_ref = refs[2 * half : 2 * half + 2]
    out_ref, act, product, sems = refs[2 * half + 2 + aliased :]
    block, parity = which
    chosen = held_place(place_ref[0], place_ref[1], block, 2 * half, n_batch)
    out_row = 2 * block + ((place_ref[1] & 1) ^ parity)
    local_rows = near[0][0].shape[0] // 2
    rows = dz_ref.shape[1]
    for e in range(half):

        @pl.when(chosen == e)
        def _():
            act[pl.ds(0, local_rows)] = near[0][e][:local_rows]
            act[pl.ds(rows, local_rows)] = near[0][e][local_rows:]
            act[pl.ds(local_rows, rows - local_rows)] = near[1][e][...]

    act[rows + local_rows :] = blocks_ref[...]
    width = act.shape[1]
    copies = []
    for i in range(width // tile):
        total = None
        for v in range(2):
            part = lax.dot_general(
                act[pl.ds(v * rows, rows), pl.ds(i * tile, tile)],
                dz_ref[v],
                (((0,), (0,)), ((), ())),
                preferred_element_type=f32,
            )
            total = part if total is None else total + part
        product[pl.ds(i * tile, tile)] = total
        start = pl.multiple_of(out_row * width + i * tile, tile)
        copies.append(
            pltpu.make_async_copy(
                product.at[pl.ds(i * tile, tile)], out_ref.at[pl.ds(start, tile)], sems.at[i]
            )
        )
        copies[-1].start()
    for copy in copies:
        copy.wait()


def weight_grad_call(place, which, near, blocks, dz, features, before):
    half = len(near[0])
    width = near[0][0].shape[1]
    _, rows, columns = dz.shape
    tile = min(256, width)
    operands = [place] + [x for group in near for x in group] + [blocks, dz]
    specs = [IN_SMEM] + [IN_VMEM] * (len(operands) - 1)
    aliases = {}
    if before is not None:
        aliases = {len(operands): 0}
        operands.append(before)
        specs.append(ANYWHERE)
    return pl.pallas_call(
        functools.partial(
            weight_grad_kernel,
            rows // (near[0][0].shape[0] // 2),
            int(before is not None),
            half,
            tile,
            which,
        ),
        out_shape=jax.ShapeDtypeStruct((features, columns), f32),
        in_specs=specs,
        out_specs=ANYWHERE,
        scratch_shapes=[
            pltpu.VMEM((2 * rows, width), bf16),
            pltpu.VMEM((width, columns), f32),
            pltpu.SemaphoreType.DMA((width // tile,)),
        ],
        input_output_aliases=aliases,
        compiler_params=params(12),
        cost_estimate=cost(4 * rows * width * columns, 4 * width * columns),
        name="weight_gradient",
    )(*operands)


def link_pieces(x, n_col):
    pieces = {0: x}
    half = x.shape[0] // 2
    for k in sorted(range(2, n_col, 2), key=lambda k: (bin(k).count("1"), k)):
        low, high = k & -k, 1 << (k.bit_length() - 1)
        if low == high:
            pieces[k] = xor_send(x, "col", k)
        else:
            first = xor_send(pieces[k ^ low][:half], "col", low)
            second = xor_send(pieces[k ^ high][half:], "col", high)
            pieces[k] = jnp.concatenate([first, second])
    return pieces


def sibling_pieces(pieces, n_col):
    for k in range(0, n_col, 2):
        if k + 1 not in pieces:
            pieces[k + 1] = xor_send(pieces[k], "col", 1)
    return pieces


def finish_kernel(n_batch, rows, *refs):
    sums, (d_pre, normalised, gain, deviation) = refs[:n_batch], refs[n_batch : n_batch + 4]
    loss_ref, gain_ref, bias_ref, out_ref = refs[n_batch + 4 :]
    both = exchange_sum(x[...] for x in sums)
    bias_ref[...] = both[0:1] + both[1:2]
    gain_ref[...] = both[2:3] + both[3:4]
    loss_ref[...] = both[4:5, 0:128]
    for v in range(2):
        factor = gain[...] * deviation[v : v + 1]
        mean_b, mean_g = both[v : v + 1] / rows, both[2 + v : 3 + v] / rows
        out_ref[v] = factor * (d_pre[v] - mean_b - normalised[v] * mean_g)


def finish_call(sums, d_pre, normalised, gain, deviation, rows):
    _, local_rows, width = d_pre.shape
    operands = list(sums) + [d_pre, normalised, gain[None], deviation[:, 0]]
    out_shape = (
        jax.ShapeDtypeStruct((1, 128), f32),
        jax.ShapeDtypeStruct((1, width), f32),
        jax.ShapeDtypeStruct((1, width), f32),
        jax.ShapeDtypeStruct(d_pre.shape, f32),
    )
    return pl.pallas_call(
        functools.partial(finish_kernel, len(sums), rows),
        out_shape=out_shape,
        in_specs=[IN_VMEM] * len(operands),
        out_specs=(IN_VMEM,) * 4,
        compiler_params=params(4),
        cost_estimate=cost(0, 8 * d_pre.size),
        name="views_gradient",
    )(*operands)


def shards(views, norm_scale_gain, norm_shift_bias, weight):
    n_batch = lax.axis_size("batch")
    n_col = lax.axis_size("col")
    place = jnp.stack([lax.axis_index("batch"), lax.axis_index("col")]).astype(jnp.int32)
    views, norm_scale_gain, norm_shift_bias, weight, place = lax.optimization_barrier(
        (views, norm_scale_gain, norm_shift_bias, weight, place)
    )
    n_view, local_rows, width = views.shape
    features, columns = weight.shape
    E = columns * n_col
    rows = local_rows * n_batch
    tall = n_view * local_rows
    scale = rows * E / 128.0
    denom = float((rows - 1) ** 2 * E)
    evens = list(range(0, n_col, 2))
    odds = [k + 1 for k in evens]
    far = evens[1:]

    with jax.named_scope("weight_load"):
        held_weight, loaded = load_call(weight, (2 * n_view, width))
    with jax.named_scope("norm_stats"):
        hidden = views.astype(f32)
        local_mean = jnp.mean(hidden, axis=1)
        local_centred = hidden - local_mean[:, None, :]
        local_spread = jnp.sum(local_centred * local_centred, axis=1)
        stats = exchange(jnp.concatenate([local_mean, local_spread]), "batch")
        stats[-1] = stats[-1] + loaded
        mean = exchange_sum(s[:n_view] for s in stats) / n_batch
        spread = exchange_sum(
            s[n_view:] + local_rows * jnp.square(s[:n_view] - mean) for s in stats
        )
        var = spread / rows
        inverse_deviation = (1.0 / jnp.sqrt(var + eps_norm))[:, None, :]
        normalised = (hidden - mean[:, None, :]) * inverse_deviation
        preactivation = norm_scale_gain * normalised + norm_shift_bias
        act = jax.nn.gelu(preactivation, approximate=True).astype(bf16)
    with jax.named_scope("act_gather"):
        own = act.reshape(tall, width)
        pieces = {0: own, 1: xor_send(own, "col", 1)}
        for k in far:
            pieces[k] = xor_send(own, "col", k)
        first, pieces[1] = lax.optimization_barrier((act[0], pieces[1]))
        others = [ring_send(first, "batch", d) for d in range(1, n_batch)]
        pieces = sibling_pieces(pieces, n_col)
    with jax.named_scope("z"):

        def z_part(source, ks, before, last=False):
            return z_call(
                place, ks, [source[k] for k in ks], held_weight, before, last, local_rows
            )

        z_own = z_part(pieces, far, z_part(pieces, [0, 1], None))
        z_own, others[-1] = lax.optimization_barrier((z_own, others[-1]))
        z_own0, z_own1 = z_part(pieces, [k + 1 for k in far], z_own, True)
        far_pieces = link_pieces(jnp.concatenate(others), n_col)
    with jax.named_scope("z_ring"):
        z_ring = [z_own1, ring_send(z_own1, "batch", 1)]
        z_ring[1], far_pieces[far[0]] = lax.optimization_barrier((z_ring[1], far_pieces[far[0]]))
        z_ring.append(ring_send(z_ring[1], "batch", 1))
    with jax.named_scope("z_far"):
        start = z_part(far_pieces, [0] + far[:-1], None)
        picked = list(pick_call(place, [pieces[k] for k in evens], n_batch, n_col))
        start, far_pieces[far[-1]], z_ring[2], picked = lax.optimization_barrier(
            (start, far_pieces[far[-1]], z_ring[2], picked)
        )
        far_pieces = sibling_pieces(far_pieces, n_col)
        for _ in range(3, n_batch):
            z_ring.append(ring_send(z_ring[-1], "batch", 1))
        z_far = z_part(far_pieces, odds[:-1] + far[-1:] + odds[-1:], start, True)
        slots = list(zip([z_own0] + list(z_far), z_ring))
    with jax.named_scope("kernel"):
        even_part, odd_part = strip_call(place, slots, n_col)
        blocks = [
            ring_send(x, "batch", 1 + i % (n_batch - 1)) for i, x in enumerate(picked)
        ]
        third = len(blocks) // 3
        odd_part, blocks[:third] = lax.optimization_barrier((odd_part, blocks[:third]))
        even_part = even_part + xor_send(odd_part, "col", 1).astype(f32)
        strip = even_part[0]
        for k in far:
            strip = strip + xor_send(even_part[k // 2].astype(bf16), "col", k).astype(f32)
        strip_b = strip.astype(bf16)
        strips = {0: strip_b}
        for k in far:
            strips[k] = xor_send(strip_b, "col", k)
        strips[far[0]], blocks[third : 2 * third] = lax.optimization_barrier(
            (strips[far[0]], blocks[third : 2 * third])
        )
        strips = sibling_pieces(strips, n_col)
    with jax.named_scope("dz"):
        constants = (
            4.0 * scale / denom,
            25.0 * scale / (2.0 * E * (rows - 1)),
            50.0 * scale / (rows * E),
            25.0 / (rows * E) / n_batch,
            25.0 / (2 * E) / n_batch,
            1.0 / denom / n_batch,
            1.0 / denom / n_batch,
        )
        dz, share = dz_call(place, strip, [strips[k] for k in range(n_col)], slots, constants)
        dz, blocks[2 * third :] = lax.optimization_barrier((dz, blocks[2 * third :]))
    with jax.named_scope("d_act"):
        (away,) = d_act_call(place, dz, share, held_weight, n_batch, n_col, None)
        got = xor_send(away, "col", 1)
        *sends, d_act = d_act_call(place, dz, share, held_weight, n_batch, n_col, got)
        arrived = [xor_send(part, "col", k) for k, part in zip(far, sends)]
    with jax.named_scope("grad_weight"):
        grad_weight = None
        for block in range(n_col // n_batch // 2):
            mine = jnp.concatenate(blocks[block * (n_batch - 1) : (block + 1) * (n_batch - 1)])
            other = xor_send(mine, "col", 1)
            for parity, ks, far_rows in ((0, evens, mine), (1, odds, other)):
                grad_weight = weight_grad_call(
                    place,
                    (block, parity),
                    [[group[k] for k in ks] for group in (pieces, far_pieces)],
                    far_rows,
                    dz,
                    features // n_batch,
                    grad_weight,
                )
    with jax.named_scope("norm_backward"):
        arrived, grad_weight = lax.optimization_barrier((arrived, grad_weight))
        share = exchange_sum(share_of(part[tall:]) for part in [d_act] + arrived)
        d_act = d_act[:tall]
        for part in arrived:
            d_act = d_act + part[:tall].astype(f32)
        d_pre = d_act.reshape(n_view, local_rows, width) * gelu_slope(preactivation)
        sums = jnp.concatenate(
            [
                jnp.sum(d_pre, axis=1),
                jnp.sum(d_pre * normalised, axis=1),
                jnp.broadcast_to(share, (2 * n_view, width)),
            ]
        )
        loss, grad_gain, grad_bias, views_gradient = finish_call(
            exchange(sums, "batch"), d_pre, normalised, norm_scale_gain, inverse_deviation, rows
        )
    return (loss[0, 0], grad_weight, grad_gain[0], grad_bias[0], views_gradient)


def solution(mesh):
    placed = (P(None, "batch", "col"), P("col"), P("col"), P(None, "col"))
    return jax.shard_map(
        shards,
        mesh=mesh,
        in_specs=placed,
        out_specs=(P(), P("batch", "col"), P("col"), P("col"), P(None, "batch", "col")),
        check_vma=False,
    )
```

```python
import functools

import jax
import jax.numpy as jnp
from jax import lax
from jax.experimental import pallas as pl
from jax.experimental.pallas import tpu as pltpu
from jax.sharding import PartitionSpec as P

eps_norm = 1e-05
eps_std = 0.0001
f32 = jnp.float32
bf16 = jnp.bfloat16
MIB = 1024 * 1024


def gelu_slope(preactivation):
    value, pullback = jax.vjp(lambda t: jax.nn.gelu(t, approximate=True), preactivation)
    return pullback(jnp.ones_like(value))[0]


def xor_send(x, axis, k):
    n = lax.axis_size(axis)
    return lax.ppermute(x, axis, [(i, i ^ k) for i in range(n)])


def ring_order(n):
    return list(range(0, n, 2)) + list(range(1, n, 2))[::-1]


def ring_send(x, axis, d):
    order = ring_order(lax.axis_size(axis))
    n = len(order)
    return lax.ppermute(x, axis, [(order[i], order[(i + d) % n]) for i in range(n)])


def exchange_sum(parts):
    parts = list(parts)
    while len(parts) > 1:
        parts = [x + y for x, y in zip(parts[::2], parts[1::2])]
    return parts[0]


def exchange(x, axis):
    return [x] + [xor_send(x, axis, k) for k in range(1, lax.axis_size(axis))]


def params(limit):
    return pltpu.CompilerParams(vmem_limit_bytes=limit * MIB)


def cost(flops, moved):
    return pl.CostEstimate(flops=flops, bytes_accessed=moved, transcendentals=0)


IN_SMEM = pl.BlockSpec(memory_space=pltpu.SMEM)
IN_VMEM = pl.BlockSpec(memory_space=pltpu.VMEM)
ANYWHERE = pl.BlockSpec(memory_space=pl.ANY)
LOADS = 8


def load_kernel(w_ref, out_ref, flag_ref, sems):
    flag_ref[...] = jnp.zeros_like(flag_ref)
    step = w_ref.shape[0] // LOADS
    copies = [
        pltpu.make_async_copy(
            w_ref.at[pl.ds(i * step, step)], out_ref.at[pl.ds(i * step, step)], sems.at[i]
        )
        for i in range(LOADS)
    ]
    for copy in copies:
        copy.start()
    for copy in copies:
        copy.wait()


def load_call(weight, flag_shape):
    return pl.pallas_call(
        load_kernel,
        out_shape=(
            pltpu.VMEM(weight.shape, weight.dtype),
            jax.ShapeDtypeStruct(flag_shape, f32),
        ),
        in_specs=[ANYWHERE],
        out_specs=(IN_VMEM, IN_VMEM),
        scratch_shapes=[pltpu.SemaphoreType.DMA((LOADS,))],
        compiler_params=params(4),
        cost_estimate=cost(0, 4 * weight.size),
        name="weight_load",
    )(pltpu.with_memory_space_constraint(weight, pltpu.HBM))


def weight_rows(place_ref, w_ref, k, width):
    return w_ref[pl.ds(pl.multiple_of((place_ref[1] ^ k) * width, width), width), :]


def z_kernel(ks, first, last, local_rows, place_ref, *refs):
    count = len(ks)
    pieces, rest = refs[:count], list(refs[count:])
    w_ref = rest.pop(0)
    total = None if first else rest.pop(0)[...]
    width = pieces[0].shape[1]
    for j in range(count):
        part = jnp.dot(
            pieces[j][...], weight_rows(place_ref, w_ref, ks[j], width), preferred_element_type=f32
        )
        total = part if total is None else total + part
    if not last:
        rest[0][...] = total
        return
    z = total.astype(bf16)
    for v, ref in enumerate(rest):
        ref[...] = z[v * local_rows : (v + 1) * local_rows]


def z_call(place, ks, pieces, weight, before, last, local_rows):
    count = len(ks)
    tall, width = pieces[0].shape
    columns = weight.shape[1]
    operands = [place] + list(pieces) + [weight] + ([] if before is None else [before])
    if last:
        groups = tall // local_rows
        out_shape = (jax.ShapeDtypeStruct((local_rows, columns), bf16),) * groups
    else:
        out_shape = jax.ShapeDtypeStruct((tall, columns), f32)
    return pl.pallas_call(
        functools.partial(z_kernel, tuple(ks), before is None, last, local_rows),
        out_shape=out_shape,
        in_specs=[IN_SMEM] + [IN_VMEM] * (len(operands) - 1),
        out_specs=jax.tree.map(lambda _: IN_VMEM, out_shape),
        compiler_params=params(8),
        cost_estimate=cost(2 * tall * width * columns * count, 2 * tall * columns),
        name="z_matmul",
    )(*operands)


def upper_blocks(n):
    return [(s, t) for s in range(n) for t in range(s, n)]


def view_strip(z_refs):
    local_rows = z_refs[0].shape[0]
    rows = local_rows * len(z_refs)
    zf = [z[...].astype(f32) for z in z_refs]
    mean = sum(jnp.sum(z, axis=0, keepdims=True) for z in zf) / rows
    rounded = jnp.concatenate([(z - mean).astype(bf16) for z in zf], axis=0)
    for s in range(len(z_refs)):
        yield lax.dot_general(
            rounded[s * local_rows : (s + 1) * local_rows],
            rounded[s * local_rows :],
            (((1,), (1,)), ((), ())),
            preferred_element_type=f32,
        )


def strip_first_kernel(*refs):
    out_ref = refs[-1]
    at = 0
    for product in view_strip(refs[:-1]):
        out_ref[:, pl.ds(at, product.shape[1])] = product
        at += product.shape[1]


def strip_first_call(z):
    local_rows, columns = z[0].shape
    wide = len(upper_blocks(len(z))) * local_rows
    return pl.pallas_call(
        strip_first_kernel,
        out_shape=jax.ShapeDtypeStruct((local_rows, wide), f32),
        in_specs=[IN_VMEM] * len(z),
        out_specs=IN_VMEM,
        compiler_params=params(12),
        cost_estimate=cost(2 * local_rows * wide * columns, 2 * local_rows * columns * len(z)),
        name="kernel_strip_0",
    )(*z)


def strip_kernel(n_batch, n_col, place_ref, *refs):
    z_refs, (first_ref, even_ref, odd_ref, strip) = refs[:n_batch], refs[n_batch:]
    local_rows = z_refs[0].shape[0]
    strip[:local_rows] = first_ref[...]
    at = 0
    for product in view_strip(z_refs):
        strip[pl.ds(local_rows, local_rows), pl.ds(at, product.shape[1])] = product
        at += product.shape[1]
    part = 2 * local_rows // n_col
    for k in range(n_col):
        start = pl.multiple_of((place_ref[1] ^ k) * part, part)
        ref = odd_ref if k % 2 else even_ref
        ref[k // 2] = strip[pl.ds(start, part), :].astype(ref.dtype)


def strip_call(place, z, first, n_col):
    n_batch = len(z)
    local_rows, columns = z[0].shape
    tall, wide = 2 * local_rows, first.shape[1]
    shape = (n_col // 2, tall // n_col, wide)
    operands = [place] + list(z) + [first]
    return pl.pallas_call(
        functools.partial(strip_kernel, n_batch, n_col),
        out_shape=(jax.ShapeDtypeStruct(shape, f32), jax.ShapeDtypeStruct(shape, bf16)),
        in_specs=[IN_SMEM] + [IN_VMEM] * (len(operands) - 1),
        out_specs=(IN_VMEM, IN_VMEM),
        scratch_shapes=[pltpu.VMEM((tall, wide), f32)],
        compiler_params=params(14),
        cost_estimate=cost(2 * local_rows * wide * columns, 2 * local_rows * columns * n_batch),
        name="kernel_strip_1",
    )(*operands)


def dz_kernel(v, n_batch, n_col, tile, constants, place_ref, own_ref, before_ref, *refs):
    coef, hinge_coef, inv_coef, inv_share, hinge_share, diag_share, block_share = constants
    strip_refs = refs[:n_col]
    z_refs = refs[n_col : n_col + n_batch]
    other_refs = refs[n_col + n_batch : n_col + 2 * n_batch]
    dz_ref, share_ref, strips, full, centred = refs[n_col + 2 * n_batch :]
    local_rows, columns = z_refs[0].shape
    rows = local_rows * n_batch
    share_ref[...] = before_ref[...]
    if v == 0:
        own = own_ref[...]
        block = lax.broadcasted_iota(jnp.int32, own.shape, 1) // local_rows
        on_diagonal = functools.reduce(
            jnp.logical_or, [block == i for i, (s, t) in enumerate(upper_blocks(n_batch)) if s == t]
        )
        own = own * own * jnp.where(on_diagonal, 1.0, 2.0)
        own = jnp.sum(jnp.sum(own, axis=0, keepdims=True), axis=1, keepdims=True)
        share_ref[...] += jnp.broadcast_to(block_share * own, share_ref.shape)
    part = 2 * local_rows // n_col
    for k in range(n_col):
        start = (place_ref[1] ^ k) * part - v * local_rows

        @pl.when(jnp.logical_and(start >= 0, start < local_rows))
        def _():
            strips[pl.ds(pl.multiple_of(start, part), part), :] = strip_refs[k][...].astype(f32)

    for i, (s, t) in enumerate(upper_blocks(n_batch)):
        here, there = pl.ds(s * local_rows, local_rows), pl.ds(t * local_rows, local_rows)
        block = strips[:, pl.ds(i * local_rows, local_rows)]
        full[here, there] = block.astype(bf16)
        if s < t:
            full[there, here] = jnp.transpose(block).astype(bf16)

    def one_tile(j, carry):
        here = pl.ds(pl.multiple_of(j * tile, tile), tile)
        zf = jnp.concatenate([z[:, here].astype(f32) for z in z_refs], axis=0)
        zc = zf - jnp.sum(zf, axis=0, keepdims=True) / rows
        std = jnp.sqrt(jnp.sum(zc * zc, axis=0, keepdims=True) / (rows - 1) + eps_std)
        zcb = zc.astype(bf16)
        centred[...] = zcb
        rounded = zcb.astype(f32)
        diag = jnp.sum(rounded * rounded, axis=0, keepdims=True)
        moved = jnp.dot(full[...], centred[...], preferred_element_type=f32)
        pull = jnp.where(std < 1.0, hinge_coef, 0.0) / std
        summed = coef * (moved - rounded * diag) - zc * pull
        grad = summed - jnp.sum(summed, axis=0, keepdims=True) / rows
        share = hinge_share * jnp.sum(jnp.maximum(1.0 - std, 0.0), axis=1, keepdims=True)
        share -= diag_share * jnp.sum(diag * diag, axis=1, keepdims=True)
        diff = zf - jnp.concatenate([z[:, here].astype(f32) for z in other_refs], axis=0)
        if v == 0:
            share += inv_share * jnp.sum(
                jnp.sum(diff * diff, axis=0, keepdims=True), axis=1, keepdims=True
            )
        share_ref[...] += jnp.broadcast_to(share, share_ref.shape)
        dz_ref[:, here] = (grad + inv_coef * diff).astype(bf16)
        return carry

    lax.fori_loop(0, columns // tile, one_tile, 0)


def dz_call(place, v, own, before, strips, z_slots, constants):
    n_col, n_batch = len(strips), len(z_slots)
    local_rows, columns = z_slots[0][0].shape
    rows = local_rows * n_batch
    tile = min(256, columns)
    operands = [place, own, before] + list(strips)
    operands += [z[v] for z in z_slots] + [z[1 - v] for z in z_slots]
    return pl.pallas_call(
        functools.partial(dz_kernel, v, n_batch, n_col, tile, constants),
        out_shape=(
            jax.ShapeDtypeStruct((rows, columns), bf16),
            jax.ShapeDtypeStruct((8, 128), f32),
        ),
        in_specs=[IN_SMEM] + [IN_VMEM] * (len(operands) - 1),
        out_specs=(IN_VMEM, IN_VMEM),
        scratch_shapes=[
            pltpu.VMEM((local_rows, strips[0].shape[1]), f32),
            pltpu.VMEM((rows, rows), bf16),
            pltpu.VMEM((rows, tile), bf16),
        ],
        compiler_params=params(16),
        cost_estimate=cost(2 * rows * rows * columns, 6 * rows * columns),
        name="embedding_gradient",
    )(*operands)


EXTRA = 16


def share_rows(share, width, kind):
    high = share.astype(bf16).astype(f32)
    middle = (share - high).astype(bf16).astype(f32)
    low = share - high - middle
    row = lax.broadcasted_iota(jnp.int32, (EXTRA, width), 0)
    rows = jnp.where(row == 0, high, jnp.where(row == 1, middle, jnp.where(row == 2, low, 0.0)))
    return rows.astype(kind)


def share_of(rows):
    return rows[0:1].astype(f32) + rows[1:2].astype(f32) + rows[2:3].astype(f32)


def d_act_kernel(adds, tall, width, count, shares, place_ref, dz_ref, *refs):
    refs = list(refs)
    share = refs.pop(0)[0:1, 0:1] if shares else None
    w_ref = refs.pop(0)
    got = refs.pop(0) if adds else None
    dz = dz_ref[:tall]
    for j in range(count):
        k = 2 * ((j + 1) % count) if adds else 2 * j + 1
        part = lax.dot_general(
            dz,
            weight_rows(place_ref, w_ref, k, width),
            (((1,), (1,)), ((), ())),
            preferred_element_type=f32,
        )
        out = refs[j] if adds else refs[0].at[j]
        whole_share = share
        if adds:
            part = part + got[k // 2, :tall].astype(f32)
            if shares:
                whole_share = share + share_of(got[k // 2, tall:])[:, 0:1]
        out[:tall] = part.astype(out.dtype)
        if shares:
            out[tall:] = share_rows(whole_share, width, out.dtype)


def d_act_call(place, dz, share, weight, n_batch, n_col, got):
    width = weight.shape[0] // n_col
    tall = dz.shape[0] // n_batch
    columns = weight.shape[1]
    count = n_col // 2
    long = tall if share is None else tall + EXTRA
    operands = [place, dz] + ([] if share is None else [share]) + [weight]
    if got is None:
        out_shape = (jax.ShapeDtypeStruct((count, long, width), bf16),)
    else:
        operands.append(got)
        out_shape = (jax.ShapeDtypeStruct((long, width), bf16),) * (count - 1)
        out_shape += (jax.ShapeDtypeStruct((long, width), f32),)
    return pl.pallas_call(
        functools.partial(d_act_kernel, got is not None, tall, width, count, share is not None),
        out_shape=out_shape,
        in_specs=[IN_SMEM] + [IN_VMEM] * (len(operands) - 1),
        out_specs=(IN_VMEM,) * len(out_shape),
        compiler_params=params(8),
        cost_estimate=cost(2 * tall * width * columns * count, 2 * count * width * tall),
        name="d_act_matmul",
    )(*operands)


def held_place(plane, c, block, n_col, n_batch):
    return (((n_col // n_batch) * plane + 2 * block) ^ (c - (c & 1))) >> 1


def pick_kernel(n_batch, n_col, local_rows, place_ref, *refs):
    half = n_col // 2
    pieces, outs = refs[:half], refs[half:]
    b, c = place_ref[0], place_ref[1]
    position = jnp.where((b & 1) == 0, b >> 1, n_batch - 1 - (b >> 1))
    i = 0
    for block in range(n_col // n_batch // 2):
        for d in range(1, n_batch):
            ahead = position + d
            ahead = jnp.where(ahead >= n_batch, ahead - n_batch, ahead)
            plane = jnp.where(2 * ahead < n_batch, 2 * ahead, 2 * (n_batch - ahead) - 1)
            chosen = held_place(plane, c, block, n_col, n_batch)
            for e in range(half):

                @pl.when(chosen == e)
                def _():
                    outs[i][...] = pieces[e][local_rows:]

            i += 1


def pick_call(place, pieces, n_batch, n_col):
    tall, width = pieces[0].shape
    count = n_col // n_batch // 2 * (n_batch - 1)
    out_shape = (jax.ShapeDtypeStruct((tall // 2, width), bf16),) * count
    return pl.pallas_call(
        functools.partial(pick_kernel, n_batch, n_col, tall // 2),
        out_shape=out_shape,
        in_specs=[IN_SMEM] + [IN_VMEM] * len(pieces),
        out_specs=(IN_VMEM,) * count,
        compiler_params=params(4),
        cost_estimate=cost(0, tall * width * count),
        name="pick_blocks",
    )(place, *pieces)


def weight_grad_kernel(n_batch, aliased, half, tile, which, place_ref, *refs):
    near = [refs[:half], refs[half : 2 * half]]
    blocks_ref, *dz_refs = refs[2 * half : 2 * half + 3]
    out_ref, act, product, sems = refs[2 * half + 3 + aliased :]
    block, parity = which
    chosen = held_place(place_ref[0], place_ref[1], block, 2 * half, n_batch)
    out_row = 2 * block + ((place_ref[1] & 1) ^ parity)
    local_rows = near[0][0].shape[0] // 2
    rows = dz_refs[0].shape[0]
    for e in range(half):

        @pl.when(chosen == e)
        def _():
            act[pl.ds(0, local_rows)] = near[0][e][:local_rows]
            act[pl.ds(rows, local_rows)] = near[0][e][local_rows:]
            act[pl.ds(local_rows, rows - local_rows)] = near[1][e][...]

    act[rows + local_rows :] = blocks_ref[...]
    width = act.shape[1]
    copies = []
    for i in range(width // tile):
        total = None
        for v in range(2):
            part = lax.dot_general(
                act[pl.ds(v * rows, rows), pl.ds(i * tile, tile)],
                dz_refs[v][...],
                (((0,), (0,)), ((), ())),
                preferred_element_type=f32,
            )
            total = part if total is None else total + part
        product[pl.ds(i * tile, tile)] = total
        start = pl.multiple_of(out_row * width + i * tile, tile)
        copies.append(
            pltpu.make_async_copy(
                product.at[pl.ds(i * tile, tile)], out_ref.at[pl.ds(start, tile)], sems.at[i]
            )
        )
        copies[-1].start()
    for copy in copies:
        copy.wait()


def weight_grad_call(place, which, near, blocks, dz, features, before):
    half = len(near[0])
    width = near[0][0].shape[1]
    rows, columns = dz[0].shape
    tile = min(256, width)
    operands = [place] + [x for group in near for x in group] + [blocks] + list(dz)
    specs = [IN_SMEM] + [IN_VMEM] * (len(operands) - 1)
    aliases = {}
    if before is not None:
        aliases = {len(operands): 0}
        operands.append(before)
        specs.append(ANYWHERE)
    return pl.pallas_call(
        functools.partial(
            weight_grad_kernel,
            rows // (near[0][0].shape[0] // 2),
            int(before is not None),
            half,
            tile,
            which,
        ),
        out_shape=jax.ShapeDtypeStruct((features, columns), f32),
        in_specs=specs,
        out_specs=ANYWHERE,
        scratch_shapes=[
            pltpu.VMEM((2 * rows, width), bf16),
            pltpu.VMEM((width, columns), f32),
            pltpu.SemaphoreType.DMA((width // tile,)),
        ],
        input_output_aliases=aliases,
        compiler_params=params(12),
        cost_estimate=cost(4 * rows * width * columns, 4 * width * columns),
        name="weight_gradient",
    )(*operands)


def link_pieces(x, n_col):
    pieces = {0: x}
    half = x.shape[0] // 2
    for k in sorted(range(2, n_col, 2), key=lambda k: (bin(k).count("1"), k)):
        low, high = k & -k, 1 << (k.bit_length() - 1)
        if low == high:
            pieces[k] = xor_send(x, "col", k)
        else:
            first = xor_send(pieces[k ^ low][:half], "col", low)
            second = xor_send(pieces[k ^ high][half:], "col", high)
            pieces[k] = jnp.concatenate([first, second])
    return pieces


def sibling_pieces(pieces, n_col):
    for k in range(0, n_col, 2):
        if k + 1 not in pieces:
            pieces[k + 1] = xor_send(pieces[k], "col", 1)
    return pieces


def finish_kernel(n_batch, rows, *refs):
    sums, (d_pre, normalised, gain, deviation) = refs[:n_batch], refs[n_batch : n_batch + 4]
    loss_ref, gain_ref, bias_ref, out_ref = refs[n_batch + 4 :]
    both = exchange_sum(x[...] for x in sums)
    bias_ref[...] = both[0:1] + both[1:2]
    gain_ref[...] = both[2:3] + both[3:4]
    loss_ref[...] = both[4:5, 0:128]
    for v in range(2):
        factor = gain[...] * deviation[v : v + 1]
        mean_b, mean_g = both[v : v + 1] / rows, both[2 + v : 3 + v] / rows
        out_ref[v] = factor * (d_pre[v] - mean_b - normalised[v] * mean_g)


def finish_call(sums, d_pre, normalised, gain, deviation, rows):
    _, local_rows, width = d_pre.shape
    operands = list(sums) + [d_pre, normalised, gain[None], deviation[:, 0]]
    out_shape = (
        jax.ShapeDtypeStruct((1, 128), f32),
        jax.ShapeDtypeStruct((1, width), f32),
        jax.ShapeDtypeStruct((1, width), f32),
        jax.ShapeDtypeStruct(d_pre.shape, f32),
    )
    return pl.pallas_call(
        functools.partial(finish_kernel, len(sums), rows),
        out_shape=out_shape,
        in_specs=[IN_VMEM] * len(operands),
        out_specs=(IN_VMEM,) * 4,
        compiler_params=params(4),
        cost_estimate=cost(0, 8 * d_pre.size),
        name="views_gradient",
    )(*operands)


def shards(views, norm_scale_gain, norm_shift_bias, weight):
    n_batch = lax.axis_size("batch")
    n_col = lax.axis_size("col")
    place = jnp.stack([lax.axis_index("batch"), lax.axis_index("col")]).astype(jnp.int32)
    views, norm_scale_gain, norm_shift_bias, weight, place = lax.optimization_barrier(
        (views, norm_scale_gain, norm_shift_bias, weight, place)
    )
    n_view, local_rows, width = views.shape
    features, columns = weight.shape
    E = columns * n_col
    rows = local_rows * n_batch
    tall = n_view * local_rows
    scale = rows * E / 128.0
    denom = float((rows - 1) ** 2 * E)
    evens = list(range(0, n_col, 2))
    odds = [k + 1 for k in evens]
    far = evens[1:]

    with jax.named_scope("weight_load"):
        held_weight, loaded = load_call(weight, (2 * n_view, width))
    with jax.named_scope("norm_stats"):
        hidden = views.astype(f32)
        local_mean = jnp.mean(hidden, axis=1)
        local_centred = hidden - local_mean[:, None, :]
        local_spread = jnp.sum(local_centred * local_centred, axis=1)
        stats = exchange(jnp.concatenate([local_mean, local_spread]), "batch")
        stats[-1] = stats[-1] + loaded
        mean = exchange_sum(s[:n_view] for s in stats) / n_batch
        spread = exchange_sum(
            s[n_view:] + local_rows * jnp.square(s[:n_view] - mean) for s in stats
        )
        var = spread / rows
        inverse_deviation = (1.0 / jnp.sqrt(var + eps_norm))[:, None, :]
        normalised = (hidden - mean[:, None, :]) * inverse_deviation
        preactivation = norm_scale_gain * normalised + norm_shift_bias
        act = jax.nn.gelu(preactivation, approximate=True).astype(bf16)
    with jax.named_scope("act_gather"):
        own = act.reshape(tall, width)
        pieces = {0: own, 1: xor_send(own, "col", 1)}
        for k in far:
            pieces[k] = xor_send(own, "col", k)
        first, pieces[1] = lax.optimization_barrier((act[0], pieces[1]))
        others = [ring_send(first, "batch", d) for d in range(1, n_batch)]
        pieces = sibling_pieces(pieces, n_col)
    with jax.named_scope("z"):

        def z_part(source, ks, before, last=False):
            return z_call(
                place, ks, [source[k] for k in ks], held_weight, before, last, local_rows
            )

        z_own = z_part(pieces, far, z_part(pieces, [0, 1], None))
        z_own, others[-1] = lax.optimization_barrier((z_own, others[-1]))
        z_own0, z_own1 = z_part(pieces, [k + 1 for k in far], z_own, True)
        far_pieces = link_pieces(jnp.concatenate(others), n_col)
    with jax.named_scope("z_ring"):
        z_ring = [z_own1, ring_send(z_own1, "batch", 1)]
        z_ring[1], far_pieces[far[0]] = lax.optimization_barrier((z_ring[1], far_pieces[far[0]]))
        z_ring.append(ring_send(z_ring[1], "batch", 1))
    with jax.named_scope("z_far"):
        start = z_part(far_pieces, [0] + far[:-1], None)
        picked = list(pick_call(place, [pieces[k] for k in evens], n_batch, n_col))
        start, far_pieces[far[-1]], z_ring[2], picked = lax.optimization_barrier(
            (start, far_pieces[far[-1]], z_ring[2], picked)
        )
        far_pieces = sibling_pieces(far_pieces, n_col)
        for _ in range(3, n_batch):
            z_ring.append(ring_send(z_ring[-1], "batch", 1))
        z_far = z_part(far_pieces, odds[:-1] + far[-1:] + odds[-1:], start, True)
        slots = list(zip([z_own0] + list(z_far), z_ring))
    with jax.named_scope("kernel"):
        first_strip = strip_first_call([z0 for z0, _ in slots])
        even_part, odd_part = strip_call(place, [z1 for _, z1 in slots], first_strip, n_col)
        blocks = [
            ring_send(x, "batch", 1 + i % (n_batch - 1)) for i, x in enumerate(picked)
        ]
        third = len(blocks) // 3
        odd_part, blocks[:third] = lax.optimization_barrier((odd_part, blocks[:third]))
        even_part = even_part + xor_send(odd_part, "col", 1).astype(f32)
        strip = even_part[0]
        for k in far:
            strip = strip + xor_send(even_part[k // 2].astype(bf16), "col", k).astype(f32)
        strip_b = strip.astype(bf16)
        strips = {0: strip_b}
        for k in far:
            strips[k] = xor_send(strip_b, "col", k)
        strips[far[0]], blocks[third : 2 * third] = lax.optimization_barrier(
            (strips[far[0]], blocks[third : 2 * third])
        )
        strips = sibling_pieces(strips, n_col)
    with jax.named_scope("dz"):
        constants = (
            4.0 * scale / denom,
            25.0 * scale / (2.0 * E * (rows - 1)),
            50.0 * scale / (rows * E),
            25.0 / (rows * E) / n_batch,
            25.0 / (2 * E) / n_batch,
            1.0 / denom / n_batch,
            1.0 / denom / n_batch,
        )
        strips = [strips[k] for k in range(n_col)]
        share = jnp.zeros((8, 128), f32)
        dz0, share = dz_call(place, 0, strip, share, strips, slots, constants)
    with jax.named_scope("d_act"):
        (away0,) = d_act_call(place, dz0, None, held_weight, n_batch, n_col, None)
        away0, share = lax.optimization_barrier((away0, share))
        got0 = xor_send(away0, "col", 1)
        dz1, share = dz_call(place, 1, strip, share, strips, slots, constants)
        dz1, blocks[2 * third :] = lax.optimization_barrier((dz1, blocks[2 * third :]))
        dz = [dz0, dz1]
        (away1,) = d_act_call(place, dz1, share, held_weight, n_batch, n_col, None)
        got1 = xor_send(away1, "col", 1)
        views_d_act, arrived = [], []
        for v, carried, got in ((0, None, got0), (1, share, got1)):
            *sends, own = d_act_call(place, dz[v], carried, held_weight, n_batch, n_col, got)
            arrived.append([xor_send(part, "col", k) for k, part in zip(far, sends)])
            views_d_act.append(own)
    with jax.named_scope("grad_weight"):
        grad_weight = None
        for block in range(n_col // n_batch // 2):
            mine = jnp.concatenate(blocks[block * (n_batch - 1) : (block + 1) * (n_batch - 1)])
            other = xor_send(mine, "col", 1)
            for parity, ks, far_rows in ((0, evens, mine), (1, odds, other)):
                grad_weight = weight_grad_call(
                    place,
                    (block, parity),
                    [[group[k] for k in ks] for group in (pieces, far_pieces)],
                    far_rows,
                    dz,
                    features // n_batch,
                    grad_weight,
                )
    with jax.named_scope("norm_backward"):
        arrived, grad_weight = lax.optimization_barrier((arrived, grad_weight))
        last = [views_d_act[1]] + arrived[1]
        share = exchange_sum(share_of(part[local_rows:]) for part in last)
        d_act = []
        for own, parts in zip(views_d_act, arrived):
            total = own[:local_rows]
            for part in parts:
                total = total + part[:local_rows].astype(f32)
            d_act.append(total)
        d_act = jnp.stack(d_act)
        d_pre = d_act * gelu_slope(preactivation)
        sums = jnp.concatenate(
            [
                jnp.sum(d_pre, axis=1),
                jnp.sum(d_pre * normalised, axis=1),
                jnp.broadcast_to(share, (2 * n_view, width)),
            ]
        )
        loss, grad_gain, grad_bias, views_gradient = finish_call(
            exchange(sums, "batch"), d_pre, normalised, norm_scale_gain, inverse_deviation, rows
        )
    return (loss[0, 0], grad_weight, grad_gain[0], grad_bias[0], views_gradient)


def solution(mesh):
    placed = (P(None, "batch", "col"), P("col"), P("col"), P(None, "col"))
    return jax.shard_map(
        shards,
        mesh=mesh,
        in_specs=placed,
        out_specs=(P(), P("batch", "col"), P("col"), P("col"), P(None, "batch", "col")),
        check_vma=False,
    )
```

```python
import functools

import jax
import jax.numpy as jnp
from jax import lax
from jax.experimental import pallas as pl
from jax.experimental.pallas import tpu as pltpu
from jax.sharding import PartitionSpec as P

eps_norm = 1e-05
eps_std = 0.0001
f32 = jnp.float32
bf16 = jnp.bfloat16
MIB = 1024 * 1024


def gelu_slope(preactivation):
    value, pullback = jax.vjp(lambda t: jax.nn.gelu(t, approximate=True), preactivation)
    return pullback(jnp.ones_like(value))[0]


def xor_send(x, axis, k):
    n = lax.axis_size(axis)
    return lax.ppermute(x, axis, [(i, i ^ k) for i in range(n)])


def ring_order(n):
    return list(range(0, n, 2)) + list(range(1, n, 2))[::-1]


def ring_send(x, axis, d):
    order = ring_order(lax.axis_size(axis))
    n = len(order)
    return lax.ppermute(x, axis, [(order[i], order[(i + d) % n]) for i in range(n)])


def exchange_sum(parts):
    parts = list(parts)
    while len(parts) > 1:
        parts = [x + y for x, y in zip(parts[::2], parts[1::2])]
    return parts[0]


def exchange(x, axis):
    return [x] + [xor_send(x, axis, k) for k in range(1, lax.axis_size(axis))]


def params(limit):
    return pltpu.CompilerParams(vmem_limit_bytes=limit * MIB)


def cost(flops, moved):
    return pl.CostEstimate(flops=flops, bytes_accessed=moved, transcendentals=0)


IN_SMEM = pl.BlockSpec(memory_space=pltpu.SMEM)
IN_VMEM = pl.BlockSpec(memory_space=pltpu.VMEM)
ANYWHERE = pl.BlockSpec(memory_space=pl.ANY)
LOADS = 8


def load_kernel(w_ref, out_ref, flag_ref, sems):
    flag_ref[...] = jnp.zeros_like(flag_ref)
    step = w_ref.shape[0] // LOADS
    copies = [
        pltpu.make_async_copy(
            w_ref.at[pl.ds(i * step, step)], out_ref.at[pl.ds(i * step, step)], sems.at[i]
        )
        for i in range(LOADS)
    ]
    for copy in copies:
        copy.start()
    for copy in copies:
        copy.wait()


def load_call(weight, flag_shape):
    return pl.pallas_call(
        load_kernel,
        out_shape=(
            pltpu.VMEM(weight.shape, weight.dtype),
            jax.ShapeDtypeStruct(flag_shape, f32),
        ),
        in_specs=[ANYWHERE],
        out_specs=(IN_VMEM, IN_VMEM),
        scratch_shapes=[pltpu.SemaphoreType.DMA((LOADS,))],
        compiler_params=params(4),
        cost_estimate=cost(0, 4 * weight.size),
        name="weight_load",
    )(pltpu.with_memory_space_constraint(weight, pltpu.HBM))


def weight_rows(place_ref, w_ref, k, width):
    return w_ref[pl.ds(pl.multiple_of((place_ref[1] ^ k) * width, width), width), :]


def z_kernel(ks, first, last, local_rows, place_ref, *refs):
    count = len(ks)
    pieces, rest = refs[:count], list(refs[count:])
    w_ref = rest.pop(0)
    total = None if first else rest.pop(0)[...]
    width = pieces[0].shape[1]
    for j in range(count):
        part = jnp.dot(
            pieces[j][...], weight_rows(place_ref, w_ref, ks[j], width), preferred_element_type=f32
        )
        total = part if total is None else total + part
    if not last:
        rest[0][...] = total
        return
    z = total.astype(bf16)
    for v, ref in enumerate(rest):
        ref[...] = z[v * local_rows : (v + 1) * local_rows]


def z_call(place, ks, pieces, weight, before, last, local_rows):
    count = len(ks)
    tall, width = pieces[0].shape
    columns = weight.shape[1]
    operands = [place] + list(pieces) + [weight] + ([] if before is None else [before])
    if last:
        groups = tall // local_rows
        out_shape = (jax.ShapeDtypeStruct((local_rows, columns), bf16),) * groups
    else:
        out_shape = jax.ShapeDtypeStruct((tall, columns), f32)
    return pl.pallas_call(
        functools.partial(z_kernel, tuple(ks), before is None, last, local_rows),
        out_shape=out_shape,
        in_specs=[IN_SMEM] + [IN_VMEM] * (len(operands) - 1),
        out_specs=jax.tree.map(lambda _: IN_VMEM, out_shape),
        compiler_params=params(8),
        cost_estimate=cost(2 * tall * width * columns * count, 2 * tall * columns),
        name="z_matmul",
    )(*operands)


def upper_blocks(n):
    return [(s, t) for s in range(n) for t in range(s, n)]


def strip_kernel(n_batch, n_col, place_ref, *refs):
    z_refs, (even_ref, odd_ref, strip) = refs[: 2 * n_batch], refs[2 * n_batch :]
    local_rows = z_refs[0].shape[0]
    rows = local_rows * n_batch
    for v in range(2):
        zf = [z[...].astype(f32) for z in z_refs[v::2]]
        mean = sum(jnp.sum(z, axis=0, keepdims=True) for z in zf) / rows
        rounded = jnp.concatenate([(z - mean).astype(bf16) for z in zf], axis=0)
        at = 0
        for s in range(n_batch):
            product = lax.dot_general(
                rounded[s * local_rows : (s + 1) * local_rows],
                rounded[s * local_rows :],
                (((1,), (1,)), ((), ())),
                preferred_element_type=f32,
            )
            strip[pl.ds(v * local_rows, local_rows), pl.ds(at, product.shape[1])] = product
            at += product.shape[1]
    part = 2 * local_rows // n_col
    for k in range(n_col):
        start = pl.multiple_of((place_ref[1] ^ k) * part, part)
        ref = odd_ref if k % 2 else even_ref
        ref[k // 2] = strip[pl.ds(start, part), :].astype(ref.dtype)


def strip_call(place, z_slots, n_col):
    n_batch = len(z_slots)
    local_rows, columns = z_slots[0][0].shape
    tall = 2 * local_rows
    wide = len(upper_blocks(n_batch)) * local_rows
    shape = (n_col // 2, tall // n_col, wide)
    operands = [place] + [z for slot in z_slots for z in slot]
    return pl.pallas_call(
        functools.partial(strip_kernel, n_batch, n_col),
        out_shape=(jax.ShapeDtypeStruct(shape, f32), jax.ShapeDtypeStruct(shape, bf16)),
        in_specs=[IN_SMEM] + [IN_VMEM] * (len(operands) - 1),
        out_specs=(IN_VMEM, IN_VMEM),
        scratch_shapes=[pltpu.VMEM((tall, wide), f32)],
        compiler_params=params(18),
        cost_estimate=cost(2 * tall * wide * columns, 2 * tall * columns * n_batch),
        name="kernel_strip",
    )(*operands)


def dz_kernel(n_batch, n_col, tile, constants, place_ref, own_ref, *refs):
    coef, hinge_coef, inv_coef, inv_share, hinge_share, diag_share, block_share = constants
    strip_refs = refs[:n_col]
    z_refs = refs[n_col : n_col + 2 * n_batch]
    dz_ref, share_ref, strips, full, centred = refs[n_col + 2 * n_batch :]
    local_rows, columns = z_refs[0].shape
    rows = local_rows * n_batch
    own = own_ref[...]
    block = lax.broadcasted_iota(jnp.int32, own.shape, 1) // local_rows
    on_diagonal = functools.reduce(
        jnp.logical_or, [block == i for i, (s, t) in enumerate(upper_blocks(n_batch)) if s == t]
    )
    own = own * own * jnp.where(on_diagonal, 1.0, 2.0)
    own = jnp.sum(jnp.sum(own, axis=0, keepdims=True), axis=1, keepdims=True)
    share_ref[...] = jnp.broadcast_to(block_share * own, share_ref.shape)
    part = 2 * local_rows // n_col
    for k in range(n_col):
        start = pl.multiple_of((place_ref[1] ^ k) * part, part)
        strips[pl.ds(start, part), :] = strip_refs[k][...].astype(f32)
    for v in range(2):
        for i, (s, t) in enumerate(upper_blocks(n_batch)):
            here, there = pl.ds(s * local_rows, local_rows), pl.ds(t * local_rows, local_rows)
            block = strips[pl.ds(v * local_rows, local_rows), pl.ds(i * local_rows, local_rows)]
            full[v, here, there] = block.astype(bf16)
            if s < t:
                full[v, there, here] = jnp.transpose(block).astype(bf16)

    def one_tile(j, carry):
        here = pl.ds(pl.multiple_of(j * tile, tile), tile)
        share = jnp.zeros((1, 1), f32)
        grads = []
        z_views = []
        for v in range(2):
            zf = jnp.concatenate([z[:, here].astype(f32) for z in z_refs[v::2]], axis=0)
            z_views.append(zf)
            zc = zf - jnp.sum(zf, axis=0, keepdims=True) / rows
            std = jnp.sqrt(jnp.sum(zc * zc, axis=0, keepdims=True) / (rows - 1) + eps_std)
            zcb = zc.astype(bf16)
            centred[...] = zcb
            rounded = zcb.astype(f32)
            diag = jnp.sum(rounded * rounded, axis=0, keepdims=True)
            moved = jnp.dot(full[v], centred[...], preferred_element_type=f32)
            pull = jnp.where(std < 1.0, hinge_coef, 0.0) / std
            summed = coef * (moved - rounded * diag) - zc * pull
            grads.append(summed - jnp.sum(summed, axis=0, keepdims=True) / rows)
            share += hinge_share * jnp.sum(jnp.maximum(1.0 - std, 0.0), axis=1, keepdims=True)
            share -= diag_share * jnp.sum(diag * diag, axis=1, keepdims=True)
        diff = z_views[0] - z_views[1]
        share += inv_share * jnp.sum(
            jnp.sum(diff * diff, axis=0, keepdims=True), axis=1, keepdims=True
        )
        share_ref[...] += jnp.broadcast_to(share, share_ref.shape)
        dz_ref[0, :, here] = (grads[0] + inv_coef * diff).astype(bf16)
        dz_ref[1, :, here] = (grads[1] - inv_coef * diff).astype(bf16)
        return carry

    lax.fori_loop(0, columns // tile, one_tile, 0)


def dz_call(place, own, strips, z_slots, constants):
    n_col, n_batch = len(strips), len(z_slots)
    local_rows, columns = z_slots[0][0].shape
    tall = 2 * local_rows
    rows = local_rows * n_batch
    tile = min(256, columns)
    operands = [place, own] + list(strips) + [z for slot in z_slots for z in slot]
    return pl.pallas_call(
        functools.partial(dz_kernel, n_batch, n_col, tile, constants),
        out_shape=(
            jax.ShapeDtypeStruct((2, rows, columns), bf16),
            jax.ShapeDtypeStruct((8, 128), f32),
        ),
        in_specs=[IN_SMEM] + [IN_VMEM] * (len(operands) - 1),
        out_specs=(IN_VMEM, IN_VMEM),
        scratch_shapes=[
            pltpu.VMEM((tall, strips[0].shape[1]), f32),
            pltpu.VMEM((2, rows, rows), bf16),
            pltpu.VMEM((rows, tile), bf16),
        ],
        compiler_params=params(24),
        cost_estimate=cost(4 * rows * rows * columns, 8 * rows * columns),
        name="embedding_gradient",
    )(*operands)


EXTRA = 16


def share_rows(share, width, kind):
    high = share.astype(bf16).astype(f32)
    middle = (share - high).astype(bf16).astype(f32)
    low = share - high - middle
    row = lax.broadcasted_iota(jnp.int32, (EXTRA, width), 0)
    rows = jnp.where(row == 0, high, jnp.where(row == 1, middle, jnp.where(row == 2, low, 0.0)))
    return rows.astype(kind)


def share_of(rows):
    return rows[0:1].astype(f32) + rows[1:2].astype(f32) + rows[2:3].astype(f32)


def d_act_kernel(ks, adds, tall, width, place_ref, dz_ref, share_ref, w_ref, *refs):
    local_rows = tall // 2
    dz = jnp.concatenate([dz_ref[0, :local_rows], dz_ref[1, :local_rows]], axis=0)
    share = share_ref[0:1, 0:1]
    for j, k in enumerate(ks):
        part = lax.dot_general(
            dz,
            weight_rows(place_ref, w_ref, k, width),
            (((1,), (1,)), ((), ())),
            preferred_element_type=f32,
        )
        whole_share = share
        out = refs[j + 1] if adds else refs[0].at[j]
        if adds:
            part = part + refs[0][j, :tall].astype(f32)
            whole_share = share + share_of(refs[0][j, tall:])[:, 0:1]
        out[:tall] = part.astype(out.dtype)
        out[tall:] = share_rows(whole_share, width, out.dtype)


def d_act_call(place, dz, share, weight, n_batch, n_col, ks, got):
    width = weight.shape[0] // n_col
    tall = 2 * dz.shape[1] // n_batch
    columns = weight.shape[1]
    long = tall + EXTRA
    operands = [place, dz, share, weight]
    if got is None:
        out_shape = (jax.ShapeDtypeStruct((len(ks), long, width), bf16),)
    else:
        operands.append(got)
        out_shape = tuple(jax.ShapeDtypeStruct((long, width), bf16 if k else f32) for k in ks)
    return pl.pallas_call(
        functools.partial(d_act_kernel, tuple(ks), got is not None, tall, width),
        out_shape=out_shape,
        in_specs=[IN_SMEM] + [IN_VMEM] * (len(operands) - 1),
        out_specs=(IN_VMEM,) * len(out_shape),
        compiler_params=params(8),
        cost_estimate=cost(2 * tall * width * columns * len(ks), 2 * len(ks) * width * tall),
        name="d_act_matmul",
    )(*operands)


def held_place(plane, c, block, n_col, n_batch):
    return (((n_col // n_batch) * plane + 2 * block) ^ (c - (c & 1))) >> 1


def pick_kernel(n_batch, n_col, local_rows, place_ref, *refs):
    half = n_col // 2
    pieces, outs = refs[:half], refs[half:]
    b, c = place_ref[0], place_ref[1]
    position = jnp.where((b & 1) == 0, b >> 1, n_batch - 1 - (b >> 1))
    i = 0
    for block in range(n_col // n_batch // 2):
        for d in range(1, n_batch):
            ahead = position + d
            ahead = jnp.where(ahead >= n_batch, ahead - n_batch, ahead)
            plane = jnp.where(2 * ahead < n_batch, 2 * ahead, 2 * (n_batch - ahead) - 1)
            chosen = held_place(plane, c, block, n_col, n_batch)
            for e in range(half):

                @pl.when(chosen == e)
                def _():
                    outs[i][...] = pieces[e][local_rows:]

            i += 1


def pick_call(place, pieces, n_batch, n_col):
    tall, width = pieces[0].shape
    count = n_col // n_batch // 2 * (n_batch - 1)
    out_shape = (jax.ShapeDtypeStruct((tall // 2, width), bf16),) * count
    return pl.pallas_call(
        functools.partial(pick_kernel, n_batch, n_col, tall // 2),
        out_shape=out_shape,
        in_specs=[IN_SMEM] + [IN_VMEM] * len(pieces),
        out_specs=(IN_VMEM,) * count,
        compiler_params=params(4),
        cost_estimate=cost(0, tall * width * count),
        name="pick_blocks",
    )(place, *pieces)


def weight_grad_kernel(n_batch, aliased, half, tile, which, place_ref, *refs):
    near = [refs[:half], refs[half : 2 * half]]
    blocks_ref, dz_ref = refs[2 * half : 2 * half + 2]
    out_ref, act, product, sems = refs[2 * half + 2 + aliased :]
    block, parity = which
    chosen = held_place(place_ref[0], place_ref[1], block, 2 * half, n_batch)
    out_row = 2 * block + ((place_ref[1] & 1) ^ parity)
    local_rows = near[0][0].shape[0] // 2
    rows = dz_ref.shape[1]
    for e in range(half):

        @pl.when(chosen == e)
        def _():
            act[pl.ds(0, local_rows)] = near[0][e][:local_rows]
            act[pl.ds(rows, local_rows)] = near[0][e][local_rows:]
            act[pl.ds(local_rows, rows - local_rows)] = near[1][e][...]

    act[rows + local_rows :] = blocks_ref[...]
    width = act.shape[1]
    copies = []
    for i in range(width // tile):
        total = None
        for v in range(2):
            part = lax.dot_general(
                act[pl.ds(v * rows, rows), pl.ds(i * tile, tile)],
                dz_ref[v],
                (((0,), (0,)), ((), ())),
                preferred_element_type=f32,
            )
            total = part if total is None else total + part
        product[pl.ds(i * tile, tile)] = total
        start = pl.multiple_of(out_row * width + i * tile, tile)
        copies.append(
            pltpu.make_async_copy(
                product.at[pl.ds(i * tile, tile)], out_ref.at[pl.ds(start, tile)], sems.at[i]
            )
        )
        copies[-1].start()
    for copy in copies:
        copy.wait()


def weight_grad_call(place, which, near, blocks, dz, features, before):
    half = len(near[0])
    width = near[0][0].shape[1]
    _, rows, columns = dz.shape
    tile = min(256, width)
    operands = [place] + [x for group in near for x in group] + [blocks, dz]
    specs = [IN_SMEM] + [IN_VMEM] * (len(operands) - 1)
    aliases = {}
    if before is not None:
        aliases = {len(operands): 0}
        operands.append(before)
        specs.append(ANYWHERE)
    return pl.pallas_call(
        functools.partial(
            weight_grad_kernel,
            rows // (near[0][0].shape[0] // 2),
            int(before is not None),
            half,
            tile,
            which,
        ),
        out_shape=jax.ShapeDtypeStruct((features, columns), f32),
        in_specs=specs,
        out_specs=ANYWHERE,
        scratch_shapes=[
            pltpu.VMEM((2 * rows, width), bf16),
            pltpu.VMEM((width, columns), f32),
            pltpu.SemaphoreType.DMA((width // tile,)),
        ],
        input_output_aliases=aliases,
        compiler_params=params(12),
        cost_estimate=cost(4 * rows * width * columns, 4 * width * columns),
        name="weight_gradient",
    )(*operands)


def link_pieces(x, n_col):
    pieces = {0: x}
    half = x.shape[0] // 2
    for k in sorted(range(2, n_col, 2), key=lambda k: (bin(k).count("1"), k)):
        low, high = k & -k, 1 << (k.bit_length() - 1)
        if low == high:
            pieces[k] = xor_send(x, "col", k)
        else:
            first = xor_send(pieces[k ^ low][:half], "col", low)
            second = xor_send(pieces[k ^ high][half:], "col", high)
            pieces[k] = jnp.concatenate([first, second])
    return pieces


def sibling_pieces(pieces, n_col):
    for k in range(0, n_col, 2):
        if k + 1 not in pieces:
            pieces[k + 1] = xor_send(pieces[k], "col", 1)
    return pieces


def finish_kernel(n_batch, rows, *refs):
    sums, (d_pre, normalised, gain, deviation) = refs[:n_batch], refs[n_batch : n_batch + 4]
    loss_ref, gain_ref, bias_ref, out_ref = refs[n_batch + 4 :]
    both = exchange_sum(x[...] for x in sums)
    bias_ref[...] = both[0:1] + both[1:2]
    gain_ref[...] = both[2:3] + both[3:4]
    loss_ref[...] = both[4:5, 0:128]
    for v in range(2):
        factor = gain[...] * deviation[v : v + 1]
        mean_b, mean_g = both[v : v + 1] / rows, both[2 + v : 3 + v] / rows
        out_ref[v] = factor * (d_pre[v] - mean_b - normalised[v] * mean_g)


def finish_call(sums, d_pre, normalised, gain, deviation, rows):
    _, local_rows, width = d_pre.shape
    operands = list(sums) + [d_pre, normalised, gain[None], deviation[:, 0]]
    out_shape = (
        jax.ShapeDtypeStruct((1, 128), f32),
        jax.ShapeDtypeStruct((1, width), f32),
        jax.ShapeDtypeStruct((1, width), f32),
        jax.ShapeDtypeStruct(d_pre.shape, f32),
    )
    return pl.pallas_call(
        functools.partial(finish_kernel, len(sums), rows),
        out_shape=out_shape,
        in_specs=[IN_VMEM] * len(operands),
        out_specs=(IN_VMEM,) * 4,
        compiler_params=params(4),
        cost_estimate=cost(0, 8 * d_pre.size),
        name="views_gradient",
    )(*operands)


def shards(views, norm_scale_gain, norm_shift_bias, weight):
    n_batch = lax.axis_size("batch")
    n_col = lax.axis_size("col")
    place = jnp.stack([lax.axis_index("batch"), lax.axis_index("col")]).astype(jnp.int32)
    views, norm_scale_gain, norm_shift_bias, weight, place = lax.optimization_barrier(
        (views, norm_scale_gain, norm_shift_bias, weight, place)
    )
    n_view, local_rows, width = views.shape
    features, columns = weight.shape
    E = columns * n_col
    rows = local_rows * n_batch
    tall = n_view * local_rows
    scale = rows * E / 128.0
    denom = float((rows - 1) ** 2 * E)
    evens = list(range(0, n_col, 2))
    odds = [k + 1 for k in evens]
    far = evens[1:]

    with jax.named_scope("weight_load"):
        held_weight, loaded = load_call(weight, (2 * n_view, width))
    with jax.named_scope("norm_stats"):
        hidden = views.astype(f32)
        local_mean = jnp.mean(hidden, axis=1)
        local_centred = hidden - local_mean[:, None, :]
        local_spread = jnp.sum(local_centred * local_centred, axis=1)
        stats = exchange(jnp.concatenate([local_mean, local_spread]), "batch")
        stats[-1] = stats[-1] + loaded
        mean = exchange_sum(s[:n_view] for s in stats) / n_batch
        spread = exchange_sum(
            s[n_view:] + local_rows * jnp.square(s[:n_view] - mean) for s in stats
        )
        var = spread / rows
        inverse_deviation = (1.0 / jnp.sqrt(var + eps_norm))[:, None, :]
        normalised = (hidden - mean[:, None, :]) * inverse_deviation
        preactivation = norm_scale_gain * normalised + norm_shift_bias
        act = jax.nn.gelu(preactivation, approximate=True).astype(bf16)
    with jax.named_scope("act_gather"):
        own = act.reshape(tall, width)
        pieces = {0: own, 1: xor_send(own, "col", 1)}
        for k in far:
            pieces[k] = xor_send(own, "col", k)
        first, pieces[1] = lax.optimization_barrier((act[0], pieces[1]))
        others = [ring_send(first, "batch", d) for d in range(1, n_batch)]
        pieces = sibling_pieces(pieces, n_col)
    with jax.named_scope("z"):

        def z_part(source, ks, before, last=False):
            return z_call(
                place, ks, [source[k] for k in ks], held_weight, before, last, local_rows
            )

        z_own = z_part(pieces, far, z_part(pieces, [0, 1], None))
        z_own, others[-1] = lax.optimization_barrier((z_own, others[-1]))
        z_own0, z_own1 = z_part(pieces, [k + 1 for k in far], z_own, True)
        far_pieces = link_pieces(jnp.concatenate(others), n_col)
    with jax.named_scope("z_ring"):
        z_ring = [z_own1, ring_send(z_own1, "batch", 1)]
        z_ring[1], far_pieces[far[0]] = lax.optimization_barrier((z_ring[1], far_pieces[far[0]]))
        z_ring.append(ring_send(z_ring[1], "batch", 1))
    with jax.named_scope("z_far"):
        start = z_part(far_pieces, [0] + far[:-1], None)
        picked = list(pick_call(place, [pieces[k] for k in evens], n_batch, n_col))
        start, far_pieces[far[-1]], z_ring[2], picked = lax.optimization_barrier(
            (start, far_pieces[far[-1]], z_ring[2], picked)
        )
        far_pieces = sibling_pieces(far_pieces, n_col)
        for _ in range(3, n_batch):
            z_ring.append(ring_send(z_ring[-1], "batch", 1))
        z_far = z_part(far_pieces, odds[:-1] + far[-1:] + odds[-1:], start, True)
        slots = list(zip([z_own0] + list(z_far), z_ring))
    with jax.named_scope("kernel"):
        even_part, odd_part = strip_call(place, slots, n_col)
        blocks = [
            ring_send(x, "batch", 1 + i % (n_batch - 1)) for i, x in enumerate(picked)
        ]
        third = len(blocks) // 3
        odd_part, blocks[:third] = lax.optimization_barrier((odd_part, blocks[:third]))
        even_part = even_part + xor_send(odd_part, "col", 1).astype(f32)
        strip = even_part[0]
        for k in far:
            strip = strip + xor_send(even_part[k // 2].astype(bf16), "col", k).astype(f32)
        strip_b = strip.astype(bf16)
        strips = {0: strip_b}
        for k in far:
            strips[k] = xor_send(strip_b, "col", k)
        strips[far[0]], blocks[third : 2 * third] = lax.optimization_barrier(
            (strips[far[0]], blocks[third : 2 * third])
        )
        strips = sibling_pieces(strips, n_col)
    with jax.named_scope("dz"):
        constants = (
            4.0 * scale / denom,
            25.0 * scale / (2.0 * E * (rows - 1)),
            50.0 * scale / (rows * E),
            25.0 / (rows * E) / n_batch,
            25.0 / (2 * E) / n_batch,
            1.0 / denom / n_batch,
            1.0 / denom / n_batch,
        )
        dz, share = dz_call(place, strip, [strips[k] for k in range(n_col)], slots, constants)
        dz, blocks[2 * third :] = lax.optimization_barrier((dz, blocks[2 * third :]))
    with jax.named_scope("d_act"):
        crossing = [k for k in far if k & (k - 1)]
        groups = [crossing, [k for k in far if k not in crossing] + [0]]
        got = []
        for ks in groups:
            (away,) = d_act_call(
                place, dz, share, held_weight, n_batch, n_col, [k + 1 for k in ks], None
            )
            away, share = lax.optimization_barrier((away, share))
            got.append(xor_send(away, "col", 1))
        arrived = {}
        for ks, part in zip(groups, got):
            summed = d_act_call(place, dz, share, held_weight, n_batch, n_col, ks, part)
            for k, piece in zip(ks, summed):
                arrived[k] = xor_send(piece, "col", k) if k else piece
        d_act = arrived.pop(0)
        arrived = [arrived[k] for k in far]
    with jax.named_scope("grad_weight"):
        grad_weight = None
        for block in range(n_col // n_batch // 2):
            mine = jnp.concatenate(blocks[block * (n_batch - 1) : (block + 1) * (n_batch - 1)])
            other = xor_send(mine, "col", 1)
            for parity, ks, far_rows in ((0, evens, mine), (1, odds, other)):
                grad_weight = weight_grad_call(
                    place,
                    (block, parity),
                    [[group[k] for k in ks] for group in (pieces, far_pieces)],
                    far_rows,
                    dz,
                    features // n_batch,
                    grad_weight,
                )
    with jax.named_scope("norm_backward"):
        arrived, grad_weight = lax.optimization_barrier((arrived, grad_weight))
        share = exchange_sum(share_of(part[tall:]) for part in [d_act] + arrived)
        d_act = d_act[:tall]
        for part in arrived:
            d_act = d_act + part[:tall].astype(f32)
        d_pre = d_act.reshape(n_view, local_rows, width) * gelu_slope(preactivation)
        sums = jnp.concatenate(
            [
                jnp.sum(d_pre, axis=1),
                jnp.sum(d_pre * normalised, axis=1),
                jnp.broadcast_to(share, (2 * n_view, width)),
            ]
        )
        loss, grad_gain, grad_bias, views_gradient = finish_call(
            exchange(sums, "batch"), d_pre, normalised, norm_scale_gain, inverse_deviation, rows
        )
    return (loss[0, 0], grad_weight, grad_gain[0], grad_bias[0], views_gradient)


def solution(mesh):
    placed = (P(None, "batch", "col"), P("col"), P("col"), P(None, "col"))
    return jax.shard_map(
        shards,
        mesh=mesh,
        in_specs=placed,
        out_specs=(P(), P("batch", "col"), P("col"), P("col"), P(None, "batch", "col")),
        check_vma=False,
    )
```

```python
import functools

import jax
import jax.numpy as jnp
from jax import lax
from jax.experimental import pallas as pl
from jax.experimental.pallas import tpu as pltpu
from jax.sharding import PartitionSpec as P

eps_norm = 1e-05
eps_std = 0.0001
f32 = jnp.float32
bf16 = jnp.bfloat16
MIB = 1024 * 1024


def gelu_slope(preactivation):
    value, pullback = jax.vjp(lambda t: jax.nn.gelu(t, approximate=True), preactivation)
    return pullback(jnp.ones_like(value))[0]


def xor_send(x, axis, k):
    n = lax.axis_size(axis)
    return lax.ppermute(x, axis, [(i, i ^ k) for i in range(n)])


def ring_order(n):
    return list(range(0, n, 2)) + list(range(1, n, 2))[::-1]


def ring_send(x, axis, d):
    order = ring_order(lax.axis_size(axis))
    n = len(order)
    return lax.ppermute(x, axis, [(order[i], order[(i + d) % n]) for i in range(n)])


def exchange_sum(parts):
    parts = list(parts)
    while len(parts) > 1:
        parts = [x + y for x, y in zip(parts[::2], parts[1::2])]
    return parts[0]


def exchange(x, axis):
    return [x] + [xor_send(x, axis, k) for k in range(1, lax.axis_size(axis))]


def params(limit):
    return pltpu.CompilerParams(vmem_limit_bytes=limit * MIB)


def cost(flops, moved):
    return pl.CostEstimate(flops=flops, bytes_accessed=moved, transcendentals=0)


IN_SMEM = pl.BlockSpec(memory_space=pltpu.SMEM)
IN_VMEM = pl.BlockSpec(memory_space=pltpu.VMEM)
ANYWHERE = pl.BlockSpec(memory_space=pl.ANY)
LOADS = 8


def load_kernel(w_ref, out_ref, flag_ref, sems):
    flag_ref[...] = jnp.zeros_like(flag_ref)
    step = w_ref.shape[0] // LOADS
    copies = [
        pltpu.make_async_copy(
            w_ref.at[pl.ds(i * step, step)], out_ref.at[pl.ds(i * step, step)], sems.at[i]
        )
        for i in range(LOADS)
    ]
    for copy in copies:
        copy.start()
    for copy in copies:
        copy.wait()


def load_call(weight, flag_shape):
    return pl.pallas_call(
        load_kernel,
        out_shape=(
            pltpu.VMEM(weight.shape, weight.dtype),
            jax.ShapeDtypeStruct(flag_shape, f32),
        ),
        in_specs=[ANYWHERE],
        out_specs=(IN_VMEM, IN_VMEM),
        scratch_shapes=[pltpu.SemaphoreType.DMA((LOADS,))],
        compiler_params=params(4),
        cost_estimate=cost(0, 4 * weight.size),
        name="weight_load",
    )(pltpu.with_memory_space_constraint(weight, pltpu.HBM))


def weight_rows(place_ref, w_ref, k, width):
    return w_ref[pl.ds(pl.multiple_of((place_ref[1] ^ k) * width, width), width), :]


def z_kernel(ks, first, last, local_rows, place_ref, *refs):
    count = len(ks)
    pieces, rest = refs[:count], list(refs[count:])
    w_ref = rest.pop(0)
    total = None if first else rest.pop(0)[...]
    width = pieces[0].shape[1]
    for j in range(count):
        part = jnp.dot(
            pieces[j][...], weight_rows(place_ref, w_ref, ks[j], width), preferred_element_type=f32
        )
        total = part if total is None else total + part
    if not last:
        rest[0][...] = total
        return
    z = total.astype(bf16)
    for v, ref in enumerate(rest):
        ref[...] = z[v * local_rows : (v + 1) * local_rows]


def z_call(place, ks, pieces, weight, before, last, local_rows):
    count = len(ks)
    tall, width = pieces[0].shape
    columns = weight.shape[1]
    operands = [place] + list(pieces) + [weight] + ([] if before is None else [before])
    if last:
        groups = tall // local_rows
        out_shape = (jax.ShapeDtypeStruct((local_rows, columns), bf16),) * groups
    else:
        out_shape = jax.ShapeDtypeStruct((tall, columns), f32)
    return pl.pallas_call(
        functools.partial(z_kernel, tuple(ks), before is None, last, local_rows),
        out_shape=out_shape,
        in_specs=[IN_SMEM] + [IN_VMEM] * (len(operands) - 1),
        out_specs=jax.tree.map(lambda _: IN_VMEM, out_shape),
        compiler_params=params(8),
        cost_estimate=cost(2 * tall * width * columns * count, 2 * tall * columns),
        name="z_matmul",
    )(*operands)


def upper_blocks(n):
    return [(s, t) for s in range(n) for t in range(s, n)]


def strip_kernel(n_batch, n_col, place_ref, *refs):
    z_refs, (even_ref, odd_ref, strip) = refs[: 2 * n_batch], refs[2 * n_batch :]
    local_rows = z_refs[0].shape[0]
    rows = local_rows * n_batch
    for v in range(2):
        zf = [z[...].astype(f32) for z in z_refs[v::2]]
        mean = sum(jnp.sum(z, axis=0, keepdims=True) for z in zf) / rows
        rounded = jnp.concatenate([(z - mean).astype(bf16) for z in zf], axis=0)
        at = 0
        for s in range(n_batch):
            product = lax.dot_general(
                rounded[s * local_rows : (s + 1) * local_rows],
                rounded[s * local_rows :],
                (((1,), (1,)), ((), ())),
                preferred_element_type=f32,
            )
            strip[pl.ds(v * local_rows, local_rows), pl.ds(at, product.shape[1])] = product
            at += product.shape[1]
    part = 2 * local_rows // n_col
    for k in range(n_col):
        start = pl.multiple_of((place_ref[1] ^ k) * part, part)
        ref = odd_ref if k % 2 else even_ref
        ref[k // 2] = strip[pl.ds(start, part), :].astype(ref.dtype)


def strip_call(place, z_slots, n_col):
    n_batch = len(z_slots)
    local_rows, columns = z_slots[0][0].shape
    tall = 2 * local_rows
    wide = len(upper_blocks(n_batch)) * local_rows
    shape = (n_col // 2, tall // n_col, wide)
    operands = [place] + [z for slot in z_slots for z in slot]
    return pl.pallas_call(
        functools.partial(strip_kernel, n_batch, n_col),
        out_shape=(jax.ShapeDtypeStruct(shape, f32), jax.ShapeDtypeStruct(shape, bf16)),
        in_specs=[IN_SMEM] + [IN_VMEM] * (len(operands) - 1),
        out_specs=(IN_VMEM, IN_VMEM),
        scratch_shapes=[pltpu.VMEM((tall, wide), f32)],
        compiler_params=params(18),
        cost_estimate=cost(2 * tall * wide * columns, 2 * tall * columns * n_batch),
        name="kernel_strip",
    )(*operands)


def dz_kernel(n_batch, n_col, tile, constants, place_ref, own_ref, *refs):
    coef, hinge_coef, inv_coef, inv_share, hinge_share, diag_share, block_share = constants
    strip_refs = refs[:n_col]
    z_refs = refs[n_col : n_col + 2 * n_batch]
    dz_ref, share_ref, strips, full, centred = refs[n_col + 2 * n_batch :]
    local_rows, columns = z_refs[0].shape
    rows = local_rows * n_batch
    own = own_ref[...]
    block = lax.broadcasted_iota(jnp.int32, own.shape, 1) // local_rows
    on_diagonal = functools.reduce(
        jnp.logical_or, [block == i for i, (s, t) in enumerate(upper_blocks(n_batch)) if s == t]
    )
    own = own * own * jnp.where(on_diagonal, 1.0, 2.0)
    own = jnp.sum(jnp.sum(own, axis=0, keepdims=True), axis=1, keepdims=True)
    share_ref[...] = jnp.broadcast_to(block_share * own, share_ref.shape)
    part = 2 * local_rows // n_col
    for k in range(n_col):
        start = pl.multiple_of((place_ref[1] ^ k) * part, part)
        strips[pl.ds(start, part), :] = strip_refs[k][...].astype(f32)
    for v in range(2):
        for i, (s, t) in enumerate(upper_blocks(n_batch)):
            here, there = pl.ds(s * local_rows, local_rows), pl.ds(t * local_rows, local_rows)
            block = strips[pl.ds(v * local_rows, local_rows), pl.ds(i * local_rows, local_rows)]
            full[v, here, there] = block.astype(bf16)
            if s < t:
                full[v, there, here] = jnp.transpose(block).astype(bf16)

    def one_tile(j, carry):
        here = pl.ds(pl.multiple_of(j * tile, tile), tile)
        share = jnp.zeros((1, 1), f32)
        grads = []
        z_views = []
        for v in range(2):
            zf = jnp.concatenate([z[:, here].astype(f32) for z in z_refs[v::2]], axis=0)
            z_views.append(zf)
            zc = zf - jnp.sum(zf, axis=0, keepdims=True) / rows
            std = jnp.sqrt(jnp.sum(zc * zc, axis=0, keepdims=True) / (rows - 1) + eps_std)
            zcb = zc.astype(bf16)
            centred[...] = zcb
            rounded = zcb.astype(f32)
            diag = jnp.sum(rounded * rounded, axis=0, keepdims=True)
            moved = jnp.dot(full[v], centred[...], preferred_element_type=f32)
            pull = jnp.where(std < 1.0, hinge_coef, 0.0) / std
            summed = coef * (moved - rounded * diag) - zc * pull
            grads.append(summed - jnp.sum(summed, axis=0, keepdims=True) / rows)
            share += hinge_share * jnp.sum(jnp.maximum(1.0 - std, 0.0), axis=1, keepdims=True)
            share -= diag_share * jnp.sum(diag * diag, axis=1, keepdims=True)
        diff = z_views[0] - z_views[1]
        share += inv_share * jnp.sum(
            jnp.sum(diff * diff, axis=0, keepdims=True), axis=1, keepdims=True
        )
        share_ref[...] += jnp.broadcast_to(share, share_ref.shape)
        dz_ref[0, :, here] = (grads[0] + inv_coef * diff).astype(bf16)
        dz_ref[1, :, here] = (grads[1] - inv_coef * diff).astype(bf16)
        return carry

    lax.fori_loop(0, columns // tile, one_tile, 0)


def dz_call(place, own, strips, z_slots, constants):
    n_col, n_batch = len(strips), len(z_slots)
    local_rows, columns = z_slots[0][0].shape
    tall = 2 * local_rows
    rows = local_rows * n_batch
    tile = min(256, columns)
    operands = [place, own] + list(strips) + [z for slot in z_slots for z in slot]
    return pl.pallas_call(
        functools.partial(dz_kernel, n_batch, n_col, tile, constants),
        out_shape=(
            jax.ShapeDtypeStruct((2, rows, columns), bf16),
            jax.ShapeDtypeStruct((8, 128), f32),
        ),
        in_specs=[IN_SMEM] + [IN_VMEM] * (len(operands) - 1),
        out_specs=(IN_VMEM, IN_VMEM),
        scratch_shapes=[
            pltpu.VMEM((tall, strips[0].shape[1]), f32),
            pltpu.VMEM((2, rows, rows), bf16),
            pltpu.VMEM((rows, tile), bf16),
        ],
        compiler_params=params(24),
        cost_estimate=cost(4 * rows * rows * columns, 8 * rows * columns),
        name="embedding_gradient",
    )(*operands)


EXTRA = 16


def share_rows(share, width, kind):
    high = share.astype(bf16).astype(f32)
    middle = (share - high).astype(bf16).astype(f32)
    low = share - high - middle
    row = lax.broadcasted_iota(jnp.int32, (EXTRA, width), 0)
    rows = jnp.where(row == 0, high, jnp.where(row == 1, middle, jnp.where(row == 2, low, 0.0)))
    return rows.astype(kind)


def share_of(rows):
    return rows[0:1].astype(f32) + rows[1:2].astype(f32) + rows[2:3].astype(f32)


def d_act_kernel(evens, odds, tall, width, place_ref, dz_ref, share_ref, w_ref, *refs):
    local_rows = tall // 2
    dz = jnp.concatenate([dz_ref[0, :local_rows], dz_ref[1, :local_rows]], axis=0)
    share = share_ref[0:1, 0:1]
    got, outs = (refs[0], refs[1:]) if evens else (None, refs)

    def product(k):
        return lax.dot_general(
            dz,
            weight_rows(place_ref, w_ref, k, width),
            (((1,), (1,)), ((), ())),
            preferred_element_type=f32,
        )

    for j, k in enumerate(evens):
        out = outs[j]
        out[:tall] = (product(k) + got[j, :tall].astype(f32)).astype(out.dtype)
        out[tall:] = share_rows(share + share_of(got[j, tall:])[:, 0:1], width, out.dtype)
    for j, k in enumerate(odds):
        outs[-1][j, :tall] = product(k).astype(bf16)
        outs[-1][j, tall:] = share_rows(share, width, bf16)


def d_act_call(place, dz, share, weight, n_batch, n_col, evens, got, odds):
    width = weight.shape[0] // n_col
    tall = 2 * dz.shape[1] // n_batch
    columns = weight.shape[1]
    long, count = tall + EXTRA, len(evens) + len(odds)
    operands = [place, dz, share, weight] + ([got] if evens else [])
    out_shape = tuple(jax.ShapeDtypeStruct((long, width), bf16 if k else f32) for k in evens)
    if odds:
        out_shape += (jax.ShapeDtypeStruct((len(odds), long, width), bf16),)
    return pl.pallas_call(
        functools.partial(d_act_kernel, tuple(evens), tuple(odds), tall, width),
        out_shape=out_shape,
        in_specs=[IN_SMEM] + [IN_VMEM] * (len(operands) - 1),
        out_specs=(IN_VMEM,) * len(out_shape),
        compiler_params=params(8),
        cost_estimate=cost(2 * tall * width * columns * count, 2 * count * width * tall),
        name="d_act_matmul",
    )(*operands)


def held_place(plane, c, block, n_col, n_batch):
    return (((n_col // n_batch) * plane + 2 * block) ^ (c - (c & 1))) >> 1


def pick_kernel(n_batch, n_col, local_rows, place_ref, *refs):
    half = n_col // 2
    pieces, outs = refs[:half], refs[half:]
    b, c = place_ref[0], place_ref[1]
    position = jnp.where((b & 1) == 0, b >> 1, n_batch - 1 - (b >> 1))
    i = 0
    for block in range(n_col // n_batch // 2):
        for d in range(1, n_batch):
            ahead = position + d
            ahead = jnp.where(ahead >= n_batch, ahead - n_batch, ahead)
            plane = jnp.where(2 * ahead < n_batch, 2 * ahead, 2 * (n_batch - ahead) - 1)
            chosen = held_place(plane, c, block, n_col, n_batch)
            for e in range(half):

                @pl.when(chosen == e)
                def _():
                    outs[i][...] = pieces[e][local_rows:]

            i += 1


def pick_call(place, pieces, n_batch, n_col):
    tall, width = pieces[0].shape
    count = n_col // n_batch // 2 * (n_batch - 1)
    out_shape = (jax.ShapeDtypeStruct((tall // 2, width), bf16),) * count
    return pl.pallas_call(
        functools.partial(pick_kernel, n_batch, n_col, tall // 2),
        out_shape=out_shape,
        in_specs=[IN_SMEM] + [IN_VMEM] * len(pieces),
        out_specs=(IN_VMEM,) * count,
        compiler_params=params(4),
        cost_estimate=cost(0, tall * width * count),
        name="pick_blocks",
    )(place, *pieces)


def weight_grad_kernel(n_batch, aliased, half, tile, which, place_ref, *refs):
    near = [refs[:half], refs[half : 2 * half]]
    blocks_ref, dz_ref = refs[2 * half : 2 * half + 2]
    out_ref, act, product, sems = refs[2 * half + 2 + aliased :]
    block, parity = which
    chosen = held_place(place_ref[0], place_ref[1], block, 2 * half, n_batch)
    out_row = 2 * block + ((place_ref[1] & 1) ^ parity)
    local_rows = near[0][0].shape[0] // 2
    rows = dz_ref.shape[1]
    for e in range(half):

        @pl.when(chosen == e)
        def _():
            act[pl.ds(0, local_rows)] = near[0][e][:local_rows]
            act[pl.ds(rows, local_rows)] = near[0][e][local_rows:]
            act[pl.ds(local_rows, rows - local_rows)] = near[1][e][...]

    act[rows + local_rows :] = blocks_ref[...]
    width = act.shape[1]
    copies = []
    for i in range(width // tile):
        total = None
        for v in range(2):
            part = lax.dot_general(
                act[pl.ds(v * rows, rows), pl.ds(i * tile, tile)],
                dz_ref[v],
                (((0,), (0,)), ((), ())),
                preferred_element_type=f32,
            )
            total = part if total is None else total + part
        product[pl.ds(i * tile, tile)] = total
        start = pl.multiple_of(out_row * width + i * tile, tile)
        copies.append(
            pltpu.make_async_copy(
                product.at[pl.ds(i * tile, tile)], out_ref.at[pl.ds(start, tile)], sems.at[i]
            )
        )
        copies[-1].start()
    for copy in copies:
        copy.wait()


def weight_grad_call(place, which, near, blocks, dz, features, before):
    half = len(near[0])
    width = near[0][0].shape[1]
    _, rows, columns = dz.shape
    tile = min(256, width)
    operands = [place] + [x for group in near for x in group] + [blocks, dz]
    specs = [IN_SMEM] + [IN_VMEM] * (len(operands) - 1)
    aliases = {}
    if before is not None:
        aliases = {len(operands): 0}
        operands.append(before)
        specs.append(ANYWHERE)
    return pl.pallas_call(
        functools.partial(
            weight_grad_kernel,
            rows // (near[0][0].shape[0] // 2),
            int(before is not None),
            half,
            tile,
            which,
        ),
        out_shape=jax.ShapeDtypeStruct((features, columns), f32),
        in_specs=specs,
        out_specs=ANYWHERE,
        scratch_shapes=[
            pltpu.VMEM((2 * rows, width), bf16),
            pltpu.VMEM((width, columns), f32),
            pltpu.SemaphoreType.DMA((width // tile,)),
        ],
        input_output_aliases=aliases,
        compiler_params=params(12),
        cost_estimate=cost(4 * rows * width * columns, 4 * width * columns),
        name="weight_gradient",
    )(*operands)


def link_pieces(x, n_col):
    pieces = {0: x}
    half = x.shape[0] // 2
    for k in sorted(range(2, n_col, 2), key=lambda k: (bin(k).count("1"), k)):
        low, high = k & -k, 1 << (k.bit_length() - 1)
        if low == high:
            pieces[k] = xor_send(x, "col", k)
        else:
            first = xor_send(pieces[k ^ low][:half], "col", low)
            second = xor_send(pieces[k ^ high][half:], "col", high)
            pieces[k] = jnp.concatenate([first, second])
    return pieces


def sibling_pieces(pieces, n_col):
    for k in range(0, n_col, 2):
        if k + 1 not in pieces:
            pieces[k + 1] = xor_send(pieces[k], "col", 1)
    return pieces


def finish_kernel(n_batch, rows, *refs):
    sums, (d_pre, normalised, gain, deviation) = refs[:n_batch], refs[n_batch : n_batch + 4]
    loss_ref, gain_ref, bias_ref, out_ref = refs[n_batch + 4 :]
    both = exchange_sum(x[...] for x in sums)
    bias_ref[...] = both[0:1] + both[1:2]
    gain_ref[...] = both[2:3] + both[3:4]
    loss_ref[...] = both[4:5, 0:128]
    for v in range(2):
        factor = gain[...] * deviation[v : v + 1]
        mean_b, mean_g = both[v : v + 1] / rows, both[2 + v : 3 + v] / rows
        out_ref[v] = factor * (d_pre[v] - mean_b - normalised[v] * mean_g)


def finish_call(sums, d_pre, normalised, gain, deviation, rows):
    _, local_rows, width = d_pre.shape
    operands = list(sums) + [d_pre, normalised, gain[None], deviation[:, 0]]
    out_shape = (
        jax.ShapeDtypeStruct((1, 128), f32),
        jax.ShapeDtypeStruct((1, width), f32),
        jax.ShapeDtypeStruct((1, width), f32),
        jax.ShapeDtypeStruct(d_pre.shape, f32),
    )
    return pl.pallas_call(
        functools.partial(finish_kernel, len(sums), rows),
        out_shape=out_shape,
        in_specs=[IN_VMEM] * len(operands),
        out_specs=(IN_VMEM,) * 4,
        compiler_params=params(4),
        cost_estimate=cost(0, 8 * d_pre.size),
        name="views_gradient",
    )(*operands)


def shards(views, norm_scale_gain, norm_shift_bias, weight):
    n_batch = lax.axis_size("batch")
    n_col = lax.axis_size("col")
    place = jnp.stack([lax.axis_index("batch"), lax.axis_index("col")]).astype(jnp.int32)
    views, norm_scale_gain, norm_shift_bias, weight, place = lax.optimization_barrier(
        (views, norm_scale_gain, norm_shift_bias, weight, place)
    )
    n_view, local_rows, width = views.shape
    features, columns = weight.shape
    E = columns * n_col
    rows = local_rows * n_batch
    tall = n_view * local_rows
    scale = rows * E / 128.0
    denom = float((rows - 1) ** 2 * E)
    evens = list(range(0, n_col, 2))
    odds = [k + 1 for k in evens]
    far = evens[1:]

    with jax.named_scope("weight_load"):
        held_weight, loaded = load_call(weight, (2 * n_view, width))
    with jax.named_scope("norm_stats"):
        hidden = views.astype(f32)
        local_mean = jnp.mean(hidden, axis=1)
        local_centred = hidden - local_mean[:, None, :]
        local_spread = jnp.sum(local_centred * local_centred, axis=1)
        stats = exchange(jnp.concatenate([local_mean, local_spread]), "batch")
        stats[-1] = stats[-1] + loaded
        mean = exchange_sum(s[:n_view] for s in stats) / n_batch
        spread = exchange_sum(
            s[n_view:] + local_rows * jnp.square(s[:n_view] - mean) for s in stats
        )
        var = spread / rows
        inverse_deviation = (1.0 / jnp.sqrt(var + eps_norm))[:, None, :]
        normalised = (hidden - mean[:, None, :]) * inverse_deviation
        preactivation = norm_scale_gain * normalised + norm_shift_bias
        act = jax.nn.gelu(preactivation, approximate=True).astype(bf16)
    with jax.named_scope("act_gather"):
        own = act.reshape(tall, width)
        pieces = {0: own, 1: xor_send(own, "col", 1)}
        for k in far:
            pieces[k] = xor_send(own, "col", k)
        first, pieces[1] = lax.optimization_barrier((act[0], pieces[1]))
        others = [ring_send(first, "batch", d) for d in range(1, n_batch)]
        pieces = sibling_pieces(pieces, n_col)
    with jax.named_scope("z"):

        def z_part(source, ks, before, last=False):
            return z_call(
                place, ks, [source[k] for k in ks], held_weight, before, last, local_rows
            )

        z_own = z_part(pieces, far, z_part(pieces, [0, 1], None))
        z_own, others[-1] = lax.optimization_barrier((z_own, others[-1]))
        z_own0, z_own1 = z_part(pieces, [k + 1 for k in far], z_own, True)
        far_pieces = link_pieces(jnp.concatenate(others), n_col)
    with jax.named_scope("z_ring"):
        z_ring = [z_own1, ring_send(z_own1, "batch", 1)]
        z_ring[1], far_pieces[far[0]] = lax.optimization_barrier((z_ring[1], far_pieces[far[0]]))
        z_ring.append(ring_send(z_ring[1], "batch", 1))
    with jax.named_scope("z_far"):
        start = z_part(far_pieces, [0] + far[:-1], None)
        picked = list(pick_call(place, [pieces[k] for k in evens], n_batch, n_col))
        start, far_pieces[far[-1]], z_ring[2], picked = lax.optimization_barrier(
            (start, far_pieces[far[-1]], z_ring[2], picked)
        )
        far_pieces = sibling_pieces(far_pieces, n_col)
        for _ in range(3, n_batch):
            z_ring.append(ring_send(z_ring[-1], "batch", 1))
        z_far = z_part(far_pieces, odds[:-1] + far[-1:] + odds[-1:], start, True)
        slots = list(zip([z_own0] + list(z_far), z_ring))
    with jax.named_scope("kernel"):
        even_part, odd_part = strip_call(place, slots, n_col)
        blocks = [
            ring_send(x, "batch", 1 + i % (n_batch - 1)) for i, x in enumerate(picked)
        ]
        third = len(blocks) // 3
        odd_part, blocks[:third] = lax.optimization_barrier((odd_part, blocks[:third]))
        even_part = even_part + xor_send(odd_part, "col", 1).astype(f32)
        strip = even_part[0]
        for k in far:
            strip = strip + xor_send(even_part[k // 2].astype(bf16), "col", k).astype(f32)
        strip_b = strip.astype(bf16)
        strips = {0: strip_b}
        for k in far:
            strips[k] = xor_send(strip_b, "col", k)
        strips[far[0]], blocks[third : 2 * third] = lax.optimization_barrier(
            (strips[far[0]], blocks[third : 2 * third])
        )
        strips = sibling_pieces(strips, n_col)
    with jax.named_scope("dz"):
        constants = (
            4.0 * scale / denom,
            25.0 * scale / (2.0 * E * (rows - 1)),
            50.0 * scale / (rows * E),
            25.0 / (rows * E) / n_batch,
            25.0 / (2 * E) / n_batch,
            1.0 / denom / n_batch,
            1.0 / denom / n_batch,
        )
        dz, share = dz_call(place, strip, [strips[k] for k in range(n_col)], slots, constants)
        dz, blocks[2 * third :] = lax.optimization_barrier((dz, blocks[2 * third :]))
    with jax.named_scope("d_act"):
        crossing = [k for k in far if k & (k - 1)]
        others = [k for k in far if k not in crossing] + [0]

        def products(evens, got, odds):
            return d_act_call(place, dz, share, held_weight, n_batch, n_col, evens, got, odds)

        (away,) = products([], None, [k + 1 for k in crossing])
        *crossed, away = products(crossing, xor_send(away, "col", 1), [k + 1 for k in others])
        summed = products(others, xor_send(away, "col", 1), [])
        arrived = {
            k: xor_send(piece, "col", k) if k else piece
            for k, piece in zip(crossing + others, list(crossed) + list(summed))
        }
        d_act = arrived.pop(0)
        arrived = [arrived[k] for k in far]
    with jax.named_scope("grad_weight"):
        grad_weight = None
        for block in range(n_col // n_batch // 2):
            mine = jnp.concatenate(blocks[block * (n_batch - 1) : (block + 1) * (n_batch - 1)])
            other = xor_send(mine, "col", 1)
            for parity, ks, far_rows in ((0, evens, mine), (1, odds, other)):
                grad_weight = weight_grad_call(
                    place,
                    (block, parity),
                    [[group[k] for k in ks] for group in (pieces, far_pieces)],
                    far_rows,
                    dz,
                    features // n_batch,
                    grad_weight,
                )
    with jax.named_scope("norm_backward"):
        arrived, grad_weight = lax.optimization_barrier((arrived, grad_weight))
        share = exchange_sum(share_of(part[tall:]) for part in [d_act] + arrived)
        d_act = d_act[:tall]
        for part in arrived:
            d_act = d_act + part[:tall].astype(f32)
        d_pre = d_act.reshape(n_view, local_rows, width) * gelu_slope(preactivation)
        sums = jnp.concatenate(
            [
                jnp.sum(d_pre, axis=1),
                jnp.sum(d_pre * normalised, axis=1),
                jnp.broadcast_to(share, (2 * n_view, width)),
            ]
        )
        k = 1
        while 2 * k < n_batch:
            sums = sums + xor_send(sums, "batch", k)
            k *= 2
        sums = [sums, xor_send(sums, "batch", k)]
        loss, grad_gain, grad_bias, views_gradient = finish_call(
            sums, d_pre, normalised, norm_scale_gain, inverse_deviation, rows
        )
    return (loss[0, 0], grad_weight, grad_gain[0], grad_bias[0], views_gradient)


def solution(mesh):
    placed = (P(None, "batch", "col"), P("col"), P("col"), P(None, "col"))
    return jax.shard_map(
        shards,
        mesh=mesh,
        in_specs=placed,
        out_specs=(P(), P("batch", "col"), P("col"), P("col"), P(None, "batch", "col")),
        check_vma=False,
    )
```

```python
import functools

import jax
import jax.numpy as jnp
from jax import lax
from jax.experimental import pallas as pl
from jax.experimental.pallas import tpu as pltpu
from jax.sharding import PartitionSpec as P

eps_norm = 1e-05
eps_std = 0.0001
f32 = jnp.float32
bf16 = jnp.bfloat16
MIB = 1024 * 1024


def gelu_slope(preactivation):
    value, pullback = jax.vjp(lambda t: jax.nn.gelu(t, approximate=True), preactivation)
    return pullback(jnp.ones_like(value))[0]


def xor_send(x, axis, k):
    n = lax.axis_size(axis)
    return lax.ppermute(x, axis, [(i, i ^ k) for i in range(n)])


def ring_order(n):
    return list(range(0, n, 2)) + list(range(1, n, 2))[::-1]


def ring_send(x, axis, d):
    order = ring_order(lax.axis_size(axis))
    n = len(order)
    return lax.ppermute(x, axis, [(order[i], order[(i + d) % n]) for i in range(n)])


def exchange_sum(parts):
    parts = list(parts)
    while len(parts) > 1:
        parts = [x + y for x, y in zip(parts[::2], parts[1::2])]
    return parts[0]


def exchange(x, axis):
    return [x] + [xor_send(x, axis, k) for k in range(1, lax.axis_size(axis))]


def params(limit):
    return pltpu.CompilerParams(vmem_limit_bytes=limit * MIB)


def cost(flops, moved):
    return pl.CostEstimate(flops=flops, bytes_accessed=moved, transcendentals=0)


IN_SMEM = pl.BlockSpec(memory_space=pltpu.SMEM)
IN_VMEM = pl.BlockSpec(memory_space=pltpu.VMEM)
ANYWHERE = pl.BlockSpec(memory_space=pl.ANY)
LOADS = 8


def load_kernel(w_ref, out_ref, flag_ref, sems):
    flag_ref[...] = jnp.zeros_like(flag_ref)
    step = w_ref.shape[0] // LOADS
    copies = [
        pltpu.make_async_copy(
            w_ref.at[pl.ds(i * step, step)], out_ref.at[pl.ds(i * step, step)], sems.at[i]
        )
        for i in range(LOADS)
    ]
    for copy in copies:
        copy.start()
    for copy in copies:
        copy.wait()


def load_call(weight, flag_shape):
    return pl.pallas_call(
        load_kernel,
        out_shape=(
            pltpu.VMEM(weight.shape, weight.dtype),
            jax.ShapeDtypeStruct(flag_shape, f32),
        ),
        in_specs=[ANYWHERE],
        out_specs=(IN_VMEM, IN_VMEM),
        scratch_shapes=[pltpu.SemaphoreType.DMA((LOADS,))],
        compiler_params=params(4),
        cost_estimate=cost(0, 4 * weight.size),
        name="weight_load",
    )(pltpu.with_memory_space_constraint(weight, pltpu.HBM))


def stats_kernel(views_ref, out_ref):
    n_view, local_rows, _ = views_ref.shape
    for v in range(n_view):
        x = views_ref[v].astype(f32)
        mean = jnp.sum(x, axis=0, keepdims=True) / local_rows
        centred = x - mean
        out_ref[v : v + 1] = mean
        out_ref[n_view + v : n_view + v + 1] = jnp.sum(centred * centred, axis=0, keepdims=True)


def stats_call(views):
    n_view, _, width = views.shape
    return pl.pallas_call(
        stats_kernel,
        out_shape=jax.ShapeDtypeStruct((2 * n_view, width), f32),
        in_specs=[IN_VMEM],
        out_specs=IN_VMEM,
        compiler_params=params(4),
        cost_estimate=cost(0, 2 * views.size),
        name="norm_statistics",
    )(views)


def weight_rows(place_ref, w_ref, k, width):
    return w_ref[pl.ds(pl.multiple_of((place_ref[1] ^ k) * width, width), width), :]


def z_kernel(ks, first, last, local_rows, place_ref, *refs):
    count = len(ks)
    pieces, rest = refs[:count], list(refs[count:])
    w_ref = rest.pop(0)
    total = None if first else rest.pop(0)[...]
    width = pieces[0].shape[1]
    for j in range(count):
        part = jnp.dot(
            pieces[j][...], weight_rows(place_ref, w_ref, ks[j], width), preferred_element_type=f32
        )
        total = part if total is None else total + part
    if not last:
        rest[0][...] = total
        return
    z = total.astype(bf16)
    for v, ref in enumerate(rest):
        ref[...] = z[v * local_rows : (v + 1) * local_rows]


def z_call(place, ks, pieces, weight, before, last, local_rows):
    count = len(ks)
    tall, width = pieces[0].shape
    columns = weight.shape[1]
    operands = [place] + list(pieces) + [weight] + ([] if before is None else [before])
    if last:
        groups = tall // local_rows
        out_shape = (jax.ShapeDtypeStruct((local_rows, columns), bf16),) * groups
    else:
        out_shape = jax.ShapeDtypeStruct((tall, columns), f32)
    return pl.pallas_call(
        functools.partial(z_kernel, tuple(ks), before is None, last, local_rows),
        out_shape=out_shape,
        in_specs=[IN_SMEM] + [IN_VMEM] * (len(operands) - 1),
        out_specs=jax.tree.map(lambda _: IN_VMEM, out_shape),
        compiler_params=params(8),
        cost_estimate=cost(2 * tall * width * columns * count, 2 * tall * columns),
        name="z_matmul",
    )(*operands)


def upper_blocks(n):
    return [(s, t) for s in range(n) for t in range(s, n)]


def strip_kernel(n_batch, n_col, place_ref, *refs):
    z_refs, (even_ref, odd_ref, strip) = refs[: 2 * n_batch], refs[2 * n_batch :]
    local_rows = z_refs[0].shape[0]
    rows = local_rows * n_batch
    for v in range(2):
        zf = [z[...].astype(f32) for z in z_refs[v::2]]
        mean = sum(jnp.sum(z, axis=0, keepdims=True) for z in zf) / rows
        rounded = jnp.concatenate([(z - mean).astype(bf16) for z in zf], axis=0)
        at = 0
        for s in range(n_batch):
            product = lax.dot_general(
                rounded[s * local_rows : (s + 1) * local_rows],
                rounded[s * local_rows :],
                (((1,), (1,)), ((), ())),
                preferred_element_type=f32,
            )
            strip[pl.ds(v * local_rows, local_rows), pl.ds(at, product.shape[1])] = product
            at += product.shape[1]
    part = 2 * local_rows // n_col
    for k in range(n_col):
        start = pl.multiple_of((place_ref[1] ^ k) * part, part)
        ref = odd_ref if k % 2 else even_ref
        ref[k // 2] = strip[pl.ds(start, part), :].astype(ref.dtype)


def strip_call(place, z_slots, n_col):
    n_batch = len(z_slots)
    local_rows, columns = z_slots[0][0].shape
    tall = 2 * local_rows
    wide = len(upper_blocks(n_batch)) * local_rows
    shape = (n_col // 2, tall // n_col, wide)
    operands = [place] + [z for slot in z_slots for z in slot]
    return pl.pallas_call(
        functools.partial(strip_kernel, n_batch, n_col),
        out_shape=(jax.ShapeDtypeStruct(shape, f32), jax.ShapeDtypeStruct(shape, bf16)),
        in_specs=[IN_SMEM] + [IN_VMEM] * (len(operands) - 1),
        out_specs=(IN_VMEM, IN_VMEM),
        scratch_shapes=[pltpu.VMEM((tall, wide), f32)],
        compiler_params=params(18),
        cost_estimate=cost(2 * tall * wide * columns, 2 * tall * columns * n_batch),
        name="kernel_strip",
    )(*operands)


def dz_kernel(n_batch, n_col, tile, constants, place_ref, own_ref, *refs):
    coef, hinge_coef, inv_coef, inv_share, hinge_share, diag_share, block_share = constants
    strip_refs = refs[:n_col]
    z_refs = refs[n_col : n_col + 2 * n_batch]
    dz_ref, share_ref, strips, full, centred = refs[n_col + 2 * n_batch :]
    local_rows, columns = z_refs[0].shape
    rows = local_rows * n_batch
    own = own_ref[...]
    block = lax.broadcasted_iota(jnp.int32, own.shape, 1) // local_rows
    on_diagonal = functools.reduce(
        jnp.logical_or, [block == i for i, (s, t) in enumerate(upper_blocks(n_batch)) if s == t]
    )
    own = own * own * jnp.where(on_diagonal, 1.0, 2.0)
    own = jnp.sum(jnp.sum(own, axis=0, keepdims=True), axis=1, keepdims=True)
    share_ref[...] = jnp.broadcast_to(block_share * own, share_ref.shape)
    part = 2 * local_rows // n_col
    for k in range(n_col):
        start = pl.multiple_of((place_ref[1] ^ k) * part, part)
        strips[pl.ds(start, part), :] = strip_refs[k][...].astype(f32)
    for v in range(2):
        for i, (s, t) in enumerate(upper_blocks(n_batch)):
            here, there = pl.ds(s * local_rows, local_rows), pl.ds(t * local_rows, local_rows)
            block = strips[pl.ds(v * local_rows, local_rows), pl.ds(i * local_rows, local_rows)]
            full[v, here, there] = block.astype(bf16)
            if s < t:
                full[v, there, here] = jnp.transpose(block).astype(bf16)

    for j in range(columns // tile):
        here = pl.ds(j * tile, tile)
        share = jnp.zeros((1, 1), f32)
        grads = []
        z_views = []
        for v in range(2):
            zf = jnp.concatenate([z[:, here].astype(f32) for z in z_refs[v::2]], axis=0)
            z_views.append(zf)
            zc = zf - jnp.sum(zf, axis=0, keepdims=True) / rows
            std = jnp.sqrt(jnp.sum(zc * zc, axis=0, keepdims=True) / (rows - 1) + eps_std)
            zcb = zc.astype(bf16)
            centred[2 * j + v] = zcb
            rounded = zcb.astype(f32)
            diag = jnp.sum(rounded * rounded, axis=0, keepdims=True)
            moved = jnp.dot(full[v], centred[2 * j + v], preferred_element_type=f32)
            pull = jnp.where(std < 1.0, hinge_coef, 0.0) / std
            summed = coef * (moved - rounded * diag) - zc * pull
            grads.append(summed - jnp.sum(summed, axis=0, keepdims=True) / rows)
            share += hinge_share * jnp.sum(jnp.maximum(1.0 - std, 0.0), axis=1, keepdims=True)
            share -= diag_share * jnp.sum(diag * diag, axis=1, keepdims=True)
        diff = z_views[0] - z_views[1]
        share += inv_share * jnp.sum(
            jnp.sum(diff * diff, axis=0, keepdims=True), axis=1, keepdims=True
        )
        share_ref[...] += jnp.broadcast_to(share, share_ref.shape)
        dz_ref[0, :, here] = (grads[0] + inv_coef * diff).astype(bf16)
        dz_ref[1, :, here] = (grads[1] - inv_coef * diff).astype(bf16)


def dz_call(place, own, strips, z_slots, constants):
    n_col, n_batch = len(strips), len(z_slots)
    local_rows, columns = z_slots[0][0].shape
    tall = 2 * local_rows
    rows = local_rows * n_batch
    tile = min(256, columns)
    operands = [place, own] + list(strips) + [z for slot in z_slots for z in slot]
    return pl.pallas_call(
        functools.partial(dz_kernel, n_batch, n_col, tile, constants),
        out_shape=(
            jax.ShapeDtypeStruct((2, rows, columns), bf16),
            jax.ShapeDtypeStruct((8, 128), f32),
        ),
        in_specs=[IN_SMEM] + [IN_VMEM] * (len(operands) - 1),
        out_specs=(IN_VMEM, IN_VMEM),
        scratch_shapes=[
            pltpu.VMEM((tall, strips[0].shape[1]), f32),
            pltpu.VMEM((2, rows, rows), bf16),
            pltpu.VMEM((2 * columns // tile, rows, tile), bf16),
        ],
        compiler_params=params(28),
        cost_estimate=cost(4 * rows * rows * columns, 8 * rows * columns),
        name="embedding_gradient",
    )(*operands)


EXTRA = 16


def share_rows(share, width, kind):
    high = share.astype(bf16).astype(f32)
    middle = (share - high).astype(bf16).astype(f32)
    low = share - high - middle
    row = lax.broadcasted_iota(jnp.int32, (EXTRA, width), 0)
    rows = jnp.where(row == 0, high, jnp.where(row == 1, middle, jnp.where(row == 2, low, 0.0)))
    return rows.astype(kind)


def share_of(rows):
    return rows[0:1].astype(f32) + rows[1:2].astype(f32) + rows[2:3].astype(f32)


def d_act_kernel(evens, odds, tall, width, place_ref, dz_ref, share_ref, w_ref, *refs):
    local_rows = tall // 2
    dz = jnp.concatenate([dz_ref[0, :local_rows], dz_ref[1, :local_rows]], axis=0)
    share = share_ref[0:1, 0:1]
    got, outs = (refs[0], refs[1:]) if evens else (None, refs)

    def product(k):
        return lax.dot_general(
            dz,
            weight_rows(place_ref, w_ref, k, width),
            (((1,), (1,)), ((), ())),
            preferred_element_type=f32,
        )

    for j, k in enumerate(evens):
        out = outs[j]
        out[:tall] = (product(k) + got[j, :tall].astype(f32)).astype(out.dtype)
        out[tall:] = share_rows(share + share_of(got[j, tall:])[:, 0:1], width, out.dtype)
    for j, k in enumerate(odds):
        outs[-1][j, :tall] = product(k).astype(bf16)
        outs[-1][j, tall:] = share_rows(share, width, bf16)


def d_act_call(place, dz, share, weight, n_batch, n_col, evens, got, odds):
    width = weight.shape[0] // n_col
    tall = 2 * dz.shape[1] // n_batch
    columns = weight.shape[1]
    long, count = tall + EXTRA, len(evens) + len(odds)
    operands = [place, dz, share, weight] + ([got] if evens else [])
    out_shape = tuple(jax.ShapeDtypeStruct((long, width), bf16 if k else f32) for k in evens)
    if odds:
        out_shape += (jax.ShapeDtypeStruct((len(odds), long, width), bf16),)
    return pl.pallas_call(
        functools.partial(d_act_kernel, tuple(evens), tuple(odds), tall, width),
        out_shape=out_shape,
        in_specs=[IN_SMEM] + [IN_VMEM] * (len(operands) - 1),
        out_specs=(IN_VMEM,) * len(out_shape),
        compiler_params=params(8),
        cost_estimate=cost(2 * tall * width * columns * count, 2 * count * width * tall),
        name="d_act_matmul",
    )(*operands)


def held_place(plane, c, block, n_col, n_batch):
    return (((n_col // n_batch) * plane + 2 * block) ^ (c - (c & 1))) >> 1


def pick_kernel(n_batch, n_col, local_rows, place_ref, *refs):
    half = n_col // 2
    pieces, outs = refs[:half], refs[half:]
    b, c = place_ref[0], place_ref[1]
    position = jnp.where((b & 1) == 0, b >> 1, n_batch - 1 - (b >> 1))
    i = 0
    for block in range(n_col // n_batch // 2):
        for d in range(1, n_batch):
            ahead = position + d
            ahead = jnp.where(ahead >= n_batch, ahead - n_batch, ahead)
            plane = jnp.where(2 * ahead < n_batch, 2 * ahead, 2 * (n_batch - ahead) - 1)
            chosen = held_place(plane, c, block, n_col, n_batch)
            for e in range(half):

                @pl.when(chosen == e)
                def _():
                    outs[i][...] = pieces[e][local_rows:]

            i += 1


def pick_call(place, pieces, n_batch, n_col):
    tall, width = pieces[0].shape
    count = n_col // n_batch // 2 * (n_batch - 1)
    out_shape = (jax.ShapeDtypeStruct((tall // 2, width), bf16),) * count
    return pl.pallas_call(
        functools.partial(pick_kernel, n_batch, n_col, tall // 2),
        out_shape=out_shape,
        in_specs=[IN_SMEM] + [IN_VMEM] * len(pieces),
        out_specs=(IN_VMEM,) * count,
        compiler_params=params(4),
        cost_estimate=cost(0, tall * width * count),
        name="pick_blocks",
    )(place, *pieces)


def weight_grad_kernel(n_batch, aliased, half, tile, which, place_ref, *refs):
    near = [refs[:half], refs[half : 2 * half]]
    blocks_ref, dz_ref = refs[2 * half : 2 * half + 2]
    out_ref, act, product, sems = refs[2 * half + 2 + aliased :]
    block, parity = which
    chosen = held_place(place_ref[0], place_ref[1], block, 2 * half, n_batch)
    out_row = 2 * block + ((place_ref[1] & 1) ^ parity)
    local_rows = near[0][0].shape[0] // 2
    rows = dz_ref.shape[1]
    for e in range(half):

        @pl.when(chosen == e)
        def _():
            act[pl.ds(0, local_rows)] = near[0][e][:local_rows]
            act[pl.ds(rows, local_rows)] = near[0][e][local_rows:]
            act[pl.ds(local_rows, rows - local_rows)] = near[1][e][...]

    act[rows + local_rows :] = blocks_ref[...]
    width = act.shape[1]
    copies = []
    for i in range(width // tile):
        total = None
        for v in range(2):
            part = lax.dot_general(
                act[pl.ds(v * rows, rows), pl.ds(i * tile, tile)],
                dz_ref[v],
                (((0,), (0,)), ((), ())),
                preferred_element_type=f32,
            )
            total = part if total is None else total + part
        product[pl.ds(i * tile, tile)] = total
        start = pl.multiple_of(out_row * width + i * tile, tile)
        copies.append(
            pltpu.make_async_copy(
                product.at[pl.ds(i * tile, tile)], out_ref.at[pl.ds(start, tile)], sems.at[i]
            )
        )
        copies[-1].start()
    for copy in copies:
        copy.wait()


def weight_grad_call(place, which, near, blocks, dz, features, before):
    half = len(near[0])
    width = near[0][0].shape[1]
    _, rows, columns = dz.shape
    tile = min(256, width)
    operands = [place] + [x for group in near for x in group] + [blocks, dz]
    specs = [IN_SMEM] + [IN_VMEM] * (len(operands) - 1)
    aliases = {}
    if before is not None:
        aliases = {len(operands): 0}
        operands.append(before)
        specs.append(ANYWHERE)
    return pl.pallas_call(
        functools.partial(
            weight_grad_kernel,
            rows // (near[0][0].shape[0] // 2),
            int(before is not None),
            half,
            tile,
            which,
        ),
        out_shape=jax.ShapeDtypeStruct((features, columns), f32),
        in_specs=specs,
        out_specs=ANYWHERE,
        scratch_shapes=[
            pltpu.VMEM((2 * rows, width), bf16),
            pltpu.VMEM((width, columns), f32),
            pltpu.SemaphoreType.DMA((width // tile,)),
        ],
        input_output_aliases=aliases,
        compiler_params=params(12),
        cost_estimate=cost(4 * rows * width * columns, 4 * width * columns),
        name="weight_gradient",
    )(*operands)


def link_pieces(x, n_col):
    pieces = {0: x}
    half = x.shape[0] // 2
    for k in sorted(range(2, n_col, 2), key=lambda k: (bin(k).count("1"), k)):
        low, high = k & -k, 1 << (k.bit_length() - 1)
        if low == high:
            pieces[k] = xor_send(x, "col", k)
        else:
            first = xor_send(pieces[k ^ low][:half], "col", low)
            second = xor_send(pieces[k ^ high][half:], "col", high)
            pieces[k] = jnp.concatenate([first, second])
    return pieces


def sibling_pieces(pieces, n_col):
    for k in range(0, n_col, 2):
        if k + 1 not in pieces:
            pieces[k + 1] = xor_send(pieces[k], "col", 1)
    return pieces


def finish_kernel(n_batch, rows, *refs):
    sums, (d_pre, normalised, gain, deviation) = refs[:n_batch], refs[n_batch : n_batch + 4]
    loss_ref, gain_ref, bias_ref, out_ref = refs[n_batch + 4 :]
    both = exchange_sum(x[...] for x in sums)
    bias_ref[...] = both[0:1] + both[1:2]
    gain_ref[...] = both[2:3] + both[3:4]
    loss_ref[...] = both[4:5, 0:128]
    for v in range(2):
        factor = gain[...] * deviation[v : v + 1]
        mean_b, mean_g = both[v : v + 1] / rows, both[2 + v : 3 + v] / rows
        out_ref[v] = factor * (d_pre[v] - mean_b - normalised[v] * mean_g)


def finish_call(sums, d_pre, normalised, gain, deviation, rows):
    _, local_rows, width = d_pre.shape
    operands = list(sums) + [d_pre, normalised, gain[None], deviation[:, 0]]
    out_shape = (
        jax.ShapeDtypeStruct((1, 128), f32),
        jax.ShapeDtypeStruct((1, width), f32),
        jax.ShapeDtypeStruct((1, width), f32),
        jax.ShapeDtypeStruct(d_pre.shape, f32),
    )
    return pl.pallas_call(
        functools.partial(finish_kernel, len(sums), rows),
        out_shape=out_shape,
        in_specs=[IN_VMEM] * len(operands),
        out_specs=(IN_VMEM,) * 4,
        compiler_params=params(4),
        cost_estimate=cost(0, 8 * d_pre.size),
        name="views_gradient",
    )(*operands)


def shards(views, norm_scale_gain, norm_shift_bias, weight):
    n_batch = lax.axis_size("batch")
    n_col = lax.axis_size("col")
    place = jnp.stack([lax.axis_index("batch"), lax.axis_index("col")]).astype(jnp.int32)
    views, norm_scale_gain, norm_shift_bias, weight, place = lax.optimization_barrier(
        (views, norm_scale_gain, norm_shift_bias, weight, place)
    )
    n_view, local_rows, width = views.shape
    features, columns = weight.shape
    E = columns * n_col
    rows = local_rows * n_batch
    tall = n_view * local_rows
    scale = rows * E / 128.0
    denom = float((rows - 1) ** 2 * E)
    evens = list(range(0, n_col, 2))
    odds = [k + 1 for k in evens]
    far = evens[1:]

    with jax.named_scope("weight_load"):
        held_weight, loaded = load_call(weight, (2 * n_view, width))
    with jax.named_scope("norm_stats"):
        hidden = views.astype(f32)
        stats = exchange(stats_call(views), "batch")
        stats[-1] = stats[-1] + loaded
        mean = exchange_sum(s[:n_view] for s in stats) / n_batch
        spread = exchange_sum(
            s[n_view:] + local_rows * jnp.square(s[:n_view] - mean) for s in stats
        )
        var = spread / rows
        inverse_deviation = (1.0 / jnp.sqrt(var + eps_norm))[:, None, :]
        normalised = (hidden - mean[:, None, :]) * inverse_deviation
        preactivation = norm_scale_gain * normalised + norm_shift_bias
        act = jax.nn.gelu(preactivation, approximate=True).astype(bf16)
    with jax.named_scope("act_gather"):
        own = act.reshape(tall, width)
        pieces = {0: own, 1: xor_send(own, "col", 1)}
        for k in far:
            pieces[k] = xor_send(own, "col", k)
        first, pieces[1] = lax.optimization_barrier((act[0], pieces[1]))
        others = [ring_send(first, "batch", d) for d in range(1, n_batch)]
        pieces = sibling_pieces(pieces, n_col)
    with jax.named_scope("z"):

        def z_part(source, ks, before, last=False):
            return z_call(
                place, ks, [source[k] for k in ks], held_weight, before, last, local_rows
            )

        z_own = z_part(pieces, far, z_part(pieces, [0, 1], None))
        z_own, others[-1] = lax.optimization_barrier((z_own, others[-1]))
        z_own0, z_own1 = z_part(pieces, [k + 1 for k in far], z_own, True)
        far_pieces = link_pieces(jnp.concatenate(others), n_col)
    with jax.named_scope("z_ring"):
        z_ring = [z_own1, ring_send(z_own1, "batch", 1)]
        z_ring[1], far_pieces[far[0]] = lax.optimization_barrier((z_ring[1], far_pieces[far[0]]))
        z_ring.append(ring_send(z_ring[1], "batch", 1))
    with jax.named_scope("z_far"):
        start = z_part(far_pieces, [0] + far[:-1], None)
        picked = list(pick_call(place, [pieces[k] for k in evens], n_batch, n_col))
        start, far_pieces[far[-1]], z_ring[2], picked = lax.optimization_barrier(
            (start, far_pieces[far[-1]], z_ring[2], picked)
        )
        far_pieces = sibling_pieces(far_pieces, n_col)
        for _ in range(3, n_batch):
            z_ring.append(ring_send(z_ring[-1], "batch", 1))
        z_far = z_part(far_pieces, odds[:-1] + far[-1:] + odds[-1:], start, True)
        slots = list(zip([z_own0] + list(z_far), z_ring))
    with jax.named_scope("kernel"):
        even_part, odd_part = strip_call(place, slots, n_col)
        blocks = [
            ring_send(x, "batch", 1 + i % (n_batch - 1)) for i, x in enumerate(picked)
        ]
        third = len(blocks) // 3
        odd_part, blocks[:third] = lax.optimization_barrier((odd_part, blocks[:third]))
        even_part = even_part + xor_send(odd_part, "col", 1).astype(f32)
        strip = even_part[0]
        for k in far:
            strip = strip + xor_send(even_part[k // 2].astype(bf16), "col", k).astype(f32)
        strip_b = strip.astype(bf16)
        strips = {0: strip_b}
        for k in far:
            strips[k] = xor_send(strip_b, "col", k)
        strips[far[0]], blocks[third : 2 * third] = lax.optimization_barrier(
            (strips[far[0]], blocks[third : 2 * third])
        )
        strips = sibling_pieces(strips, n_col)
    with jax.named_scope("dz"):
        constants = (
            4.0 * scale / denom,
            25.0 * scale / (2.0 * E * (rows - 1)),
            50.0 * scale / (rows * E),
            25.0 / (rows * E) / n_batch,
            25.0 / (2 * E) / n_batch,
            1.0 / denom / n_batch,
            1.0 / denom / n_batch,
        )
        dz, share = dz_call(place, strip, [strips[k] for k in range(n_col)], slots, constants)
        dz, blocks[2 * third :] = lax.optimization_barrier((dz, blocks[2 * third :]))
    with jax.named_scope("d_act"):
        crossing = [k for k in far if k & (k - 1)]
        others = [k for k in far if k not in crossing] + [0]

        def products(evens, got, odds):
            return d_act_call(place, dz, share, held_weight, n_batch, n_col, evens, got, odds)

        (away,) = products([], None, [k + 1 for k in crossing])
        *crossed, away = products(crossing, xor_send(away, "col", 1), [k + 1 for k in others])
        summed = products(others, xor_send(away, "col", 1), [])
        arrived = {
            k: xor_send(piece, "col", k) if k else piece
            for k, piece in zip(crossing + others, list(crossed) + list(summed))
        }
        d_act = arrived.pop(0)
        arrived = [arrived[k] for k in far]
    with jax.named_scope("grad_weight"):
        grad_weight = None
        for block in range(n_col // n_batch // 2):
            mine = jnp.concatenate(blocks[block * (n_batch - 1) : (block + 1) * (n_batch - 1)])
            other = xor_send(mine, "col", 1)
            for parity, ks, far_rows in ((0, evens, mine), (1, odds, other)):
                grad_weight = weight_grad_call(
                    place,
                    (block, parity),
                    [[group[k] for k in ks] for group in (pieces, far_pieces)],
                    far_rows,
                    dz,
                    features // n_batch,
                    grad_weight,
                )
    with jax.named_scope("norm_backward"):
        arrived, grad_weight = lax.optimization_barrier((arrived, grad_weight))
        share = exchange_sum(share_of(part[tall:]) for part in [d_act] + arrived)
        d_act = d_act[:tall]
        for part in arrived:
            d_act = d_act + part[:tall].astype(f32)
        d_pre = d_act.reshape(n_view, local_rows, width) * gelu_slope(preactivation)
        sums = jnp.concatenate(
            [
                jnp.sum(d_pre, axis=1),
                jnp.sum(d_pre * normalised, axis=1),
                jnp.broadcast_to(share, (2 * n_view, width)),
            ]
        )
        loss, grad_gain, grad_bias, views_gradient = finish_call(
            exchange(sums, "batch"), d_pre, normalised, norm_scale_gain, inverse_deviation, rows
        )
    return (loss[0, 0], grad_weight, grad_gain[0], grad_bias[0], views_gradient)


def solution(mesh):
    placed = (P(None, "batch", "col"), P("col"), P("col"), P(None, "col"))
    return jax.shard_map(
        shards,
        mesh=mesh,
        in_specs=placed,
        out_specs=(P(), P("batch", "col"), P("col"), P("col"), P(None, "batch", "col")),
        check_vma=False,
    )
```

```python
import functools

import jax
import jax.numpy as jnp
from jax import lax
from jax.experimental import pallas as pl
from jax.experimental.pallas import tpu as pltpu
from jax.sharding import PartitionSpec as P

eps_norm = 1e-05
eps_std = 0.0001
f32 = jnp.float32
bf16 = jnp.bfloat16
MIB = 1024 * 1024


def gelu_slope(preactivation):
    value, pullback = jax.vjp(lambda t: jax.nn.gelu(t, approximate=True), preactivation)
    return pullback(jnp.ones_like(value))[0]


def xor_send(x, axis, k):
    n = lax.axis_size(axis)
    return lax.ppermute(x, axis, [(i, i ^ k) for i in range(n)])


def ring_order(n):
    return list(range(0, n, 2)) + list(range(1, n, 2))[::-1]


def ring_send(x, axis, d):
    order = ring_order(lax.axis_size(axis))
    n = len(order)
    return lax.ppermute(x, axis, [(order[i], order[(i + d) % n]) for i in range(n)])


def exchange_sum(parts):
    parts = list(parts)
    while len(parts) > 1:
        parts = [x + y for x, y in zip(parts[::2], parts[1::2])]
    return parts[0]


def exchange(x, axis):
    return [x] + [xor_send(x, axis, k) for k in range(1, lax.axis_size(axis))]


def params(limit):
    return pltpu.CompilerParams(vmem_limit_bytes=limit * MIB)


def cost(flops, moved):
    return pl.CostEstimate(flops=flops, bytes_accessed=moved, transcendentals=0)


IN_SMEM = pl.BlockSpec(memory_space=pltpu.SMEM)
IN_VMEM = pl.BlockSpec(memory_space=pltpu.VMEM)
ANYWHERE = pl.BlockSpec(memory_space=pl.ANY)
LOADS = 8


def load_kernel(w_ref, out_ref, flag_ref, sems):
    flag_ref[...] = jnp.zeros_like(flag_ref)
    step = w_ref.shape[0] // LOADS
    copies = [
        pltpu.make_async_copy(
            w_ref.at[pl.ds(i * step, step)], out_ref.at[pl.ds(i * step, step)], sems.at[i]
        )
        for i in range(LOADS)
    ]
    for copy in copies:
        copy.start()
    for copy in copies:
        copy.wait()


def load_call(weight, flag_shape):
    return pl.pallas_call(
        load_kernel,
        out_shape=(
            pltpu.VMEM(weight.shape, weight.dtype),
            jax.ShapeDtypeStruct(flag_shape, f32),
        ),
        in_specs=[ANYWHERE],
        out_specs=(IN_VMEM, IN_VMEM),
        scratch_shapes=[pltpu.SemaphoreType.DMA((LOADS,))],
        compiler_params=params(4),
        cost_estimate=cost(0, 4 * weight.size),
        name="weight_load",
    )(pltpu.with_memory_space_constraint(weight, pltpu.HBM))


def stats_kernel(views_ref, out_ref):
    n_view, local_rows, _ = views_ref.shape
    for v in range(n_view):
        x = views_ref[v].astype(f32)
        mean = jnp.sum(x, axis=0, keepdims=True) / local_rows
        centred = x - mean
        out_ref[v : v + 1] = mean
        out_ref[n_view + v : n_view + v + 1] = jnp.sum(centred * centred, axis=0, keepdims=True)


def stats_call(views):
    n_view, _, width = views.shape
    return pl.pallas_call(
        stats_kernel,
        out_shape=jax.ShapeDtypeStruct((2 * n_view, width), f32),
        in_specs=[IN_VMEM],
        out_specs=IN_VMEM,
        compiler_params=params(4),
        cost_estimate=cost(0, 2 * views.size),
        name="norm_statistics",
    )(views)


def weight_rows(place_ref, w_ref, k, width):
    return w_ref[pl.ds(pl.multiple_of((place_ref[1] ^ k) * width, width), width), :]


def z_kernel(ks, first, last, local_rows, place_ref, *refs):
    count = len(ks)
    pieces, rest = refs[:count], list(refs[count:])
    w_ref = rest.pop(0)
    total = None if first else rest.pop(0)[...]
    width = pieces[0].shape[1]
    for j in range(count):
        part = jnp.dot(
            pieces[j][...], weight_rows(place_ref, w_ref, ks[j], width), preferred_element_type=f32
        )
        total = part if total is None else total + part
    if not last:
        rest[0][...] = total
        return
    z = total.astype(bf16)
    for v, ref in enumerate(rest):
        ref[...] = z[v * local_rows : (v + 1) * local_rows]


def z_call(place, ks, pieces, weight, before, last, local_rows):
    count = len(ks)
    tall, width = pieces[0].shape
    columns = weight.shape[1]
    operands = [place] + list(pieces) + [weight] + ([] if before is None else [before])
    if last:
        groups = tall // local_rows
        out_shape = (jax.ShapeDtypeStruct((local_rows, columns), bf16),) * groups
    else:
        out_shape = jax.ShapeDtypeStruct((tall, columns), f32)
    return pl.pallas_call(
        functools.partial(z_kernel, tuple(ks), before is None, last, local_rows),
        out_shape=out_shape,
        in_specs=[IN_SMEM] + [IN_VMEM] * (len(operands) - 1),
        out_specs=jax.tree.map(lambda _: IN_VMEM, out_shape),
        compiler_params=params(8),
        cost_estimate=cost(2 * tall * width * columns * count, 2 * tall * columns),
        name="z_matmul",
    )(*operands)


def upper_blocks(n):
    return [(s, t) for s in range(n) for t in range(s, n)]


def strip_kernel(n_batch, n_col, place_ref, *refs):
    z_refs, (even_ref, odd_ref, strip) = refs[: 2 * n_batch], refs[2 * n_batch :]
    local_rows = z_refs[0].shape[0]
    rows = local_rows * n_batch
    for v in range(2):
        zf = [z[...].astype(f32) for z in z_refs[v::2]]
        mean = sum(jnp.sum(z, axis=0, keepdims=True) for z in zf) / rows
        rounded = jnp.concatenate([(z - mean).astype(bf16) for z in zf], axis=0)
        at = 0
        for s in range(n_batch):
            product = lax.dot_general(
                rounded[s * local_rows : (s + 1) * local_rows],
                rounded[s * local_rows :],
                (((1,), (1,)), ((), ())),
                preferred_element_type=f32,
            )
            strip[pl.ds(v * local_rows, local_rows), pl.ds(at, product.shape[1])] = product
            at += product.shape[1]
    part = 2 * local_rows // n_col
    for k in range(n_col):
        start = pl.multiple_of((place_ref[1] ^ k) * part, part)
        ref = odd_ref if k % 2 else even_ref
        ref[k // 2] = strip[pl.ds(start, part), :].astype(ref.dtype)


def strip_call(place, z_slots, n_col):
    n_batch = len(z_slots)
    local_rows, columns = z_slots[0][0].shape
    tall = 2 * local_rows
    wide = len(upper_blocks(n_batch)) * local_rows
    shape = (n_col // 2, tall // n_col, wide)
    operands = [place] + [z for slot in z_slots for z in slot]
    return pl.pallas_call(
        functools.partial(strip_kernel, n_batch, n_col),
        out_shape=(jax.ShapeDtypeStruct(shape, f32), jax.ShapeDtypeStruct(shape, bf16)),
        in_specs=[IN_SMEM] + [IN_VMEM] * (len(operands) - 1),
        out_specs=(IN_VMEM, IN_VMEM),
        scratch_shapes=[pltpu.VMEM((tall, wide), f32)],
        compiler_params=params(18),
        cost_estimate=cost(2 * tall * wide * columns, 2 * tall * columns * n_batch),
        name="kernel_strip",
    )(*operands)


def dz_kernel(n_batch, n_col, tile, constants, place_ref, own_ref, *refs):
    coef, hinge_coef, inv_coef, inv_share, hinge_share, diag_share, block_share = constants
    strip_refs = refs[:n_col]
    z_refs = refs[n_col : n_col + 2 * n_batch]
    dz_ref, share_ref, strips, full, centred = refs[n_col + 2 * n_batch :]
    local_rows, columns = z_refs[0].shape
    rows = local_rows * n_batch
    own = own_ref[...]
    block = lax.broadcasted_iota(jnp.int32, own.shape, 1) // local_rows
    on_diagonal = functools.reduce(
        jnp.logical_or, [block == i for i, (s, t) in enumerate(upper_blocks(n_batch)) if s == t]
    )
    own = own * own * jnp.where(on_diagonal, 1.0, 2.0)
    own = jnp.sum(jnp.sum(own, axis=0, keepdims=True), axis=1, keepdims=True)
    share_ref[...] = jnp.broadcast_to(block_share * own, share_ref.shape)
    part = 2 * local_rows // n_col
    for k in range(n_col):
        start = pl.multiple_of((place_ref[1] ^ k) * part, part)
        strips[pl.ds(start, part), :] = strip_refs[k][...].astype(f32)
    for v in range(2):
        for i, (s, t) in enumerate(upper_blocks(n_batch)):
            here, there = pl.ds(s * local_rows, local_rows), pl.ds(t * local_rows, local_rows)
            block = strips[pl.ds(v * local_rows, local_rows), pl.ds(i * local_rows, local_rows)]
            full[v, here, there] = block.astype(bf16)
            if s < t:
                full[v, there, here] = jnp.transpose(block).astype(bf16)

    for j in range(columns // tile):
        here = pl.ds(j * tile, tile)
        share = jnp.zeros((1, 1), f32)
        grads = []
        z_views = []
        for v in range(2):
            zf = jnp.concatenate([z[:, here].astype(f32) for z in z_refs[v::2]], axis=0)
            z_views.append(zf)
            zc = zf - jnp.sum(zf, axis=0, keepdims=True) / rows
            std = jnp.sqrt(jnp.sum(zc * zc, axis=0, keepdims=True) / (rows - 1) + eps_std)
            zcb = zc.astype(bf16)
            centred[2 * j + v] = zcb
            rounded = zcb.astype(f32)
            diag = jnp.sum(rounded * rounded, axis=0, keepdims=True)
            moved = jnp.dot(full[v], centred[2 * j + v], preferred_element_type=f32)
            pull = jnp.where(std < 1.0, hinge_coef, 0.0) / std
            summed = coef * (moved - rounded * diag) - zc * pull
            grads.append(summed - jnp.sum(summed, axis=0, keepdims=True) / rows)
            share += hinge_share * jnp.sum(jnp.maximum(1.0 - std, 0.0), axis=1, keepdims=True)
            share -= diag_share * jnp.sum(diag * diag, axis=1, keepdims=True)
        diff = z_views[0] - z_views[1]
        share += inv_share * jnp.sum(
            jnp.sum(diff * diff, axis=0, keepdims=True), axis=1, keepdims=True
        )
        share_ref[...] += jnp.broadcast_to(share, share_ref.shape)
        dz_ref[0, :, here] = (grads[0] + inv_coef * diff).astype(bf16)
        dz_ref[1, :, here] = (grads[1] - inv_coef * diff).astype(bf16)


def dz_call(place, own, strips, z_slots, constants):
    n_col, n_batch = len(strips), len(z_slots)
    local_rows, columns = z_slots[0][0].shape
    tall = 2 * local_rows
    rows = local_rows * n_batch
    tile = min(256, columns)
    operands = [place, own] + list(strips) + [z for slot in z_slots for z in slot]
    return pl.pallas_call(
        functools.partial(dz_kernel, n_batch, n_col, tile, constants),
        out_shape=(
            jax.ShapeDtypeStruct((2, rows, columns), bf16),
            jax.ShapeDtypeStruct((8, 128), f32),
        ),
        in_specs=[IN_SMEM] + [IN_VMEM] * (len(operands) - 1),
        out_specs=(IN_VMEM, IN_VMEM),
        scratch_shapes=[
            pltpu.VMEM((tall, strips[0].shape[1]), f32),
            pltpu.VMEM((2, rows, rows), bf16),
            pltpu.VMEM((2 * columns // tile, rows, tile), bf16),
        ],
        compiler_params=params(28),
        cost_estimate=cost(4 * rows * rows * columns, 8 * rows * columns),
        name="embedding_gradient",
    )(*operands)


EXTRA = 16


def share_rows(share, width, kind):
    high = share.astype(bf16).astype(f32)
    middle = (share - high).astype(bf16).astype(f32)
    low = share - high - middle
    row = lax.broadcasted_iota(jnp.int32, (EXTRA, width), 0)
    rows = jnp.where(row == 0, high, jnp.where(row == 1, middle, jnp.where(row == 2, low, 0.0)))
    return rows.astype(kind)


def share_of(rows):
    return rows[0:1].astype(f32) + rows[1:2].astype(f32) + rows[2:3].astype(f32)


def d_act_kernel(evens, odds, tall, width, place_ref, dz_ref, share_ref, w_ref, *refs):
    local_rows = tall // 2
    dz = jnp.concatenate([dz_ref[0, :local_rows], dz_ref[1, :local_rows]], axis=0)
    share = share_ref[0:1, 0:1]
    got, outs = (refs[0], refs[1:]) if evens else (None, refs)

    def product(k):
        return lax.dot_general(
            dz,
            weight_rows(place_ref, w_ref, k, width),
            (((1,), (1,)), ((), ())),
            preferred_element_type=f32,
        )

    for j, k in enumerate(evens):
        out = outs[j]
        out[:tall] = (product(k) + got[j, :tall].astype(f32)).astype(out.dtype)
        out[tall:] = share_rows(share + share_of(got[j, tall:])[:, 0:1], width, out.dtype)
    for j, k in enumerate(odds):
        outs[-1][j, :tall] = product(k).astype(bf16)
        outs[-1][j, tall:] = share_rows(share, width, bf16)


def d_act_call(place, dz, share, weight, n_batch, n_col, evens, got, odds):
    width = weight.shape[0] // n_col
    tall = 2 * dz.shape[1] // n_batch
    columns = weight.shape[1]
    long, count = tall + EXTRA, len(evens) + len(odds)
    operands = [place, dz, share, weight] + ([got] if evens else [])
    out_shape = tuple(jax.ShapeDtypeStruct((long, width), bf16 if k else f32) for k in evens)
    if odds:
        out_shape += (jax.ShapeDtypeStruct((len(odds), long, width), bf16),)
    return pl.pallas_call(
        functools.partial(d_act_kernel, tuple(evens), tuple(odds), tall, width),
        out_shape=out_shape,
        in_specs=[IN_SMEM] + [IN_VMEM] * (len(operands) - 1),
        out_specs=(IN_VMEM,) * len(out_shape),
        compiler_params=params(8),
        cost_estimate=cost(2 * tall * width * columns * count, 2 * count * width * tall),
        name="d_act_matmul",
    )(*operands)


def held_place(plane, c, block, n_col, n_batch):
    return (((n_col // n_batch) * plane + 2 * block) ^ (c - (c & 1))) >> 1


def pick_kernel(n_batch, n_col, local_rows, place_ref, *refs):
    half = n_col // 2
    pieces, outs = refs[:half], refs[half:]
    b, c = place_ref[0], place_ref[1]
    position = jnp.where((b & 1) == 0, b >> 1, n_batch - 1 - (b >> 1))
    i = 0
    for block in range(n_col // n_batch // 2):
        for d in range(1, n_batch):
            ahead = position + d
            ahead = jnp.where(ahead >= n_batch, ahead - n_batch, ahead)
            plane = jnp.where(2 * ahead < n_batch, 2 * ahead, 2 * (n_batch - ahead) - 1)
            chosen = held_place(plane, c, block, n_col, n_batch)
            for e in range(half):

                @pl.when(chosen == e)
                def _():
                    outs[i][...] = pieces[e][local_rows:]

            i += 1


def pick_call(place, pieces, n_batch, n_col):
    tall, width = pieces[0].shape
    count = n_col // n_batch // 2 * (n_batch - 1)
    out_shape = (jax.ShapeDtypeStruct((tall // 2, width), bf16),) * count
    return pl.pallas_call(
        functools.partial(pick_kernel, n_batch, n_col, tall // 2),
        out_shape=out_shape,
        in_specs=[IN_SMEM] + [IN_VMEM] * len(pieces),
        out_specs=(IN_VMEM,) * count,
        compiler_params=params(4),
        cost_estimate=cost(0, tall * width * count),
        name="pick_blocks",
    )(place, *pieces)


def weight_grad_kernel(n_batch, aliased, half, tile, which, place_ref, *refs):
    near = [refs[:half], refs[half : 2 * half]]
    blocks_ref, dz_ref = refs[2 * half : 2 * half + 2]
    out_ref, act, product, sems = refs[2 * half + 2 + aliased :]
    block, parity = which
    chosen = held_place(place_ref[0], place_ref[1], block, 2 * half, n_batch)
    out_row = 2 * block + ((place_ref[1] & 1) ^ parity)
    local_rows = near[0][0].shape[0] // 2
    rows = dz_ref.shape[1]
    for e in range(half):

        @pl.when(chosen == e)
        def _():
            act[pl.ds(0, local_rows)] = near[0][e][:local_rows]
            act[pl.ds(rows, local_rows)] = near[0][e][local_rows:]
            act[pl.ds(local_rows, rows - local_rows)] = near[1][e][...]

    act[rows + local_rows :] = blocks_ref[...]
    width = act.shape[1]
    copies = []
    for i in range(width // tile):
        total = None
        for v in range(2):
            part = lax.dot_general(
                act[pl.ds(v * rows, rows), pl.ds(i * tile, tile)],
                dz_ref[v],
                (((0,), (0,)), ((), ())),
                preferred_element_type=f32,
            )
            total = part if total is None else total + part
        product[pl.ds(i * tile, tile)] = total
        start = pl.multiple_of(out_row * width + i * tile, tile)
        copies.append(
            pltpu.make_async_copy(
                product.at[pl.ds(i * tile, tile)], out_ref.at[pl.ds(start, tile)], sems.at[i]
            )
        )
        copies[-1].start()
    for copy in copies:
        copy.wait()


def weight_grad_call(place, which, near, blocks, dz, features, before):
    half = len(near[0])
    width = near[0][0].shape[1]
    _, rows, columns = dz.shape
    tile = min(256, width)
    operands = [place] + [x for group in near for x in group] + [blocks, dz]
    specs = [IN_SMEM] + [IN_VMEM] * (len(operands) - 1)
    aliases = {}
    if before is not None:
        aliases = {len(operands): 0}
        operands.append(before)
        specs.append(ANYWHERE)
    return pl.pallas_call(
        functools.partial(
            weight_grad_kernel,
            rows // (near[0][0].shape[0] // 2),
            int(before is not None),
            half,
            tile,
            which,
        ),
        out_shape=jax.ShapeDtypeStruct((features, columns), f32),
        in_specs=specs,
        out_specs=ANYWHERE,
        scratch_shapes=[
            pltpu.VMEM((2 * rows, width), bf16),
            pltpu.VMEM((width, columns), f32),
            pltpu.SemaphoreType.DMA((width // tile,)),
        ],
        input_output_aliases=aliases,
        compiler_params=params(12),
        cost_estimate=cost(4 * rows * width * columns, 4 * width * columns),
        name="weight_gradient",
    )(*operands)


def link_pieces(x, n_col):
    pieces = {0: x}
    half = x.shape[0] // 2
    for k in sorted(range(2, n_col, 2), key=lambda k: (bin(k).count("1"), k)):
        low, high = k & -k, 1 << (k.bit_length() - 1)
        if low == high:
            pieces[k] = xor_send(x, "col", k)
        else:
            first = xor_send(pieces[k ^ low][:half], "col", low)
            second = xor_send(pieces[k ^ high][half:], "col", high)
            pieces[k] = jnp.concatenate([first, second])
    return pieces


def sibling_pieces(pieces, n_col):
    for k in range(0, n_col, 2):
        if k + 1 not in pieces:
            pieces[k + 1] = xor_send(pieces[k], "col", 1)
    return pieces


def finish_kernel(n_batch, rows, *refs):
    sums, (d_pre, normalised, gain, deviation) = refs[:n_batch], refs[n_batch : n_batch + 4]
    loss_ref, gain_ref, bias_ref, out_ref = refs[n_batch + 4 :]
    both = exchange_sum(x[...] for x in sums)
    bias_ref[...] = both[0:1] + both[1:2]
    gain_ref[...] = both[2:3] + both[3:4]
    loss_ref[...] = both[4:5, 0:128]
    for v in range(2):
        factor = gain[...] * deviation[v : v + 1]
        mean_b, mean_g = both[v : v + 1] / rows, both[2 + v : 3 + v] / rows
        out_ref[v] = factor * (d_pre[v] - mean_b - normalised[v] * mean_g)


def finish_call(sums, d_pre, normalised, gain, deviation, rows):
    _, local_rows, width = d_pre.shape
    operands = list(sums) + [d_pre, normalised, gain[None], deviation[:, 0]]
    out_shape = (
        jax.ShapeDtypeStruct((1, 128), f32),
        jax.ShapeDtypeStruct((1, width), f32),
        jax.ShapeDtypeStruct((1, width), f32),
        jax.ShapeDtypeStruct(d_pre.shape, f32),
    )
    return pl.pallas_call(
        functools.partial(finish_kernel, len(sums), rows),
        out_shape=out_shape,
        in_specs=[IN_VMEM] * len(operands),
        out_specs=(IN_VMEM,) * 4,
        compiler_params=params(4),
        cost_estimate=cost(0, 8 * d_pre.size),
        name="views_gradient",
    )(*operands)


def shards(views, norm_scale_gain, norm_shift_bias, weight):
    n_batch = lax.axis_size("batch")
    n_col = lax.axis_size("col")
    place = jnp.stack([lax.axis_index("batch"), lax.axis_index("col")]).astype(jnp.int32)
    views, norm_scale_gain, norm_shift_bias, weight, place = lax.optimization_barrier(
        (views, norm_scale_gain, norm_shift_bias, weight, place)
    )
    n_view, local_rows, width = views.shape
    features, columns = weight.shape
    E = columns * n_col
    rows = local_rows * n_batch
    tall = n_view * local_rows
    scale = rows * E / 128.0
    denom = float((rows - 1) ** 2 * E)
    evens = list(range(0, n_col, 2))
    odds = [k + 1 for k in evens]
    far = evens[1:]

    with jax.named_scope("weight_load"):
        held_weight, loaded = load_call(weight, (2 * n_view, width))
    with jax.named_scope("norm_stats"):
        hidden = views.astype(f32)
        stats = exchange(stats_call(views), "batch")
        stats[-1] = stats[-1] + loaded
        mean = exchange_sum(s[:n_view] for s in stats) / n_batch
        spread = exchange_sum(
            s[n_view:] + local_rows * jnp.square(s[:n_view] - mean) for s in stats
        )
        var = spread / rows
        inverse_deviation = (1.0 / jnp.sqrt(var + eps_norm))[:, None, :]
        normalised = (hidden - mean[:, None, :]) * inverse_deviation
        preactivation = norm_scale_gain * normalised + norm_shift_bias
        act = jax.nn.gelu(preactivation, approximate=True).astype(bf16)
    with jax.named_scope("act_gather"):
        own = act.reshape(tall, width)
        pieces = {0: own, 1: xor_send(own, "col", 1)}
        for k in far:
            pieces[k] = xor_send(own, "col", k)
        first, pieces[1] = lax.optimization_barrier((act[0], pieces[1]))
        others = [ring_send(first, "batch", d) for d in range(1, n_batch)]
        pieces = sibling_pieces(pieces, n_col)
    with jax.named_scope("z"):

        def z_part(source, ks, before, last=False):
            return z_call(
                place, ks, [source[k] for k in ks], held_weight, before, last, local_rows
            )

        z_own = z_part(pieces, far, z_part(pieces, [0, 1], None))
        z_own, others[-1] = lax.optimization_barrier((z_own, others[-1]))
        z_own0, z_own1 = z_part(pieces, [k + 1 for k in far], z_own, True)
        far_pieces = link_pieces(jnp.concatenate(others), n_col)
    with jax.named_scope("z_ring"):
        z_ring = [z_own1, ring_send(z_own1, "batch", 1)]
        reach = n_batch // 2
        back = [ring_send(z_own1, "batch", n_batch - 1)]
        z_ring[1], far_pieces[far[0]], back[0] = lax.optimization_barrier(
            (z_ring[1], far_pieces[far[0]], back[0])
        )
        z_ring.append(ring_send(z_ring[1], "batch", 1))
        for _ in range(reach + 2, n_batch):
            back.append(ring_send(back[-1], "batch", n_batch - 1))
    with jax.named_scope("z_far"):
        start = z_part(far_pieces, [0] + far[:-1], None)
        picked = list(pick_call(place, [pieces[k] for k in evens], n_batch, n_col))
        start, far_pieces[far[-1]], z_ring[2], picked = lax.optimization_barrier(
            (start, far_pieces[far[-1]], z_ring[2], picked)
        )
        far_pieces = sibling_pieces(far_pieces, n_col)
        for _ in range(3, reach + 1):
            z_ring.append(ring_send(z_ring[-1], "batch", 1))
        z_ring += back[::-1]
        z_far = z_part(far_pieces, odds[:-1] + far[-1:] + odds[-1:], start, True)
        slots = list(zip([z_own0] + list(z_far), z_ring))
    with jax.named_scope("kernel"):
        even_part, odd_part = strip_call(place, slots, n_col)
        blocks = [
            ring_send(x, "batch", 1 + i % (n_batch - 1)) for i, x in enumerate(picked)
        ]
        third = len(blocks) // 3
        odd_part, blocks[:third] = lax.optimization_barrier((odd_part, blocks[:third]))
        even_part = even_part + xor_send(odd_part, "col", 1).astype(f32)
        strip = even_part[0]
        for k in far:
            strip = strip + xor_send(even_part[k // 2].astype(bf16), "col", k).astype(f32)
        strip_b = strip.astype(bf16)
        strips = {0: strip_b}
        for k in far:
            strips[k] = xor_send(strip_b, "col", k)
        strips[far[0]], blocks[third : 2 * third] = lax.optimization_barrier(
            (strips[far[0]], blocks[third : 2 * third])
        )
        strips = sibling_pieces(strips, n_col)
    with jax.named_scope("dz"):
        constants = (
            4.0 * scale / denom,
            25.0 * scale / (2.0 * E * (rows - 1)),
            50.0 * scale / (rows * E),
            25.0 / (rows * E) / n_batch,
            25.0 / (2 * E) / n_batch,
            1.0 / denom / n_batch,
            1.0 / denom / n_batch,
        )
        dz, share = dz_call(place, strip, [strips[k] for k in range(n_col)], slots, constants)
        dz, blocks[2 * third :] = lax.optimization_barrier((dz, blocks[2 * third :]))
    with jax.named_scope("d_act"):
        crossing = [k for k in far if k & (k - 1)]
        others = [k for k in far if k not in crossing] + [0]

        def products(evens, got, odds):
            return d_act_call(place, dz, share, held_weight, n_batch, n_col, evens, got, odds)

        (away,) = products([], None, [k + 1 for k in crossing])
        *crossed, away = products(crossing, xor_send(away, "col", 1), [k + 1 for k in others])
        summed = products(others, xor_send(away, "col", 1), [])
        arrived = {
            k: xor_send(piece, "col", k) if k else piece
            for k, piece in zip(crossing + others, list(crossed) + list(summed))
        }
        d_act = arrived.pop(0)
        arrived = [arrived[k] for k in far]
    with jax.named_scope("grad_weight"):
        grad_weight = None
        for block in range(n_col // n_batch // 2):
            mine = jnp.concatenate(blocks[block * (n_batch - 1) : (block + 1) * (n_batch - 1)])
            other = xor_send(mine, "col", 1)
            for parity, ks, far_rows in ((0, evens, mine), (1, odds, other)):
                grad_weight = weight_grad_call(
                    place,
                    (block, parity),
                    [[group[k] for k in ks] for group in (pieces, far_pieces)],
                    far_rows,
                    dz,
                    features // n_batch,
                    grad_weight,
                )
    with jax.named_scope("norm_backward"):
        arrived, grad_weight = lax.optimization_barrier((arrived, grad_weight))
        share = exchange_sum(share_of(part[tall:]) for part in [d_act] + arrived)
        d_act = d_act[:tall]
        for part in arrived:
            d_act = d_act + part[:tall].astype(f32)
        d_pre = d_act.reshape(n_view, local_rows, width) * gelu_slope(preactivation)
        sums = jnp.concatenate(
            [
                jnp.sum(d_pre, axis=1),
                jnp.sum(d_pre * normalised, axis=1),
                jnp.broadcast_to(share, (2 * n_view, width)),
            ]
        )
        loss, grad_gain, grad_bias, views_gradient = finish_call(
            exchange(sums, "batch"), d_pre, normalised, norm_scale_gain, inverse_deviation, rows
        )
    return (loss[0, 0], grad_weight, grad_gain[0], grad_bias[0], views_gradient)


def solution(mesh):
    placed = (P(None, "batch", "col"), P("col"), P("col"), P(None, "col"))
    return jax.shard_map(
        shards,
        mesh=mesh,
        in_specs=placed,
        out_specs=(P(), P("batch", "col"), P("col"), P("col"), P(None, "batch", "col")),
        check_vma=False,
    )
```
